32 devices in a mesh: dp: 8 (over z, core), seq: 4 (over y, x).
Axes of the slice: x: 2, y: 2, z: 4, core: 2. Of those that a mesh axis runs over, the one named last changes fastest.
Arguments:
- inputs: bfloat16 [16, 1024, 512], P('dp', 'seq'), may hold values from -3 to 3
- segment_ids: int32 [16, 1024], P('dp', 'seq'), may hold values from 0 to 3, never falling along the last dimension, each value on 1 to 800 neighbouring positions
- cotangent: bfloat16 [16, 1024, 512], P('dp', 'seq'), may hold values from -6 to 6
- norm_gain: bfloat16 [4, 512], P(None, 'seq'), may hold values from 0.5 to 1.5
- norm_bias: bfloat16 [4, 512], P(None, 'seq'), may hold values from -1.5 to 1.5
- glu_weight: bfloat16 [512, 1024], P('seq'), may hold values from -0.25 to 0.25
- left_weight: bfloat16 [512, 2048], P('seq'), may hold values from -0.25 to 0.25
- conv_weight: bfloat16 [3, 512, 256], P(None, 'seq'), may hold values from -0.75 to 0.75
- mid_gain: bfloat16 [2048], P('seq'), may hold values from 0.5 to 1.5
- mid_bias: bfloat16 [2048], P('seq'), may hold values from -1.5 to 1.5
- depth_weight: bfloat16 [9, 2048], P(None, 'seq'), may hold values from -2 to 2
- point_weight: bfloat16 [2048, 512], P('seq'), may hold values from -0.125 to 0.125
- qkv_weight: bfloat16 [512, 1536], P('seq'), may hold values from -0.25 to 0.25
- out_weight: bfloat16 [512, 512], P('seq'), may hold values from -1 to 1
- ffn_in: bfloat16 [512, 2048], P('seq'), may hold values from -0.25 to 0.25
- ffn_out: bfloat16 [2048, 512], P('seq'), may hold values from -0.1875 to 0.1875
Outputs:
- output: float32 [16, 1024, 512], P('dp', 'seq')
- input_grad: float32 [16, 1024, 512], P('dp', 'seq')
- grad_norm_gain: float32 [4, 512], P(None, 'seq')
- grad_norm_bias: float32 [4, 512], P(None, 'seq')
- grad_glu_weight: float32 [512, 1024], P('seq')
- grad_left_weight: float32 [512, 2048], P('seq')
- grad_conv_weight: float32 [3, 512, 256], P(None, 'seq')
- grad_mid_gain: float32 [2048], P('seq')
- grad_mid_bias: float32 [2048], P('seq')
- grad_depth_weight: float32 [9, 2048], P(None, 'seq')
- grad_point_weight: float32 [2048, 512], P('seq')
- grad_qkv_weight: float32 [512, 1536], P('seq')
- grad_out_weight: float32 [512, 512], P('seq')
- grad_ffn_in: float32 [512, 2048], P('seq')
- grad_ffn_out: float32 [2048, 512], P('seq')
The draws below stay inside these ranges and needn't reach their ends.
Inputs may be any that keep to these rules, and one draw needn't show every extreme that they name: `segment_ids`: along each sequence of 1024 tokens the segment ids never fall and take every value from 0 to 3; each document has 1 to 800 tokens, and one document of every sequence has exactly 800.
All inputs are finite; a program needn't handle non-finite values.
Results may differ from the reference program's by a relative error of at most 0.02.
Values may be sent and summed in bfloat16 or wider, within the bound.
A program may use at most 192 MiB of HBM per device.

```python
import math
import jax
import jax.numpy as jnp
import numpy as np
from jax import lax

D = 512
FF = 2048
HEADS = 8
HEAD_DIM = 64
HALF = 256
LEN = 1024
DOCS = 4
DOC_MOST = 800
SEQS_ALL = 16


def shard_levels(rng, dims, cuts, least, high):
    def one(position, blocks):
        draws = jax.random.uniform(jax.random.fold_in(jax.random.fold_in(rng, 6), position), (blocks,), jnp.float32, least / len(cuts), high / len(cuts))
        return jnp.repeat(jnp.exp(draws), dims[position] // blocks).reshape((-1,) + (1,) * (len(dims) - position - 1))

    loudness = one(*cuts[0])
    for cut in cuts[1:]:
        loudness = loudness * one(*cut)
    return loudness


def split_up(count, total, reach, lean):
    loads = [(1 << 20) // math.isqrt(grade ** lean) + 1 for grade in range(2, count + 1)]
    rest, counts = total - reach - (count - 1), [1] * (count - 1)
    while rest > 0:
        movable = [i for i in range(count - 1) if counts[i] < reach]
        mass, remaining = sum([loads[i] for i in movable]), rest
        for i in movable:
            addition = min(reach - counts[i], max(1, remaining * loads[i] // mass), rest)
            counts[i] = counts[i] + addition
            rest = rest - addition
    return np.array([reach] + counts)


def uneven_parts(own_key, amount, total, reach, skew):
    if amount == 2:
        one = jax.random.randint(own_key, (), max(1, total - reach), min(reach, total - 1) + 1)
        return jnp.stack([one, total - one])
    tallies = jnp.asarray(split_up(amount, total, reach, skew), jnp.int32)
    couples = (amount - 1) // 2
    giver, sink = tallies[1:1 + 2 * couples:2], tallies[2:2 + 2 * couples:2]
    slack = jnp.minimum(giver - 1, reach - sink)
    moved = jax.random.randint(jax.random.fold_in(own_key, 1), (couples,), 0, 1 << 20) % (slack + 1)
    tallies = tallies.at[1:1 + 2 * couples:2].set(giver - moved).at[2:2 + 2 * couples:2].set(sink + moved)
    return tallies[jax.random.permutation(jax.random.fold_in(own_key, 2), amount)]


def noise(own_key, dims, width, most, split=(), held_as=jnp.bfloat16):
    values = jax.random.normal(own_key, dims, jnp.float32) * width
    if len(split) > 0:
        values = shard_levels(own_key, dims, split, -0.22, 0.18) * values
    return jnp.clip(values, min=-most, max=most).astype(held_as)


def setup_inputs(seed: int = 0) -> dict:
    splits = jax.random.split(jax.random.key(seed), 17)
    return {
        "inputs": noise(splits[0], (SEQS_ALL, LEN, D), 0.5, 3.0, ((0, 8), (1, 4))),
        "segment_ids": jax.vmap(lambda own: jnp.searchsorted(jnp.cumsum(uneven_parts(own, DOCS, LEN, DOC_MOST, 2)), jnp.arange(LEN), side="right"))(jax.random.split(splits[1], SEQS_ALL)).reshape((SEQS_ALL, LEN)).astype(jnp.int32),
        "cotangent": noise(splits[2], (SEQS_ALL, LEN, D), 1.0, 6.0, ((0, 8), (1, 4))),
        "norm_gain": jnp.clip(1.0 + 0.1 * jax.random.normal(splits[3], (4, D), jnp.float32), 0.5, 1.5).astype(jnp.bfloat16),
        "norm_bias": noise(splits[4], (4, D), 0.3, 1.5, ((1, 4),)),
        "glu_weight": noise(splits[5], (D, 2 * D), D ** -0.5, 0.25, ((0, 4),)),
        "left_weight": noise(splits[6], (D, FF), D ** -0.5, 0.25, ((0, 4),)),
        "conv_weight": noise(splits[7], (3, D, HALF), (D // 8) ** -0.5, 0.75, ((1, 4),)),
        "mid_gain": jnp.clip(1.0 + 0.1 * jax.random.normal(splits[8], (FF,), jnp.float32), 0.5, 1.5).astype(jnp.bfloat16),
        "mid_bias": noise(splits[9], (FF,), 0.3, 1.5, ((0, 4),)),
        "depth_weight": noise(splits[10], (9, FF), 9 ** -0.5, 2.0, ((1, 4),)),
        "point_weight": noise(splits[11], (FF, D), FF ** -0.5, 0.125, ((0, 4),)),
        "qkv_weight": noise(splits[12], (D, 3 * D), D ** -0.5, 0.25, ((0, 4),)),
        "out_weight": noise(splits[13], (D, D), (D // 16) ** -0.5, 1.0, ((0, 4),)),
        "ffn_in": noise(splits[14], (D, FF), D ** -0.5, 0.25, ((0, 4),)),
        "ffn_out": noise(splits[15], (FF, D), (FF // 2) ** -0.5, 0.1875, ((0, 4),)),
    }


@jax.custom_vjp
def low(v):
    return lax.optimization_barrier(v.astype(jnp.bfloat16)).astype(jnp.float32)

@jax.custom_vjp
def low_back(v):
    return v

def low_keep(v):
    return (low(v), None)

def low_pass(kept, grad):
    return (grad,)

def back_keep(v):
    return (v, None)

def back_low(kept, grad):
    return (low(grad),)
low.defvjp(low_keep, low_pass)
low_back.defvjp(back_keep, back_low)
EPS = 1e-06
NEG = -1000000000.0
PRECISION = lax.Precision.HIGHEST

def layer_norm(values, gain, bias):
    average = lax.optimization_barrier(jnp.mean(values, axis=-1, keepdims=True))
    centred = values - average
    spread = lax.optimization_barrier(jnp.mean(centred * centred, axis=-1, keepdims=True))
    return centred * lax.rsqrt(spread + EPS) * gain + bias

def product(left, right):
    return jnp.matmul(left, right, precision=PRECISION)

def shifted(values, offset, radius):
    length = values.shape[1]
    padded = jnp.pad(values, ((0, 0), (radius, radius), (0, 0)))
    return padded[:, radius + offset:radius + offset + length]

def tap_masks(segments, radius):
    length = segments.shape[1]
    padded = jnp.pad(segments, ((0, 0), (radius, radius)), constant_values=-1)
    return [(padded[:, radius + offset:radius + offset + length] == segments).astype(jnp.float32)[..., None] for offset in range(-radius, radius + 1)]

def one_sequence(entry):
    queries, keys_in, values_in, segments = entry
    length = queries.shape[0]
    heads_query = queries.reshape(length, HEADS, HEAD_DIM)
    heads_key = keys_in.reshape(length, HEADS, HEAD_DIM)
    heads_value = values_in.reshape(length, HEADS, HEAD_DIM)
    scores = low_back(jnp.einsum('qhd,khd->hqk', heads_query, heads_key, precision=PRECISION))
    same_doc = (segments[:, None] == segments[None, :])[None]
    scores = jnp.where(same_doc, scores, NEG)
    probabilities = jax.nn.softmax(scores, axis=-1)
    context = jnp.einsum('hqk,khd->qhd', low(probabilities), heads_value, precision=PRECISION)
    return low(low_back(context.reshape(length, D)))

def forward(stream, segments, params):
    norm_gain, norm_bias, glu_weight, left_weight, conv_weight, mid_gain, mid_bias, depth_weight, point_weight, qkv_weight, out_weight, ffn_in, ffn_out = params
    act1 = low(layer_norm(stream, norm_gain[0], norm_bias[0]))
    pre1 = low_back(product(act1, glu_weight))
    glu_out = pre1[..., :D] * jax.nn.sigmoid(pre1[..., D:])
    stream1 = stream + glu_out
    act2 = low(layer_norm(stream1, norm_gain[1], norm_bias[1]))
    left_act = jax.nn.gelu(low_back(product(act2, left_weight)))
    narrow = tap_masks(segments, 1)
    right_pre = sum((product(shifted(act2, offset, 1) * narrow[offset + 1], conv_weight[offset + 1]) for offset in (-1, 0, 1)))
    right_act = jax.nn.gelu(low_back(right_pre))
    middle = left_act + jnp.pad(right_act, ((0, 0), (0, 0), (0, FF - HALF)))
    act3 = low(layer_norm(middle, mid_gain, mid_bias))
    wide = tap_masks(segments, 4)
    separable = sum((shifted(act3, offset, 4) * wide[offset + 4] * depth_weight[offset + 4] for offset in range(-4, 5)))
    sep_hidden = low(low_back(separable))
    sep_out = low_back(product(sep_hidden, point_weight))
    stream2 = stream1 + sep_out
    act4 = low(layer_norm(stream2, norm_gain[2], norm_bias[2]))
    qkv = low_back(product(act4, qkv_weight))
    queries = low(qkv[..., :D] * (1.0 / math.sqrt(HEAD_DIM)))
    keys_in = low(qkv[..., D:2 * D])
    values_in = low(qkv[..., 2 * D:])
    context = lax.map(jax.checkpoint(one_sequence), (queries, keys_in, values_in, segments))
    attn_out = low_back(product(context, out_weight))
    stream3 = stream2 + attn_out
    act5 = low(layer_norm(stream3, norm_gain[3], norm_bias[3]))
    hidden = low(jax.nn.gelu(low_back(product(act5, ffn_in))))
    feed_out = low_back(product(hidden, ffn_out))
    return stream3 + feed_out

def reference(inputs, segment_ids, cotangent, norm_gain, norm_bias, glu_weight, left_weight, conv_weight, mid_gain, mid_bias, depth_weight, point_weight, qkv_weight, out_weight, ffn_in, ffn_out):
    params = tuple((weight.astype(jnp.float32) for weight in (norm_gain, norm_bias, glu_weight, left_weight, conv_weight, mid_gain, mid_bias, depth_weight, point_weight, qkv_weight, out_weight, ffn_in, ffn_out)))
    per_group = 4 if SEQS_ALL % 4 == 0 else 1
    groups = SEQS_ALL // per_group
    streams = inputs.astype(jnp.float32).reshape(groups, per_group, LEN, D)
    cotangents = cotangent.astype(jnp.float32).reshape(groups, per_group, LEN, D)
    segments_all = segment_ids.reshape(groups, per_group, LEN)

    def step(grads, entry):
        values_in, segments, cot_in = entry
        result, pullback = jax.vjp(lambda xs, ps: forward(xs, segments, ps), values_in, params)
        d_values, d_params = pullback(cot_in)
        grads = jax.tree.map(lambda totals, term: totals + term, grads, d_params)
        return (grads, (result, d_values))
    start = jax.tree.map(jnp.zeros_like, params)
    grads, (outputs, input_grads) = lax.scan(step, start, (streams, segments_all, cotangents))
    return (outputs.reshape(SEQS_ALL, LEN, D), input_grads.reshape(SEQS_ALL, LEN, D), grads[0], grads[1], grads[2], grads[3], grads[4], grads[5], grads[6], grads[7], grads[8], grads[9], grads[10], grads[11], grads[12])
```

```python
import math

import jax
import jax.numpy as jnp
from jax import lax
from jax.experimental import pallas as pl
from jax.experimental.pallas import tpu as pltpu
from jax.sharding import PartitionSpec as P

HEADS = 8
EPS = 1e-06
NEG = -1000000000.0
MESH = pl.DeviceIdType.MESH
F32 = jnp.float32
BF16 = jnp.bfloat16

GLU, CONV, LEFT, POINT, QKV, OUT, FIN, FOUT = range(8)
WEIGHTS = 8
SMALL = 8


def mm(a, b):
    return lax.dot_general(a, b, (((1,), (0,)), ((), ())), preferred_element_type=F32)


def mm_t(a, b):
    return lax.dot_general(a, b, (((1,), (1,)), ((), ())), preferred_element_type=F32)


def mm_tn(a, b):
    return lax.dot_general(a, b, (((0,), (0,)), ((), ())), preferred_element_type=F32)


def normed(v):
    centred = v - jnp.mean(v, axis=-1, keepdims=True)
    r = lax.rsqrt(jnp.mean(centred * centred, axis=-1, keepdims=True) + EPS)
    return centred * r, r


def gelu_both(v):
    c = math.sqrt(2.0 / math.pi)
    sq = v * v
    t = jnp.tanh(v * (c + (c * 0.044715) * sq))
    half = 0.5 * t + 0.5
    value = v * half
    slope = half + (0.5 * v) * (1.0 - t * t) * (c + (3.0 * c * 0.044715) * sq)
    return value, slope


def sigmoid(v):
    return 0.5 * jnp.tanh(0.5 * v) + 0.5


class Buffers:
    pass


class Plan:
    def __init__(self, dp, n, seqs, span, width, hidden, half):
        self.n, self.Z = n, dp // 2
        self.S, self.span = seqs, span
        self.D, self.FF, self.HALF = width, hidden, half
        self.LEN = span * n
        self.T = self.LEN // 2
        self.PH = n // 2
        self.B = math.isqrt(n)
        self.A = n // self.B
        assert self.A == self.B and n == 2 * seqs and dp % 2 == 0
        self.sw = max(span, 128)
        self.sr = self.sw // span
        dn = width // n
        self.nw = max(dn, 128)
        self.nr = self.nw // dn
        self.FFn = hidden // n
        self.dims = [
            (width, 2 * width),
            (width, half),
            (width, hidden),
            (hidden, width),
            (width, 3 * width),
            (width, width),
            (width, hidden),
            (hidden, width),
        ]

    def whole(self, w):
        k, cols = self.dims[w]
        return (3, k, cols) if w == CONV else (k, cols)

    def kr(self, w):
        return self.dims[w][0] // self.n

    def hr(self, w):
        return self.kr(w) // 2

    def piece(self, w, rows):
        cols = self.dims[w][1]
        return (3, rows, cols) if w == CONV else (rows, cols)

    def buffers(self, take):
        T, D, FF, H, n = self.T, self.D, self.FF, self.HALF, self.n
        r = Buffers()

        def vm(shape, dtype):
            return take(pltpu.VMEM(shape, dtype))

        def sem(*shape):
            return take(pltpu.SemaphoreType.DMA(shape))

        every = range(WEIGHTS)
        parts = [(self.piece(w, self.hr(w)), BF16) for w in every] + [((8, FF), F32)]
        r.w = [vm(self.whole(w), BF16) for w in every]
        r.g8 = vm((16, FF), F32)
        r.g = r.w + [r.g8]
        r.r = [vm(self.piece(w, n * self.hr(w)), BF16) for w in every] + [vm((8, FF), F32)]
        r.p = [vm((n - 1,) + shape, dtype) for shape, dtype in parts]
        if self.Z > 1:
            r.u = [vm(shape, dtype) for shape, dtype in parts]
            r.d = [vm(shape, dtype) for shape, dtype in parts]
        r.segbuf = vm((n, 8, self.sw), F32)
        r.segrow = vm((8, self.LEN), F32)
        r.segq = vm((8, T), F32)
        r.segcol = vm((self.LEN + 16, 128), F32)
        r.segloc = vm((T + 16, 128), F32)
        r.mext = vm((4, T + 16, 128), F32)
        r.smallbuf = vm((n, 32, self.FFn), BF16)
        r.nrm = vm((8, D), F32)
        r.midp = vm((16, FF), F32)
        r.xin = vm((T, D), BF16)
        r.cot = vm((T, D), BF16)
        r.a1 = vm((T, D), BF16)
        r.sg = vm((T, 2 * D), BF16)
        r.y1 = vm((T, D), F32)
        r.a2 = vm((T, D), BF16)
        r.pext = vm((3, T + 16, H), F32)
        r.dgl = vm((T, FF), BF16)
        r.dgr = vm((T, H), BF16)
        r.nm = vm((T, FF), BF16)
        r.rm = vm((T, 1), F32)
        r.big = vm((T + 16, FF), F32)
        r.sep = vm((T, FF), BF16)
        r.y2 = vm((T, D), F32)
        r.a4 = vm((T, D), BF16)
        r.qb = vm((T, D), BF16)
        r.kvb = vm((2, T, 2 * D), BF16)
        r.lse = vm((T, 128), F32)
        r.lset = vm((HEADS // 2, 8, T), F32)
        r.ctx = vm((T, D), BF16)
        r.y3 = vm((T, D), F32)
        r.a5 = vm((T, D), BF16)
        r.hid = vm((T, FF), BF16)
        r.dg = vm((T, FF), BF16)
        r.osend = vm((T, D), BF16)
        r.gs = vm((T, D), F32)
        r.dkvr = vm((T, 2 * D), BF16)
        r.acc = vm((2, self.LEN, 128), F32)
        r.tr = vm((D, T), BF16)
        r.col = vm((T, 128), F32)
        wides = (H, FF, FF, H)
        r.es = [vm((8, wide), F32) for wide in wides]
        r.er = [vm((8, wide), F32) for wide in wides]
        r.s_loc = sem(WEIGHTS)
        r.s_as = sem(WEIGHTS, self.B)
        r.s_ar = sem(WEIGHTS, self.B)
        r.s_bs = sem(WEIGHTS, self.A * self.B)
        r.s_br = sem(WEIGHTS, self.A * self.B)
        r.s_ds = sem(WEIGHTS, n)
        r.s_dr = sem(WEIGHTS, n)
        r.s_rs = sem(WEIGHTS + 1, n)
        r.s_rr = sem(WEIGHTS + 1, n)
        r.s_ps = sem(WEIGHTS + 1, n)
        r.s_pr = sem(WEIGHTS + 1, n)
        r.s_zs = sem(WEIGHTS + 1, 2)
        r.s_zr = sem(WEIGHTS + 1, 2)
        r.s_fs = sem(WEIGHTS + 1)
        r.s_fr = sem(WEIGHTS + 1)
        r.s_fl = sem(WEIGHTS + 1)
        r.s_xs = sem(4, self.S)
        r.s_xr = sem(4, max(self.PH, self.S))
        r.s_gs = sem(2 * self.S)
        r.s_gr = sem(n)
        r.s_ms = sem(n)
        r.s_mr = sem(n)
        r.s_es = sem(4)
        r.s_er = sem(4)
        r.s_ks = sem(2)
        r.s_kr = sem(2)
        return r


INPUTS = 4 + WEIGHTS
OUTPUTS = 2 + WEIGHTS + 1


def kernel(plan, *refs):
    ins, outs = refs[:INPUTS], refs[INPUTS : INPUTS + OUTPUTS]
    scratch = iter(refs[INPUTS + OUTPUTS :])
    r = plan.buffers(lambda shape: next(scratch))
    r.x, r.seg, r.ct, r.small = ins[:4]
    r.h = ins[4:]
    r.o_out, r.o_ig = outs[:2]
    r.o = outs[2:]
    n, Z, S, span = plan.n, plan.Z, plan.S, plan.span
    T, D, FF, H, PH = plan.T, plan.D, plan.FF, plan.HALF, plan.PH
    A, B = plan.A, plan.B
    dp, q = lax.axis_index("dp"), lax.axis_index("seq")
    z, c = dp // 2, dp % 2
    oc = 1 - c

    def aligned(v, m=16):
        return pl.multiple_of(v, m)

    def dev(core, chip, plane=None):
        return ((z if plane is None else plane) * 2 + core, chip)

    sibling = dev(oc, q)

    def remote(src, dst, ss, rs, to):
        return pltpu.make_async_remote_copy(
            src_ref=src, dst_ref=dst, send_sem=ss, recv_sem=rs, device_id=to, device_id_type=MESH
        )

    barrier = pltpu.get_barrier_semaphore()
    for core in range(2):

        def greet(t, _, core=core):
            chip = lax.rem(q + t, n)
            to = (z * 2 + (c + core) % 2, chip)
            pl.semaphore_signal(barrier, inc=1, device_id=to, device_id_type=MESH)
            return 0

        lax.fori_loop(1 - core, n, greet, 0)
    if Z > 1:

        @pl.when(z > 0)
        def _():
            pl.semaphore_signal(barrier, inc=1, device_id=dev(c, q, z - 1), device_id_type=MESH)

        @pl.when(z < Z - 1)
        def _():
            pl.semaphore_signal(barrier, inc=1, device_id=dev(c, q, z + 1), device_id_type=MESH)

    pl.semaphore_wait(barrier, 2 * n - 1 + (z + Z - 1) // Z + (2 * Z - 2 - z) // Z)

    def vrows(ref, w, row0, rows):
        ds = pl.ds(aligned(row0), rows)
        return ref.at[:, ds] if w == CONV else ref.at[ds]

    def wblock(w, shard, half):
        return vrows(r.w[w], w, shard * plan.kr(w) + half * plan.hr(w), plan.hr(w))

    def qof(core, f, g):
        f, g = f % B, g % B
        return core * (f * B + g) + (1 - core) * (g * B + f)

    b_, a_ = q % B, q // B
    f_, g_ = c * a_ + oc * b_, c * b_ + oc * a_
    of_, og_ = oc * a_ + c * b_, oc * b_ + c * a_

    def copy_a(w, t):
        src = vrows(r.h[w], w, c * plan.hr(w), plan.hr(w))
        return remote(
            src,
            wblock(w, q, c),
            r.s_as.at[w, t],
            r.s_ar.at[w, t],
            dev(c, qof(c, f_ + t, g_)),
        )

    def arrived_a(w, t):
        blk = wblock(w, qof(c, f_ + B - t, g_), c)
        return remote(blk, blk, r.s_as.at[w, t], r.s_ar.at[w, t], sibling)

    def copy_b(w, u, t):
        shard = qof(c, f_ + B - t, g_)
        if t == 0:
            src = vrows(r.h[w], w, c * plan.hr(w), plan.hr(w))
        else:
            src = wblock(w, shard, c)
        i = u * B + t
        return remote(
            src,
            wblock(w, shard, c),
            r.s_bs.at[w, i],
            r.s_br.at[w, i],
            dev(c, qof(c, f_, g_ + u)),
        )

    def arrived_b(w, u, t):
        blk = wblock(w, qof(c, f_ + B - t, g_ + B - u), c)
        i = u * B + t
        return remote(blk, blk, r.s_bs.at[w, i], r.s_br.at[w, i], sibling)

    def copy_d(w, u, t):
        blk = wblock(w, qof(c, f_ + B - t, g_ + B - u), c)
        i = u * B + t
        return remote(blk, blk, r.s_ds.at[w, i], r.s_dr.at[w, i], sibling)

    def arrived_d(w, u, t):
        blk = wblock(w, qof(oc, of_ + B - t, og_ + B - u), oc)
        i = u * B + t
        return remote(blk, blk, r.s_ds.at[w, i], r.s_dr.at[w, i], sibling)

    def local_shard(w):
        dst = vrows(r.w[w], w, q * plan.kr(w), plan.kr(w))
        return pltpu.make_async_copy(r.h[w], dst, r.s_loc.at[w])

    def g0(w):
        local_shard(w).start()
        for t in range(1, B):
            copy_a(w, t).start()
        for u in range(1, A):
            copy_b(w, u, 0).start()

    def g1(w):
        for t in range(1, B):
            arrived_a(w, t).wait_recv()
            for u in range(1, A):
                copy_b(w, u, t).start()
            copy_d(w, 0, t).start()

    def g2(w):
        for u in range(1, A):
            for t in range(B):
                arrived_b(w, u, t).wait_recv()
                copy_d(w, u, t).start()

    def g3(w):
        local_shard(w).wait()
        for u in range(A):
            for t in range(B):
                if (u, t) != (0, 0):
                    arrived_d(w, u, t).wait_recv()

    def gather_sent(w):
        for t in range(1, B):
            copy_a(w, t).wait_send()
        for u in range(A):
            for t in range(B):
                if u > 0:
                    copy_b(w, u, t).wait_send()
                if (u, t) != (0, 0):
                    copy_d(w, u, t).wait_send()

    def token_rows(ref, slot):
        return ref.at[pl.ds(aligned(slot * span), span)]

    def tokens_in(src, dst, k):
        for j in range(S):
            chip, core, slot = S * c + j, q // PH, q % PH
            here = jnp.logical_and(chip == q, core == c)
            there = token_rows(dst, slot)

            @pl.when(here)
            def _():
                pltpu.make_async_copy(src.at[j], there, r.s_xr.at[k, slot]).start()

            @pl.when(jnp.logical_not(here))
            def _():
                remote(
                    src.at[j], there, r.s_xs.at[k, j], r.s_xr.at[k, slot], dev(core, chip)
                ).start()

    def tokens_in_done(dst, k):
        for slot in range(PH):
            blk = token_rows(dst, slot)
            pltpu.make_async_copy(blk, blk, r.s_xr.at[k, slot]).wait()

    def tokens_in_sent(src, dst, k):
        for j in range(S):
            chip, core, slot = S * c + j, q // PH, q % PH
            here = jnp.logical_and(chip == q, core == c)

            @pl.when(jnp.logical_not(here))
            def _():
                remote(
                    src.at[j],
                    token_rows(dst, slot),
                    r.s_xs.at[k, j],
                    r.s_xr.at[k, slot],
                    dev(core, chip),
                ).wait_send()

    def tokens_out(src, dst, k):
        for p in range(PH):
            chip, core, slot = c * PH + p, q // S, q % S
            here = jnp.logical_and(chip == q, core == c)

            @pl.when(here)
            def _():
                pltpu.make_async_copy(token_rows(src, p), dst.at[slot], r.s_xr.at[k, slot]).start()

            @pl.when(jnp.logical_not(here))
            def _():
                remote(
                    token_rows(src, p),
                    dst.at[slot],
                    r.s_xs.at[k, p],
                    r.s_xr.at[k, slot],
                    dev(core, chip),
                ).start()

    def tokens_out_done(src, dst, k):
        for j in range(S):
            pltpu.make_async_copy(dst.at[j], dst.at[j], r.s_xr.at[k, j]).wait()
        for p in range(PH):
            chip, core, slot = c * PH + p, q // S, q % S
            here = jnp.logical_and(chip == q, core == c)

            @pl.when(jnp.logical_not(here))
            def _():
                remote(
                    token_rows(src, p),
                    dst.at[slot],
                    r.s_xs.at[k, p],
                    r.s_xr.at[k, slot],
                    dev(core, chip),
                ).wait_send()

    def seg_send():
        for j in range(S):
            for core in range(2):
                chip = S * c + j
                here = jnp.logical_and(chip == q, c == core)
                i = 2 * j + core

                @pl.when(here)
                def _():
                    pltpu.make_async_copy(r.seg.at[j], r.segbuf.at[q], r.s_gr.at[q]).start()

                @pl.when(jnp.logical_not(here))
                def _():
                    remote(
                        r.seg.at[j],
                        r.segbuf.at[q],
                        r.s_gs.at[i],
                        r.s_gr.at[q],
                        dev(core, chip),
                    ).start()

    def seg_sent():
        for j in range(S):
            for core in range(2):
                chip = S * c + j
                here = jnp.logical_and(chip == q, c == core)

                @pl.when(jnp.logical_not(here))
                def _():
                    remote(
                        r.seg.at[j],
                        r.segbuf.at[q],
                        r.s_gs.at[2 * j + core],
                        r.s_gr.at[q],
                        dev(core, chip),
                    ).wait_send()

    def small_copy(t):
        return remote(
            r.small,
            r.smallbuf.at[q],
            r.s_ms.at[t],
            r.s_mr.at[t],
            dev(c, (q + t) % n),
        )

    def small_arrived(t):
        blk = r.smallbuf.at[(q + n - t) % n]
        return remote(blk, blk, r.s_ms.at[t], r.s_mr.at[t], sibling)

    def edge_copy(i):
        return remote(r.es[i], r.er[i], r.s_es.at[i], r.s_er.at[i], sibling)

    def edge_send(i, last, first):
        r.es[i][...] = jnp.where(c == 0, last, first)
        edge_copy(i).start()

    def edge_take(i):
        edge_copy(i).wait()
        got = r.er[i][...]
        return jnp.where(c == 1, got, 0.0), jnp.where(c == 0, got, 0.0)

    def gpiece(w, shard, half):
        if w == SMALL:
            return r.g8.at[pl.ds(pl.multiple_of(half * 8, 8), 8)]
        return vrows(r.w[w], w, shard * plan.kr(w) + half * plan.hr(w), plan.hr(w))

    def rpiece(w, shard):
        if w == SMALL:
            return r.r[SMALL]
        return vrows(r.r[w], w, shard * plan.hr(w), plan.hr(w))

    def copy_r(w, s):
        return remote(
            gpiece(w, s, oc), rpiece(w, s), r.s_rs.at[w, s], r.s_rr.at[w, s], sibling
        )

    def copy_p(w, t):
        chip = lax.rem(q + t, n)
        return remote(
            gpiece(w, chip, c),
            r.p[w].at[t - 1],
            r.s_ps.at[w, t],
            r.s_pr.at[w, t],
            dev(c, chip),
        )

    def shards(w):
        return 1 if w == SMALL else n

    def red0(w):
        for s in range(shards(w)):
            copy_r(w, s).start()

    def add_core(w, s):
        copy_r(w, s).wait_recv()
        mine = gpiece(w, s, c)
        total = mine[...].astype(F32) + rpiece(w, s)[...].astype(F32)
        mine[...] = total.astype(mine.dtype)

    def red1(w):
        if w == SMALL:
            add_core(w, 0)

        def one(t, _):
            if w != SMALL:
                add_core(w, lax.rem(q + t, n))
            copy_p(w, t).start()
            return 0

        lax.fori_loop(1, n, one, 0)
        if w != SMALL:
            add_core(w, q)

    def red2(w):
        buf = r.p[w]
        mine = gpiece(w, q, c)
        total = mine[...].astype(F32)
        for t in range(1, n):
            copy_p(w, t).wait_recv()
            total = total + buf[t - 1].astype(F32)
        buf[0] = total.astype(buf.dtype)

    def copy_z(w, way):
        plane = z + 1 if way == 0 else z - 1
        return remote(
            r.p[w].at[1 + way],
            (r.u, r.d)[way][w],
            r.s_zs.at[w, way],
            r.s_zr.at[w, way],
            dev(c, q, plane),
        )

    def red_hop(w, h):
        buf = r.p[w]

        @pl.when(z == h)
        def _():
            if h == 0:
                buf[1] = buf[0]
            else:
                copy_z(w, 0).wait_recv()
                buf[1] = (buf[0].astype(F32) + r.u[w][...].astype(F32)).astype(buf.dtype)
            if h < Z - 1:
                copy_z(w, 0).start()

        @pl.when(z == Z - 1 - h)
        def _():
            if h == 0:
                buf[2] = buf[0]
            else:
                copy_z(w, 1).wait_recv()
                if h < Z - 1:
                    buf[2] = (buf[0].astype(F32) + r.d[w][...].astype(F32)).astype(buf.dtype)
            if h < Z - 1:
                copy_z(w, 1).start()

    def final_rows(w, ref):
        if w == SMALL:
            return ref.at[pl.ds(pl.multiple_of(c * 8, 8), 8)]
        return vrows(ref, w, c * plan.hr(w), plan.hr(w))

    def final_local(w):
        return pltpu.make_async_copy(
            r.p[w].at[0], final_rows(w, r.o[w]), r.s_fl.at[w]
        )

    def final_remote(w):
        return remote(
            r.p[w].at[0],
            final_rows(w, r.o[w]),
            r.s_fs.at[w],
            r.s_fr.at[w],
            sibling,
        )

    def red_final(w):
        buf = r.p[w]
        if Z > 1:

            @pl.when(z == Z - 1)
            def _():
                buf[0] = buf[1]

            @pl.when(z < Z - 1)
            def _():
                buf[0] = (buf[1].astype(F32) + r.d[w][...].astype(F32)).astype(buf.dtype)

        final_local(w).start()
        final_remote(w).start()

    def red_end(w):
        final_local(w).wait()
        final_remote(w).wait()
        for s in range(shards(w)):
            copy_r(w, s).wait_send()
        for t in range(1, n):
            copy_p(w, t).wait_send()
        if Z > 1:

            @pl.when(z < Z - 1)
            def _():
                copy_z(w, 0).wait_send()

            @pl.when(z > 0)
            def _():
                copy_z(w, 1).wait_send()

    active = []

    def reduce_start(w):
        red0(w)
        steps = [red1, red2]
        if Z > 1:
            steps += [lambda k, h=h: red_hop(k, h) for h in range(Z)]
        steps.append(red_final)
        active.append((w, steps))

    def pump(times=1):
        for _ in range(times):
            for w, steps in active:
                if steps:
                    steps.pop(0)(w)

    def loop(count, body):
        def step(i, _):
            body(i)
            return 0

        lax.fori_loop(0, count, step, 0)

    RB = 256
    NB = T // RB

    def rows_of(i, size=RB, base=0):
        return pl.ds(pl.multiple_of(i * size + base, 8 if base else size), size)

    small_local = pltpu.make_async_copy(r.small, r.smallbuf.at[q], r.s_mr.at[0])
    small_local.start()
    for t in range(1, n):
        small_copy(t).start()
    seg_send()
    tokens_in(r.x, r.xin, 0)
    g0(GLU)
    g0(CONV)
    r.g8[...] = jnp.zeros((16, FF), F32)

    for s in range(n):
        blk = r.segbuf.at[s]
        pltpu.make_async_copy(blk, blk, r.s_gr.at[s]).wait()
    for grp in range(n // plan.sr):
        got = r.segbuf[grp * plan.sr]
        for k in range(1, plan.sr):
            got = got + r.segbuf[grp * plan.sr + k]
        r.segrow[:, grp * plan.sw : (grp + 1) * plan.sw] = got
    r.segq[...] = r.segrow[:, pl.ds(pl.multiple_of(c * T, 128), T)]
    r.segcol[0:8] = jnp.full((8, 128), -1.0, F32)
    r.segcol[plan.LEN + 8 : plan.LEN + 16] = jnp.full((8, 128), -1.0, F32)
    for k in range(plan.LEN // 128):
        row = r.segrow[0:1, k * 128 : (k + 1) * 128]
        r.segcol[8 + k * 128 : 8 + (k + 1) * 128] = jnp.broadcast_to(row, (128, 128)).T
    r.segloc[...] = r.segcol[pl.ds(pl.multiple_of(c * T, 8), T + 16)]
    for o in range(1, 5):
        same = r.segloc[0 : T + 8] == r.segloc[o : T + 8 + o]
        r.mext[o - 1, 0 : T + 8] = jnp.where(same, 1.0, 0.0)

    def mask(o, start, rows):
        if o > 0:
            return r.mext[o - 1, 8 + start : 8 + start + rows]
        return r.mext[-o - 1, 8 + start + o : 8 + start + o + rows]

    small_local.wait()
    for t in range(1, n):
        small_arrived(t).wait_recv()
    for grp in range(n // plan.nr):
        got = r.smallbuf[grp * plan.nr].astype(F32)[0:8, 0 : plan.nw]
        for k in range(1, plan.nr):
            got = got + r.smallbuf[grp * plan.nr + k].astype(F32)[0:8, 0 : plan.nw]
        r.nrm[:, grp * plan.nw : (grp + 1) * plan.nw] = got
    for s in range(n):
        r.midp[:, s * plan.FFn : (s + 1) * plan.FFn] = r.smallbuf[s].astype(F32)[8:24]

    def ln_out(k, v):
        unit, _ = normed(v)
        return (unit * r.nrm[k : k + 1] + r.nrm[4 + k : 5 + k]).astype(BF16)

    def ln_back(k, e, v):
        unit, rs = normed(v)
        eg = e * r.nrm[k : k + 1]
        m1 = jnp.mean(eg, axis=-1, keepdims=True)
        m2 = jnp.mean(eg * unit, axis=-1, keepdims=True)
        cols = slice(k * D, (k + 1) * D)
        r.g8[11:12, cols] += jnp.sum(e * unit, axis=0, keepdims=True)
        r.g8[12:13, cols] += jnp.sum(e, axis=0, keepdims=True)
        return rs * (eg - m1 - unit * m2)

    g1(GLU)
    g0(LEFT)
    g2(GLU)
    g1(CONV)
    tokens_in_done(r.xin, 0)
    g3(GLU)

    def glu(i):
        rows = rows_of(i)
        x = r.xin[rows].astype(F32)
        a1 = ln_out(0, x)
        r.a1[rows] = a1
        value = mm(a1, r.w[GLU][:, 0:D])
        gate = sigmoid(mm(a1, r.w[GLU][:, D : 2 * D]))
        r.sg[rows, 0:D] = gate.astype(BF16)
        r.sg[rows, D : 2 * D] = (value * gate * (1.0 - gate)).astype(BF16)
        y1 = x + value * gate
        r.y1[rows] = y1
        r.a2[rows] = ln_out(1, y1)

    loop(NB, glu)
    g0(POINT)
    g2(CONV)
    g1(LEFT)
    g3(CONV)

    def conv(i):
        a2 = r.a2[rows_of(i)]
        for o in range(3):
            r.pext[o, rows_of(i, RB, 8)] = mm(a2, r.w[CONV][o])

    loop(NB, conv)
    edge_send(0, r.pext[0, T : T + 8], r.pext[2, 8:16])
    g0(QKV)
    g2(LEFT)
    g1(POINT)
    top, bottom = edge_take(0)
    r.pext[0, 0:8] = top
    r.pext[2, T + 8 : T + 16] = bottom
    for k in range(T // 128):
        lo = k * 128
        before = mask(-1, lo, 128)
        after = mask(1, lo, 128)
        pre = (
            r.pext[0, lo + 7 : lo + 135] * jnp.concatenate([before] * (H // 128), axis=1)
            + r.pext[1, lo + 8 : lo + 136]
            + r.pext[2, lo + 9 : lo + 137] * jnp.concatenate([after] * (H // 128), axis=1)
        )
        value, slope = gelu_both(pre)
        r.pext[1, lo + 8 : lo + 136] = value
        r.dgr[lo : lo + 128] = slope.astype(BF16)
    g3(LEFT)

    CH = 512
    RM = 128

    def left(i):
        rows, erows = rows_of(i, RM), rows_of(i, RM, 8)
        a2 = r.a2[rows]
        for k in range(FF // CH):
            value, slope = gelu_both(mm(a2, r.w[LEFT][:, k * CH : (k + 1) * CH]))
            r.dgl[rows, k * CH : (k + 1) * CH] = slope.astype(BF16)
            r.big[erows, k * CH : (k + 1) * CH] = value
        r.big[erows, 0:H] += r.pext[1, erows]
        unit, rs = normed(r.big[erows])
        r.nm[rows] = unit.astype(BF16)
        r.rm[rows] = rs
        r.big[erows] = (unit * r.midp[0:1] + r.midp[1:2]).astype(BF16).astype(F32)

    loop(T // RM, left)
    edge_send(1, r.big[T : T + 8], r.big[8:16])
    g0(OUT)
    g2(POINT)
    g1(QKV)
    top, bottom = edge_take(1)
    r.big[0:8] = top
    r.big[T + 8 : T + 16] = bottom

    RC = 64

    def depthwise(j):
        cols = pl.ds(pl.multiple_of(j * 128, 128), 128)
        for k in range(T // RC):
            lo = k * RC
            total = r.big[lo + 8 : lo + 8 + RC, cols] * r.midp[6:7, cols]
            for o in (-4, -3, -2, -1, 1, 2, 3, 4):
                cells = r.big[lo + 8 + o : lo + 8 + o + RC, cols]
                total = total + cells * mask(o, lo, RC) * r.midp[6 + o : 7 + o, cols]
            r.sep[lo : lo + RC, cols] = total.astype(BF16)

    loop(FF // 128, depthwise)
    g0(FIN)
    g2(QKV)
    g1(OUT)
    g3(POINT)

    def point(i):
        rows = rows_of(i)
        y2 = r.y1[rows] + mm(r.sep[rows], r.w[POINT][...])
        r.y2[rows] = y2
        r.a4[rows] = ln_out(2, y2)

    loop(NB, point)
    g0(FOUT)
    g2(OUT)
    g1(FIN)
    g3(QKV)
    scale = 1.0 / math.sqrt(D // HEADS)

    def qkv(i):
        rows = rows_of(i)
        a4 = r.a4[rows]
        r.qb[rows] = (mm(a4, r.w[QKV][:, 0:D]) * scale).astype(BF16)
        r.kvb[c, rows, 0:D] = mm(a4, r.w[QKV][:, D : 2 * D]).astype(BF16)
        r.kvb[c, rows, D : 2 * D] = mm(a4, r.w[QKV][:, 2 * D : 3 * D]).astype(BF16)

    loop(NB, qkv)

    def kv_copy():
        blk = r.kvb.at[c]
        return remote(blk, blk, r.s_ks.at[0], r.s_kr.at[0], sibling)

    kv_copy().start()
    tokens_in(r.ct, r.cot, 1)
    lane = lax.broadcasted_iota(jnp.int32, (1, 128), 1)
    heads_lanes = [lane < 64, lane >= 64]
    g2(FIN)
    g1(FOUT)
    kv_copy().wait()

    def pair_cols(j, base=0):
        return pl.ds(pl.multiple_of(j * 128 + base, 128), 128)

    def one_head(q2, part, mine, key_row):
        def scores(keys, segs):
            raw = mm_t(q2, keys)
            same = jnp.concatenate([mine] * (T // 128), axis=1) == segs
            return jnp.where(same, raw, NEG)

        s0 = scores(part[0], key_row[:, 0:T])
        s1 = scores(part[1], key_row[:, T : 2 * T])
        most = jnp.maximum(
            jnp.max(s0, axis=-1, keepdims=True), jnp.max(s1, axis=-1, keepdims=True)
        )
        e0, e1 = jnp.exp(s0 - most), jnp.exp(s1 - most)
        total = jnp.sum(e0, axis=-1, keepdims=True) + jnp.sum(e1, axis=-1, keepdims=True)
        got = mm(e0.astype(BF16), part[2]) + mm(e1.astype(BF16), part[3])
        return got / total, most + jnp.log(total)

    def attend(j):
        cols, vcols = pair_cols(j), pair_cols(j, D)
        part = [r.kvb[0, :, cols], r.kvb[1, :, cols], r.kvb[0, :, vcols], r.kvb[1, :, vcols]]
        key_row = r.segrow[0:1]
        for k in range(T // RB):
            rows = slice(k * RB, (k + 1) * RB)
            q2 = r.qb[rows, cols]
            mine = r.segloc[8 + k * RB : 8 + (k + 1) * RB]
            got = []
            for e in range(2):
                context, lse = one_head(
                    jnp.where(heads_lanes[e], q2, jnp.zeros_like(q2)), part, mine, key_row
                )
                got.append(context)
                r.lse[rows] = jnp.where(lane == 2 * j + e, lse, r.lse[rows])
            r.ctx[rows, cols] = jnp.where(heads_lanes[0], got[0], got[1]).astype(BF16)

    r.lse[...] = jnp.zeros((T, 128), F32)
    loop(HEADS // 2, attend)
    turned = r.lse[...].T
    for j in range(HEADS // 2):
        r.lset[j, 0:2] = turned[2 * j : 2 * j + 2]
    g2(FOUT)
    g3(OUT)

    def out(i):
        rows = rows_of(i)
        y3 = r.y2[rows] + mm(r.ctx[rows], r.w[OUT][...])
        r.y3[rows] = y3
        r.a5[rows] = ln_out(3, y3)

    loop(NB, out)
    g3(FIN)

    def ffn_in(i):
        rows = rows_of(i)
        a5 = r.a5[rows]
        for k in range(FF // CH):
            value, slope = gelu_both(mm(a5, r.w[FIN][:, k * CH : (k + 1) * CH]))
            r.hid[rows, k * CH : (k + 1) * CH] = value.astype(BF16)
            r.dg[rows, k * CH : (k + 1) * CH] = slope.astype(BF16)

    loop(NB, ffn_in)
    g3(FOUT)

    def ffn_out(i):
        rows = rows_of(i)
        r.osend[rows] = (r.y3[rows] + mm(r.hid[rows], r.w[FOUT][...])).astype(BF16)

    loop(NB, ffn_out)
    tokens_out(r.osend, r.o_out, 2)
    for w in range(WEIGHTS):
        gather_sent(w)

    tokens_in_done(r.cot, 1)

    def ffn_back(i):
        rows = rows_of(i)
        f4 = r.cot[rows]
        for k in range(FF // CH):
            cols = slice(k * CH, (k + 1) * CH)
            up = mm_t(f4, r.w[FOUT][cols])
            r.dg[rows, cols] = (up * r.dg[rows, cols].astype(F32)).astype(BF16)
        e = mm_t(r.dg[rows], r.w[FIN][...])
        r.gs[rows] = f4.astype(F32) + ln_back(3, e, r.y3[rows])

    loop(NB, ffn_back)
    GC = 256

    def grad_outer(k):
        cols = rows_of(k, GC)
        r.w[FOUT][cols] = mm_tn(r.hid[:, cols], r.cot[...]).astype(BF16)

    loop(FF // GC, grad_outer)
    reduce_start(FOUT)
    r.tr[...] = r.a5[...].T

    def grad_inner(k):
        cols = rows_of(k, GC)
        r.w[FIN][:, cols] = mm(r.tr[...], r.dg[:, cols]).astype(BF16)

    loop(FF // GC, grad_inner)
    reduce_start(FIN)
    pump()

    def out_back(i):
        rows = rows_of(i)
        f3 = r.gs[rows].astype(BF16)
        r.a5[rows] = f3
        r.hid[rows, 3 * D : 4 * D] = mm_t(f3, r.w[OUT][...]).astype(BF16)

    loop(NB, out_back)
    r.w[OUT][...] = mm_tn(r.ctx[...], r.a5[...]).astype(BF16)
    reduce_start(OUT)
    pump()

    QB = 256

    def attend_back(j):
        cols, vcols = pair_cols(j), pair_cols(j, D)
        for k in range(T // QB):
            rows = slice(k * QB, (k + 1) * QB)
            q2 = r.qb[rows, cols]
            d2 = r.hid[rows, pair_cols(j, 3 * D)]
            dq = jnp.zeros((QB, 128), F32)
            for e in range(2):
                qe = jnp.where(heads_lanes[e], q2, jnp.zeros_like(q2))
                de = jnp.where(heads_lanes[e], d2, jnp.zeros_like(d2))
                lse = r.lset[j, e : e + 1, rows]
                probs, dprobs = [], []
                for kk in range(2):
                    keys = r.kvb[kk, :, cols]
                    values = r.kvb[kk, :, vcols]
                    segs = r.segcol[8 + kk * T : 8 + (kk + 1) * T]
                    same = jnp.concatenate([segs] * (QB // 128), axis=1) == r.segq[0:1, rows]
                    probs.append(jnp.where(same, jnp.exp(mm_t(keys, qe) - lse), 0.0))
                    dprobs.append(mm_t(values, de))
                delta = jnp.sum(probs[0] * dprobs[0], axis=0, keepdims=True) + jnp.sum(
                    probs[1] * dprobs[1], axis=0, keepdims=True
                )
                for kk in range(2):
                    keys = r.kvb[kk, :, cols]
                    ds = (probs[kk] * (dprobs[kk] - delta)).astype(BF16)
                    span_k = slice(kk * T, (kk + 1) * T)
                    dk = mm(ds, qe)
                    dv = mm(probs[kk].astype(BF16), de)
                    if k == 0 and e == 0:
                        r.acc[0, span_k] = dk
                        r.acc[1, span_k] = dv
                    else:
                        r.acc[0, span_k] += dk
                        r.acc[1, span_k] += dv
                    ke = jnp.where(heads_lanes[e], keys, jnp.zeros_like(keys))
                    dq = dq + mm_tn(ds, ke)
            r.hid[rows, cols] = (dq * scale).astype(BF16)
        own = pl.ds(pl.multiple_of(c * T, T), T)
        other = pl.ds(pl.multiple_of(oc * T, T), T)
        r.big[0:T, cols] = r.acc[0, own]
        r.big[0:T, vcols] = r.acc[1, own]
        r.dg[:, cols] = r.acc[0, other].astype(BF16)
        r.dg[:, vcols] = r.acc[1, other].astype(BF16)

    for half in range(2):
        lax.fori_loop(half * 2, half * 2 + 2, lambda j, _: (attend_back(j), 0)[1], 0)
        pump(2)

    def dkv_copy():
        return remote(
            r.dg.at[:, pl.ds(0, 2 * D)], r.dkvr, r.s_ks.at[1], r.s_kr.at[1], sibling
        )

    dkv_copy().start()
    pump()
    dkv_copy().wait()

    def qkv_back(i):
        rows = rows_of(i)
        total = r.big[rows, 0 : 2 * D] + r.dkvr[rows].astype(F32)
        r.hid[rows, D : 3 * D] = total.astype(BF16)
        e = mm_t(r.hid[rows, 0 : 3 * D], r.w[QKV][...])
        r.gs[rows] += ln_back(2, e, r.y2[rows])

    loop(NB, qkv_back)
    r.tr[...] = r.a4[...].T

    def grad_qkv(k):
        cols = rows_of(k, GC)
        r.w[QKV][:, cols] = mm(r.tr[...], r.hid[:, cols]).astype(BF16)

    loop(3 * D // GC, grad_qkv)
    reduce_start(QKV)
    pump()

    def point_back(i):
        rows = rows_of(i)
        f2 = r.gs[rows].astype(BF16)
        r.a4[rows] = f2
        for k in range(FF // CH):
            cols = slice(k * CH, (k + 1) * CH)
            d = mm_t(f2, r.w[POINT][cols])
            r.big[rows_of(i, RB, 8), cols] = d.astype(BF16).astype(F32)

    loop(NB, point_back)
    edge_send(2, r.big[T : T + 8], r.big[8:16])

    def grad_point(k):
        cols = rows_of(k, GC)
        r.w[POINT][cols] = mm_tn(r.sep[:, cols], r.a4[...]).astype(BF16)

    loop(FF // GC, grad_point)
    reduce_start(POINT)
    pump()
    top, bottom = edge_take(2)
    r.big[0:8] = top
    r.big[T + 8 : T + 16] = bottom

    def depth_back(j):
        cols = pl.ds(pl.multiple_of(j * 128, 128), 128)
        gain, shift = r.midp[0:1, cols], r.midp[1:2, cols]
        sums = [jnp.zeros((8, 128), F32) for _ in range(9)]
        for k in range(T // RC):
            lo = k * RC
            a3 = r.nm[lo : lo + RC, cols].astype(F32) * gain + shift
            total = jnp.zeros((RC, 128), F32)
            for o in range(-4, 5):
                moved = r.big[lo + 8 - o : lo + 8 - o + RC, cols]
                if o:
                    moved = moved * mask(-o, lo, RC)
                total = total + moved * r.midp[6 + o : 7 + o, cols]
                part = moved * a3
                for b in range(RC // 8):
                    sums[o + 4] = sums[o + 4] + part[b * 8 : (b + 1) * 8]
            r.col[lo : lo + RC] = total
        for o in range(9):
            r.g8[2 + o : 3 + o, cols] = jnp.sum(sums[o], axis=0, keepdims=True)
        r.big[8 : T + 8, cols] = r.col[...]

    loop(FF // 128, depth_back)
    pump()

    def mid_back(i):
        rows, erows = rows_of(i, RM), rows_of(i, RM, 8)
        e = r.big[erows]
        unit = r.nm[rows].astype(F32)
        eg = e * r.midp[0:1]
        m1 = jnp.mean(eg, axis=-1, keepdims=True)
        m2 = jnp.mean(eg * unit, axis=-1, keepdims=True)
        r.g8[0:1] += jnp.sum(e * unit, axis=0, keepdims=True)
        r.g8[1:2] += jnp.sum(e, axis=0, keepdims=True)
        dmid = r.rm[rows] * (eg - m1 - unit * m2)
        r.dgl[rows] = (dmid * r.dgl[rows].astype(F32)).astype(BF16)
        right = dmid[:, 0:H] * r.dgr[rows].astype(F32)
        r.pext[0, erows] = right.astype(BF16).astype(F32)

    loop(T // RM, mid_back)
    edge_send(3, r.pext[0, T : T + 8], r.pext[0, 8:16])
    pump()
    top, bottom = edge_take(3)
    r.pext[0, 0:8] = top
    r.pext[0, T + 8 : T + 16] = bottom
    for k in range(T // 128):
        lo = k * 128
        for o in (-1, 0, 1):
            moved = r.pext[0, lo + 8 - o : lo + 136 - o]
            if o:
                moved = moved * jnp.concatenate([mask(-o, lo, 128)] * (H // 128), axis=1)
            r.hid[lo : lo + 128, (o + 1) * H : (o + 2) * H] = moved.astype(BF16)

    def branch_back(i):
        rows = rows_of(i)
        e = mm_t(r.dgl[rows], r.w[LEFT][...])
        for o in range(3):
            e = e + mm_t(r.hid[rows, o * H : (o + 1) * H], r.w[CONV][o])
        r.gs[rows] += ln_back(1, e, r.y1[rows])

    loop(NB, branch_back)
    r.tr[...] = r.a2[...].T

    def grad_left(k):
        cols = rows_of(k, GC)
        r.w[LEFT][:, cols] = mm(r.tr[...], r.dgl[:, cols]).astype(BF16)

    loop(FF // GC, grad_left)
    reduce_start(LEFT)
    for o in range(3):
        r.w[CONV][o] = mm(r.tr[...], r.hid[:, o * H : (o + 1) * H]).astype(BF16)
    reduce_start(CONV)
    pump()

    def glu_back(i):
        rows = rows_of(i)
        g = r.gs[rows]
        r.sg[rows, 0:D] = (g * r.sg[rows, 0:D].astype(F32)).astype(BF16)
        r.sg[rows, D : 2 * D] = (g * r.sg[rows, D : 2 * D].astype(F32)).astype(BF16)
        e = mm_t(r.sg[rows], r.w[GLU][...])
        total = g + ln_back(0, e, r.xin[rows].astype(F32))
        r.a5[rows] = total.astype(BF16)

    loop(NB, glu_back)
    tokens_out(r.a5, r.o_ig, 3)
    r.tr[...] = r.a1[...].T

    def grad_glu(k):
        cols = rows_of(k, GC)
        r.w[GLU][:, cols] = mm(r.tr[...], r.sg[:, cols]).astype(BF16)

    loop(2 * D // GC, grad_glu)
    reduce_start(GLU)
    reduce_start(SMALL)
    while any(steps for _, steps in active):
        pump()

    for w in range(WEIGHTS + 1):
        red_end(w)
    tokens_out_done(r.osend, r.o_out, 2)
    tokens_out_done(r.a5, r.o_ig, 3)
    tokens_in_sent(r.x, r.xin, 0)
    tokens_in_sent(r.ct, r.cot, 1)
    seg_sent()
    for t in range(1, n):
        small_copy(t).wait_send()


def local(
    inputs,
    segment_ids,
    cotangent,
    norm_gain,
    norm_bias,
    glu_weight,
    left_weight,
    conv_weight,
    mid_gain,
    mid_bias,
    depth_weight,
    point_weight,
    qkv_weight,
    out_weight,
    ffn_in,
    ffn_out,
):
    seqs, span, width = inputs.shape
    n = lax.axis_size("seq")
    plan = Plan(
        lax.axis_size("dp"), n, seqs, span, width, ffn_in.shape[1], conv_weight.shape[2]
    )
    q = lax.axis_index("seq")

    def placed(piece, repeats):
        if repeats == 1:
            return piece
        size = piece.shape[-1]
        tiled = jnp.tile(piece, (1,) * (piece.ndim - 1) + (repeats,))
        at = lax.broadcasted_iota(jnp.int32, tiled.shape, tiled.ndim - 1) // size
        return jnp.where(at == q % repeats, tiled, jnp.zeros_like(tiled))

    segs = placed(segment_ids.astype(F32), plan.sr)
    segs = jnp.broadcast_to(segs[:, None, :], (seqs, 8, plan.sw))
    norms = placed(jnp.concatenate([norm_gain, norm_bias], 0), plan.nr)
    norms = jnp.pad(norms, ((0, 0), (0, plan.FFn - plan.nw)))
    small = jnp.concatenate([norms, mid_gain[None], mid_bias[None], depth_weight], 0)
    small = jnp.pad(small, ((0, 32 - small.shape[0]), (0, 0)))
    weights = [None] * WEIGHTS
    weights[GLU], weights[CONV], weights[LEFT] = glu_weight, conv_weight, left_weight
    weights[POINT], weights[QKV], weights[OUT] = point_weight, qkv_weight, out_weight
    weights[FIN], weights[FOUT] = ffn_in, ffn_out

    shapes = []
    plan.buffers(shapes.append)
    out_shape = [jax.ShapeDtypeStruct(inputs.shape, BF16)] * 2
    out_shape += [jax.ShapeDtypeStruct(w.shape, BF16) for w in weights]
    out_shape += [jax.ShapeDtypeStruct((16, plan.FF), F32)]
    hbm = pl.BlockSpec(memory_space=pl.ANY)
    got = pl.pallas_call(
        lambda *refs: kernel(plan, *refs),
        out_shape=out_shape,
        in_specs=[hbm] * INPUTS,
        out_specs=[hbm] * OUTPUTS,
        scratch_shapes=shapes,
        compiler_params=pltpu.CompilerParams(
            collective_id=0, has_side_effects=True, vmem_limit_bytes=64 << 20
        ),
        name="cell",
    )(inputs, segs, cotangent, small, *weights)
    output, input_grad = got[0].astype(F32), got[1].astype(F32)
    grads = [g.astype(F32) for g in got[2 : 2 + WEIGHTS]]
    rest = got[2 + WEIGHTS]
    mids = lax.dynamic_slice_in_dim(rest[0:11], q * plan.FFn, plan.FFn, 1)
    dn = width // n
    g_gain = lax.dynamic_slice_in_dim(rest[11].reshape(4, width), q * dn, dn, 1)
    g_bias = lax.dynamic_slice_in_dim(rest[12].reshape(4, width), q * dn, dn, 1)
    return (
        output,
        input_grad,
        g_gain,
        g_bias,
        grads[GLU],
        grads[LEFT],
        grads[CONV],
        mids[0],
        mids[1],
        mids[2:11],
        grads[POINT],
        grads[QKV],
        grads[OUT],
        grads[FIN],
        grads[FOUT],
    )


def solution(mesh):
    in_specs = (
        P("dp", "seq", None),
        P("dp", "seq"),
        P("dp", "seq", None),
        P(None, "seq"),
        P(None, "seq"),
        P("seq", None),
        P("seq", None),
        P(None, "seq", None),
        P("seq"),
        P("seq"),
        P(None, "seq"),
        P("seq", None),
        P("seq", None),
        P("seq", None),
        P("seq", None),
        P("seq", None),
    )
    out_specs = (
        P("dp", "seq", None),
        P("dp", "seq", None),
        P(None, "seq"),
        P(None, "seq"),
        P("seq", None),
        P("seq", None),
        P(None, "seq", None),
        P("seq"),
        P("seq"),
        P(None, "seq"),
        P("seq", None),
        P("seq", None),
        P("seq", None),
        P("seq", None),
        P("seq", None),
    )
    return jax.shard_map(local, mesh=mesh, in_specs=in_specs, out_specs=out_specs, check_vma=False)
```

```python
import math

import jax
import jax.numpy as jnp
from jax import lax
from jax.experimental import pallas as pl
from jax.experimental.pallas import tpu as pltpu
from jax.sharding import PartitionSpec as P

HEADS = 8
EPS = 1e-06
NEG = -1000000000.0
MESH = pl.DeviceIdType.MESH
F32 = jnp.float32
BF16 = jnp.bfloat16

GLU, CONV, LEFT, POINT, QKV, OUT, FIN, FOUT = range(8)
WEIGHTS = 8
(U_GLU0, U_GLU1, U_CONV, U_LEFT0, U_LEFT1, U_POINT0, U_POINT1, U_QKV, U_OUT, U_FIN, U_FOUT, SMALL) = range(12)
UNITS = 12
UNIT_WEIGHT = (GLU, GLU, CONV, LEFT, LEFT, POINT, POINT, QKV, OUT, FIN, FOUT, WEIGHTS)
UNIT_PART = (0, 1, None, 0, 1, 0, 1, None, None, None, None, None)


def mm(a, b):
    return lax.dot_general(a, b, (((1,), (0,)), ((), ())), preferred_element_type=F32)


def mm_t(a, b):
    return lax.dot_general(a, b, (((1,), (1,)), ((), ())), preferred_element_type=F32)


def mm_tn(a, b):
    return lax.dot_general(a, b, (((0,), (0,)), ((), ())), preferred_element_type=F32)


def normed(v):
    centred = v - jnp.mean(v, axis=-1, keepdims=True)
    r = lax.rsqrt(jnp.mean(centred * centred, axis=-1, keepdims=True) + EPS)
    return centred * r, r


def gelu_both(v):
    c = math.sqrt(2.0 / math.pi)
    sq = v * v
    t = jnp.tanh(v * (c + (c * 0.044715) * sq))
    half = 0.5 * t + 0.5
    value = v * half
    slope = half + (0.5 * v) * (1.0 - t * t) * (c + (3.0 * c * 0.044715) * sq)
    return value, slope


def sigmoid(v):
    return 0.5 * jnp.tanh(0.5 * v) + 0.5


class Buffers:
    pass


class Plan:
    def __init__(self, dp, n, seqs, span, width, hidden, half):
        self.n, self.Z = n, dp // 2
        self.S, self.span = seqs, span
        self.D, self.FF, self.HALF = width, hidden, half
        self.LEN = span * n
        self.T = self.LEN // 2
        self.PH = n // 2
        self.B = math.isqrt(n)
        self.A = n // self.B
        assert self.A == self.B and n == 2 * seqs and dp % 2 == 0
        self.sw = max(span, 128)
        self.sr = self.sw // span
        dn = width // n
        self.nw = max(dn, 128)
        self.nr = self.nw // dn
        self.FFn = hidden // n
        self.dims = [
            (width, 2 * width),
            (width, half),
            (width, hidden),
            (hidden, width),
            (width, 3 * width),
            (width, width),
            (width, hidden),
            (hidden, width),
        ]

    def whole(self, w):
        k, cols = self.dims[w]
        return (3, k, cols) if w == CONV else (k, cols)

    def kr(self, w):
        return self.dims[w][0] // self.n

    def hr(self, w):
        return self.kr(w) // 2

    def piece(self, w, rows):
        cols = self.dims[w][1]
        return (3, rows, cols) if w == CONV else (rows, cols)

    def buffers(self, take):
        T, D, FF, H, n = self.T, self.D, self.FF, self.HALF, self.n
        r = Buffers()

        def vm(shape, dtype):
            return take(pltpu.VMEM(shape, dtype))

        def sem(*shape):
            return take(pltpu.SemaphoreType.DMA(shape))

        every = range(WEIGHTS)
        parts = [(self.piece(w, self.hr(w)), BF16) for w in every] + [((8, FF), F32)]
        r.w = [vm(self.whole(w), BF16) for w in every]
        r.g8 = vm((16, FF), F32)
        r.r = [None] * WEIGHTS + [vm((8, FF), F32)]
        for w in (CONV, QKV, OUT, FIN, FOUT):
            r.r[w] = vm(self.piece(w, n * self.hr(w)), BF16)
        r.r[LEFT], r.r[POINT], r.r[GLU] = r.r[FIN], r.r[FOUT], r.r[QKV]
        r.p = [vm((n - 1,) + shape, dtype) for shape, dtype in parts]
        if self.Z > 1:
            r.u = [vm(shape, dtype) for shape, dtype in parts]
            r.d = [vm(shape, dtype) for shape, dtype in parts]
        r.segbuf = vm((n, 8, self.sw), F32)
        r.segrow = vm((8, self.LEN), F32)
        r.segq = vm((8, T), F32)
        r.segcol = vm((self.LEN + 16, 128), F32)
        r.segloc = vm((T + 16, 128), F32)
        r.mext = vm((4, T + 16, 128), F32)
        r.smallbuf = vm((n, 32, self.FFn), BF16)
        r.nrm = vm((8, D), F32)
        r.midp = vm((16, FF), F32)
        r.xin = vm((T, D), BF16)
        r.cot = vm((T, D), BF16)
        r.a1 = vm((T, D), BF16)
        r.sg = vm((T, 2 * D), BF16)
        r.y1 = vm((T, D), F32)
        r.a2 = vm((T, D), BF16)
        r.pext = vm((3, T + 16, H), F32)
        r.dgl = vm((T, FF), BF16)
        r.dgr = vm((T, H), BF16)
        r.nm = vm((T, FF), BF16)
        r.rm = vm((T, 1), F32)
        r.big = vm((T + 16, FF), F32)
        r.sep = vm((T, FF), BF16)
        r.y2 = vm((T, D), F32)
        r.a4 = vm((T, D), BF16)
        r.qb = vm((T, D), BF16)
        r.kvb = vm((2, T, 2 * D), BF16)
        r.lse = vm((T, 128), F32)
        r.lset = vm((HEADS // 2, 8, T), F32)
        r.ctx = vm((T, D), BF16)
        r.y3 = vm((T, D), F32)
        r.a5 = vm((T, D), BF16)
        r.hid = vm((T, FF), BF16)
        r.dg = vm((T, FF), BF16)
        r.osend = vm((T, D), BF16)
        r.gs = vm((T, D), F32)
        r.dkvr = vm((T, 2 * D), BF16)
        r.acc = vm((2, self.LEN, 128), F32)
        r.tr = vm((D, T), BF16)
        r.col = vm((T, 128), F32)
        wides = (H, FF, FF, H)
        r.es = [vm((8, wide), F32) for wide in wides]
        r.er = [vm((8, wide), F32) for wide in wides]
        r.s_loc = sem(WEIGHTS)
        r.s_as = sem(WEIGHTS, self.B)
        r.s_ar = sem(WEIGHTS, self.B)
        r.s_bs = sem(WEIGHTS, self.A * self.B)
        r.s_br = sem(WEIGHTS, self.A * self.B)
        r.s_ds = sem(WEIGHTS, n)
        r.s_dr = sem(WEIGHTS, n)
        r.s_rs = sem(UNITS, n)
        r.s_rr = sem(UNITS, n)
        r.s_ps = sem(UNITS, n)
        r.s_pr = sem(UNITS, n)
        r.s_zs = sem(UNITS, 2)
        r.s_zr = sem(UNITS, 2)
        r.s_fs = sem(UNITS)
        r.s_fr = sem(UNITS)
        r.s_fl = sem(UNITS)
        r.s_xs = sem(4, self.S)
        r.s_xr = sem(4, max(self.PH, self.S))
        r.s_gs = sem(2 * self.S)
        r.s_gr = sem(n)
        r.s_ms = sem(n)
        r.s_mr = sem(n)
        r.s_es = sem(4)
        r.s_er = sem(4)
        r.s_ks = sem(2)
        r.s_kr = sem(2)
        return r


INPUTS = 4 + WEIGHTS
OUTPUTS = 2 + WEIGHTS + 1


def kernel(plan, *refs):
    ins, outs = refs[:INPUTS], refs[INPUTS : INPUTS + OUTPUTS]
    scratch = iter(refs[INPUTS + OUTPUTS :])
    r = plan.buffers(lambda shape: next(scratch))
    r.x, r.seg, r.ct, r.small = ins[:4]
    r.h = ins[4:]
    r.o_out, r.o_ig = outs[:2]
    r.o = outs[2:]
    n, Z, S, span = plan.n, plan.Z, plan.S, plan.span
    T, D, FF, H, PH = plan.T, plan.D, plan.FF, plan.HALF, plan.PH
    A, B = plan.A, plan.B
    dp, q = lax.axis_index("dp"), lax.axis_index("seq")
    z, c = dp // 2, dp % 2
    oc = 1 - c

    def aligned(v, m=16):
        return pl.multiple_of(v, m)

    def dev(core, chip, plane=None):
        return ((z if plane is None else plane) * 2 + core, chip)

    sibling = dev(oc, q)

    def remote(src, dst, ss, rs, to):
        return pltpu.make_async_remote_copy(
            src_ref=src, dst_ref=dst, send_sem=ss, recv_sem=rs, device_id=to, device_id_type=MESH
        )

    barrier = pltpu.get_barrier_semaphore()
    for core in range(2):

        def greet(t, _, core=core):
            chip = lax.rem(q + t, n)
            to = (z * 2 + (c + core) % 2, chip)
            pl.semaphore_signal(barrier, inc=1, device_id=to, device_id_type=MESH)
            return 0

        lax.fori_loop(1 - core, n, greet, 0)
    if Z > 1:

        @pl.when(z > 0)
        def _():
            pl.semaphore_signal(barrier, inc=1, device_id=dev(c, q, z - 1), device_id_type=MESH)

        @pl.when(z < Z - 1)
        def _():
            pl.semaphore_signal(barrier, inc=1, device_id=dev(c, q, z + 1), device_id_type=MESH)

    pl.semaphore_wait(barrier, 2 * n - 1 + (z + Z - 1) // Z + (2 * Z - 2 - z) // Z)

    def vrows(ref, w, row0, rows):
        ds = pl.ds(aligned(row0), rows)
        return ref.at[:, ds] if w == CONV else ref.at[ds]

    def wblock(w, shard, half):
        return vrows(r.w[w], w, shard * plan.kr(w) + half * plan.hr(w), plan.hr(w))

    def qof(core, f, g):
        f, g = f % B, g % B
        return core * (f * B + g) + (1 - core) * (g * B + f)

    b_, a_ = q % B, q // B
    f_, g_ = c * a_ + oc * b_, c * b_ + oc * a_
    of_, og_ = oc * a_ + c * b_, oc * b_ + c * a_

    def copy_a(w, t):
        src = vrows(r.h[w], w, c * plan.hr(w), plan.hr(w))
        return remote(
            src,
            wblock(w, q, c),
            r.s_as.at[w, t],
            r.s_ar.at[w, t],
            dev(c, qof(c, f_ + t, g_)),
        )

    def arrived_a(w, t):
        blk = wblock(w, qof(c, f_ + B - t, g_), c)
        return remote(blk, blk, r.s_as.at[w, t], r.s_ar.at[w, t], sibling)

    def copy_b(w, u, t):
        shard = qof(c, f_ + B - t, g_)
        if t == 0:
            src = vrows(r.h[w], w, c * plan.hr(w), plan.hr(w))
        else:
            src = wblock(w, shard, c)
        i = u * B + t
        return remote(
            src,
            wblock(w, shard, c),
            r.s_bs.at[w, i],
            r.s_br.at[w, i],
            dev(c, qof(c, f_, g_ + u)),
        )

    def arrived_b(w, u, t):
        blk = wblock(w, qof(c, f_ + B - t, g_ + B - u), c)
        i = u * B + t
        return remote(blk, blk, r.s_bs.at[w, i], r.s_br.at[w, i], sibling)

    def copy_d(w, u, t):
        blk = wblock(w, qof(c, f_ + B - t, g_ + B - u), c)
        i = u * B + t
        return remote(blk, blk, r.s_ds.at[w, i], r.s_dr.at[w, i], sibling)

    def arrived_d(w, u, t):
        blk = wblock(w, qof(oc, of_ + B - t, og_ + B - u), oc)
        i = u * B + t
        return remote(blk, blk, r.s_ds.at[w, i], r.s_dr.at[w, i], sibling)

    def local_shard(w):
        dst = vrows(r.w[w], w, q * plan.kr(w), plan.kr(w))
        return pltpu.make_async_copy(r.h[w], dst, r.s_loc.at[w])

    def g0(w):
        local_shard(w).start()
        for t in range(1, B):
            copy_a(w, t).start()
        for u in range(1, A):
            copy_b(w, u, 0).start()

    def g1(w):
        for t in range(1, B):
            arrived_a(w, t).wait_recv()
            for u in range(1, A):
                copy_b(w, u, t).start()
            copy_d(w, 0, t).start()

    def g2(w):
        for u in range(1, A):
            for t in range(B):
                arrived_b(w, u, t).wait_recv()
                copy_d(w, u, t).start()

    def g3(w):
        local_shard(w).wait()
        for u in range(A):
            for t in range(B):
                if (u, t) != (0, 0):
                    arrived_d(w, u, t).wait_recv()

    def gather_sent(w):
        for t in range(1, B):
            copy_a(w, t).wait_send()
        for u in range(A):
            for t in range(B):
                if u > 0:
                    copy_b(w, u, t).wait_send()
                if (u, t) != (0, 0):
                    copy_d(w, u, t).wait_send()

    def token_rows(ref, slot):
        return ref.at[pl.ds(aligned(slot * span), span)]

    def tokens_in(src, dst, k):
        for j in range(S):
            chip, core, slot = S * c + j, q // PH, q % PH
            here = jnp.logical_and(chip == q, core == c)
            there = token_rows(dst, slot)

            @pl.when(here)
            def _():
                pltpu.make_async_copy(src.at[j], there, r.s_xr.at[k, slot]).start()

            @pl.when(jnp.logical_not(here))
            def _():
                remote(
                    src.at[j], there, r.s_xs.at[k, j], r.s_xr.at[k, slot], dev(core, chip)
                ).start()

    def tokens_in_done(dst, k):
        for slot in range(PH):
            blk = token_rows(dst, slot)
            pltpu.make_async_copy(blk, blk, r.s_xr.at[k, slot]).wait()

    def tokens_in_sent(src, dst, k):
        for j in range(S):
            chip, core, slot = S * c + j, q // PH, q % PH
            here = jnp.logical_and(chip == q, core == c)

            @pl.when(jnp.logical_not(here))
            def _():
                remote(
                    src.at[j],
                    token_rows(dst, slot),
                    r.s_xs.at[k, j],
                    r.s_xr.at[k, slot],
                    dev(core, chip),
                ).wait_send()

    def tokens_out(src, dst, k):
        for p in range(PH):
            chip, core, slot = c * PH + p, q // S, q % S
            here = jnp.logical_and(chip == q, core == c)

            @pl.when(here)
            def _():
                pltpu.make_async_copy(token_rows(src, p), dst.at[slot], r.s_xr.at[k, slot]).start()

            @pl.when(jnp.logical_not(here))
            def _():
                remote(
                    token_rows(src, p),
                    dst.at[slot],
                    r.s_xs.at[k, p],
                    r.s_xr.at[k, slot],
                    dev(core, chip),
                ).start()

    def tokens_out_done(src, dst, k):
        for j in range(S):
            pltpu.make_async_copy(dst.at[j], dst.at[j], r.s_xr.at[k, j]).wait()
        for p in range(PH):
            chip, core, slot = c * PH + p, q // S, q % S
            here = jnp.logical_and(chip == q, core == c)

            @pl.when(jnp.logical_not(here))
            def _():
                remote(
                    token_rows(src, p),
                    dst.at[slot],
                    r.s_xs.at[k, p],
                    r.s_xr.at[k, slot],
                    dev(core, chip),
                ).wait_send()

    def seg_send():
        for j in range(S):
            for core in range(2):
                chip = S * c + j
                here = jnp.logical_and(chip == q, c == core)
                i = 2 * j + core

                @pl.when(here)
                def _():
                    pltpu.make_async_copy(r.seg.at[j], r.segbuf.at[q], r.s_gr.at[q]).start()

                @pl.when(jnp.logical_not(here))
                def _():
                    remote(
                        r.seg.at[j],
                        r.segbuf.at[q],
                        r.s_gs.at[i],
                        r.s_gr.at[q],
                        dev(core, chip),
                    ).start()

    def seg_sent():
        for j in range(S):
            for core in range(2):
                chip = S * c + j
                here = jnp.logical_and(chip == q, c == core)

                @pl.when(jnp.logical_not(here))
                def _():
                    remote(
                        r.seg.at[j],
                        r.segbuf.at[q],
                        r.s_gs.at[2 * j + core],
                        r.s_gr.at[q],
                        dev(core, chip),
                    ).wait_send()

    def small_copy(t):
        return remote(
            r.small,
            r.smallbuf.at[q],
            r.s_ms.at[t],
            r.s_mr.at[t],
            dev(c, (q + t) % n),
        )

    def small_arrived(t):
        blk = r.smallbuf.at[(q + n - t) % n]
        return remote(blk, blk, r.s_ms.at[t], r.s_mr.at[t], sibling)

    def edge_copy(i):
        return remote(r.es[i], r.er[i], r.s_es.at[i], r.s_er.at[i], sibling)

    def edge_send(i, last, first):
        r.es[i][...] = jnp.where(c == 0, last, first)
        edge_copy(i).start()

    def edge_take(i):
        edge_copy(i).wait()
        got = r.er[i][...]
        return jnp.where(c == 1, got, 0.0), jnp.where(c == 0, got, 0.0)

    def columns(u):
        half = UNIT_PART[u]
        if half is None:
            return None
        size = plan.dims[UNIT_WEIGHT[u]][1] // 2
        return pl.ds(half * size, size)

    def urows(ref, u, row0, rows):
        cols = columns(u)
        if cols is None:
            return vrows(ref, UNIT_WEIGHT[u], row0, rows)
        return ref.at[pl.ds(aligned(row0), rows), cols]

    def gpiece(u, shard, half):
        if u == SMALL:
            return r.g8.at[pl.ds(pl.multiple_of(half * 8, 8), 8)]
        w = UNIT_WEIGHT[u]
        row0 = shard * plan.kr(w) + half * plan.hr(w)
        if w == GLU:
            size = plan.D
            cols = pl.ds(2 * D + UNIT_PART[u] * size, size)
            return r.hid.at[pl.ds(aligned(row0), plan.hr(w)), cols]
        return urows(r.dg if w == LEFT else r.w[w], u, row0, plan.hr(w))

    def rpiece(u, shard):
        w = UNIT_WEIGHT[u]
        if u == SMALL:
            return r.r[w]
        return urows(r.r[w], u, shard * plan.hr(w), plan.hr(w))

    def ppiece(u, slot):
        cols = columns(u)
        buf = r.p[UNIT_WEIGHT[u]]
        return buf.at[slot] if cols is None else buf.at[slot, :, cols]

    def zpiece(u, way):
        cols = columns(u)
        buf = (r.u, r.d)[way][UNIT_WEIGHT[u]]
        return buf if cols is None else buf.at[:, cols]

    def copy_r(u, s):
        return remote(
            gpiece(u, s, oc), rpiece(u, s), r.s_rs.at[u, s], r.s_rr.at[u, s], sibling
        )

    def copy_p(u, t):
        chip = lax.rem(q + t, n)
        return remote(
            gpiece(u, chip, c),
            ppiece(u, t - 1),
            r.s_ps.at[u, t],
            r.s_pr.at[u, t],
            dev(c, chip),
        )

    def shards(u):
        return 1 if u == SMALL else n

    def red0(u):
        for s in range(shards(u)):
            copy_r(u, s).start()

    def plus(a, b):
        return a[...].astype(F32) + b[...].astype(F32)

    def add_core(u, s):
        copy_r(u, s).wait_recv()
        mine = gpiece(u, s, c)
        mine[...] = plus(mine, rpiece(u, s)).astype(mine.dtype)

    def red1(u):
        if u == SMALL:
            add_core(u, 0)

        def one(t, _):
            if u != SMALL:
                add_core(u, lax.rem(q + t, n))
            copy_p(u, t).start()
            return 0

        lax.fori_loop(1, n, one, 0)
        if u != SMALL:
            add_core(u, q)

    def red2(u):
        total = gpiece(u, q, c)[...].astype(F32)
        for t in range(1, n):
            copy_p(u, t).wait_recv()
            total = total + ppiece(u, t - 1)[...].astype(F32)
        mine = ppiece(u, 0)
        mine[...] = total.astype(mine.dtype)

    def copy_z(u, way):
        return remote(
            ppiece(u, 1 + way),
            zpiece(u, way),
            r.s_zs.at[u, way],
            r.s_zr.at[u, way],
            dev(c, q, z + 1 if way == 0 else z - 1),
        )

    def red_hop(u, h):
        own, up, down = ppiece(u, 0), ppiece(u, 1), ppiece(u, 2)

        @pl.when(z == h)
        def _():
            if h == 0:
                up[...] = own[...]
            else:
                copy_z(u, 0).wait_recv()
                up[...] = plus(own, zpiece(u, 0)).astype(up.dtype)
            if h < Z - 1:
                copy_z(u, 0).start()

        @pl.when(z == Z - 1 - h)
        def _():
            if h == 0:
                down[...] = own[...]
            else:
                copy_z(u, 1).wait_recv()
                if h < Z - 1:
                    down[...] = plus(own, zpiece(u, 1)).astype(down.dtype)
            if h < Z - 1:
                copy_z(u, 1).start()

    def final_rows(u):
        w = UNIT_WEIGHT[u]
        if u == SMALL:
            return r.o[w].at[pl.ds(pl.multiple_of(c * 8, 8), 8)]
        return urows(r.o[w], u, c * plan.hr(w), plan.hr(w))

    def final_local(u):
        return pltpu.make_async_copy(ppiece(u, 0), final_rows(u), r.s_fl.at[u])

    def final_remote(u):
        return remote(ppiece(u, 0), final_rows(u), r.s_fs.at[u], r.s_fr.at[u], sibling)

    def red_final(u):
        if Z > 1:
            own, up = ppiece(u, 0), ppiece(u, 1)

            @pl.when(z == Z - 1)
            def _():
                own[...] = up[...]

            @pl.when(z < Z - 1)
            def _():
                own[...] = plus(up, zpiece(u, 1)).astype(own.dtype)

        final_local(u).start()
        final_remote(u).start()

    def red_end(u):
        final_local(u).wait()
        final_remote(u).wait()
        for s in range(shards(u)):
            copy_r(u, s).wait_send()
        for t in range(1, n):
            copy_p(u, t).wait_send()
        if Z > 1:

            @pl.when(z < Z - 1)
            def _():
                copy_z(u, 0).wait_send()

            @pl.when(z > 0)
            def _():
                copy_z(u, 1).wait_send()

    ahead = {}

    def last_hop(u):
        red_hop(u, Z - 1)
        red_final(u)

    def reduce_start(*units):
        for u in units:
            red0(u)
            ahead[u] = [red1, red2]
            if Z > 1:
                ahead[u] += [lambda k, h=h: red_hop(k, h) for h in range(Z - 1)]
            ahead[u].append(last_hop if Z > 1 else red_final)

    def move(*units):
        for u in units:
            if ahead[u]:
                ahead[u].pop(0)(u)

    def loop(count, body, after=()):
        def step(i, _):
            body(i)
            for k, act in after:
                pl.when(i == k)(act)
            return 0

        lax.fori_loop(0, count, step, 0)

    RB = 256
    NB = T // RB

    def rows_of(i, size=RB, base=0):
        return pl.ds(pl.multiple_of(i * size + base, 8 if base else size), size)

    small_local = pltpu.make_async_copy(r.small, r.smallbuf.at[q], r.s_mr.at[0])
    small_local.start()
    for t in range(1, n):
        small_copy(t).start()
    seg_send()
    tokens_in(r.x, r.xin, 0)
    g0(GLU)
    g0(CONV)
    r.g8[...] = jnp.zeros((16, FF), F32)

    for s in range(n):
        blk = r.segbuf.at[s]
        pltpu.make_async_copy(blk, blk, r.s_gr.at[s]).wait()
    for grp in range(n // plan.sr):
        got = r.segbuf[grp * plan.sr]
        for k in range(1, plan.sr):
            got = got + r.segbuf[grp * plan.sr + k]
        r.segrow[:, grp * plan.sw : (grp + 1) * plan.sw] = got
    r.segq[...] = r.segrow[:, pl.ds(pl.multiple_of(c * T, 128), T)]
    r.segcol[0:8] = jnp.full((8, 128), -1.0, F32)
    r.segcol[plan.LEN + 8 : plan.LEN + 16] = jnp.full((8, 128), -1.0, F32)
    for k in range(plan.LEN // 128):
        row = r.segrow[0:1, k * 128 : (k + 1) * 128]
        r.segcol[8 + k * 128 : 8 + (k + 1) * 128] = jnp.broadcast_to(row, (128, 128)).T
    r.segloc[...] = r.segcol[pl.ds(pl.multiple_of(c * T, 8), T + 16)]
    for o in range(1, 5):
        same = r.segloc[0 : T + 8] == r.segloc[o : T + 8 + o]
        r.mext[o - 1, 0 : T + 8] = jnp.where(same, 1.0, 0.0)

    def mask(o, start, rows):
        if o > 0:
            return r.mext[o - 1, 8 + start : 8 + start + rows]
        return r.mext[-o - 1, 8 + start + o : 8 + start + o + rows]

    small_local.wait()
    for t in range(1, n):
        small_arrived(t).wait_recv()
    for grp in range(n // plan.nr):
        got = r.smallbuf[grp * plan.nr].astype(F32)[0:8, 0 : plan.nw]
        for k in range(1, plan.nr):
            got = got + r.smallbuf[grp * plan.nr + k].astype(F32)[0:8, 0 : plan.nw]
        r.nrm[:, grp * plan.nw : (grp + 1) * plan.nw] = got
    for s in range(n):
        r.midp[:, s * plan.FFn : (s + 1) * plan.FFn] = r.smallbuf[s].astype(F32)[8:24]

    def ln_out(k, v):
        unit, _ = normed(v)
        return (unit * r.nrm[k : k + 1] + r.nrm[4 + k : 5 + k]).astype(BF16)

    def ln_back(k, e, v):
        unit, rs = normed(v)
        eg = e * r.nrm[k : k + 1]
        m1 = jnp.mean(eg, axis=-1, keepdims=True)
        m2 = jnp.mean(eg * unit, axis=-1, keepdims=True)
        cols = slice(k * D, (k + 1) * D)
        r.g8[11:12, cols] += jnp.sum(e * unit, axis=0, keepdims=True)
        r.g8[12:13, cols] += jnp.sum(e, axis=0, keepdims=True)
        return rs * (eg - m1 - unit * m2)

    g1(GLU)
    g0(LEFT)
    g2(GLU)
    g1(CONV)
    tokens_in_done(r.xin, 0)
    g3(GLU)

    def glu(i):
        rows = rows_of(i)
        x = r.xin[rows].astype(F32)
        a1 = ln_out(0, x)
        r.a1[rows] = a1
        value = mm(a1, r.w[GLU][:, 0:D])
        gate = sigmoid(mm(a1, r.w[GLU][:, D : 2 * D]))
        r.sg[rows, 0:D] = gate.astype(BF16)
        r.sg[rows, D : 2 * D] = (value * gate * (1.0 - gate)).astype(BF16)
        y1 = x + value * gate
        r.y1[rows] = y1
        r.a2[rows] = ln_out(1, y1)

    loop(NB, glu)
    g2(CONV)
    g1(LEFT)
    g0(POINT)
    g3(CONV)

    def conv(i):
        a2 = r.a2[rows_of(i)]
        for o in range(3):
            r.pext[o, rows_of(i, RB, 8)] = mm(a2, r.w[CONV][o])

    loop(NB, conv)
    edge_send(0, r.pext[0, T : T + 8], r.pext[2, 8:16])
    g2(LEFT)
    g1(POINT)
    g0(QKV)
    top, bottom = edge_take(0)
    r.pext[0, 0:8] = top
    r.pext[2, T + 8 : T + 16] = bottom
    for k in range(T // 128):
        lo = k * 128
        before = mask(-1, lo, 128)
        after = mask(1, lo, 128)
        pre = (
            r.pext[0, lo + 7 : lo + 135] * jnp.concatenate([before] * (H // 128), axis=1)
            + r.pext[1, lo + 8 : lo + 136]
            + r.pext[2, lo + 9 : lo + 137] * jnp.concatenate([after] * (H // 128), axis=1)
        )
        value, slope = gelu_both(pre)
        r.pext[1, lo + 8 : lo + 136] = value
        r.dgr[lo : lo + 128] = slope.astype(BF16)
    g3(LEFT)

    CH = 512
    RM = 128

    def left(i):
        rows, erows = rows_of(i, RM), rows_of(i, RM, 8)
        a2 = r.a2[rows]
        for k in range(FF // CH):
            value, slope = gelu_both(mm(a2, r.w[LEFT][:, k * CH : (k + 1) * CH]))
            r.dgl[rows, k * CH : (k + 1) * CH] = slope.astype(BF16)
            r.big[erows, k * CH : (k + 1) * CH] = value
        r.big[erows, 0:H] += r.pext[1, erows]
        unit, rs = normed(r.big[erows])
        r.nm[rows] = unit.astype(BF16)
        r.rm[rows] = rs
        r.big[erows] = (unit * r.midp[0:1] + r.midp[1:2]).astype(BF16).astype(F32)

    loop(T // RM, left)
    edge_send(1, r.big[T : T + 8], r.big[8:16])
    g2(POINT)
    g1(QKV)
    g0(OUT)
    top, bottom = edge_take(1)
    r.big[0:8] = top
    r.big[T + 8 : T + 16] = bottom

    RC = 64

    def depthwise(j):
        cols = pl.ds(pl.multiple_of(j * 128, 128), 128)
        for k in range(T // RC):
            lo = k * RC
            total = r.big[lo + 8 : lo + 8 + RC, cols] * r.midp[6:7, cols]
            for o in (-4, -3, -2, -1, 1, 2, 3, 4):
                cells = r.big[lo + 8 + o : lo + 8 + o + RC, cols]
                total = total + cells * mask(o, lo, RC) * r.midp[6 + o : 7 + o, cols]
            r.sep[lo : lo + RC, cols] = total.astype(BF16)

    def ahead_qkv():
        g2(QKV)
        g1(OUT)
        g0(FIN)

    loop(FF // 128, depthwise, [(7, ahead_qkv)])
    g2(OUT)
    g3(POINT)

    def point(i):
        rows = rows_of(i)
        y2 = r.y1[rows] + mm(r.sep[rows], r.w[POINT][...])
        r.y2[rows] = y2
        r.a4[rows] = ln_out(2, y2)

    loop(NB, point)
    g3(QKV)
    scale = 1.0 / math.sqrt(D // HEADS)

    def qkv(i):
        rows = rows_of(i)
        a4 = r.a4[rows]
        r.qb[rows] = (mm(a4, r.w[QKV][:, 0:D]) * scale).astype(BF16)
        r.kvb[c, rows, 0:D] = mm(a4, r.w[QKV][:, D : 2 * D]).astype(BF16)
        r.kvb[c, rows, D : 2 * D] = mm(a4, r.w[QKV][:, 2 * D : 3 * D]).astype(BF16)

    loop(NB, qkv)

    def kv_copy():
        blk = r.kvb.at[c]
        return remote(blk, blk, r.s_ks.at[0], r.s_kr.at[0], sibling)

    kv_copy().start()
    tokens_in(r.ct, r.cot, 1)
    lane = lax.broadcasted_iota(jnp.int32, (1, 128), 1)
    heads_lanes = [lane < 64, lane >= 64]
    g1(FIN)
    g0(FOUT)
    kv_copy().wait()

    def pair_cols(j, base=0):
        return pl.ds(pl.multiple_of(j * 128 + base, 128), 128)

    def one_head(q2, part, mine, key_row):
        def scores(keys, segs):
            raw = mm_t(q2, keys)
            same = jnp.concatenate([mine] * (T // 128), axis=1) == segs
            return jnp.where(same, raw, NEG)

        s0 = scores(part[0], key_row[:, 0:T])
        s1 = scores(part[1], key_row[:, T : 2 * T])
        most = jnp.maximum(
            jnp.max(s0, axis=-1, keepdims=True), jnp.max(s1, axis=-1, keepdims=True)
        )
        e0, e1 = jnp.exp(s0 - most), jnp.exp(s1 - most)
        total = jnp.sum(e0, axis=-1, keepdims=True) + jnp.sum(e1, axis=-1, keepdims=True)
        got = mm(e0.astype(BF16), part[2]) + mm(e1.astype(BF16), part[3])
        return got / total, most + jnp.log(total)

    def attend(j):
        cols, vcols = pair_cols(j), pair_cols(j, D)
        part = [r.kvb[0, :, cols], r.kvb[1, :, cols], r.kvb[0, :, vcols], r.kvb[1, :, vcols]]
        key_row = r.segrow[0:1]
        for k in range(T // RB):
            rows = slice(k * RB, (k + 1) * RB)
            q2 = r.qb[rows, cols]
            mine = r.segloc[8 + k * RB : 8 + (k + 1) * RB]
            got = []
            for e in range(2):
                context, lse = one_head(
                    jnp.where(heads_lanes[e], q2, jnp.zeros_like(q2)), part, mine, key_row
                )
                got.append(context)
                r.lse[rows] = jnp.where(lane == 2 * j + e, lse, r.lse[rows])
            r.ctx[rows, cols] = jnp.where(heads_lanes[0], got[0], got[1]).astype(BF16)

    r.lse[...] = jnp.zeros((T, 128), F32)
    def ahead_fin():
        g2(FIN)
        g1(FOUT)

    loop(HEADS // 2, attend, [(1, ahead_fin)])
    turned = r.lse[...].T
    for j in range(HEADS // 2):
        r.lset[j, 0:2] = turned[2 * j : 2 * j + 2]
    g2(FOUT)
    g3(OUT)

    def out(i):
        rows = rows_of(i)
        y3 = r.y2[rows] + mm(r.ctx[rows], r.w[OUT][...])
        r.y3[rows] = y3
        r.a5[rows] = ln_out(3, y3)

    loop(NB, out)
    g3(FIN)

    def ffn_in(i):
        rows = rows_of(i)
        a5 = r.a5[rows]
        for k in range(FF // CH):
            value, slope = gelu_both(mm(a5, r.w[FIN][:, k * CH : (k + 1) * CH]))
            r.hid[rows, k * CH : (k + 1) * CH] = value.astype(BF16)
            r.dg[rows, k * CH : (k + 1) * CH] = slope.astype(BF16)

    loop(NB, ffn_in)
    g3(FOUT)

    def ffn_out(i):
        rows = rows_of(i)
        r.osend[rows] = (r.y3[rows] + mm(r.hid[rows], r.w[FOUT][...])).astype(BF16)

    loop(NB, ffn_out)
    tokens_out(r.osend, r.o_out, 2)
    for w in range(WEIGHTS):
        gather_sent(w)

    tokens_in_done(r.cot, 1)

    def ffn_back(i):
        rows = rows_of(i)
        f4 = r.cot[rows]
        for k in range(FF // CH):
            cols = slice(k * CH, (k + 1) * CH)
            up = mm_t(f4, r.w[FOUT][cols])
            r.dg[rows, cols] = (up * r.dg[rows, cols].astype(F32)).astype(BF16)
        e = mm_t(r.dg[rows], r.w[FIN][...])
        r.gs[rows] = f4.astype(F32) + ln_back(3, e, r.y3[rows])

    loop(NB, ffn_back)
    GC = 256

    def grad_outer(k):
        cols = rows_of(k, GC)
        r.w[FOUT][cols] = mm_tn(r.hid[:, cols], r.cot[...]).astype(BF16)

    loop(FF // GC, grad_outer)
    reduce_start(U_FOUT)
    r.tr[...] = r.a5[...].T

    def grad_inner(k):
        cols = rows_of(k, GC)
        r.w[FIN][:, cols] = mm(r.tr[...], r.dg[:, cols]).astype(BF16)

    loop(FF // GC, grad_inner)
    reduce_start(U_FIN)
    move(U_FOUT)

    def out_back(i):
        rows = rows_of(i)
        f3 = r.gs[rows].astype(BF16)
        r.a5[rows] = f3
        r.hid[rows, 3 * D : 4 * D] = mm_t(f3, r.w[OUT][...]).astype(BF16)

    loop(NB, out_back)
    r.w[OUT][...] = mm_tn(r.ctx[...], r.a5[...]).astype(BF16)
    reduce_start(U_OUT)

    QB = 256

    def attend_back(j):
        cols, vcols = pair_cols(j), pair_cols(j, D)
        for k in range(T // QB):
            rows = slice(k * QB, (k + 1) * QB)
            q2 = r.qb[rows, cols]
            d2 = r.hid[rows, pair_cols(j, 3 * D)]
            dq = jnp.zeros((QB, 128), F32)
            for e in range(2):
                qe = jnp.where(heads_lanes[e], q2, jnp.zeros_like(q2))
                de = jnp.where(heads_lanes[e], d2, jnp.zeros_like(d2))
                lse = r.lset[j, e : e + 1, rows]
                probs, dprobs = [], []
                for kk in range(2):
                    keys = r.kvb[kk, :, cols]
                    values = r.kvb[kk, :, vcols]
                    segs = r.segcol[8 + kk * T : 8 + (kk + 1) * T]
                    same = jnp.concatenate([segs] * (QB // 128), axis=1) == r.segq[0:1, rows]
                    probs.append(jnp.where(same, jnp.exp(mm_t(keys, qe) - lse), 0.0))
                    dprobs.append(mm_t(values, de))
                delta = jnp.sum(probs[0] * dprobs[0], axis=0, keepdims=True) + jnp.sum(
                    probs[1] * dprobs[1], axis=0, keepdims=True
                )
                for kk in range(2):
                    keys = r.kvb[kk, :, cols]
                    ds = (probs[kk] * (dprobs[kk] - delta)).astype(BF16)
                    span_k = slice(kk * T, (kk + 1) * T)
                    dk = mm(ds, qe)
                    dv = mm(probs[kk].astype(BF16), de)
                    if k == 0 and e == 0:
                        r.acc[0, span_k] = dk
                        r.acc[1, span_k] = dv
                    else:
                        r.acc[0, span_k] += dk
                        r.acc[1, span_k] += dv
                    ke = jnp.where(heads_lanes[e], keys, jnp.zeros_like(keys))
                    dq = dq + mm_tn(ds, ke)
            r.hid[rows, cols] = (dq * scale).astype(BF16)
        own = pl.ds(pl.multiple_of(c * T, T), T)
        other = pl.ds(pl.multiple_of(oc * T, T), T)
        r.big[0:T, cols] = r.acc[0, own]
        r.big[0:T, vcols] = r.acc[1, own]
        r.dg[:, cols] = r.acc[0, other].astype(BF16)
        r.dg[:, vcols] = r.acc[1, other].astype(BF16)

    loop(
        HEADS // 2,
        attend_back,
        [
            (1, lambda: move(U_FIN)),
            (2, lambda: move(U_FOUT, U_FOUT)),
            (3, lambda: move(U_OUT)),
        ],
    )

    def dkv_copy():
        return remote(
            r.dg.at[:, pl.ds(0, 2 * D)], r.dkvr, r.s_ks.at[1], r.s_kr.at[1], sibling
        )

    dkv_copy().start()
    dkv_copy().wait()

    def qkv_back(i):
        rows = rows_of(i)
        total = r.big[rows, 0 : 2 * D] + r.dkvr[rows].astype(F32)
        r.hid[rows, D : 3 * D] = total.astype(BF16)
        e = mm_t(r.hid[rows, 0 : 3 * D], r.w[QKV][...])
        r.gs[rows] += ln_back(2, e, r.y2[rows])

    loop(NB, qkv_back)
    r.tr[...] = r.a4[...].T

    def grad_qkv(k):
        cols = rows_of(k, GC)
        r.w[QKV][:, cols] = mm(r.tr[...], r.hid[:, cols]).astype(BF16)

    loop(3 * D // GC, grad_qkv)
    reduce_start(U_QKV)

    def point_back(i):
        rows = rows_of(i)
        f2 = r.gs[rows].astype(BF16)
        r.a4[rows] = f2
        for k in range(FF // CH):
            cols = slice(k * CH, (k + 1) * CH)
            d = mm_t(f2, r.w[POINT][cols])
            r.big[rows_of(i, RB, 8), cols] = d.astype(BF16).astype(F32)

    loop(NB, point_back)
    edge_send(2, r.big[T : T + 8], r.big[8:16])
    move(U_FIN, U_FOUT, U_FIN, U_QKV)

    def grad_point(k):
        cols = rows_of(k, GC)
        r.w[POINT][cols] = mm_tn(r.sep[:, cols], r.a4[...]).astype(BF16)

    loop(FF // GC, grad_point)
    reduce_start(U_POINT0, U_POINT1)
    move(U_OUT, U_OUT)
    top, bottom = edge_take(2)
    r.big[0:8] = top
    r.big[T + 8 : T + 16] = bottom

    def depth_back(j):
        cols = pl.ds(pl.multiple_of(j * 128, 128), 128)
        gain, shift = r.midp[0:1, cols], r.midp[1:2, cols]
        sums = [jnp.zeros((8, 128), F32) for _ in range(9)]
        for k in range(T // RC):
            lo = k * RC
            a3 = r.nm[lo : lo + RC, cols].astype(F32) * gain + shift
            total = jnp.zeros((RC, 128), F32)
            for o in range(-4, 5):
                moved = r.big[lo + 8 - o : lo + 8 - o + RC, cols]
                if o:
                    moved = moved * mask(-o, lo, RC)
                total = total + moved * r.midp[6 + o : 7 + o, cols]
                part = moved * a3
                for b in range(RC // 8):
                    sums[o + 4] = sums[o + 4] + part[b * 8 : (b + 1) * 8]
            r.col[lo : lo + RC] = total
        for o in range(9):
            r.g8[2 + o : 3 + o, cols] = jnp.sum(sums[o], axis=0, keepdims=True)
        r.big[8 : T + 8, cols] = r.col[...]

    loop(
        FF // 128,
        depth_back,
        [
            (3, lambda: move(U_POINT0, U_POINT1)),
            (7, lambda: move(U_FOUT, U_FIN, U_OUT, U_QKV, U_QKV)),
            (13, lambda: move(U_FOUT, U_FIN, U_OUT, U_QKV)),
        ],
    )
    move(U_POINT0, U_POINT0)

    def mid_back(i):
        rows, erows = rows_of(i, RM), rows_of(i, RM, 8)
        e = r.big[erows]
        unit = r.nm[rows].astype(F32)
        eg = e * r.midp[0:1]
        m1 = jnp.mean(eg, axis=-1, keepdims=True)
        m2 = jnp.mean(eg * unit, axis=-1, keepdims=True)
        r.g8[0:1] += jnp.sum(e * unit, axis=0, keepdims=True)
        r.g8[1:2] += jnp.sum(e, axis=0, keepdims=True)
        dmid = r.rm[rows] * (eg - m1 - unit * m2)
        r.dgl[rows] = (dmid * r.dgl[rows].astype(F32)).astype(BF16)
        right = dmid[:, 0:H] * r.dgr[rows].astype(F32)
        r.pext[0, erows] = right.astype(BF16).astype(F32)

    loop(T // RM, mid_back)
    edge_send(3, r.pext[0, T : T + 8], r.pext[0, 8:16])
    move(U_POINT1, U_POINT1, U_QKV)
    r.tr[...] = r.a2[...].T

    def grad_left(k):
        cols = rows_of(k, GC)
        r.dg[:, cols] = mm(r.tr[...], r.dgl[:, cols]).astype(BF16)

    for half in range(2):
        lax.fori_loop(
            half * (FF // GC // 2), (half + 1) * (FF // GC // 2), lambda k, _: (grad_left(k), 0)[1], 0
        )
        reduce_start((U_LEFT0, U_LEFT1)[half])
    move(U_POINT0, U_FIN, U_OUT)
    top, bottom = edge_take(3)
    r.pext[0, 0:8] = top
    r.pext[0, T + 8 : T + 16] = bottom
    for k in range(T // 128):
        lo = k * 128
        for o in (-1, 0, 1):
            moved = r.pext[0, lo + 8 - o : lo + 136 - o]
            if o:
                moved = moved * jnp.concatenate([mask(-o, lo, 128)] * (H // 128), axis=1)
            r.hid[lo : lo + 128, (o + 1) * H : (o + 2) * H] = moved.astype(BF16)

    def branch_back(i):
        rows = rows_of(i)
        e = mm_t(r.dgl[rows], r.w[LEFT][...])
        for o in range(3):
            e = e + mm_t(r.hid[rows, o * H : (o + 1) * H], r.w[CONV][o])
        r.gs[rows] += ln_back(1, e, r.y1[rows])

    loop(NB, branch_back, [(0, lambda: move(U_LEFT0))])
    move(U_LEFT1, U_QKV, U_POINT1)
    for o in range(3):
        r.w[CONV][o] = mm(r.tr[...], r.hid[:, o * H : (o + 1) * H]).astype(BF16)
    reduce_start(U_CONV)
    move(U_POINT0)

    def gate_back(i):
        rows = rows_of(i)
        g = r.gs[rows]
        r.sg[rows, 0:D] = (g * r.sg[rows, 0:D].astype(F32)).astype(BF16)
        r.sg[rows, D : 2 * D] = (g * r.sg[rows, D : 2 * D].astype(F32)).astype(BF16)

    loop(NB, gate_back)
    r.tr[...] = r.a1[...].T

    def grad_glu(k):
        cols = rows_of(k, GC)
        to = pl.ds(pl.multiple_of(k * GC + 2 * D, GC), GC)
        r.hid[:, to] = mm(r.tr[...], r.sg[:, cols]).astype(BF16)

    loop(2 * D // GC, grad_glu)
    move(U_CONV)
    reduce_start(U_GLU0, U_GLU1)

    def glu_back(i):
        rows = rows_of(i)
        e = mm_t(r.sg[rows], r.w[GLU][...])
        total = r.gs[rows] + ln_back(0, e, r.xin[rows].astype(F32))
        r.a5[rows] = total.astype(BF16)

    loop(NB, glu_back)
    reduce_start(SMALL)
    move(U_POINT1, U_LEFT0, U_LEFT0, U_GLU0, U_GLU1, SMALL)
    tokens_out(r.a5, r.o_ig, 3)
    move(U_POINT0, U_LEFT1, U_LEFT1, U_LEFT0, U_POINT1, U_CONV, U_CONV, U_LEFT1, U_LEFT0)
    move(U_CONV, U_GLU0, U_GLU0, U_LEFT1, U_GLU1, U_GLU1, SMALL, SMALL, U_LEFT0, U_CONV)
    move(U_GLU0, U_LEFT1, U_GLU1, SMALL, U_CONV, U_GLU0, U_GLU1, SMALL, U_GLU0, U_GLU1, SMALL)
    while any(ahead.values()):
        move(*range(UNITS))

    for u in range(UNITS):
        red_end(u)
    tokens_out_done(r.osend, r.o_out, 2)
    tokens_out_done(r.a5, r.o_ig, 3)
    tokens_in_sent(r.x, r.xin, 0)
    tokens_in_sent(r.ct, r.cot, 1)
    seg_sent()
    for t in range(1, n):
        small_copy(t).wait_send()


def local(
    inputs,
    segment_ids,
    cotangent,
    norm_gain,
    norm_bias,
    glu_weight,
    left_weight,
    conv_weight,
    mid_gain,
    mid_bias,
    depth_weight,
    point_weight,
    qkv_weight,
    out_weight,
    ffn_in,
    ffn_out,
):
    seqs, span, width = inputs.shape
    n = lax.axis_size("seq")
    plan = Plan(
        lax.axis_size("dp"), n, seqs, span, width, ffn_in.shape[1], conv_weight.shape[2]
    )
    q = lax.axis_index("seq")

    def placed(piece, repeats):
        if repeats == 1:
            return piece
        size = piece.shape[-1]
        tiled = jnp.tile(piece, (1,) * (piece.ndim - 1) + (repeats,))
        at = lax.broadcasted_iota(jnp.int32, tiled.shape, tiled.ndim - 1) // size
        return jnp.where(at == q % repeats, tiled, jnp.zeros_like(tiled))

    segs = placed(segment_ids.astype(F32), plan.sr)
    segs = jnp.broadcast_to(segs[:, None, :], (seqs, 8, plan.sw))
    norms = placed(jnp.concatenate([norm_gain, norm_bias], 0), plan.nr)
    norms = jnp.pad(norms, ((0, 0), (0, plan.FFn - plan.nw)))
    small = jnp.concatenate([norms, mid_gain[None], mid_bias[None], depth_weight], 0)
    small = jnp.pad(small, ((0, 32 - small.shape[0]), (0, 0)))
    weights = [None] * WEIGHTS
    weights[GLU], weights[CONV], weights[LEFT] = glu_weight, conv_weight, left_weight
    weights[POINT], weights[QKV], weights[OUT] = point_weight, qkv_weight, out_weight
    weights[FIN], weights[FOUT] = ffn_in, ffn_out

    shapes = []
    plan.buffers(shapes.append)
    out_shape = [jax.ShapeDtypeStruct(inputs.shape, BF16)] * 2
    out_shape += [jax.ShapeDtypeStruct(w.shape, BF16) for w in weights]
    out_shape += [jax.ShapeDtypeStruct((16, plan.FF), F32)]
    hbm = pl.BlockSpec(memory_space=pl.ANY)
    got = pl.pallas_call(
        lambda *refs: kernel(plan, *refs),
        out_shape=out_shape,
        in_specs=[hbm] * INPUTS,
        out_specs=[hbm] * OUTPUTS,
        scratch_shapes=shapes,
        compiler_params=pltpu.CompilerParams(
            collective_id=0, has_side_effects=True, vmem_limit_bytes=64 << 20
        ),
        name="cell",
    )(inputs, segs, cotangent, small, *weights)
    out = unpacked(plan, got)
    return (
        out[0],
        out[1],
        out[2 + WEIGHTS],
        out[3 + WEIGHTS],
        out[2 + GLU],
        out[2 + LEFT],
        out[2 + CONV],
        out[4 + WEIGHTS].reshape(-1),
        out[5 + WEIGHTS].reshape(-1),
        out[6 + WEIGHTS],
        out[2 + POINT],
        out[2 + QKV],
        out[2 + OUT],
        out[2 + FIN],
        out[2 + FOUT],
    )


def unpacked(plan, parts):
    count = 2 + WEIGHTS
    dn = plan.D // plan.n
    wide = [jax.ShapeDtypeStruct(p.shape, F32) for p in parts[:count]]
    tiny = [(4, dn), (4, dn), (1, plan.FFn), (1, plan.FFn), (9, plan.FFn)]
    out_shape = wide + [jax.ShapeDtypeStruct(shape, F32) for shape in tiny]

    def body(*refs):
        ins, outs = refs[:count], refs[count + 1 : 2 * count + 1]
        sums, tinies = refs[count], refs[2 * count + 1 : 2 * count + 6]
        near, far = refs[2 * count + 6 : 3 * count + 6], refs[3 * count + 6 : 4 * count + 6]
        came, went = refs[4 * count + 6], refs[4 * count + 7]

        def arrive(i):
            return pltpu.make_async_copy(ins[i], near[i], came.at[i])

        def leave(i):
            return pltpu.make_async_copy(far[i], outs[i], went.at[i])

        for i in range(count):
            arrive(i).start()
        q = lax.axis_index("seq")
        rolled = pltpu.roll(sums[...], (plan.FF - q * plan.FFn) % plan.FF, 1)[:, 0 : plan.FFn]
        tinies[2][...] = rolled[0:1]
        tinies[3][...] = rolled[1:2]
        tinies[4][...] = rolled[2:11]
        for k in range(2):
            row = sums[11 + k : 12 + k]
            rows = [row[:, i * plan.D : (i + 1) * plan.D] for i in range(4)]
            both = jnp.concatenate(rows + rows, axis=0)
            tinies[k][...] = pltpu.roll(both, (plan.D - q * dn) % plan.D, 1)[0:4, 0:dn]
        for i in range(count):
            arrive(i).wait()
            far[i][...] = near[i][...].astype(F32)
            leave(i).start()
        for i in range(count):
            leave(i).wait()

    hbm = pl.BlockSpec(memory_space=pl.ANY)
    vmem = pl.BlockSpec(memory_space=pltpu.VMEM)
    return pl.pallas_call(
        body,
        out_shape=out_shape,
        in_specs=[hbm] * count + [vmem],
        out_specs=[hbm] * count + [vmem] * len(tiny),
        scratch_shapes=[pltpu.VMEM(p.shape, BF16) for p in parts[:count]]
        + [pltpu.VMEM(p.shape, F32) for p in parts[:count]]
        + [pltpu.SemaphoreType.DMA((count,))] * 2,
        compiler_params=pltpu.CompilerParams(vmem_limit_bytes=64 << 20),
    )(*parts)


def solution(mesh):
    in_specs = (
        P("dp", "seq", None),
        P("dp", "seq"),
        P("dp", "seq", None),
        P(None, "seq"),
        P(None, "seq"),
        P("seq", None),
        P("seq", None),
        P(None, "seq", None),
        P("seq"),
        P("seq"),
        P(None, "seq"),
        P("seq", None),
        P("seq", None),
        P("seq", None),
        P("seq", None),
        P("seq", None),
    )
    out_specs = (
        P("dp", "seq", None),
        P("dp", "seq", None),
        P(None, "seq"),
        P(None, "seq"),
        P("seq", None),
        P("seq", None),
        P(None, "seq", None),
        P("seq"),
        P("seq"),
        P(None, "seq"),
        P("seq", None),
        P("seq", None),
        P("seq", None),
        P("seq", None),
        P("seq", None),
    )
    return jax.shard_map(local, mesh=mesh, in_specs=in_specs, out_specs=out_specs, check_vma=False)
```

```python
import math

import jax
import jax.numpy as jnp
from jax import lax
from jax.experimental import pallas as pl
from jax.experimental.pallas import tpu as pltpu
from jax.sharding import PartitionSpec as P

HEADS = 8
EPS = 1e-06
MESH = pl.DeviceIdType.MESH
F32 = jnp.float32
BF16 = jnp.bfloat16

GLU, CONV, LEFT, POINT, QKV, OUT, FIN, FOUT = range(8)
WEIGHTS = 8
(U_GLU0, U_GLU1, U_CONV, U_LEFT0, U_LEFT1, U_POINT0, U_POINT1, U_QKV, U_OUT, U_FIN, U_FOUT, SMALL) = range(12)
UNITS = 12

MB, MW = 128, 256
FAR = -(2.0**30)
UNIT_WEIGHT = (GLU, GLU, CONV, LEFT, LEFT, POINT, POINT, QKV, OUT, FIN, FOUT, WEIGHTS)
UNIT_PART = (0, 1, None, 0, 1, 0, 1, None, None, None, None, None)


def mm(a, b):
    return lax.dot_general(a, b, (((1,), (0,)), ((), ())), preferred_element_type=F32)


def mm_t(a, b):
    return lax.dot_general(a, b, (((1,), (1,)), ((), ())), preferred_element_type=F32)


def mm_tn(a, b):
    return lax.dot_general(a, b, (((0,), (0,)), ((), ())), preferred_element_type=F32)


def normed(v):
    centred = v - jnp.mean(v, axis=-1, keepdims=True)
    r = lax.rsqrt(jnp.mean(centred * centred, axis=-1, keepdims=True) + EPS)
    return centred * r, r


def gelu_both(v):
    c = math.sqrt(2.0 / math.pi)
    sq = v * v
    t = jnp.tanh(v * (c + (c * 0.044715) * sq))
    half = 0.5 * t + 0.5
    value = v * half
    slope = half + (0.5 * v) * (1.0 - t * t) * (c + (3.0 * c * 0.044715) * sq)
    return value, slope


def sigmoid(v):
    return 0.5 * jnp.tanh(0.5 * v) + 0.5


class Buffers:
    pass


class Plan:
    def __init__(self, dp, n, seqs, span, width, hidden, half):
        self.n, self.Z = n, dp // 2
        self.S, self.span = seqs, span
        self.D, self.FF, self.HALF = width, hidden, half
        self.LEN = span * n
        self.T = self.LEN // 2
        self.PH = n // 2
        self.B = math.isqrt(n)
        self.A = n // self.B
        assert self.A == self.B and n == 2 * seqs and dp % 2 == 0
        self.shared = (LEFT, POINT, FIN, FOUT) if self.Z % 2 == 0 else ()
        self.sw = max(span, 128)
        self.sr = self.sw // span
        dn = width // n
        self.nw = max(dn, 128)
        self.nr = self.nw // dn
        self.FFn = hidden // n
        self.dims = [
            (width, 2 * width),
            (width, half),
            (width, hidden),
            (hidden, width),
            (width, 3 * width),
            (width, width),
            (width, hidden),
            (hidden, width),
        ]

    def whole(self, w):
        k, cols = self.dims[w]
        return (3, k, cols) if w == CONV else (k, cols)

    def kr(self, w):
        return self.dims[w][0] // self.n

    def hr(self, w):
        return self.kr(w) // 2

    def piece(self, w, rows):
        cols = self.dims[w][1]
        return (3, rows, cols) if w == CONV else (rows, cols)

    def buffers(self, take):
        T, D, FF, H, n = self.T, self.D, self.FF, self.HALF, self.n
        r = Buffers()

        def vm(shape, dtype):
            return take(pltpu.VMEM(shape, dtype))

        def sem(*shape):
            return take(pltpu.SemaphoreType.DMA(shape))

        every = range(WEIGHTS)
        parts = [(self.piece(w, self.hr(w)), BF16) for w in every] + [((8, FF), F32)]
        r.w = [vm(self.whole(w), BF16) for w in every]
        r.g8 = vm((16, FF), F32)
        r.r = [None] * WEIGHTS + [vm((8, FF), F32)]
        for w in (CONV, QKV, OUT, FIN, FOUT):
            r.r[w] = vm(self.piece(w, n * self.hr(w)), BF16)
        r.r[LEFT], r.r[POINT], r.r[GLU] = r.r[FIN], r.r[FOUT], r.r[QKV]
        r.p = [vm((n - 1,) + shape, dtype) for shape, dtype in parts]
        if self.Z > 1:
            r.u = [vm(shape, dtype) for shape, dtype in parts]
            r.d = [vm(shape, dtype) for shape, dtype in parts]
        r.segbuf = vm((n, 8, self.sw), F32)
        r.segrow = vm((8, self.LEN), F32)
        r.segcol = vm((self.LEN + 16, 128), F32)
        r.segloc = vm((T + 16, 128), F32)
        r.mext = vm((T + 16, 128), F32)
        r.ms = vm((T // MB, 9 * MB, MW), BF16)
        r.qenc = vm((T, 128), BF16)
        r.kenc = vm((self.LEN, 128), BF16)
        r.smallbuf = vm((n, 32, self.FFn), BF16)
        r.nrm = vm((8, D), F32)
        r.midp = vm((16, FF), F32)
        r.xin = vm((T, D), BF16)
        r.cot = vm((T, D), BF16)
        r.a1 = vm((T, D), BF16)
        r.sg = vm((T, 2 * D), BF16)
        r.y1 = vm((T, D), F32)
        r.a2 = vm((T, D), BF16)
        r.pext = vm((3, T + 16, H), F32)
        r.dgl = vm((T, FF), BF16)
        r.dgr = vm((T, H), BF16)
        r.nm = vm((T, FF), BF16)
        r.rm = vm((T, 1), F32)
        r.big = vm((T + 16, FF), F32)
        r.sep = vm((T, FF), BF16)
        r.y2 = vm((T, D), F32)
        r.a4 = vm((T, D), BF16)
        r.qb = vm((T, D), BF16)
        r.kvb = vm((self.LEN, 2 * D), BF16)
        r.lse = vm((T, 128), F32)
        r.ctx = vm((T, D), BF16)
        r.y3 = vm((T, D), F32)
        r.a5 = vm((T, D), BF16)
        r.hid = vm((T + 32, FF), BF16)
        r.dg = vm((T, FF), BF16)
        r.osend = vm((T, D), BF16)
        r.gs = r.y3
        r.dkvr = vm((T, 2 * D), BF16)
        r.tr = vm((D, T), BF16)
        edges = (((8, H), F32), ((16, FF), BF16), ((16, FF), BF16), ((8, H), F32))
        r.es = [vm(shape, dtype) for shape, dtype in edges]
        r.er = [vm(shape, dtype) for shape, dtype in edges]
        r.s_loc = sem(WEIGHTS)
        r.s_as = sem(WEIGHTS)
        r.s_ar = sem(WEIGHTS, self.B - 1)
        r.s_br = sem(WEIGHTS, (self.A - 1) * self.B)
        r.s_ds = sem(WEIGHTS)
        r.s_dr = sem(WEIGHTS)
        if self.shared:
            r.s_hs = sem(WEIGHTS)
            r.s_hr = sem(WEIGHTS)
        r.s_rs = sem(UNITS)
        r.s_rr = sem(UNITS)
        r.s_ps = sem(UNITS, 2)
        r.s_pr = sem(UNITS, 2)
        if self.Z > 1:
            r.s_zs = sem(UNITS, 2)
            r.s_zr = sem(UNITS, 2)
        r.s_fs = sem(UNITS)
        r.s_fr = sem(UNITS)
        r.s_fl = sem(UNITS)
        r.s_xs = sem(4, self.S)
        r.s_xr = sem(4, max(self.PH, self.S))
        r.s_gs = sem(2 * self.S)
        r.s_gr = sem(n)
        r.s_ms = sem(n)
        r.s_mr = sem(n)
        r.s_es = sem(4)
        r.s_er = sem(4)
        r.s_ks = sem(2)
        r.s_kr = sem(2)
        return r


INPUTS = 4 + WEIGHTS
OUTPUTS = 2 + WEIGHTS + 1


def kernel(plan, *refs):
    ins, outs = refs[:INPUTS], refs[INPUTS : INPUTS + OUTPUTS]
    scratch = iter(refs[INPUTS + OUTPUTS :])
    r = plan.buffers(lambda shape: next(scratch))
    r.x, r.seg, r.ct, r.small = ins[:4]
    r.h = ins[4:]
    r.o_out, r.o_ig = outs[:2]
    r.o = outs[2:]
    n, Z, S, span = plan.n, plan.Z, plan.S, plan.span
    T, D, FF, H, PH = plan.T, plan.D, plan.FF, plan.HALF, plan.PH
    A, B = plan.A, plan.B
    dp, q = lax.axis_index("dp"), lax.axis_index("seq")
    z, c = dp // 2, dp % 2
    oc = 1 - c

    def aligned(v, m=16):
        return pl.multiple_of(v, m)

    def dev(core, chip, plane=None):
        return ((z if plane is None else plane) * 2 + core, chip)

    sibling = dev(oc, q)

    def remote(src, dst, ss, rs, to):
        return pltpu.make_async_remote_copy(
            src_ref=src, dst_ref=dst, send_sem=ss, recv_sem=rs, device_id=to, device_id_type=MESH
        )

    barrier = pltpu.get_barrier_semaphore()
    for core in range(2):

        def greet(t, _, core=core):
            chip = lax.rem(q + t, n)
            to = (z * 2 + (c + core) % 2, chip)
            pl.semaphore_signal(barrier, inc=1, device_id=to, device_id_type=MESH)
            return 0

        lax.fori_loop(1 - core, n, greet, 0)
    if Z > 1:

        @pl.when(z > 0)
        def _():
            pl.semaphore_signal(barrier, inc=1, device_id=dev(c, q, z - 1), device_id_type=MESH)

        @pl.when(z < Z - 1)
        def _():
            pl.semaphore_signal(barrier, inc=1, device_id=dev(c, q, z + 1), device_id_type=MESH)

    pl.semaphore_wait(barrier, 2 * n - 1 + (z + Z - 1) // Z + (2 * Z - 2 - z) // Z)

    def vrows(ref, w, row0, rows):
        ds = pl.ds(aligned(row0), rows)
        return ref.at[:, ds] if w == CONV else ref.at[ds]

    def bytes_of(view, semaphore):
        return pltpu.make_async_copy(view, view, semaphore)

    def qof(core, f, g):
        f, g = f % B, g % B
        return core * (f * B + g) + (1 - core) * (g * B + f)

    b_, a_ = q % B, q // B
    f_, g_ = c * a_ + oc * b_, c * b_ + oc * a_
    par = z % 2
    partner = dev(c, q, z + 1 - 2 * par)

    def wrows(ref, w, row0, rows, side):
        if w not in plan.shared:
            return vrows(ref, w, row0, rows)
        size = plan.dims[w][1] // 2
        cols = pl.ds(pl.multiple_of(side * size, 128), size)
        return ref.at[pl.ds(aligned(row0), rows), cols]

    def wblock(w, shard, side=par):
        return wrows(r.w[w], w, shard * plan.kr(w) + c * plan.hr(w), plan.hr(w), side)

    def own_block(w):
        return wrows(r.h[w], w, c * plan.hr(w), plan.hr(w), par)

    def copy_a(w, t):
        to = dev(c, qof(c, f_ + t, g_))
        return remote(own_block(w), wblock(w, q), r.s_as.at[w], r.s_ar.at[w, t - 1], to)

    def copy_b(w, u, t):
        blk = wblock(w, qof(c, f_ + B - t, g_))
        src = own_block(w) if t == 0 else blk
        to = dev(c, qof(c, f_, g_ + u))
        return remote(src, blk, r.s_as.at[w], r.s_br.at[w, (u - 1) * B + t], to)

    def shard_from(u, t):
        return qof(c, f_ + B - t, g_ + B - u)

    def pass_on(w, u, t):
        blk = wblock(w, shard_from(u, t))
        remote(blk, blk, r.s_ds.at[w], r.s_dr.at[w], sibling).start()
        if w in plan.shared:
            remote(blk, blk, r.s_hs.at[w], r.s_hr.at[w], partner).start()

    def local_shard(w):
        dst = vrows(r.w[w], w, q * plan.kr(w), plan.kr(w))
        return pltpu.make_async_copy(r.h[w], dst, r.s_loc.at[w])

    def g0(w):
        local_shard(w).start()
        for t in range(1, B):
            copy_a(w, t).start()
        for u in range(1, A):
            copy_b(w, u, 0).start()

    def g1(w):
        for t in range(1, B):
            bytes_of(wblock(w, shard_from(0, t)), r.s_ar.at[w, t - 1]).wait()
            for u in range(1, A):
                copy_b(w, u, t).start()
            pass_on(w, 0, t)

    def g2(w):
        for u in range(1, A):
            for t in range(B):
                bytes_of(wblock(w, shard_from(u, t)), r.s_br.at[w, (u - 1) * B + t]).wait()
                pass_on(w, u, t)

    def others(w):
        return wrows(r.w[w], w, 0, (n - 1) * plan.hr(w), 0)

    def gz(w):
        if w not in plan.shared:
            return
        bytes_of(others(w), r.s_hr.at[w]).wait()
        for u in range(A):
            for t in range(B):
                if (u, t) != (0, 0):
                    blk = wblock(w, shard_from(u, t), 1 - par)
                    remote(blk, blk, r.s_ds.at[w], r.s_dr.at[w], sibling).start()

    def g3(w):
        local_shard(w).wait()
        bytes_of(vrows(r.w[w], w, 0, (n - 1) * plan.hr(w)), r.s_dr.at[w]).wait()

    def gather_sent(w):
        bytes_of(others(w), r.s_as.at[w]).wait()
        bytes_of(vrows(r.w[w], w, 0, (n - 1) * plan.hr(w)), r.s_ds.at[w]).wait()
        if w in plan.shared:
            bytes_of(others(w), r.s_hs.at[w]).wait()

    def token_rows(ref, slot):
        return ref.at[pl.ds(aligned(slot * span), span)]

    def tokens_in(src, dst, k):
        for j in range(S):
            chip, core, slot = S * c + j, q // PH, q % PH
            here = jnp.logical_and(chip == q, core == c)
            there = token_rows(dst, slot)

            @pl.when(here)
            def _():
                pltpu.make_async_copy(src.at[j], there, r.s_xr.at[k, slot]).start()

            @pl.when(jnp.logical_not(here))
            def _():
                remote(
                    src.at[j], there, r.s_xs.at[k, j], r.s_xr.at[k, slot], dev(core, chip)
                ).start()

    def tokens_in_done(dst, k):
        for slot in range(PH):
            blk = token_rows(dst, slot)
            pltpu.make_async_copy(blk, blk, r.s_xr.at[k, slot]).wait()

    def tokens_in_sent(src, dst, k):
        for j in range(S):
            chip, core, slot = S * c + j, q // PH, q % PH
            here = jnp.logical_and(chip == q, core == c)

            @pl.when(jnp.logical_not(here))
            def _():
                remote(
                    src.at[j],
                    token_rows(dst, slot),
                    r.s_xs.at[k, j],
                    r.s_xr.at[k, slot],
                    dev(core, chip),
                ).wait_send()

    def tokens_out(src, dst, k):
        for p in range(PH):
            chip, core, slot = c * PH + p, q // S, q % S
            here = jnp.logical_and(chip == q, core == c)

            @pl.when(here)
            def _():
                pltpu.make_async_copy(token_rows(src, p), dst.at[slot], r.s_xr.at[k, slot]).start()

            @pl.when(jnp.logical_not(here))
            def _():
                remote(
                    token_rows(src, p),
                    dst.at[slot],
                    r.s_xs.at[k, p],
                    r.s_xr.at[k, slot],
                    dev(core, chip),
                ).start()

    def tokens_out_done(src, dst, k):
        for j in range(S):
            pltpu.make_async_copy(dst.at[j], dst.at[j], r.s_xr.at[k, j]).wait()
        for p in range(PH):
            chip, core, slot = c * PH + p, q // S, q % S
            here = jnp.logical_and(chip == q, core == c)

            @pl.when(jnp.logical_not(here))
            def _():
                remote(
                    token_rows(src, p),
                    dst.at[slot],
                    r.s_xs.at[k, p],
                    r.s_xr.at[k, slot],
                    dev(core, chip),
                ).wait_send()

    def seg_send():
        for j in range(S):
            for core in range(2):
                chip = S * c + j
                here = jnp.logical_and(chip == q, c == core)
                i = 2 * j + core

                @pl.when(here)
                def _():
                    pltpu.make_async_copy(r.seg.at[j], r.segbuf.at[q], r.s_gr.at[q]).start()

                @pl.when(jnp.logical_not(here))
                def _():
                    remote(
                        r.seg.at[j],
                        r.segbuf.at[q],
                        r.s_gs.at[i],
                        r.s_gr.at[q],
                        dev(core, chip),
                    ).start()

    def seg_sent():
        for j in range(S):
            for core in range(2):
                chip = S * c + j
                here = jnp.logical_and(chip == q, c == core)

                @pl.when(jnp.logical_not(here))
                def _():
                    remote(
                        r.seg.at[j],
                        r.segbuf.at[q],
                        r.s_gs.at[2 * j + core],
                        r.s_gr.at[q],
                        dev(core, chip),
                    ).wait_send()

    def small_copy(t):
        return remote(
            r.small,
            r.smallbuf.at[q],
            r.s_ms.at[t],
            r.s_mr.at[t],
            dev(c, (q + t) % n),
        )

    def small_arrived(t):
        blk = r.smallbuf.at[(q + n - t) % n]
        return remote(blk, blk, r.s_ms.at[t], r.s_mr.at[t], sibling)

    def edge_copy(i):
        return remote(r.es[i], r.er[i], r.s_es.at[i], r.s_er.at[i], sibling)

    def edge_send(i, last, first):
        r.es[i][...] = jnp.where(c == 0, last, first)
        edge_copy(i).start()

    def edge_take(i):
        edge_copy(i).wait()
        got = r.er[i][...]
        none = jnp.zeros_like(got)
        return jnp.where(c == 1, got, none), jnp.where(c == 0, got, none)

    def columns(u):
        half = UNIT_PART[u]
        if half is None:
            return None
        size = plan.dims[UNIT_WEIGHT[u]][1] // 2
        return pl.ds(half * size, size)

    def urows(ref, u, row0, rows):
        cols = columns(u)
        if cols is None:
            return vrows(ref, UNIT_WEIGHT[u], row0, rows)
        return ref.at[pl.ds(aligned(row0), rows), cols]

    def gpiece(u, shard, half):
        if u == SMALL:
            return r.g8.at[pl.ds(pl.multiple_of(half * 8, 8), 8)]
        w = UNIT_WEIGHT[u]
        row0 = shard * plan.kr(w) + half * plan.hr(w)
        if w == GLU:
            size = plan.D
            cols = pl.ds(2 * D + UNIT_PART[u] * size, size)
            return r.hid.at[pl.ds(aligned(row0), plan.hr(w)), cols]
        return urows(r.dg if w == LEFT else r.w[w], u, row0, plan.hr(w))

    def rpiece(u, shard):
        w = UNIT_WEIGHT[u]
        if u == SMALL:
            return r.r[w]
        return urows(r.r[w], u, shard * plan.hr(w), plan.hr(w))

    def ppiece(u, slot):
        cols = columns(u)
        buf = r.p[UNIT_WEIGHT[u]]
        return buf.at[slot] if cols is None else buf.at[slot, :, cols]

    def zpiece(u, way):
        cols = columns(u)
        buf = (r.u, r.d)[way][UNIT_WEIGHT[u]]
        return buf if cols is None else buf.at[:, cols]

    def copy_r(u, s):
        return remote(gpiece(u, s, oc), rpiece(u, s), r.s_rs.at[u], r.s_rr.at[u], sibling)

    def all_r(u, semaphore):
        w = UNIT_WEIGHT[u]
        view = r.r[w] if u == SMALL else urows(r.r[w], u, 0, n * plan.hr(w))
        return bytes_of(view, semaphore.at[u])

    def shards(u):
        return 1 if u == SMALL else n

    def red0(u):
        for s in range(shards(u)):
            copy_r(u, s).start()

    def plus(a, b):
        return a[...].astype(F32) + b[...].astype(F32)

    def add_core(u, s):
        mine = gpiece(u, s, c)
        mine[...] = plus(mine, rpiece(u, s)).astype(mine.dtype)

    def slot1(u, t):
        return (u - 1) * B + t

    def slot2(t):
        return (A - 1) * B + t - 1

    def copy_p1(u, k, t):
        return remote(
            gpiece(u, qof(c, f_ + t, g_ + k), c),
            ppiece(u, slot1(k, t)),
            r.s_ps.at[u, 0],
            r.s_pr.at[u, 0],
            dev(c, qof(c, f_, g_ + k)),
        )

    def copy_p2(u, t):
        to = qof(c, f_ + t, g_)
        return remote(
            r.r[WEIGHTS] if u == SMALL else gpiece(u, to, c),
            ppiece(u, slot2(t)),
            r.s_ps.at[u, 1],
            r.s_pr.at[u, 1],
            dev(c, to),
        )

    def all_p(u, step, semaphore):
        count = B - 1 if step else A - 1 if u == SMALL else (A - 1) * B
        cols = columns(u)
        buf = r.p[UNIT_WEIGHT[u]]
        view = buf.at[pl.ds(0, count)] if cols is None else buf.at[pl.ds(0, count), :, cols]
        return bytes_of(view, semaphore.at[u, step])

    def red1(u):
        all_r(u, r.s_rr).wait()
        if u == SMALL:
            add_core(u, 0)
            for k in range(1, A):
                copy_p1(u, k, 0).start()
            return

        def send(i, _):
            k, t = i // B + 1, i % B
            add_core(u, qof(c, f_ + t, g_ + k))
            copy_p1(u, k, t).start()
            return 0

        lax.fori_loop(0, (A - 1) * B, send, 0)
        lax.fori_loop(0, B, lambda t, _: (add_core(u, qof(c, f_ + t, g_)), 0)[1], 0)

    def red1b(u):
        all_p(u, 0, r.s_pr).wait()

        def send(t, _):
            if u == SMALL:
                total, to = r.g8[pl.ds(pl.multiple_of(c * 8, 8), 8)], r.r[WEIGHTS]
            else:
                to = gpiece(u, qof(c, f_ + t, g_), c)
                total = to[...].astype(F32)
            for k in range(1, A):
                total = total + ppiece(u, slot1(k, 0 if u == SMALL else t))[...].astype(F32)
            to[...] = total.astype(to.dtype)
            if u != SMALL:
                copy_p2(u, t).start()
            return 0

        if u == SMALL:
            send(0, 0)
            for t in range(1, B):
                copy_p2(u, t).start()
        else:
            lax.fori_loop(1, B, send, 0)

    def red2(u):
        all_p(u, 1, r.s_pr).wait()
        total = (r.r[WEIGHTS] if u == SMALL else gpiece(u, q, c))[...].astype(F32)
        if u != SMALL:
            for k in range(1, A):
                total = total + ppiece(u, slot1(k, 0))[...].astype(F32)
        for t in range(1, B):
            total = total + ppiece(u, slot2(t))[...].astype(F32)
        mine = ppiece(u, 0)
        mine[...] = total.astype(mine.dtype)

    def copy_z(u, way):
        return remote(
            ppiece(u, 1 + way),
            zpiece(u, way),
            r.s_zs.at[u, way],
            r.s_zr.at[u, way],
            dev(c, q, z + 1 if way == 0 else z - 1),
        )

    def red_hop(u, h):
        own, up, down = ppiece(u, 0), ppiece(u, 1), ppiece(u, 2)

        @pl.when(z == h)
        def _():
            if h == 0:
                up[...] = own[...]
            else:
                copy_z(u, 0).wait_recv()
                up[...] = plus(own, zpiece(u, 0)).astype(up.dtype)
            if h < Z - 1:
                copy_z(u, 0).start()

        @pl.when(z == Z - 1 - h)
        def _():
            if h == 0:
                down[...] = own[...]
            else:
                copy_z(u, 1).wait_recv()
                if h < Z - 1:
                    down[...] = plus(own, zpiece(u, 1)).astype(down.dtype)
            if h < Z - 1:
                copy_z(u, 1).start()

    def final_rows(u):
        w = UNIT_WEIGHT[u]
        if u == SMALL:
            return r.o[w].at[pl.ds(pl.multiple_of(c * 8, 8), 8)]
        return urows(r.o[w], u, c * plan.hr(w), plan.hr(w))

    def final_local(u):
        return pltpu.make_async_copy(ppiece(u, 0), final_rows(u), r.s_fl.at[u])

    def final_remote(u):
        return remote(ppiece(u, 0), final_rows(u), r.s_fs.at[u], r.s_fr.at[u], sibling)

    def red_final(u):
        if Z > 1:
            own, up = ppiece(u, 0), ppiece(u, 1)

            @pl.when(z == Z - 1)
            def _():
                own[...] = up[...]

            @pl.when(z < Z - 1)
            def _():
                own[...] = plus(up, zpiece(u, 1)).astype(own.dtype)

        final_local(u).start()
        final_remote(u).start()

    def red_end(u):
        final_local(u).wait()
        final_remote(u).wait()
        all_r(u, r.s_rs).wait()
        all_p(u, 0, r.s_ps).wait()
        all_p(u, 1, r.s_ps).wait()
        if Z > 1:

            @pl.when(z < Z - 1)
            def _():
                copy_z(u, 0).wait_send()

            @pl.when(z > 0)
            def _():
                copy_z(u, 1).wait_send()

    ahead = {}

    def last_hop(u):
        red_hop(u, Z - 1)
        red_final(u)

    def reduce_start(*units):
        for u in units:
            red0(u)
            ahead[u] = [red1, red1b, red2]
            if Z > 1:
                ahead[u] += [lambda k, h=h: red_hop(k, h) for h in range(Z - 1)]
            ahead[u].append(last_hop if Z > 1 else red_final)

    def move(*units):
        for u in units:
            if ahead[u]:
                ahead[u].pop(0)(u)

    def loop(count, body, after=()):
        def step(i, _):
            body(i)
            for k, act in after:
                pl.when(i == k)(act)
            return 0

        lax.fori_loop(0, count, step, 0)

    RB = 256
    NB = T // RB

    def rows_of(i, size=RB, base=0):
        return pl.ds(pl.multiple_of(i * size + base, base or size), size)

    g0(GLU)
    seg_send()
    small_local = pltpu.make_async_copy(r.small, r.smallbuf.at[q], r.s_mr.at[0])
    small_local.start()
    for t in range(1, n):
        small_copy(t).start()
    tokens_in(r.x, r.xin, 0)
    r.g8[...] = jnp.zeros((16, FF), F32)
    g1(GLU)

    for s in range(n):
        blk = r.segbuf.at[s]
        pltpu.make_async_copy(blk, blk, r.s_gr.at[s]).wait()
    for grp in range(n // plan.sr):
        got = r.segbuf[grp * plan.sr]
        for k in range(1, plan.sr):
            got = got + r.segbuf[grp * plan.sr + k]
        r.segrow[:, grp * plan.sw : (grp + 1) * plan.sw] = got
    r.segcol[0:8] = jnp.full((8, 128), -1.0, F32)
    r.segcol[plan.LEN + 8 : plan.LEN + 16] = jnp.full((8, 128), -1.0, F32)
    for k in range(plan.LEN // 128):
        row = r.segrow[0:1, k * 128 : (k + 1) * 128]
        r.segcol[8 + k * 128 : 8 + (k + 1) * 128] = jnp.broadcast_to(row, (128, 128)).T
    r.segloc[...] = r.segcol[pl.ds(pl.multiple_of(c * T, 8), T + 16)]
    r.mext[0 : T + 8] = jnp.where(r.segloc[0 : T + 8] == r.segloc[1 : T + 9], 1.0, 0.0)

    def mask(o, start, rows):
        first = 8 + start + (0 if o > 0 else o)
        return r.mext[first : first + rows]

    small_local.wait()
    for t in range(1, n):
        small_arrived(t).wait_recv()
    for grp in range(n // plan.nr):
        got = r.smallbuf[grp * plan.nr].astype(F32)[0:8, 0 : plan.nw]
        for k in range(1, plan.nr):
            got = got + r.smallbuf[grp * plan.nr + k].astype(F32)[0:8, 0 : plan.nw]
        r.nrm[:, grp * plan.nw : (grp + 1) * plan.nw] = got
    for s in range(n):
        r.midp[:, s * plan.FFn : (s + 1) * plan.FFn] = r.smallbuf[s].astype(F32)[8:24]

    def ln_out(k, v):
        unit, _ = normed(v)
        return (unit * r.nrm[k : k + 1] + r.nrm[4 + k : 5 + k]).astype(BF16)

    def ln_back(k, e, v):
        unit, rs = normed(v)
        eg = e * r.nrm[k : k + 1]
        m1 = jnp.mean(eg, axis=-1, keepdims=True)
        m2 = jnp.mean(eg * unit, axis=-1, keepdims=True)
        cols = slice(k * D, (k + 1) * D)
        r.g8[11:12, cols] += jnp.sum(e * unit, axis=0, keepdims=True)
        r.g8[12:13, cols] += jnp.sum(e, axis=0, keepdims=True)
        return rs * (eg - m1 - unit * m2)

    g0(LEFT)
    g2(GLU)
    g0(CONV)

    def window(b):
        return min(max(b * MB - (MW - MB) // 2 + 16, 0), T + 32 - MW)

    ahead_of = lax.broadcasted_iota(jnp.int32, (MB, MW), 1) - lax.broadcasted_iota(
        jnp.int32, (MB, MW), 0
    )
    for b in range(T // MB):
        home = r.segloc[8 + b * MB : 8 + (b + 1) * MB]
        for o in range(-4, 5):
            there = r.segloc[8 + b * MB + o : 8 + (b + 1) * MB + o]
            same = jnp.where(home == there, 1.0, 0.0)
            hit = ahead_of == b * MB + 16 - window(b) + o
            tap = jnp.where(hit, jnp.concatenate([same] * (MW // 128), axis=1), 0.0)
            r.ms[b, (o + 4) * MB : (o + 5) * MB] = tap.astype(BF16)

    lane = lax.broadcasted_iota(jnp.int32, (1, 128), 1)
    lane_f = lane.astype(F32)
    own_doc = r.segloc[8 : T + 8] == lane_f
    r.qenc[...] = jnp.where(jnp.logical_and(lane < 4, jnp.logical_not(own_doc)), FAR, 0.0).astype(BF16)
    ones = jnp.logical_and(lane >= 4, lane < 7)
    r.kenc[...] = jnp.where(
        jnp.logical_or(r.segcol[8 : plan.LEN + 8] == lane_f, ones), 1.0, 0.0
    ).astype(BF16)

    tokens_in_done(r.xin, 0)
    g3(GLU)
    g1(LEFT)
    g0(POINT)

    def glu(i):
        rows = rows_of(i)
        x = r.xin[rows].astype(F32)
        a1 = ln_out(0, x)
        r.a1[rows] = a1
        value = mm(a1, r.w[GLU][:, 0:D])
        gate = sigmoid(mm(a1, r.w[GLU][:, D : 2 * D]))
        r.sg[rows, 0:D] = gate.astype(BF16)
        r.sg[rows, D : 2 * D] = (value * gate * (1.0 - gate)).astype(BF16)
        y1 = x + value * gate
        r.y1[rows] = y1
        r.a2[rows] = ln_out(1, y1)

    loop(NB, glu, [(0, lambda: g1(CONV))])
    g2(LEFT)
    g2(CONV)
    g3(CONV)

    def conv(i):
        a2 = r.a2[rows_of(i)]
        for o in range(3):
            r.pext[o, rows_of(i, RB, 8)] = mm(a2, r.w[CONV][o])

    loop(NB, conv)
    edge_send(0, r.pext[0, T : T + 8], r.pext[2, 8:16])
    g1(POINT)
    g0(QKV)
    top, bottom = edge_take(0)
    r.pext[0, 0:8] = top
    r.pext[2, T + 8 : T + 16] = bottom
    for k in range(T // 128):
        lo = k * 128
        before = mask(-1, lo, 128)
        after = mask(1, lo, 128)
        pre = (
            r.pext[0, lo + 7 : lo + 135] * jnp.concatenate([before] * (H // 128), axis=1)
            + r.pext[1, lo + 8 : lo + 136]
            + r.pext[2, lo + 9 : lo + 137] * jnp.concatenate([after] * (H // 128), axis=1)
        )
        value, slope = gelu_both(pre)
        r.pext[1, lo + 8 : lo + 136] = value
        r.dgr[lo : lo + 128] = slope.astype(BF16)
    gz(LEFT)
    g3(LEFT)

    CH = 512
    RM = 128

    def left(i):
        rows, erows = rows_of(i, RM), rows_of(i, RM, 8)
        a2 = r.a2[rows]
        for k in range(FF // CH):
            value, slope = gelu_both(mm(a2, r.w[LEFT][:, k * CH : (k + 1) * CH]))
            r.dgl[rows, k * CH : (k + 1) * CH] = slope.astype(BF16)
            r.big[erows, k * CH : (k + 1) * CH] = value
        r.big[erows, 0:H] += r.pext[1, erows]
        unit, rs = normed(r.big[erows])
        r.nm[rows] = unit.astype(BF16)
        r.rm[rows] = rs
        r.hid[rows_of(i, RM, 16)] = (unit * r.midp[0:1] + r.midp[1:2]).astype(BF16)

    def ahead_point():
        g2(POINT)
        g1(QKV)
        g0(OUT)

    loop(T // RM, left, [(1, ahead_point)])
    edge_send(1, r.hid[T : T + 16], r.hid[16:32])
    gz(POINT)
    r.hid[0:16], r.hid[T + 16 : T + 32] = edge_take(1)

    def depthwise(j):
        cols = pl.ds(pl.multiple_of(j * 256, 256), 256)
        for b in range(T // MB):
            near = r.hid[window(b) : window(b) + MW, cols]
            taps = mm(r.ms[b], near)
            total = taps[0:MB] * r.midp[2:3, cols]
            for o in range(1, 9):
                total = total + taps[o * MB : (o + 1) * MB] * r.midp[2 + o : 3 + o, cols]
            r.sep[b * MB : (b + 1) * MB, cols] = total.astype(BF16)

    def ahead_qkv():
        g2(QKV)
        g1(OUT)
        g0(FIN)

    def ahead_out():
        g2(OUT)
        g1(FIN)
        g0(FOUT)

    loop(FF // 256, depthwise, [(1, ahead_qkv), (5, ahead_out)])
    g3(POINT)

    def point(i):
        rows = rows_of(i)
        y2 = r.y1[rows] + mm(r.sep[rows], r.w[POINT][...])
        r.y2[rows] = y2
        r.a4[rows] = ln_out(2, y2)

    loop(NB, point)
    g3(QKV)
    scale = 1.0 / math.sqrt(D // HEADS)

    def qkv(i):
        rows = rows_of(i)
        a4 = r.a4[rows]
        r.qb[rows] = (mm(a4, r.w[QKV][:, 0:D]) * scale).astype(BF16)
        here = pl.ds(pl.multiple_of(c * T + i * RB, RB), RB)
        r.kvb[here, 0:D] = mm(a4, r.w[QKV][:, D : 2 * D]).astype(BF16)
        r.kvb[here, D : 2 * D] = mm(a4, r.w[QKV][:, 2 * D : 3 * D]).astype(BF16)

    loop(NB, qkv)

    def kv_copy():
        blk = r.kvb.at[pl.ds(aligned(c * T), T)]
        return remote(blk, blk, r.s_ks.at[0], r.s_kr.at[0], sibling)

    kv_copy().start()
    tokens_in(r.ct, r.cot, 1)
    heads_lanes = [lane < 64, lane >= 64]
    g2(FIN)
    kv_copy().wait()

    def pair_cols(j, base=0):
        return pl.ds(pl.multiple_of(j * 128 + base, 128), 128)

    def head_lanes(e, v):
        return jnp.where(heads_lanes[e], v, jnp.zeros_like(v))

    def attend(j):
        cols, vcols = pair_cols(j), pair_cols(j, D)
        keys = jnp.concatenate([r.kvb[:, cols], r.kenc[...]], axis=1)
        for k in range(T // RB):
            rows = slice(k * RB, (k + 1) * RB)
            q2 = r.qb[rows, cols]
            got = []
            for e in range(2):
                score = mm_t(jnp.concatenate([head_lanes(e, q2), r.qenc[rows]], axis=1), keys)
                most = jnp.max(score, axis=-1, keepdims=True)
                power = jnp.exp(score - most)
                total = jnp.sum(power, axis=-1, keepdims=True)
                got.append(mm(power.astype(BF16), r.kvb[:, vcols]) / total)
                lse = most + jnp.log(total)
                r.lse[rows] = jnp.where(lane == 2 * j + e, lse, r.lse[rows])
            r.ctx[rows, cols] = jnp.where(heads_lanes[0], got[0], got[1]).astype(BF16)

    r.lse[...] = jnp.zeros((T, 128), F32)

    loop(
        HEADS // 2,
        attend,
        [(0, lambda: g1(FOUT)), (1, lambda: gz(FIN)), (2, lambda: g2(FOUT))],
    )
    g3(OUT)

    def out(i):
        rows = rows_of(i)
        y3 = r.y2[rows] + mm(r.ctx[rows], r.w[OUT][...])
        r.y3[rows] = y3
        r.a5[rows] = ln_out(3, y3)

    loop(NB, out)
    g3(FIN)

    def ffn_in(i):
        rows = rows_of(i)
        a5 = r.a5[rows]
        for k in range(FF // CH):
            value, slope = gelu_both(mm(a5, r.w[FIN][:, k * CH : (k + 1) * CH]))
            r.hid[rows, k * CH : (k + 1) * CH] = value.astype(BF16)
            r.dg[rows, k * CH : (k + 1) * CH] = slope.astype(BF16)

    loop(NB, ffn_in, [(0, lambda: gz(FOUT))])
    g3(FOUT)

    def ffn_out(i):
        rows = rows_of(i)
        r.osend[rows] = (r.y3[rows] + mm(r.hid[rows], r.w[FOUT][...])).astype(BF16)

    loop(NB, ffn_out)
    tokens_out(r.osend, r.o_out, 2)
    for w in range(WEIGHTS):
        gather_sent(w)

    tokens_in_done(r.cot, 1)

    def ffn_back(i):
        rows = rows_of(i)
        f4 = r.cot[rows]
        for k in range(FF // CH):
            cols = slice(k * CH, (k + 1) * CH)
            up = mm_t(f4, r.w[FOUT][cols])
            r.dg[rows, cols] = (up * r.dg[rows, cols].astype(F32)).astype(BF16)
        e = mm_t(r.dg[rows], r.w[FIN][...])
        r.gs[rows] = f4.astype(F32) + ln_back(3, e, r.y3[rows])

    loop(NB, ffn_back)
    GC = 256

    def grad_outer(k):
        cols = rows_of(k, GC)
        r.w[FOUT][cols] = mm_tn(r.hid[0:T, cols], r.cot[...]).astype(BF16)

    loop(FF // GC, grad_outer)
    reduce_start(U_FOUT)
    r.tr[...] = r.a5[...].T

    def grad_inner(k):
        cols = rows_of(k, GC)
        r.w[FIN][:, cols] = mm(r.tr[...], r.dg[:, cols]).astype(BF16)

    loop(FF // GC, grad_inner)
    reduce_start(U_FIN)
    move(U_FOUT)

    def out_back(i):
        rows = rows_of(i)
        f3 = r.gs[rows].astype(BF16)
        r.a5[rows] = f3
        r.hid[rows, 3 * D : 4 * D] = mm_t(f3, r.w[OUT][...]).astype(BF16)

    loop(NB, out_back)
    r.w[OUT][...] = mm_tn(r.ctx[...], r.a5[...]).astype(BF16)
    reduce_start(U_OUT)

    QB = 256

    def with_terms(extra, v):
        high = v.astype(BF16).astype(F32)
        mid = (v - high).astype(BF16).astype(F32)
        low = v - high - mid
        terms = jnp.where(lane == 4, high, jnp.where(lane == 5, mid, jnp.where(lane == 6, low, 0.0)))
        return extra - terms.astype(BF16)

    def attend_back(j):
        cols, vcols = pair_cols(j), pair_cols(j, D)
        k2 = r.kvb[:, cols]
        keys = jnp.concatenate([k2, r.kenc[...]], axis=1)
        values = jnp.concatenate([r.kvb[:, vcols], r.kenc[...]], axis=1)
        for k in range(T // QB):
            rows = slice(k * QB, (k + 1) * QB)
            q2 = r.qb[rows, cols]
            d2 = r.hid[rows, pair_cols(j, 3 * D)]
            inner = d2.astype(F32) * r.ctx[rows, cols].astype(F32)
            dq = jnp.zeros((QB, 128), F32)
            for e in range(2):
                qe, de = head_lanes(e, q2), head_lanes(e, d2)
                lse = jnp.sum(
                    jnp.where(lane == 2 * j + e, r.lse[rows], 0.0), axis=-1, keepdims=True
                )
                delta = jnp.sum(head_lanes(e, inner), axis=-1, keepdims=True)
                shifted = mm_t(keys, jnp.concatenate([qe, with_terms(r.qenc[rows], lse)], axis=1))
                probs = jnp.exp(shifted)
                none = jnp.zeros((QB, 128), BF16)
                moved = mm_t(values, jnp.concatenate([de, with_terms(none, delta)], axis=1))
                ds = (probs * moved).astype(BF16)
                dk = mm(ds, qe)
                dv = mm(probs.astype(BF16), de)
                for kk in range(2):
                    half = slice(kk * T, (kk + 1) * T)
                    at = 2 * D + kk * 128
                    if k == 0 and e == 0:
                        r.big[0:T, at : at + 128] = dk[half]
                        r.big[0:T, at + 256 : at + 384] = dv[half]
                    else:
                        r.big[0:T, at : at + 128] += dk[half]
                        r.big[0:T, at + 256 : at + 384] += dv[half]
                dq = dq + mm_tn(ds, head_lanes(e, k2))
            r.hid[rows, cols] = (dq * scale).astype(BF16)

        def part(core, what):
            at = pl.multiple_of(2 * D + core * 128 + what * 256, 128)
            return r.big[0:T, pl.ds(at, 128)]

        r.big[0:T, cols] = part(c, 0)
        r.big[0:T, vcols] = part(c, 1)
        r.dg[:, cols] = part(oc, 0).astype(BF16)
        r.dg[:, vcols] = part(oc, 1).astype(BF16)

    loop(
        HEADS // 2,
        attend_back,
        [
            (0, lambda: move(U_FIN)),
            (1, lambda: move(U_FOUT)),
            (2, lambda: move(U_OUT)),
            (3, lambda: move(U_FOUT, U_FOUT, U_FIN)),
        ],
    )

    def dkv_copy():
        return remote(
            r.dg.at[:, pl.ds(0, 2 * D)], r.dkvr, r.s_ks.at[1], r.s_kr.at[1], sibling
        )

    dkv_copy().start()
    dkv_copy().wait()
    move(U_OUT)

    def qkv_back(i):
        rows = rows_of(i)
        total = r.big[rows, 0 : 2 * D] + r.dkvr[rows].astype(F32)
        r.hid[rows, D : 3 * D] = total.astype(BF16)
        e = mm_t(r.hid[rows, 0 : 3 * D], r.w[QKV][...])
        r.gs[rows] += ln_back(2, e, r.y2[rows])

    loop(NB, qkv_back)
    r.tr[...] = r.a4[...].T

    def grad_qkv(k):
        cols = rows_of(k, GC)
        r.w[QKV][:, cols] = mm(r.tr[...], r.hid[0:T, cols]).astype(BF16)

    loop(3 * D // GC, grad_qkv)
    reduce_start(U_QKV)

    def point_back(i):
        rows = rows_of(i)
        f2 = r.gs[rows].astype(BF16)
        r.a4[rows] = f2
        for k in range(FF // CH):
            cols = slice(k * CH, (k + 1) * CH)
            d = mm_t(f2, r.w[POINT][cols])
            r.hid[rows_of(i, RB, 16), cols] = d.astype(BF16)

    loop(NB, point_back)
    edge_send(2, r.hid[T : T + 16], r.hid[16:32])
    move(U_FIN, U_FIN, U_QKV)

    def grad_point(k):
        cols = rows_of(k, GC)
        r.w[POINT][cols] = mm_tn(r.sep[:, cols], r.a4[...]).astype(BF16)

    loop(FF // GC, grad_point)
    reduce_start(U_POINT0, U_POINT1)
    move(U_FOUT, U_OUT, U_OUT)
    r.hid[0:16], r.hid[T + 16 : T + 32] = edge_take(2)

    def depth_back(j):
        cols = pl.ds(pl.multiple_of(j * 256, 256), 256)
        gain, shift = r.midp[0:1, cols], r.midp[1:2, cols]
        sums = [jnp.zeros((8, 256), F32) for _ in range(9)]
        for b in range(T // MB):
            lo = b * MB
            taps = mm(r.ms[b], r.hid[window(b) : window(b) + MW, cols])
            a3 = r.nm[lo : lo + MB, cols].astype(F32) * gain + shift
            total = jnp.zeros((MB, 256), F32)
            for o in range(9):
                moved = taps[(8 - o) * MB : (9 - o) * MB]
                total = total + moved * r.midp[2 + o : 3 + o, cols]
                part = moved * a3
                for g in range(MB // 8):
                    sums[o] = sums[o] + part[g * 8 : (g + 1) * 8]
            r.big[lo + 8 : lo + 8 + MB, cols] = total
        for o in range(9):
            r.g8[2 + o : 3 + o, cols] = jnp.sum(sums[o], axis=0, keepdims=True)

    loop(
        FF // 256,
        depth_back,
        [
            (1, lambda: move(U_POINT0)),
            (2, lambda: move(U_POINT1)),
            (3, lambda: move(U_OUT)),
            (4, lambda: move(U_QKV, U_FOUT)),
            (6, lambda: move(U_FIN)),
            (7, lambda: move(U_POINT0, U_OUT)),
        ],
    )

    def mid_back(i):
        rows, erows = rows_of(i, RM), rows_of(i, RM, 8)
        e = r.big[erows]
        unit = r.nm[rows].astype(F32)
        eg = e * r.midp[0:1]
        m1 = jnp.mean(eg, axis=-1, keepdims=True)
        m2 = jnp.mean(eg * unit, axis=-1, keepdims=True)
        r.g8[0:1] += jnp.sum(e * unit, axis=0, keepdims=True)
        r.g8[1:2] += jnp.sum(e, axis=0, keepdims=True)
        dmid = r.rm[rows] * (eg - m1 - unit * m2)
        r.dgl[rows] = (dmid * r.dgl[rows].astype(F32)).astype(BF16)
        right = dmid[:, 0:H] * r.dgr[rows].astype(F32)
        r.pext[0, erows] = right.astype(BF16).astype(F32)

    loop(T // RM, mid_back)
    edge_send(3, r.pext[0, T : T + 8], r.pext[0, 8:16])
    move(U_QKV, U_QKV, U_POINT1)
    r.tr[...] = r.a2[...].T

    def grad_left(k):
        cols = rows_of(k, GC)
        r.dg[:, cols] = mm(r.tr[...], r.dgl[:, cols]).astype(BF16)

    for half in range(2):
        lax.fori_loop(
            half * (FF // GC // 2), (half + 1) * (FF // GC // 2), lambda k, _: (grad_left(k), 0)[1], 0
        )
        reduce_start((U_LEFT0, U_LEFT1)[half])
        move((U_FIN, U_FOUT)[half])
    move(U_LEFT0, U_POINT0, U_POINT0, U_OUT)
    top, bottom = edge_take(3)
    r.pext[0, 0:8] = top
    r.pext[0, T + 8 : T + 16] = bottom
    for k in range(T // 128):
        lo = k * 128
        for o in (-1, 0, 1):
            moved = r.pext[0, lo + 8 - o : lo + 136 - o]
            if o:
                moved = moved * jnp.concatenate([mask(-o, lo, 128)] * (H // 128), axis=1)
            r.hid[lo : lo + 128, (o + 1) * H : (o + 2) * H] = moved.astype(BF16)

    def branch_back(i):
        rows = rows_of(i)
        e = mm_t(r.dgl[rows], r.w[LEFT][...])
        for o in range(3):
            e = e + mm_t(r.hid[rows, o * H : (o + 1) * H], r.w[CONV][o])
        r.gs[rows] += ln_back(1, e, r.y1[rows])

    loop(NB, branch_back, [(0, lambda: move(U_LEFT1)), (1, lambda: move(U_LEFT0, U_POINT1, U_POINT1))])
    for o in range(3):
        r.w[CONV][o] = mm(r.tr[...], r.hid[0:T, o * H : (o + 1) * H]).astype(BF16)
    reduce_start(U_CONV)

    def gate_back(i):
        rows = rows_of(i)
        g = r.gs[rows]
        r.sg[rows, 0:D] = (g * r.sg[rows, 0:D].astype(F32)).astype(BF16)
        r.sg[rows, D : 2 * D] = (g * r.sg[rows, D : 2 * D].astype(F32)).astype(BF16)

    loop(NB, gate_back)
    r.tr[...] = r.a1[...].T

    def grad_glu(k):
        cols = rows_of(k, GC)
        to = pl.ds(pl.multiple_of(k * GC + 2 * D, GC), GC)
        r.hid[0:T, to] = mm(r.tr[...], r.sg[:, cols]).astype(BF16)

    loop(2 * D // GC, grad_glu)
    move(U_CONV)
    reduce_start(U_GLU0, U_GLU1)
    move(U_QKV)

    def glu_back(i):
        rows = rows_of(i)
        e = mm_t(r.sg[rows], r.w[GLU][...])
        total = r.gs[rows] + ln_back(0, e, r.xin[rows].astype(F32))
        r.a5[rows] = total.astype(BF16)

    loop(NB, glu_back)
    reduce_start(SMALL)
    move(U_GLU0, U_GLU1, SMALL, U_LEFT0, U_LEFT0, U_LEFT1, U_POINT0, U_POINT1, U_CONV)
    move(U_LEFT1, U_LEFT1, U_GLU0, U_GLU1, SMALL, U_QKV, U_LEFT0, U_POINT0, U_CONV, U_CONV)
    move(U_POINT1, U_GLU0, U_GLU0, U_LEFT1, U_GLU1, U_GLU1, SMALL, SMALL, U_LEFT0, U_CONV)
    tokens_out(r.a5, r.o_ig, 3)
    move(U_GLU0, U_LEFT1, U_GLU1, SMALL, U_CONV, U_GLU0, U_GLU1, SMALL)
    move(U_FIN, U_QKV, U_POINT0, U_POINT1, U_LEFT0, U_LEFT1, U_CONV, U_GLU0, U_GLU1, SMALL)
    while any(ahead.values()):
        move(*range(UNITS))

    for u in range(UNITS):
        red_end(u)
    tokens_out_done(r.osend, r.o_out, 2)
    tokens_out_done(r.a5, r.o_ig, 3)
    tokens_in_sent(r.x, r.xin, 0)
    tokens_in_sent(r.ct, r.cot, 1)
    seg_sent()
    for t in range(1, n):
        small_copy(t).wait_send()


def local(
    inputs,
    segment_ids,
    cotangent,
    norm_gain,
    norm_bias,
    glu_weight,
    left_weight,
    conv_weight,
    mid_gain,
    mid_bias,
    depth_weight,
    point_weight,
    qkv_weight,
    out_weight,
    ffn_in,
    ffn_out,
):
    seqs, span, width = inputs.shape
    n = lax.axis_size("seq")
    plan = Plan(
        lax.axis_size("dp"), n, seqs, span, width, ffn_in.shape[1], conv_weight.shape[2]
    )
    q = lax.axis_index("seq")

    def placed(piece, repeats):
        if repeats == 1:
            return piece
        size = piece.shape[-1]
        tiled = jnp.tile(piece, (1,) * (piece.ndim - 1) + (repeats,))
        at = lax.broadcasted_iota(jnp.int32, tiled.shape, tiled.ndim - 1) // size
        return jnp.where(at == q % repeats, tiled, jnp.zeros_like(tiled))

    segs = placed(segment_ids.astype(F32), plan.sr)
    segs = jnp.broadcast_to(segs[:, None, :], (seqs, 8, plan.sw))
    norms = placed(jnp.concatenate([norm_gain, norm_bias], 0), plan.nr)
    norms = jnp.pad(norms, ((0, 0), (0, plan.FFn - plan.nw)))
    small = jnp.concatenate([norms, mid_gain[None], mid_bias[None], depth_weight], 0)
    small = jnp.pad(small, ((0, 32 - small.shape[0]), (0, 0)))
    weights = [None] * WEIGHTS
    weights[GLU], weights[CONV], weights[LEFT] = glu_weight, conv_weight, left_weight
    weights[POINT], weights[QKV], weights[OUT] = point_weight, qkv_weight, out_weight
    weights[FIN], weights[FOUT] = ffn_in, ffn_out

    shapes = []
    plan.buffers(shapes.append)
    out_shape = [jax.ShapeDtypeStruct(inputs.shape, BF16)] * 2
    out_shape += [jax.ShapeDtypeStruct(w.shape, BF16) for w in weights]
    out_shape += [jax.ShapeDtypeStruct((16, plan.FF), F32)]
    hbm = pl.BlockSpec(memory_space=pl.ANY)
    got = pl.pallas_call(
        lambda *refs: kernel(plan, *refs),
        out_shape=out_shape,
        in_specs=[hbm] * INPUTS,
        out_specs=[hbm] * OUTPUTS,
        scratch_shapes=shapes,
        compiler_params=pltpu.CompilerParams(
            collective_id=0, has_side_effects=True, vmem_limit_bytes=64 << 20
        ),
        name="cell",
    )(inputs, segs, cotangent, small, *weights)
    out = unpacked(plan, got)
    return (
        out[0],
        out[1],
        out[2 + WEIGHTS],
        out[3 + WEIGHTS],
        out[2 + GLU],
        out[2 + LEFT],
        out[2 + CONV],
        out[4 + WEIGHTS].reshape(-1),
        out[5 + WEIGHTS].reshape(-1),
        out[6 + WEIGHTS],
        out[2 + POINT],
        out[2 + QKV],
        out[2 + OUT],
        out[2 + FIN],
        out[2 + FOUT],
    )


def unpacked(plan, parts):
    count = 2 + WEIGHTS
    dn = plan.D // plan.n
    wide = [jax.ShapeDtypeStruct(p.shape, F32) for p in parts[:count]]
    tiny = [(4, dn), (4, dn), (1, plan.FFn), (1, plan.FFn), (9, plan.FFn)]
    out_shape = wide + [jax.ShapeDtypeStruct(shape, F32) for shape in tiny]

    def body(*refs):
        ins, outs = refs[:count], refs[count + 1 : 2 * count + 1]
        sums, tinies = refs[count], refs[2 * count + 1 : 2 * count + 6]
        near, far = refs[2 * count + 6 : 3 * count + 6], refs[3 * count + 6 : 4 * count + 6]
        came, went = refs[4 * count + 6], refs[4 * count + 7]

        def arrive(i):
            return pltpu.make_async_copy(ins[i], near[i], came.at[i])

        def leave(i):
            return pltpu.make_async_copy(far[i], outs[i], went.at[i])

        for i in range(count):
            arrive(i).start()
        q = lax.axis_index("seq")
        rolled = pltpu.roll(sums[...], (plan.FF - q * plan.FFn) % plan.FF, 1)[:, 0 : plan.FFn]
        tinies[2][...] = rolled[0:1]
        tinies[3][...] = rolled[1:2]
        tinies[4][...] = rolled[2:11]
        for k in range(2):
            row = sums[11 + k : 12 + k]
            rows = [row[:, i * plan.D : (i + 1) * plan.D] for i in range(4)]
            both = jnp.concatenate(rows + rows, axis=0)
            tinies[k][...] = pltpu.roll(both, (plan.D - q * dn) % plan.D, 1)[0:4, 0:dn]
        for i in range(count):
            arrive(i).wait()
            far[i][...] = near[i][...].astype(F32)
            leave(i).start()
        for i in range(count):
            leave(i).wait()

    hbm = pl.BlockSpec(memory_space=pl.ANY)
    vmem = pl.BlockSpec(memory_space=pltpu.VMEM)
    return pl.pallas_call(
        body,
        out_shape=out_shape,
        in_specs=[hbm] * count + [vmem],
        out_specs=[hbm] * count + [vmem] * len(tiny),
        scratch_shapes=[pltpu.VMEM(p.shape, BF16) for p in parts[:count]]
        + [pltpu.VMEM(p.shape, F32) for p in parts[:count]]
        + [pltpu.SemaphoreType.DMA((count,))] * 2,
        compiler_params=pltpu.CompilerParams(vmem_limit_bytes=64 << 20),
    )(*parts)


def solution(mesh):
    in_specs = (
        P("dp", "seq", None),
        P("dp", "seq"),
        P("dp", "seq", None),
        P(None, "seq"),
        P(None, "seq"),
        P("seq", None),
        P("seq", None),
        P(None, "seq", None),
        P("seq"),
        P("seq"),
        P(None, "seq"),
        P("seq", None),
        P("seq", None),
        P("seq", None),
        P("seq", None),
        P("seq", None),
    )
    out_specs = (
        P("dp", "seq", None),
        P("dp", "seq", None),
        P(None, "seq"),
        P(None, "seq"),
        P("seq", None),
        P("seq", None),
        P(None, "seq", None),
        P("seq"),
        P("seq"),
        P(None, "seq"),
        P("seq", None),
        P("seq", None),
        P("seq", None),
        P("seq", None),
        P("seq", None),
    )
    return jax.shard_map(local, mesh=mesh, in_specs=in_specs, out_specs=out_specs, check_vma=False)
```

```python
import math

import jax
import jax.numpy as jnp
from jax import lax
from jax.experimental import pallas as pl
from jax.experimental.pallas import tpu as pltpu
from jax.sharding import PartitionSpec as P

HEADS = 8
EPS = 1e-06
MESH = pl.DeviceIdType.MESH
F32 = jnp.float32
BF16 = jnp.bfloat16

GLU, CONV, LEFT, POINT, QKV, OUT, FIN, FOUT = range(8)
WEIGHTS = 8
(U_GLU0, U_GLU1, U_CONV, U_LEFT0, U_LEFT1, U_POINT0, U_POINT1, U_QKV0, U_QKV1, U_OUT, U_FIN, U_FOUT, SMALL) = range(13)
UNITS = 13
UNIT_WEIGHT = (GLU, GLU, CONV, LEFT, LEFT, POINT, POINT, QKV, QKV, OUT, FIN, FOUT, WEIGHTS)
UNIT_PART = (0, 1, None, 0, 1, 0, 1, 0, 1, None, None, None, None)

SCHEDULE = (
    (),
    (),
    (U_FOUT,),
    (U_FIN, U_OUT,),
    (U_FOUT,),
    (),
    (U_FOUT, U_FIN, U_OUT,),
    (U_QKV0,),
    (U_QKV1, U_FIN,),
    (U_OUT, U_FOUT, U_QKV0,),
    (),
    (U_QKV1, U_POINT0,),
    (U_QKV0, U_POINT1,),
    (U_FIN,),
    (U_QKV1, U_OUT,),
    (),
    (U_FOUT, U_QKV0, U_POINT0,),
    (),
    (),
    (U_QKV1, U_POINT1,),
    (),
    (U_POINT0,),
    (U_FIN,),
    (U_OUT, U_POINT1,),
    (U_QKV0, U_LEFT0,),
    (U_POINT0, U_LEFT1,),
    (U_QKV1, U_CONV,),
    (U_POINT1,),
    (),
    (U_LEFT0,),
    (U_POINT0, U_GLU0, U_GLU1,),
)
TAIL = (
    (SMALL, U_LEFT1, U_POINT1, U_CONV, U_LEFT0, U_GLU0, U_GLU1, SMALL),
    (U_LEFT1, U_LEFT0, U_CONV, U_GLU0, U_GLU1, SMALL, U_LEFT1, U_LEFT0, U_CONV, U_GLU0, U_GLU1, U_LEFT1, SMALL, U_CONV, U_GLU0, U_GLU1, SMALL, U_FOUT, U_FIN, U_OUT, U_QKV0, U_QKV1, U_POINT0, U_POINT1, U_LEFT0, U_LEFT1, U_CONV, U_GLU0, U_GLU1, SMALL),
)

MB, MW = 128, 256
FAR = -(2.0**30)


def mm(a, b):
    return lax.dot_general(a, b, (((1,), (0,)), ((), ())), preferred_element_type=F32)


def mm_t(a, b):
    return lax.dot_general(a, b, (((1,), (1,)), ((), ())), preferred_element_type=F32)


def mm_tn(a, b):
    return lax.dot_general(a, b, (((0,), (0,)), ((), ())), preferred_element_type=F32)


def normed(v):
    centred = v - jnp.mean(v, axis=-1, keepdims=True)
    r = lax.rsqrt(jnp.mean(centred * centred, axis=-1, keepdims=True) + EPS)
    return centred * r, r


def gelu_both(v):
    c = math.sqrt(2.0 / math.pi)
    sq = v * v
    t = jnp.tanh(v * (c + (c * 0.044715) * sq))
    half = 0.5 * t + 0.5
    value = v * half
    slope = half + (0.5 * v) * (1.0 - t * t) * (c + (3.0 * c * 0.044715) * sq)
    return value, slope


def sigmoid(v):
    return 0.5 * jnp.tanh(0.5 * v) + 0.5


class Buffers:
    pass


class Plan:
    def __init__(self, dp, n, seqs, span, width, hidden, half):
        self.n, self.Z = n, dp // 2
        self.S, self.span = seqs, span
        self.D, self.FF, self.HALF = width, hidden, half
        self.LEN = span * n
        self.T = self.LEN // 2
        self.PH = n // 2
        self.B = math.isqrt(n)
        self.A = n // self.B
        assert self.A == self.B and n == 2 * seqs and dp % 2 == 0
        self.shared = (LEFT, POINT, FIN, FOUT) if self.Z % 2 == 0 else ()
        self.sw = max(span, 128)
        self.sr = self.sw // span
        dn = width // n
        self.nw = max(dn, 128)
        self.nr = self.nw // dn
        self.FFn = hidden // n
        self.dims = [
            (width, 2 * width),
            (width, half),
            (width, hidden),
            (hidden, width),
            (width, 3 * width),
            (width, width),
            (width, hidden),
            (hidden, width),
        ]

    def whole(self, w):
        k, cols = self.dims[w]
        return (3, k, cols) if w == CONV else (k, cols)

    def kr(self, w):
        return self.dims[w][0] // self.n

    def hr(self, w):
        return self.kr(w) // 2

    def gcols(self, w):
        return self.dims[w][1] * (3 if w == CONV else 1)

    def piece(self, w, rows):
        return (rows, self.gcols(w))

    def buffers(self, take):
        T, D, FF, H, n = self.T, self.D, self.FF, self.HALF, self.n
        r = Buffers()

        def vm(shape, dtype):
            return take(pltpu.VMEM(shape, dtype))

        def sem(*shape):
            return take(pltpu.SemaphoreType.DMA(shape))

        every = range(WEIGHTS)
        parts = [(self.piece(w, self.hr(w)), BF16) for w in every] + [((16, FF // 2), BF16)]
        r.w = [vm(self.whole(w), BF16) for w in every]
        r.g8 = vm((16, FF), F32)
        r.gsm = vm((32, FF // 2), BF16)
        r.r = [None] * WEIGHTS + [vm((16, FF // 2), BF16)]
        for w in (CONV, QKV, OUT, FIN, FOUT):
            r.r[w] = vm(self.piece(w, n * self.hr(w)), BF16)
        r.r[LEFT], r.r[POINT], r.r[GLU] = r.r[FIN], r.r[FOUT], r.r[QKV]
        r.p = [vm((n - 1,) + shape, dtype) for shape, dtype in parts]
        if self.Z > 1:
            r.u = [vm(shape, dtype) for shape, dtype in parts]
            r.d = [vm(shape, dtype) for shape, dtype in parts]
        r.segbuf = vm((n, 8, self.sw), F32)
        r.segrow = vm((8, self.LEN), F32)
        r.segcol = vm((self.LEN + 16, 128), F32)
        r.segloc = vm((T + 16, 128), F32)
        r.mext = vm((T + 16, 128), F32)
        r.ms = vm((T // MB, 9 * MB, MW), BF16)
        r.qenc = vm((T, 128), BF16)
        r.kenc = vm((self.LEN, 128), BF16)
        r.smallbuf = vm((n, 32, self.FFn), BF16)
        r.nrm = vm((8, D), F32)
        r.midp = vm((16, FF), F32)
        r.xin = vm((T, D), BF16)
        r.cot = vm((T, D), BF16)
        r.a1 = vm((T, D), BF16)
        r.sg = vm((T, 2 * D), BF16)
        r.y1 = vm((T, D), F32)
        r.a2 = vm((T, D), BF16)
        r.pext = vm((3, T + 16, H), F32)
        r.dgl = vm((T, FF), BF16)
        r.dgr = vm((T, H), BF16)
        r.nm = vm((T, FF), BF16)
        r.rm = vm((T, 1), F32)
        r.big = vm((T + 16, FF), F32)
        r.sep = vm((T, FF), BF16)
        r.y2 = vm((T, D), F32)
        r.a4 = vm((T, D), BF16)
        r.qb = vm((T, D), BF16)
        r.kvb = vm((self.LEN, 2 * D), BF16)
        r.lse = vm((T, 128), F32)
        r.ctx = vm((T, D), BF16)
        r.y3 = vm((T, D), F32)
        r.a5 = vm((T, D), BF16)
        r.hid = vm((T + 32, FF), BF16)
        r.dg = vm((T, FF), BF16)
        r.osend = vm((T, D), BF16)
        r.gs = r.y3
        r.dkvr = vm((T, 2 * D), BF16)
        r.tr = vm((D, T), BF16)
        edges = (((8, H), F32), ((16, FF), BF16), ((16, FF), BF16), ((8, H), F32))
        r.es = [vm(shape, dtype) for shape, dtype in edges]
        r.er = [vm(shape, dtype) for shape, dtype in edges]
        r.s_loc = sem(WEIGHTS)
        r.s_as = sem(WEIGHTS)
        r.s_ar = sem(WEIGHTS, self.B - 1)
        r.s_br = sem(WEIGHTS, (self.A - 1) * self.B)
        r.s_ds = sem(WEIGHTS)
        r.s_dr = sem(WEIGHTS)
        if self.shared:
            r.s_hs = sem(WEIGHTS)
            r.s_hr = sem(WEIGHTS)
        r.s_rs = sem(UNITS)
        r.s_rr = sem(UNITS)
        r.s_ps = sem(UNITS, 2)
        r.s_pr = sem(UNITS, 2)
        if self.Z > 1:
            r.s_zs = sem(UNITS, 2)
            r.s_zr = sem(UNITS, 2)
        r.s_fs = sem(UNITS)
        r.s_fr = sem(UNITS)
        r.s_fl = sem(UNITS)
        r.s_xs = sem(4, self.S)
        r.s_xr = sem(4, max(self.PH, self.S))
        r.s_gs = sem(2 * self.S)
        r.s_gr = sem(n)
        r.s_ms = sem(n)
        r.s_mr = sem(n)
        r.s_es = sem(4)
        r.s_er = sem(4)
        r.s_ks = sem(1)
        r.s_kr = sem(1)
        r.s_js = sem(HEADS // 2)
        r.s_jr = sem(HEADS // 2)
        return r


INPUTS = 4 + WEIGHTS
OUTPUTS = 2 + WEIGHTS + 1


def kernel(plan, *refs):
    ins, outs = refs[:INPUTS], refs[INPUTS : INPUTS + OUTPUTS]
    scratch = iter(refs[INPUTS + OUTPUTS :])
    r = plan.buffers(lambda shape: next(scratch))
    r.x, r.seg, r.ct, r.small = ins[:4]
    r.h = ins[4:]
    r.o_out, r.o_ig = outs[:2]
    r.o = outs[2:]
    n, Z, S, span = plan.n, plan.Z, plan.S, plan.span
    T, D, FF, H, PH = plan.T, plan.D, plan.FF, plan.HALF, plan.PH
    A, B = plan.A, plan.B
    dp, q = lax.axis_index("dp"), lax.axis_index("seq")
    z, c = dp // 2, dp % 2
    oc = 1 - c

    def aligned(v, m=16):
        return pl.multiple_of(v, m)

    def dev(core, chip, plane=None):
        return ((z if plane is None else plane) * 2 + core, chip)

    sibling = dev(oc, q)

    def remote(src, dst, ss, rs, to):
        return pltpu.make_async_remote_copy(
            src_ref=src, dst_ref=dst, send_sem=ss, recv_sem=rs, device_id=to, device_id_type=MESH
        )

    barrier = pltpu.get_barrier_semaphore()
    for core in range(2):

        def greet(t, _, core=core):
            chip = lax.rem(q + t, n)
            to = (z * 2 + (c + core) % 2, chip)
            pl.semaphore_signal(barrier, inc=1, device_id=to, device_id_type=MESH)
            return 0

        lax.fori_loop(1 - core, n, greet, 0)
    if Z > 1:

        @pl.when(z > 0)
        def _():
            pl.semaphore_signal(barrier, inc=1, device_id=dev(c, q, z - 1), device_id_type=MESH)

        @pl.when(z < Z - 1)
        def _():
            pl.semaphore_signal(barrier, inc=1, device_id=dev(c, q, z + 1), device_id_type=MESH)

    pl.semaphore_wait(barrier, 2 * n - 1 + (z + Z - 1) // Z + (2 * Z - 2 - z) // Z)

    def vrows(ref, w, row0, rows):
        ds = pl.ds(aligned(row0), rows)
        return ref.at[:, ds] if w == CONV else ref.at[ds]

    def bytes_of(view, semaphore):
        return pltpu.make_async_copy(view, view, semaphore)

    def qof(core, f, g):
        f, g = f % B, g % B
        return core * (f * B + g) + (1 - core) * (g * B + f)

    b_, a_ = q % B, q // B
    f_, g_ = c * a_ + oc * b_, c * b_ + oc * a_
    par = z % 2
    partner = dev(c, q, z + 1 - 2 * par)

    def wrows(ref, w, row0, rows, side):
        if w not in plan.shared:
            return vrows(ref, w, row0, rows)
        size = plan.dims[w][1] // 2
        cols = pl.ds(pl.multiple_of(side * size, 128), size)
        return ref.at[pl.ds(aligned(row0), rows), cols]

    def wblock(w, shard, side=par):
        return wrows(r.w[w], w, shard * plan.kr(w) + c * plan.hr(w), plan.hr(w), side)

    def own_block(w):
        return wrows(r.h[w], w, c * plan.hr(w), plan.hr(w), par)

    def copy_a(w, t):
        to = dev(c, qof(c, f_ + t, g_))
        return remote(own_block(w), wblock(w, q), r.s_as.at[w], r.s_ar.at[w, t - 1], to)

    def copy_b(w, u, t):
        blk = wblock(w, qof(c, f_ + B - t, g_))
        src = own_block(w) if t == 0 else blk
        to = dev(c, qof(c, f_, g_ + u))
        return remote(src, blk, r.s_as.at[w], r.s_br.at[w, (u - 1) * B + t], to)

    def shard_from(u, t):
        return qof(c, f_ + B - t, g_ + B - u)

    def pass_on(w, u, t):
        blk = wblock(w, shard_from(u, t))
        remote(blk, blk, r.s_ds.at[w], r.s_dr.at[w], sibling).start()
        if w in plan.shared:
            remote(blk, blk, r.s_hs.at[w], r.s_hr.at[w], partner).start()

    def local_shard(w):
        dst = vrows(r.w[w], w, q * plan.kr(w), plan.kr(w))
        return pltpu.make_async_copy(r.h[w], dst, r.s_loc.at[w])

    def g0(w):
        local_shard(w).start()
        for t in range(1, B):
            copy_a(w, t).start()
        for u in range(1, A):
            copy_b(w, u, 0).start()

    def g1(w):
        for t in range(1, B):
            bytes_of(wblock(w, shard_from(0, t)), r.s_ar.at[w, t - 1]).wait()
            for u in range(1, A):
                copy_b(w, u, t).start()
            pass_on(w, 0, t)

    def g2(w):
        for u in range(1, A):
            for t in range(B):
                bytes_of(wblock(w, shard_from(u, t)), r.s_br.at[w, (u - 1) * B + t]).wait()
                pass_on(w, u, t)

    def others(w):
        return wrows(r.w[w], w, 0, (n - 1) * plan.hr(w), 0)

    def gz(w):
        if w not in plan.shared:
            return
        bytes_of(others(w), r.s_hr.at[w]).wait()
        for u in range(A):
            for t in range(B):
                if (u, t) != (0, 0):
                    blk = wblock(w, shard_from(u, t), 1 - par)
                    remote(blk, blk, r.s_ds.at[w], r.s_dr.at[w], sibling).start()

    def g3(w):
        local_shard(w).wait()
        bytes_of(vrows(r.w[w], w, 0, (n - 1) * plan.hr(w)), r.s_dr.at[w]).wait()

    def gather_sent(w):
        bytes_of(others(w), r.s_as.at[w]).wait()
        bytes_of(vrows(r.w[w], w, 0, (n - 1) * plan.hr(w)), r.s_ds.at[w]).wait()
        if w in plan.shared:
            bytes_of(others(w), r.s_hs.at[w]).wait()

    def token_rows(ref, slot):
        return ref.at[pl.ds(aligned(slot * span), span)]

    def tokens_in(src, dst, k):
        for j in range(S):
            chip, core, slot = S * c + j, q // PH, q % PH
            here = jnp.logical_and(chip == q, core == c)
            there = token_rows(dst, slot)

            @pl.when(here)
            def _():
                pltpu.make_async_copy(src.at[j], there, r.s_xr.at[k, slot]).start()

            @pl.when(jnp.logical_not(here))
            def _():
                remote(
                    src.at[j], there, r.s_xs.at[k, j], r.s_xr.at[k, slot], dev(core, chip)
                ).start()

    def tokens_in_done(dst, k):
        for slot in range(PH):
            blk = token_rows(dst, slot)
            pltpu.make_async_copy(blk, blk, r.s_xr.at[k, slot]).wait()

    def tokens_in_sent(src, dst, k):
        for j in range(S):
            chip, core, slot = S * c + j, q // PH, q % PH
            here = jnp.logical_and(chip == q, core == c)

            @pl.when(jnp.logical_not(here))
            def _():
                remote(
                    src.at[j],
                    token_rows(dst, slot),
                    r.s_xs.at[k, j],
                    r.s_xr.at[k, slot],
                    dev(core, chip),
                ).wait_send()

    def tokens_out(src, dst, k):
        for p in range(PH):
            chip, core, slot = c * PH + p, q // S, q % S
            here = jnp.logical_and(chip == q, core == c)

            @pl.when(here)
            def _():
                pltpu.make_async_copy(token_rows(src, p), dst.at[slot], r.s_xr.at[k, slot]).start()

            @pl.when(jnp.logical_not(here))
            def _():
                remote(
                    token_rows(src, p),
                    dst.at[slot],
                    r.s_xs.at[k, p],
                    r.s_xr.at[k, slot],
                    dev(core, chip),
                ).start()

    def tokens_out_done(src, dst, k):
        for j in range(S):
            pltpu.make_async_copy(dst.at[j], dst.at[j], r.s_xr.at[k, j]).wait()
        for p in range(PH):
            chip, core, slot = c * PH + p, q // S, q % S
            here = jnp.logical_and(chip == q, core == c)

            @pl.when(jnp.logical_not(here))
            def _():
                remote(
                    token_rows(src, p),
                    dst.at[slot],
                    r.s_xs.at[k, p],
                    r.s_xr.at[k, slot],
                    dev(core, chip),
                ).wait_send()

    def seg_send():
        for j in range(S):
            for core in range(2):
                chip = S * c + j
                here = jnp.logical_and(chip == q, c == core)
                i = 2 * j + core

                @pl.when(here)
                def _():
                    pltpu.make_async_copy(r.seg.at[j], r.segbuf.at[q], r.s_gr.at[q]).start()

                @pl.when(jnp.logical_not(here))
                def _():
                    remote(
                        r.seg.at[j],
                        r.segbuf.at[q],
                        r.s_gs.at[i],
                        r.s_gr.at[q],
                        dev(core, chip),
                    ).start()

    def seg_sent():
        for j in range(S):
            for core in range(2):
                chip = S * c + j
                here = jnp.logical_and(chip == q, c == core)

                @pl.when(jnp.logical_not(here))
                def _():
                    remote(
                        r.seg.at[j],
                        r.segbuf.at[q],
                        r.s_gs.at[2 * j + core],
                        r.s_gr.at[q],
                        dev(core, chip),
                    ).wait_send()

    def small_copy(t):
        return remote(
            r.small,
            r.smallbuf.at[q],
            r.s_ms.at[t],
            r.s_mr.at[t],
            dev(c, (q + t) % n),
        )

    def small_arrived(t):
        blk = r.smallbuf.at[(q + n - t) % n]
        return remote(blk, blk, r.s_ms.at[t], r.s_mr.at[t], sibling)

    def edge_copy(i):
        return remote(r.es[i], r.er[i], r.s_es.at[i], r.s_er.at[i], sibling)

    def edge_send(i, last, first):
        r.es[i][...] = jnp.where(c == 0, last, first)
        edge_copy(i).start()

    def edge_take(i):
        edge_copy(i).wait()
        got = r.er[i][...]
        none = jnp.zeros_like(got)
        return jnp.where(c == 1, got, none), jnp.where(c == 0, got, none)

    def columns(u):
        w, half = UNIT_WEIGHT[u], UNIT_PART[u]
        size = plan.gcols(w)
        return (0, size) if half is None else (half * (size // 2), size // 2)

    def urows(ref, u, row0, rows, shift=0):
        col0, size = columns(u)
        return ref.at[pl.ds(aligned(row0), rows), pl.ds(col0 + shift, size)]

    grad_home = {GLU: (r.hid, 2 * D), CONV: (r.dkvr, 0), LEFT: (r.sep, 0), QKV: (r.dg, 0)}

    def gpiece(u, shard, half):
        if u == SMALL:
            return r.gsm.at[pl.ds(pl.multiple_of(half * 16, 16), 16)]
        w = UNIT_WEIGHT[u]
        ref, shift = grad_home.get(w, (r.w[w] if w < WEIGHTS else None, 0))
        return urows(ref, u, shard * plan.kr(w) + half * plan.hr(w), plan.hr(w), shift)

    def rpiece(u, shard):
        w = UNIT_WEIGHT[u]
        if u == SMALL:
            return r.r[w]
        return urows(r.r[w], u, shard * plan.hr(w), plan.hr(w))

    def slots(u, first, count):
        buf = r.p[UNIT_WEIGHT[u]]
        if u == SMALL:
            return buf.at[pl.ds(first, count)]
        col0, size = columns(u)
        return buf.at[pl.ds(first, count), :, pl.ds(col0, size)]

    def ppiece(u, slot):
        buf = r.p[UNIT_WEIGHT[u]]
        if u == SMALL:
            return buf.at[slot]
        col0, size = columns(u)
        return buf.at[slot, :, pl.ds(col0, size)]

    def zpiece(u, way):
        buf = (r.u, r.d)[way][UNIT_WEIGHT[u]]
        if u == SMALL:
            return buf
        col0, size = columns(u)
        return buf.at[:, pl.ds(col0, size)]

    def copy_r(u, s):
        return remote(gpiece(u, s, oc), rpiece(u, s), r.s_rs.at[u], r.s_rr.at[u], sibling)

    def all_r(u, semaphore):
        w = UNIT_WEIGHT[u]
        view = r.r[w] if u == SMALL else urows(r.r[w], u, 0, n * plan.hr(w))
        return bytes_of(view, semaphore.at[u])

    def shards(u):
        return 1 if u == SMALL else n

    def red0(u):
        for s in range(shards(u)):
            copy_r(u, s).start()

    def plus(a, b):
        return a[...].astype(F32) + b[...].astype(F32)

    def add_core(u, s):
        mine = gpiece(u, s, c)
        mine[...] = plus(mine, rpiece(u, s)).astype(mine.dtype)

    def slot1(u, t):
        return (u - 1) * B + t

    def slot2(t):
        return (A - 1) * B + t - 1

    def copy_p1(u, k, t):
        return remote(
            gpiece(u, qof(c, f_ + t, g_ + k), c),
            ppiece(u, slot1(k, t)),
            r.s_ps.at[u, 0],
            r.s_pr.at[u, 0],
            dev(c, qof(c, f_, g_ + k)),
        )

    def copy_p2(u, t):
        to = qof(c, f_ + t, g_)
        return remote(
            r.r[WEIGHTS] if u == SMALL else gpiece(u, to, c),
            ppiece(u, slot2(t)),
            r.s_ps.at[u, 1],
            r.s_pr.at[u, 1],
            dev(c, to),
        )

    def all_p(u, step, semaphore):
        count = B - 1 if step else A - 1 if u == SMALL else (A - 1) * B
        return bytes_of(slots(u, 0, count), semaphore.at[u, step])

    def red1(u):
        all_r(u, r.s_rr).wait()
        if u == SMALL:
            add_core(u, 0)
            for k in range(1, A):
                copy_p1(u, k, 0).start()
            return

        def send(i, _):
            k, t = i // B + 1, i % B
            add_core(u, qof(c, f_ + t, g_ + k))
            copy_p1(u, k, t).start()
            return 0

        lax.fori_loop(0, (A - 1) * B, send, 0)
        lax.fori_loop(0, B, lambda t, _: (add_core(u, qof(c, f_ + t, g_)), 0)[1], 0)

    def red1b(u):
        all_p(u, 0, r.s_pr).wait()

        def send(t, _):
            if u == SMALL:
                total, to = gpiece(u, 0, c)[...].astype(F32), r.r[WEIGHTS]
            else:
                to = gpiece(u, qof(c, f_ + t, g_), c)
                total = to[...].astype(F32)
            for k in range(1, A):
                total = total + ppiece(u, slot1(k, 0 if u == SMALL else t))[...].astype(F32)
            to[...] = total.astype(to.dtype)
            if u != SMALL:
                copy_p2(u, t).start()
            return 0

        if u == SMALL:
            send(0, 0)
            for t in range(1, B):
                copy_p2(u, t).start()
        else:
            lax.fori_loop(1, B, send, 0)

    def red2(u):
        all_p(u, 1, r.s_pr).wait()
        total = (r.r[WEIGHTS] if u == SMALL else gpiece(u, q, c))[...].astype(F32)
        if u != SMALL:
            for k in range(1, A):
                total = total + ppiece(u, slot1(k, 0))[...].astype(F32)
        for t in range(1, B):
            total = total + ppiece(u, slot2(t))[...].astype(F32)
        mine = ppiece(u, 0)
        mine[...] = total.astype(mine.dtype)

    def copy_z(u, way):
        return remote(
            ppiece(u, 1 + way),
            zpiece(u, way),
            r.s_zs.at[u, way],
            r.s_zr.at[u, way],
            dev(c, q, z + 1 if way == 0 else z - 1),
        )

    def red_hop(u, h):
        own, up, down = ppiece(u, 0), ppiece(u, 1), ppiece(u, 2)

        @pl.when(z == h)
        def _():
            if h == 0:
                up[...] = own[...]
            else:
                copy_z(u, 0).wait_recv()
                up[...] = plus(own, zpiece(u, 0)).astype(up.dtype)
            if h < Z - 1:
                copy_z(u, 0).start()

        @pl.when(z == Z - 1 - h)
        def _():
            if h == 0:
                down[...] = own[...]
            else:
                copy_z(u, 1).wait_recv()
                if h < Z - 1:
                    down[...] = plus(own, zpiece(u, 1)).astype(down.dtype)
            if h < Z - 1:
                copy_z(u, 1).start()

    def final_rows(u):
        w = UNIT_WEIGHT[u]
        if u == SMALL:
            return r.o[w].at[pl.ds(pl.multiple_of(c * 16, 16), 16)]
        return urows(r.o[w], u, c * plan.hr(w), plan.hr(w))

    def final_local(u):
        return pltpu.make_async_copy(ppiece(u, 0), final_rows(u), r.s_fl.at[u])

    def final_remote(u):
        return remote(ppiece(u, 0), final_rows(u), r.s_fs.at[u], r.s_fr.at[u], sibling)

    def red_final(u):
        if Z > 1:
            own, up = ppiece(u, 0), ppiece(u, 1)

            @pl.when(z == Z - 1)
            def _():
                own[...] = up[...]

            @pl.when(z < Z - 1)
            def _():
                own[...] = plus(up, zpiece(u, 1)).astype(own.dtype)

        final_local(u).start()
        final_remote(u).start()

    def red_end(u):
        final_local(u).wait()
        final_remote(u).wait()
        all_r(u, r.s_rs).wait()
        all_p(u, 0, r.s_ps).wait()
        all_p(u, 1, r.s_ps).wait()
        if Z > 1:

            @pl.when(z < Z - 1)
            def _():
                copy_z(u, 0).wait_send()

            @pl.when(z > 0)
            def _():
                copy_z(u, 1).wait_send()

    def red2_hop(u):
        red2(u)
        red_hop(u, 0)

    def last_hop(u):
        red_hop(u, Z - 1)
        red_final(u)

    ahead = {}
    turns = iter(SCHEDULE)

    def reduce_start(*units):
        for u in units:
            red0(u)
            if Z > 1:
                ahead[u] = [red1, red1b, red2_hop]
                ahead[u] += [lambda k, h=h: red_hop(k, h) for h in range(1, Z - 1)]
                ahead[u].append(last_hop)
            else:
                ahead[u] = [red1, red1b, red2, red_final]

    def steps_of(units):
        return [(ahead[u].pop(0), u) for u in units if ahead[u]]

    def move(units):
        for step, u in steps_of(units):
            step(u)

    def turn():
        move(next(turns))

    def turns_of(count):
        acts = []
        for k in range(count):
            steps = steps_of(next(turns))
            if steps:
                acts.append((k, lambda steps=steps: [step(u) for step, u in steps][:0]))
        return acts

    def loop(count, body, after=()):
        def step(i, _):
            body(i)
            for k, act in after:
                pl.when(i == k)(lambda act=act: (act(), None)[1])
            return 0

        lax.fori_loop(0, count, step, 0)

    RB = 256
    NB = T // RB

    def rows_of(i, size=RB, base=0):
        return pl.ds(pl.multiple_of(i * size + base, base or size), size)

    g0(GLU)
    seg_send()
    small_local = pltpu.make_async_copy(r.small, r.smallbuf.at[q], r.s_mr.at[0])
    small_local.start()
    for t in range(1, n):
        small_copy(t).start()
    tokens_in(r.x, r.xin, 0)
    r.g8[...] = jnp.zeros((16, FF), F32)
    g1(GLU)

    for s in range(n):
        blk = r.segbuf.at[s]
        pltpu.make_async_copy(blk, blk, r.s_gr.at[s]).wait()
    for grp in range(n // plan.sr):
        got = r.segbuf[grp * plan.sr]
        for k in range(1, plan.sr):
            got = got + r.segbuf[grp * plan.sr + k]
        r.segrow[:, grp * plan.sw : (grp + 1) * plan.sw] = got
    r.segcol[0:8] = jnp.full((8, 128), -1.0, F32)
    r.segcol[plan.LEN + 8 : plan.LEN + 16] = jnp.full((8, 128), -1.0, F32)
    for k in range(plan.LEN // 128):
        row = r.segrow[0:1, k * 128 : (k + 1) * 128]
        r.segcol[8 + k * 128 : 8 + (k + 1) * 128] = jnp.broadcast_to(row, (128, 128)).T
    r.segloc[...] = r.segcol[pl.ds(pl.multiple_of(c * T, 8), T + 16)]
    r.mext[0 : T + 8] = jnp.where(r.segloc[0 : T + 8] == r.segloc[1 : T + 9], 1.0, 0.0)

    def mask(o, start, rows):
        first = 8 + start + (0 if o > 0 else o)
        return r.mext[first : first + rows]

    small_local.wait()
    for t in range(1, n):
        small_arrived(t).wait_recv()
    for grp in range(n // plan.nr):
        got = r.smallbuf[grp * plan.nr].astype(F32)[0:8, 0 : plan.nw]
        for k in range(1, plan.nr):
            got = got + r.smallbuf[grp * plan.nr + k].astype(F32)[0:8, 0 : plan.nw]
        r.nrm[:, grp * plan.nw : (grp + 1) * plan.nw] = got
    for s in range(n):
        r.midp[:, s * plan.FFn : (s + 1) * plan.FFn] = r.smallbuf[s].astype(F32)[8:24]

    def ln_out(k, v):
        unit, _ = normed(v)
        return (unit * r.nrm[k : k + 1] + r.nrm[4 + k : 5 + k]).astype(BF16)

    def ln_back(k, e, v):
        unit, rs = normed(v)
        eg = e * r.nrm[k : k + 1]
        m1 = jnp.mean(eg, axis=-1, keepdims=True)
        m2 = jnp.mean(eg * unit, axis=-1, keepdims=True)
        cols = slice(k * D, (k + 1) * D)
        r.g8[11:12, cols] += jnp.sum(e * unit, axis=0, keepdims=True)
        r.g8[12:13, cols] += jnp.sum(e, axis=0, keepdims=True)
        return rs * (eg - m1 - unit * m2)

    g0(LEFT)
    g2(GLU)
    g0(CONV)

    def window(b):
        return min(max(b * MB - (MW - MB) // 2 + 16, 0), T + 32 - MW)

    ahead_of = lax.broadcasted_iota(jnp.int32, (MB, MW), 1) - lax.broadcasted_iota(
        jnp.int32, (MB, MW), 0
    )
    for b in range(T // MB):
        home = r.segloc[8 + b * MB : 8 + (b + 1) * MB]
        for o in range(-4, 5):
            there = r.segloc[8 + b * MB + o : 8 + (b + 1) * MB + o]
            same = jnp.where(home == there, 1.0, 0.0)
            hit = ahead_of == b * MB + 16 - window(b) + o
            tap = jnp.where(hit, jnp.concatenate([same] * (MW // 128), axis=1), 0.0)
            r.ms[b, (o + 4) * MB : (o + 5) * MB] = tap.astype(BF16)

    lane = lax.broadcasted_iota(jnp.int32, (1, 128), 1)
    lane_f = lane.astype(F32)
    own_doc = r.segloc[8 : T + 8] == lane_f
    r.qenc[...] = jnp.where(jnp.logical_and(lane < 4, jnp.logical_not(own_doc)), FAR, 0.0).astype(BF16)
    ones = jnp.logical_and(lane >= 4, lane < 7)
    r.kenc[...] = jnp.where(
        jnp.logical_or(r.segcol[8 : plan.LEN + 8] == lane_f, ones), 1.0, 0.0
    ).astype(BF16)

    tokens_in_done(r.xin, 0)
    g3(GLU)
    g1(LEFT)
    g0(POINT)

    def glu(i):
        rows = rows_of(i)
        x = r.xin[rows].astype(F32)
        a1 = ln_out(0, x)
        r.a1[rows] = a1
        value = mm(a1, r.w[GLU][:, 0:D])
        gate = sigmoid(mm(a1, r.w[GLU][:, D : 2 * D]))
        r.sg[rows, 0:D] = gate.astype(BF16)
        r.sg[rows, D : 2 * D] = (value * gate * (1.0 - gate)).astype(BF16)
        y1 = x + value * gate
        r.y1[rows] = y1
        r.a2[rows] = ln_out(1, y1)

    loop(NB, glu, [(0, lambda: g1(CONV))])
    g2(LEFT)
    g2(CONV)
    g3(CONV)

    def conv(i):
        a2 = r.a2[rows_of(i)]
        for o in range(3):
            r.pext[o, rows_of(i, RB, 8)] = mm(a2, r.w[CONV][o])

    loop(NB, conv)
    edge_send(0, r.pext[0, T : T + 8], r.pext[2, 8:16])
    g1(POINT)
    g0(QKV)
    top, bottom = edge_take(0)
    r.pext[0, 0:8] = top
    r.pext[2, T + 8 : T + 16] = bottom
    for k in range(T // 128):
        lo = k * 128
        before = mask(-1, lo, 128)
        after = mask(1, lo, 128)
        pre = (
            r.pext[0, lo + 7 : lo + 135] * jnp.concatenate([before] * (H // 128), axis=1)
            + r.pext[1, lo + 8 : lo + 136]
            + r.pext[2, lo + 9 : lo + 137] * jnp.concatenate([after] * (H // 128), axis=1)
        )
        value, slope = gelu_both(pre)
        r.pext[1, lo + 8 : lo + 136] = value
        r.dgr[lo : lo + 128] = slope.astype(BF16)
    gz(LEFT)
    g3(LEFT)

    CH = 512
    RM = 128

    def left(i):
        rows, erows = rows_of(i, RM), rows_of(i, RM, 8)
        a2 = r.a2[rows]
        for k in range(FF // CH):
            value, slope = gelu_both(mm(a2, r.w[LEFT][:, k * CH : (k + 1) * CH]))
            r.dgl[rows, k * CH : (k + 1) * CH] = slope.astype(BF16)
            r.big[erows, k * CH : (k + 1) * CH] = value
        r.big[erows, 0:H] += r.pext[1, erows]
        unit, rs = normed(r.big[erows])
        r.nm[rows] = unit.astype(BF16)
        r.rm[rows] = rs
        r.hid[rows_of(i, RM, 16)] = (unit * r.midp[0:1] + r.midp[1:2]).astype(BF16)

    def ahead_point():
        g2(POINT)
        g0(OUT)

    def ahead_qkv():
        g1(QKV)
        g0(FIN)

    loop(T // RM, left, [(0, ahead_point), (1, ahead_qkv)])
    edge_send(1, r.hid[T : T + 16], r.hid[16:32])
    r.hid[0:16], r.hid[T + 16 : T + 32] = edge_take(1)

    def depthwise(j):
        cols = pl.ds(pl.multiple_of(j * 256, 256), 256)
        for b in range(T // MB):
            near = r.hid[window(b) : window(b) + MW, cols]
            taps = mm(r.ms[b], near)
            total = taps[0:MB] * r.midp[2:3, cols]
            for o in range(1, 9):
                total = total + taps[o * MB : (o + 1) * MB] * r.midp[2 + o : 3 + o, cols]
            r.sep[b * MB : (b + 1) * MB, cols] = total.astype(BF16)

    def ahead_out():
        g2(QKV)
        g1(OUT)
        g0(FOUT)

    def ahead_fin():
        g2(OUT)
        g1(FIN)

    loop(
        FF // 256,
        depthwise,
        [(0, ahead_out), (2, ahead_fin), (4, lambda: gz(POINT)), (7, lambda: g2(FIN))],
    )
    g3(POINT)

    def point(i):
        rows = rows_of(i)
        y2 = r.y1[rows] + mm(r.sep[rows], r.w[POINT][...])
        r.y2[rows] = y2
        r.a4[rows] = ln_out(2, y2)

    loop(NB, point)
    g3(QKV)
    scale = 1.0 / math.sqrt(D // HEADS)

    def qkv(i):
        rows = rows_of(i)
        a4 = r.a4[rows]
        r.qb[rows] = (mm(a4, r.w[QKV][:, 0:D]) * scale).astype(BF16)
        here = pl.ds(pl.multiple_of(c * T + i * RB, RB), RB)
        r.kvb[here, 0:D] = mm(a4, r.w[QKV][:, D : 2 * D]).astype(BF16)
        r.kvb[here, D : 2 * D] = mm(a4, r.w[QKV][:, 2 * D : 3 * D]).astype(BF16)

    loop(NB, qkv)

    def kv_copy():
        blk = r.kvb.at[pl.ds(aligned(c * T), T)]
        return remote(blk, blk, r.s_ks.at[0], r.s_kr.at[0], sibling)

    kv_copy().start()
    tokens_in(r.ct, r.cot, 1)
    heads_lanes = [lane < 64, lane >= 64]
    g1(FOUT)
    kv_copy().wait()

    def pair_cols(j, base=0):
        return pl.ds(pl.multiple_of(j * 128 + base, 128), 128)

    def head_lanes(e, v):
        return jnp.where(heads_lanes[e], v, jnp.zeros_like(v))

    def attend(j):
        cols, vcols = pair_cols(j), pair_cols(j, D)
        keys = jnp.concatenate([r.kvb[:, cols], r.kenc[...]], axis=1)
        for k in range(T // RB):
            rows = slice(k * RB, (k + 1) * RB)
            q2 = r.qb[rows, cols]
            got = []
            for e in range(2):
                score = mm_t(jnp.concatenate([head_lanes(e, q2), r.qenc[rows]], axis=1), keys)
                most = jnp.max(score, axis=-1, keepdims=True)
                power = jnp.exp(score - most)
                total = jnp.sum(power, axis=-1, keepdims=True)
                got.append(mm(power.astype(BF16), r.kvb[:, vcols]) / total)
                lse = most + jnp.log(total)
                r.lse[rows] = jnp.where(lane == 2 * j + e, lse, r.lse[rows])
            r.ctx[rows, cols] = jnp.where(heads_lanes[0], got[0], got[1]).astype(BF16)

    r.lse[...] = jnp.zeros((T, 128), F32)

    loop(
        HEADS // 2,
        attend,
        [(0, lambda: gz(FIN)), (1, lambda: g2(FOUT)), (3, lambda: gz(FOUT))],
    )
    g3(OUT)

    def out(i):
        rows = rows_of(i)
        y3 = r.y2[rows] + mm(r.ctx[rows], r.w[OUT][...])
        r.y3[rows] = y3
        r.a5[rows] = ln_out(3, y3)

    loop(NB, out)
    g3(FIN)

    def ffn_in(i):
        rows = rows_of(i)
        a5 = r.a5[rows]
        for k in range(FF // CH):
            value, slope = gelu_both(mm(a5, r.w[FIN][:, k * CH : (k + 1) * CH]))
            r.hid[rows, k * CH : (k + 1) * CH] = value.astype(BF16)
            r.dg[rows, k * CH : (k + 1) * CH] = slope.astype(BF16)

    loop(NB, ffn_in)
    g3(FOUT)

    def ffn_out(i):
        rows = rows_of(i)
        r.osend[rows] = (r.y3[rows] + mm(r.hid[rows], r.w[FOUT][...])).astype(BF16)

    loop(NB, ffn_out)
    tokens_out(r.osend, r.o_out, 2)
    for w in range(WEIGHTS):
        gather_sent(w)

    tokens_in_done(r.cot, 1)

    def ffn_back(i):
        rows = rows_of(i)
        f4 = r.cot[rows]
        for k in range(FF // CH):
            cols = slice(k * CH, (k + 1) * CH)
            up = mm_t(f4, r.w[FOUT][cols])
            r.dg[rows, cols] = (up * r.dg[rows, cols].astype(F32)).astype(BF16)
        e = mm_t(r.dg[rows], r.w[FIN][...])
        r.gs[rows] = f4.astype(F32) + ln_back(3, e, r.y3[rows])

    loop(NB, ffn_back)
    GC = 256

    def grad_outer(k):
        cols = rows_of(k, GC)
        r.w[FOUT][cols] = mm_tn(r.hid[0:T, cols], r.cot[...]).astype(BF16)

    loop(FF // GC, grad_outer)
    reduce_start(U_FOUT)
    turn()
    r.tr[...] = r.a5[...].T

    def grad_inner(k):
        cols = rows_of(k, GC)
        r.w[FIN][:, cols] = mm(r.tr[...], r.dg[:, cols]).astype(BF16)

    loop(FF // GC, grad_inner)
    reduce_start(U_FIN)
    turn()

    def out_back(i):
        rows = rows_of(i)
        f3 = r.gs[rows].astype(BF16)
        r.a5[rows] = f3
        r.hid[rows, 3 * D : 4 * D] = mm_t(f3, r.w[OUT][...]).astype(BF16)

    loop(NB, out_back)
    r.w[OUT][...] = mm_tn(r.ctx[...], r.a5[...]).astype(BF16)
    reduce_start(U_OUT)
    turn()
    r.tr[...] = r.a4[...].T

    QB = 256

    def with_terms(extra, v):
        high = v.astype(BF16).astype(F32)
        mid = (v - high).astype(BF16).astype(F32)
        low = v - high - mid
        terms = jnp.where(lane == 4, high, jnp.where(lane == 5, mid, jnp.where(lane == 6, low, 0.0)))
        return extra - terms.astype(BF16)

    def attend_back(j):
        cols, vcols = pair_cols(j), pair_cols(j, D)
        k2 = r.kvb[:, cols]
        keys = jnp.concatenate([k2, r.kenc[...]], axis=1)
        values = jnp.concatenate([r.kvb[:, vcols], r.kenc[...]], axis=1)
        for k in range(T // QB):
            rows = slice(k * QB, (k + 1) * QB)
            q2 = r.qb[rows, cols]
            d2 = r.hid[rows, pair_cols(j, 3 * D)]
            inner = d2.astype(F32) * r.ctx[rows, cols].astype(F32)
            dq = jnp.zeros((QB, 128), F32)
            for e in range(2):
                qe, de = head_lanes(e, q2), head_lanes(e, d2)
                lse = jnp.sum(
                    jnp.where(lane == 2 * j + e, r.lse[rows], 0.0), axis=-1, keepdims=True
                )
                delta = jnp.sum(head_lanes(e, inner), axis=-1, keepdims=True)
                shifted = mm_t(keys, jnp.concatenate([qe, with_terms(r.qenc[rows], lse)], axis=1))
                probs = jnp.exp(shifted)
                none = jnp.zeros((QB, 128), BF16)
                moved = mm_t(values, jnp.concatenate([de, with_terms(none, delta)], axis=1))
                ds = (probs * moved).astype(BF16)
                dk = mm(ds, qe)
                dv = mm(probs.astype(BF16), de)
                for kk in range(2):
                    half = slice(kk * T, (kk + 1) * T)
                    at = 2 * D + kk * 128
                    if k == 0 and e == 0:
                        r.big[0:T, at : at + 128] = dk[half]
                        r.big[0:T, at + 256 : at + 384] = dv[half]
                    else:
                        r.big[0:T, at : at + 128] += dk[half]
                        r.big[0:T, at + 256 : at + 384] += dv[half]
                dq = dq + mm_tn(ds, head_lanes(e, k2))
            r.hid[rows, cols] = (dq * scale).astype(BF16)

        def part(core, what):
            at = pl.multiple_of(2 * D + core * 128 + what * 256, 128)
            return r.big[0:T, pl.ds(at, 128)]

        for what in range(2):
            mine = pl.ds(pl.multiple_of(j * 256 + what * 128, 128), 128)
            r.big[0:T, mine] = part(c, what)
            r.cot[:, pl.ds(pl.multiple_of(lax.rem(j, 2) * 256 + what * 128, 128), 128)] = part(
                oc, what
            ).astype(BF16)
        dkv_copy(j).start()

        @pl.when(j > 0)
        def _():
            pair_back(j - 1)

    def dkv_copy(j):
        slot = lax.rem(j, 2)
        return remote(
            r.cot.at[:, pl.ds(pl.multiple_of(slot * 256, 128), 256)],
            r.dkvr.at[:, pl.ds(pl.multiple_of(j * 256, 128), 256)],
            r.s_js.at[j],
            r.s_jr.at[j],
            sibling,
        )

    def pair_back(j):
        dkv_copy(j).wait()
        both = pl.ds(pl.multiple_of(j * 256, 256), 256)
        dkv = (r.big[0:T, both] + r.dkvr[:, both].astype(F32)).astype(BF16)
        pair = jnp.concatenate([r.hid[0:T, pair_cols(j)], dkv], axis=1)
        weight = jnp.concatenate([r.w[QKV][:, pair_cols(j, base)] for base in (0, D, 2 * D)], axis=1)
        share = mm_t(pair, weight)

        @pl.when(j == 0)
        def _():
            r.big[0:T, 3 * D : 4 * D] = share

        @pl.when(j > 0)
        def _():
            r.big[0:T, 3 * D : 4 * D] += share

        grad = mm(r.tr[...], pair)
        r.dg[:, pl.ds(pl.multiple_of(j * 384, 128), 384)] = grad.astype(BF16)

    loop(3, attend_back, turns_of(3))
    reduce_start(U_QKV0)
    attend_back(3)
    turn()
    pair_back(3)
    reduce_start(U_QKV1)
    turn()

    def qkv_back(i):
        rows = rows_of(i)
        r.gs[rows] += ln_back(2, r.big[rows, 3 * D : 4 * D], r.y2[rows])

    loop(NB, qkv_back)

    def point_back(i):
        rows = rows_of(i)
        f2 = r.gs[rows].astype(BF16)
        r.a4[rows] = f2
        for k in range(FF // CH):
            cols = slice(k * CH, (k + 1) * CH)
            d = mm_t(f2, r.w[POINT][cols])
            r.hid[rows_of(i, RB, 16), cols] = d.astype(BF16)

    loop(NB, point_back)
    edge_send(2, r.hid[T : T + 16], r.hid[16:32])
    turn()

    def grad_point(k):
        cols = rows_of(k, GC)
        r.w[POINT][cols] = mm_tn(r.sep[:, cols], r.a4[...]).astype(BF16)

    loop(FF // GC, grad_point)
    reduce_start(U_POINT0, U_POINT1)
    turn()
    r.hid[0:16], r.hid[T + 16 : T + 32] = edge_take(2)

    def depth_back(j):
        cols = pl.ds(pl.multiple_of(j * 256, 256), 256)
        gain, shift = r.midp[0:1, cols], r.midp[1:2, cols]
        sums = [jnp.zeros((8, 256), F32) for _ in range(9)]
        for b in range(T // MB):
            lo = b * MB
            taps = mm(r.ms[b], r.hid[window(b) : window(b) + MW, cols])
            a3 = r.nm[lo : lo + MB, cols].astype(F32) * gain + shift
            total = jnp.zeros((MB, 256), F32)
            for o in range(9):
                moved = taps[(8 - o) * MB : (9 - o) * MB]
                total = total + moved * r.midp[2 + o : 3 + o, cols]
                part = moved * a3
                for g in range(MB // 8):
                    sums[o] = sums[o] + part[g * 8 : (g + 1) * 8]
            r.big[lo + 8 : lo + 8 + MB, cols] = total
        for o in range(9):
            r.g8[2 + o : 3 + o, cols] = jnp.sum(sums[o], axis=0, keepdims=True)

    loop(FF // 256, depth_back, turns_of(FF // 256))

    def mid_back(i):
        rows, erows = rows_of(i, RM), rows_of(i, RM, 8)
        e = r.big[erows]
        unit = r.nm[rows].astype(F32)
        eg = e * r.midp[0:1]
        m1 = jnp.mean(eg, axis=-1, keepdims=True)
        m2 = jnp.mean(eg * unit, axis=-1, keepdims=True)
        r.g8[0:1] += jnp.sum(e * unit, axis=0, keepdims=True)
        r.g8[1:2] += jnp.sum(e, axis=0, keepdims=True)
        dmid = r.rm[rows] * (eg - m1 - unit * m2)
        r.dgl[rows] = (dmid * r.dgl[rows].astype(F32)).astype(BF16)
        right = dmid[:, 0:H] * r.dgr[rows].astype(F32)
        r.pext[0, erows] = right.astype(BF16).astype(F32)

    loop(T // RM, mid_back, turns_of(T // RM))
    edge_send(3, r.pext[0, T : T + 8], r.pext[0, 8:16])
    r.tr[...] = r.a2[...].T

    def grad_left(k):
        cols = rows_of(k, GC)
        r.sep[:, cols] = mm(r.tr[...], r.dgl[:, cols]).astype(BF16)

    half = FF // GC // 2
    lax.fori_loop(0, half, lambda k, _: (grad_left(k), 0)[1], 0)
    reduce_start(U_LEFT0)
    turn()
    lax.fori_loop(half, 2 * half, lambda k, _: (grad_left(k), 0)[1], 0)
    reduce_start(U_LEFT1)
    turn()
    top, bottom = edge_take(3)
    r.pext[0, 0:8] = top
    r.pext[0, T + 8 : T + 16] = bottom
    for k in range(T // 128):
        lo = k * 128
        for o in (-1, 0, 1):
            moved = r.pext[0, lo + 8 - o : lo + 136 - o]
            if o:
                moved = moved * jnp.concatenate([mask(-o, lo, 128)] * (H // 128), axis=1)
            r.hid[lo : lo + 128, (o + 1) * H : (o + 2) * H] = moved.astype(BF16)
    for o in range(3):
        cols = slice(o * H, (o + 1) * H)
        r.dkvr[:, cols] = mm(r.tr[...], r.hid[0:T, cols]).astype(BF16)
    reduce_start(U_CONV)
    turn()

    def branch_back(i):
        rows = rows_of(i)
        e = mm_t(r.dgl[rows], r.w[LEFT][...])
        for o in range(3):
            e = e + mm_t(r.hid[rows, o * H : (o + 1) * H], r.w[CONV][o])
        r.gs[rows] += ln_back(1, e, r.y1[rows])

    loop(NB, branch_back, turns_of(NB))

    def gate_back(i):
        rows = rows_of(i)
        g = r.gs[rows]
        r.sg[rows, 0:D] = (g * r.sg[rows, 0:D].astype(F32)).astype(BF16)
        r.sg[rows, D : 2 * D] = (g * r.sg[rows, D : 2 * D].astype(F32)).astype(BF16)

    loop(NB, gate_back)
    r.tr[...] = r.a1[...].T

    def grad_glu(k):
        cols = rows_of(k, GC)
        to = pl.ds(pl.multiple_of(k * GC + 2 * D, GC), GC)
        r.hid[0:T, to] = mm(r.tr[...], r.sg[:, cols]).astype(BF16)

    lax.fori_loop(0, D // GC, lambda k, _: (grad_glu(k), 0)[1], 0)
    reduce_start(U_GLU0)
    turn()
    lax.fori_loop(D // GC, 2 * D // GC, lambda k, _: (grad_glu(k), 0)[1], 0)
    reduce_start(U_GLU1)
    turn()

    def glu_back(i):
        rows = rows_of(i)
        e = mm_t(r.sg[rows], r.w[GLU][...])
        total = r.gs[rows] + ln_back(0, e, r.xin[rows].astype(F32))
        r.a5[rows] = total.astype(BF16)

    loop(NB, glu_back, turns_of(NB))
    r.gsm[0:16] = r.g8[:, 0 : FF // 2].astype(BF16)
    r.gsm[16:32] = r.g8[:, FF // 2 : FF].astype(BF16)
    reduce_start(SMALL)
    move(TAIL[0])
    tokens_out(r.a5, r.o_ig, 3)
    move(TAIL[1])
    while any(ahead.values()):
        move(range(UNITS))

    for u in range(UNITS):
        red_end(u)
    tokens_out_done(r.osend, r.o_out, 2)
    tokens_out_done(r.a5, r.o_ig, 3)
    tokens_in_sent(r.x, r.xin, 0)
    tokens_in_sent(r.ct, r.cot, 1)
    seg_sent()
    for t in range(1, n):
        small_copy(t).wait_send()


def local(
    inputs,
    segment_ids,
    cotangent,
    norm_gain,
    norm_bias,
    glu_weight,
    left_weight,
    conv_weight,
    mid_gain,
    mid_bias,
    depth_weight,
    point_weight,
    qkv_weight,
    out_weight,
    ffn_in,
    ffn_out,
):
    seqs, span, width = inputs.shape
    n = lax.axis_size("seq")
    plan = Plan(
        lax.axis_size("dp"), n, seqs, span, width, ffn_in.shape[1], conv_weight.shape[2]
    )
    q = lax.axis_index("seq")

    def placed(piece, repeats):
        if repeats == 1:
            return piece
        size = piece.shape[-1]
        tiled = jnp.tile(piece, (1,) * (piece.ndim - 1) + (repeats,))
        at = lax.broadcasted_iota(jnp.int32, tiled.shape, tiled.ndim - 1) // size
        return jnp.where(at == q % repeats, tiled, jnp.zeros_like(tiled))

    segs = placed(segment_ids.astype(F32), plan.sr)
    segs = jnp.broadcast_to(segs[:, None, :], (seqs, 8, plan.sw))
    norms = placed(jnp.concatenate([norm_gain, norm_bias], 0), plan.nr)
    norms = jnp.pad(norms, ((0, 0), (0, plan.FFn - plan.nw)))
    small = jnp.concatenate([norms, mid_gain[None], mid_bias[None], depth_weight], 0)
    small = jnp.pad(small, ((0, 32 - small.shape[0]), (0, 0)))
    weights = [None] * WEIGHTS
    weights[GLU], weights[CONV], weights[LEFT] = glu_weight, conv_weight, left_weight
    weights[POINT], weights[QKV], weights[OUT] = point_weight, qkv_weight, out_weight
    weights[FIN], weights[FOUT] = ffn_in, ffn_out

    shapes = []
    plan.buffers(shapes.append)
    out_shape = [jax.ShapeDtypeStruct(inputs.shape, BF16)] * 2
    out_shape += [jax.ShapeDtypeStruct(plan.piece(w, plan.kr(w)), BF16) for w in range(WEIGHTS)]
    out_shape += [jax.ShapeDtypeStruct((32, plan.FF // 2), BF16)]
    hbm = pl.BlockSpec(memory_space=pl.ANY)
    got = pl.pallas_call(
        lambda *refs: kernel(plan, *refs),
        out_shape=out_shape,
        in_specs=[hbm] * INPUTS,
        out_specs=[hbm] * OUTPUTS,
        scratch_shapes=shapes,
        compiler_params=pltpu.CompilerParams(
            collective_id=0, has_side_effects=True, vmem_limit_bytes=64 << 20
        ),
        name="cell",
    )(inputs, segs, cotangent, small, *weights)
    out = unpacked(plan, got)
    return (
        out[0],
        out[1],
        out[2 + WEIGHTS],
        out[3 + WEIGHTS],
        out[2 + GLU],
        out[2 + LEFT],
        out[2 + CONV],
        out[4 + WEIGHTS].reshape(-1),
        out[5 + WEIGHTS].reshape(-1),
        out[6 + WEIGHTS],
        out[2 + POINT],
        out[2 + QKV],
        out[2 + OUT],
        out[2 + FIN],
        out[2 + FOUT],
    )


def unpacked(plan, parts):
    count = 2 + WEIGHTS
    dn = plan.D // plan.n
    wide = [jax.ShapeDtypeStruct(p.shape, F32) for p in parts[:count]]
    conv, qkv, H = 2 + CONV, 2 + QKV, plan.HALF
    wide[conv] = jax.ShapeDtypeStruct((3, plan.kr(CONV), H), F32)
    tiny = [(4, dn), (4, dn), (1, plan.FFn), (1, plan.FFn), (9, plan.FFn)]
    out_shape = wide + [jax.ShapeDtypeStruct(shape, F32) for shape in tiny]

    def body(*refs):
        ins, outs = refs[:count], refs[count + 1 : 2 * count + 1]
        sums, tinies = refs[count], refs[2 * count + 1 : 2 * count + 6]
        near, far = refs[2 * count + 6 : 3 * count + 6], refs[3 * count + 6 : 4 * count + 6]
        came, went = refs[4 * count + 6], refs[4 * count + 7]

        def arrive(i):
            return pltpu.make_async_copy(ins[i], near[i], came.at[i])

        def leave(i):
            return pltpu.make_async_copy(far[i], outs[i], went.at[i])

        for i in range(count):
            arrive(i).start()
        q = lax.axis_index("seq")
        whole = jnp.concatenate([sums[0:16].astype(F32), sums[16:32].astype(F32)], axis=1)
        rolled = pltpu.roll(whole, (plan.FF - q * plan.FFn) % plan.FF, 1)[:, 0 : plan.FFn]
        tinies[2][...] = rolled[0:1]
        tinies[3][...] = rolled[1:2]
        tinies[4][...] = rolled[2:11]
        for k in range(2):
            row = whole[11 + k : 12 + k]
            rows = [row[:, i * plan.D : (i + 1) * plan.D] for i in range(4)]
            both = jnp.concatenate(rows + rows, axis=0)
            tinies[k][...] = pltpu.roll(both, (plan.D - q * dn) % plan.D, 1)[0:4, 0:dn]
        for i in range(count):
            arrive(i).wait()
            if i == conv:
                for k in range(3):
                    far[i][k] = near[i][:, k * H : (k + 1) * H].astype(F32)
            elif i == qkv:
                for k in range(12):
                    to = (k % 3) * plan.D + k // 3 * 128
                    far[i][:, to : to + 128] = near[i][:, k * 128 : (k + 1) * 128].astype(F32)
            else:
                far[i][...] = near[i][...].astype(F32)
            leave(i).start()
        for i in range(count):
            leave(i).wait()

    hbm = pl.BlockSpec(memory_space=pl.ANY)
    vmem = pl.BlockSpec(memory_space=pltpu.VMEM)
    return pl.pallas_call(
        body,
        out_shape=out_shape,
        in_specs=[hbm] * count + [vmem],
        out_specs=[hbm] * count + [vmem] * len(tiny),
        scratch_shapes=[pltpu.VMEM(p.shape, BF16) for p in parts[:count]]
        + [pltpu.VMEM(shape.shape, F32) for shape in wide]
        + [pltpu.SemaphoreType.DMA((count,))] * 2,
        compiler_params=pltpu.CompilerParams(vmem_limit_bytes=64 << 20),
    )(*parts)


def solution(mesh):
    in_specs = (
        P("dp", "seq", None),
        P("dp", "seq"),
        P("dp", "seq", None),
        P(None, "seq"),
        P(None, "seq"),
        P("seq", None),
        P("seq", None),
        P(None, "seq", None),
        P("seq"),
        P("seq"),
        P(None, "seq"),
        P("seq", None),
        P("seq", None),
        P("seq", None),
        P("seq", None),
        P("seq", None),
    )
    out_specs = (
        P("dp", "seq", None),
        P("dp", "seq", None),
        P(None, "seq"),
        P(None, "seq"),
        P("seq", None),
        P("seq", None),
        P(None, "seq", None),
        P("seq"),
        P("seq"),
        P(None, "seq"),
        P("seq", None),
        P("seq", None),
        P("seq", None),
        P("seq", None),
        P("seq", None),
    )
    return jax.shard_map(local, mesh=mesh, in_specs=in_specs, out_specs=out_specs, check_vma=False)
```

```python
import math

import jax
import jax.numpy as jnp
from jax import lax
from jax.experimental import pallas as pl
from jax.experimental.pallas import tpu as pltpu
from jax.sharding import PartitionSpec as P

HEADS = 8
EPS = 1e-06
MESH = pl.DeviceIdType.MESH
F32 = jnp.float32
BF16 = jnp.bfloat16

GLU, CONV, LEFT, POINT, QKV, OUT, FIN, FOUT = range(8)
WEIGHTS = 8
(U_GLU0, U_GLU1, U_CONV, U_LEFT0, U_LEFT1, U_POINT0, U_POINT1, U_QKV0, U_QKV1, U_OUT, U_FIN, U_FOUT, SMALL) = range(13)
UNITS = 13
UNIT_WEIGHT = (GLU, GLU, CONV, LEFT, LEFT, POINT, POINT, QKV, QKV, OUT, FIN, FOUT, WEIGHTS)
UNIT_PART = (0, 1, None, 0, 1, 0, 1, 0, 1, None, None, None, None)

SHARED = (GLU, LEFT, POINT, FIN,)
SMALLS, TOKENS = 8, 9
START = (GLU, SMALLS, LEFT, TOKENS)
FORWARD = (
    ((1, GLU),),
    (),
    (),
    ((1, LEFT), (2, GLU), (0, CONV), (2, LEFT), (0, POINT), (1, CONV), (0, QKV), (3, GLU)),
    (),
    ((1, POINT),),
    (),
    ((2, CONV), (3, LEFT), (0, OUT)),
    ((1, QKV),),
    (),
    (),
    (),
    ((0, FIN),),
    ((1, OUT), (2, POINT)),
    (),
    ((0, FOUT),),
    ((2, QKV),),
    ((1, FIN),),
    (),
    (),
    ((2, OUT),),
    (),
    ((3, POINT),),
    ((0, TOKENS),),
    (),
    (),
    ((1, FOUT),),
    (),
    ((2, FIN),),
    (),
    (),
    (),
    ((2, FOUT), (3, FIN)),
    (),
    (),
    (),
    (),
    (),
    (),
    (),
    (),
)
SCHEDULE = (
    (),
    (),
    (),
    (U_FOUT, U_FIN, U_OUT),
    (),
    (U_FOUT,),
    (),
    (U_FIN,),
    (U_FOUT, U_OUT, U_QKV0, U_QKV1),
    (),
    (U_FIN,),
    (U_OUT, U_POINT0),
    (U_QKV0, U_POINT1),
    (),
    (U_QKV1, U_FOUT),
    (),
    (),
    (U_QKV0,),
    (U_POINT0,),
    (U_QKV1,),
    (U_FIN,),
    (),
    (U_OUT, U_POINT1),
    (U_FOUT, U_POINT0),
    (U_QKV0,),
    (U_LEFT0, U_LEFT1, U_QKV1),
    (U_POINT1, U_CONV),
    (),
    (U_POINT0, U_FIN),
    (),
    (U_OUT, U_GLU0),
)
TAIL = (
    (U_GLU1, U_LEFT0, SMALL, U_QKV0, U_POINT1, U_LEFT1, U_QKV1, U_LEFT0, U_POINT0, U_CONV, U_LEFT1, U_POINT1, U_GLU0, U_LEFT0, U_GLU1, U_CONV, SMALL),
    (U_GLU0, U_LEFT1, U_GLU1, SMALL, U_LEFT0, U_CONV, U_GLU0, U_LEFT1, U_GLU1, SMALL, U_CONV, U_GLU0, U_GLU1, SMALL, U_FOUT, U_FIN, U_OUT, U_QKV0, U_QKV1, U_POINT0, U_POINT1, U_LEFT0, U_LEFT1, U_CONV, U_GLU0, U_GLU1, SMALL),
)

MB, MW = 128, 256
FAR = -(2.0**30)


def mm(a, b):
    return lax.dot_general(a, b, (((1,), (0,)), ((), ())), preferred_element_type=F32)


def mm_t(a, b):
    return lax.dot_general(a, b, (((1,), (1,)), ((), ())), preferred_element_type=F32)


def mm_tn(a, b):
    return lax.dot_general(a, b, (((0,), (0,)), ((), ())), preferred_element_type=F32)


def normed(v):
    centred = v - jnp.mean(v, axis=-1, keepdims=True)
    r = lax.rsqrt(jnp.mean(centred * centred, axis=-1, keepdims=True) + EPS)
    return centred * r, r


def gelu_both(v):
    c = math.sqrt(2.0 / math.pi)
    sq = v * v
    t = jnp.tanh(v * (c + (c * 0.044715) * sq))
    half = 0.5 * t + 0.5
    value = v * half
    slope = half + (0.5 * v) * (1.0 - t * t) * (c + (3.0 * c * 0.044715) * sq)
    return value, slope


def sigmoid(v):
    return 0.5 * jnp.tanh(0.5 * v) + 0.5


class Buffers:
    pass


class Plan:
    def __init__(self, dp, n, seqs, span, width, hidden, half):
        self.n, self.Z = n, dp // 2
        self.S, self.span = seqs, span
        self.D, self.FF, self.HALF = width, hidden, half
        self.LEN = span * n
        self.T = self.LEN // 2
        self.PH = n // 2
        self.B = math.isqrt(n)
        self.A = n // self.B
        assert self.A == self.B and n == 2 * seqs and dp % 2 == 0
        self.shared = SHARED if self.Z % 2 == 0 else ()
        self.sw = max(span, 128)
        self.sr = self.sw // span
        dn = width // n
        self.nw = max(dn, 128)
        self.nr = self.nw // dn
        self.FFn = hidden // n
        self.dims = [
            (width, 2 * width),
            (width, half),
            (width, hidden),
            (hidden, width),
            (width, 3 * width),
            (width, width),
            (width, hidden),
            (hidden, width),
        ]

    def whole(self, w):
        k, cols = self.dims[w]
        return (3, k, cols) if w == CONV else (k, cols)

    def kr(self, w):
        return self.dims[w][0] // self.n

    def hr(self, w):
        return self.kr(w) // 2

    def gcols(self, w):
        return self.dims[w][1] * (3 if w == CONV else 1)

    def piece(self, w, rows):
        return (rows, self.gcols(w))

    def buffers(self, take):
        T, D, FF, H, n = self.T, self.D, self.FF, self.HALF, self.n
        r = Buffers()

        def vm(shape, dtype):
            return take(pltpu.VMEM(shape, dtype))

        def sem(*shape):
            return take(pltpu.SemaphoreType.DMA(shape))

        every = range(WEIGHTS)
        parts = [(self.piece(w, self.hr(w)), BF16) for w in every] + [((16, FF // 2), BF16)]
        r.w = [vm(self.whole(w), BF16) for w in every]
        r.g8 = vm((16, FF), F32)
        r.gsm = vm((32, FF // 2), BF16)
        r.r = [None] * WEIGHTS + [vm((16, FF // 2), BF16)]
        for w in (CONV, QKV, OUT, FIN, FOUT):
            r.r[w] = vm(self.piece(w, n * self.hr(w)), BF16)
        r.r[LEFT], r.r[POINT], r.r[GLU] = r.r[FIN], r.r[FOUT], r.r[QKV]
        r.p = [vm((n - 1,) + shape, dtype) for shape, dtype in parts]
        if self.Z > 1:
            r.u = [vm(shape, dtype) for shape, dtype in parts]
            r.d = [vm(shape, dtype) for shape, dtype in parts]
        r.segbuf = vm((n, 8, self.sw), F32)
        r.segrow = vm((8, self.LEN), F32)
        r.segcol = vm((self.LEN + 16, 128), F32)
        r.segloc = vm((T + 16, 128), F32)
        r.mext = vm((T + 16, 128), F32)
        r.ms = vm((T // MB, 9 * MB, MW), BF16)
        r.qenc = vm((T, 128), BF16)
        r.kenc = vm((self.LEN, 128), BF16)
        r.smallbuf = vm((n, 32, self.FFn), BF16)
        r.nrm = vm((8, D), F32)
        r.midp = vm((16, FF), F32)
        r.xin = vm((T, D), BF16)
        r.cot = vm((T, D), BF16)
        r.a1 = vm((T, D), BF16)
        r.sg = vm((T, 2 * D), BF16)
        r.y1 = vm((T, D), F32)
        r.a2 = vm((T, D), BF16)
        r.pext = vm((3, T + 16, H), F32)
        r.dgl = vm((T, FF), BF16)
        r.dgr = vm((T, H), BF16)
        r.nm = vm((T, FF), BF16)
        r.rm = vm((T, 1), F32)
        r.big = vm((T + 16, FF), F32)
        r.sep = vm((T, FF), BF16)
        r.y2 = vm((T, D), F32)
        r.a4 = vm((T, D), BF16)
        r.qb = vm((T, D), BF16)
        r.kvb = vm((self.LEN, 2 * D), BF16)
        r.lse = vm((T, 128), F32)
        r.ctx = vm((T, D), BF16)
        r.y3 = vm((T, D), F32)
        r.a5 = vm((T, D), BF16)
        r.hid = vm((T + 32, FF), BF16)
        r.dg = vm((T, FF), BF16)
        r.osend = vm((T, D), BF16)
        r.gs = r.y3
        r.dkvr = vm((T, 2 * D), BF16)
        r.tr = vm((D, T), BF16)
        edges = (((8, H), F32), ((16, FF), BF16), ((16, FF), BF16), ((8, H), F32))
        r.es = [vm(shape, dtype) for shape, dtype in edges]
        r.er = [vm(shape, dtype) for shape, dtype in edges]
        r.s_loc = sem(WEIGHTS)
        r.s_as = sem(WEIGHTS)
        r.s_ar = sem(WEIGHTS, self.B - 1)
        r.s_br = sem(WEIGHTS, (self.A - 1) * self.B)
        r.s_ds = sem(WEIGHTS)
        r.s_dr = sem(WEIGHTS)
        if self.shared:
            r.s_hs = sem(WEIGHTS)
            r.s_hr = sem(WEIGHTS)
        r.s_rs = sem(UNITS)
        r.s_rr = sem(UNITS)
        r.s_ps = sem(UNITS, 2)
        r.s_pr = sem(UNITS, 2)
        if self.Z > 1:
            r.s_zs = sem(UNITS, 2)
            r.s_zr = sem(UNITS, 2)
        r.s_fs = sem(UNITS)
        r.s_fr = sem(UNITS)
        r.s_fl = sem(UNITS)
        r.s_xs = sem(4, self.S)
        r.s_xr = sem(4, max(self.PH, self.S))
        r.s_gs = sem(2 * self.S)
        r.s_gr = sem(n)
        r.s_ms = sem(n)
        r.s_mr = sem(n)
        r.s_es = sem(4)
        r.s_er = sem(4)
        r.s_ks = sem(1)
        r.s_kr = sem(1)
        r.s_js = sem(HEADS // 2)
        r.s_jr = sem(HEADS // 2)
        return r


INPUTS = 4 + WEIGHTS
OUTPUTS = 2 + WEIGHTS + 1


def kernel(plan, *refs):
    ins, outs = refs[:INPUTS], refs[INPUTS : INPUTS + OUTPUTS]
    scratch = iter(refs[INPUTS + OUTPUTS :])
    r = plan.buffers(lambda shape: next(scratch))
    r.x, r.seg, r.ct, r.small = ins[:4]
    r.h = ins[4:]
    r.o_out, r.o_ig = outs[:2]
    r.o = outs[2:]
    n, Z, S, span = plan.n, plan.Z, plan.S, plan.span
    T, D, FF, H, PH = plan.T, plan.D, plan.FF, plan.HALF, plan.PH
    A, B = plan.A, plan.B
    dp, q = lax.axis_index("dp"), lax.axis_index("seq")
    z, c = dp // 2, dp % 2
    oc = 1 - c

    def aligned(v, m=16):
        return pl.multiple_of(v, m)

    def dev(core, chip, plane=None):
        return ((z if plane is None else plane) * 2 + core, chip)

    sibling = dev(oc, q)

    def remote(src, dst, ss, rs, to):
        return pltpu.make_async_remote_copy(
            src_ref=src, dst_ref=dst, send_sem=ss, recv_sem=rs, device_id=to, device_id_type=MESH
        )

    barrier = pltpu.get_barrier_semaphore()
    for core in range(2):

        def greet(t, _, core=core):
            chip = lax.rem(q + t, n)
            to = (z * 2 + (c + core) % 2, chip)
            pl.semaphore_signal(barrier, inc=1, device_id=to, device_id_type=MESH)
            return 0

        lax.fori_loop(1 - core, n, greet, 0)
    if Z > 1:

        @pl.when(z > 0)
        def _():
            pl.semaphore_signal(barrier, inc=1, device_id=dev(c, q, z - 1), device_id_type=MESH)

        @pl.when(z < Z - 1)
        def _():
            pl.semaphore_signal(barrier, inc=1, device_id=dev(c, q, z + 1), device_id_type=MESH)

    pl.semaphore_wait(barrier, 2 * n - 1 + (z + Z - 1) // Z + (2 * Z - 2 - z) // Z)

    def vrows(ref, w, row0, rows):
        ds = pl.ds(aligned(row0), rows)
        return ref.at[:, ds] if w == CONV else ref.at[ds]

    def bytes_of(view, semaphore):
        return pltpu.make_async_copy(view, view, semaphore)

    def qof(core, f, g):
        f, g = f % B, g % B
        return core * (f * B + g) + (1 - core) * (g * B + f)

    b_, a_ = q % B, q // B
    f_, g_ = c * a_ + oc * b_, c * b_ + oc * a_
    par = z % 2
    partner = dev(c, q, z + 1 - 2 * par)

    def wrows(ref, w, row0, rows, side):
        if w not in plan.shared:
            return vrows(ref, w, row0, rows)
        size = plan.dims[w][1] // 2
        cols = pl.ds(pl.multiple_of(side * size, 128), size)
        if w == CONV:
            return ref.at[:, pl.ds(aligned(row0), rows), cols]
        return ref.at[pl.ds(aligned(row0), rows), cols]

    def wblock(w, shard, side=par):
        return wrows(r.w[w], w, shard * plan.kr(w) + c * plan.hr(w), plan.hr(w), side)

    def own_block(w):
        return wrows(r.h[w], w, c * plan.hr(w), plan.hr(w), par)

    def copy_a(w, t):
        to = dev(c, qof(c, f_ + t, g_))
        return remote(own_block(w), wblock(w, q), r.s_as.at[w], r.s_ar.at[w, t - 1], to)

    def copy_b(w, u, t):
        blk = wblock(w, qof(c, f_ + B - t, g_))
        src = own_block(w) if t == 0 else blk
        to = dev(c, qof(c, f_, g_ + u))
        return remote(src, blk, r.s_as.at[w], r.s_br.at[w, (u - 1) * B + t], to)

    def shard_from(u, t):
        return qof(c, f_ + B - t, g_ + B - u)

    def pass_on(w, u, t):
        blk = wblock(w, shard_from(u, t))
        remote(blk, blk, r.s_ds.at[w], r.s_dr.at[w], sibling).start()
        if w in plan.shared:
            remote(blk, blk, r.s_hs.at[w], r.s_hr.at[w], partner).start()

    def local_shard(w):
        dst = vrows(r.w[w], w, q * plan.kr(w), plan.kr(w))
        return pltpu.make_async_copy(r.h[w], dst, r.s_loc.at[w])

    def g0(w):
        local_shard(w).start()
        for t in range(1, B):
            copy_a(w, t).start()
        for u in range(1, A):
            copy_b(w, u, 0).start()

    def g1(w):
        for t in range(1, B):
            bytes_of(wblock(w, shard_from(0, t)), r.s_ar.at[w, t - 1]).wait()
            for u in range(1, A):
                copy_b(w, u, t).start()
            pass_on(w, 0, t)

    def g2(w):
        for u in range(1, A):
            for t in range(B):
                bytes_of(wblock(w, shard_from(u, t)), r.s_br.at[w, (u - 1) * B + t]).wait()
                pass_on(w, u, t)

    def others(w):
        return wrows(r.w[w], w, 0, (n - 1) * plan.hr(w), 0)

    def gz(w):
        if w not in plan.shared:
            return
        bytes_of(others(w), r.s_hr.at[w]).wait()
        for u in range(A):
            for t in range(B):
                if (u, t) != (0, 0):
                    blk = wblock(w, shard_from(u, t), 1 - par)
                    remote(blk, blk, r.s_ds.at[w], r.s_dr.at[w], sibling).start()

    def g3(w):
        local_shard(w).wait()
        bytes_of(vrows(r.w[w], w, 0, (n - 1) * plan.hr(w)), r.s_dr.at[w]).wait()

    gather_steps = (g0, g1, g2, gz)
    forward_turns = iter(FORWARD)

    def gather(steps):
        for k, w in steps:
            if w == TOKENS:
                tokens_in(r.ct, r.cot, 1)
            else:
                gather_steps[k](w)

    def pass_turn():
        gather(next(forward_turns))

    def pass_turns(count):
        every = [(k, next(forward_turns)) for k in range(count)]
        return [(k, lambda steps=steps: gather(steps)) for k, steps in every if steps]

    def gather_sent(w):
        bytes_of(others(w), r.s_as.at[w]).wait()
        bytes_of(vrows(r.w[w], w, 0, (n - 1) * plan.hr(w)), r.s_ds.at[w]).wait()
        if w in plan.shared:
            bytes_of(others(w), r.s_hs.at[w]).wait()

    def token_rows(ref, slot):
        return ref.at[pl.ds(aligned(slot * span), span)]

    def tokens_in(src, dst, k):
        for j in range(S):
            chip, core, slot = S * c + j, q // PH, q % PH
            here = jnp.logical_and(chip == q, core == c)
            there = token_rows(dst, slot)

            @pl.when(here)
            def _():
                pltpu.make_async_copy(src.at[j], there, r.s_xr.at[k, slot]).start()

            @pl.when(jnp.logical_not(here))
            def _():
                remote(
                    src.at[j], there, r.s_xs.at[k, j], r.s_xr.at[k, slot], dev(core, chip)
                ).start()

    def tokens_in_done(dst, k):
        for slot in range(PH):
            blk = token_rows(dst, slot)
            pltpu.make_async_copy(blk, blk, r.s_xr.at[k, slot]).wait()

    def tokens_in_sent(src, dst, k):
        for j in range(S):
            chip, core, slot = S * c + j, q // PH, q % PH
            here = jnp.logical_and(chip == q, core == c)

            @pl.when(jnp.logical_not(here))
            def _():
                remote(
                    src.at[j],
                    token_rows(dst, slot),
                    r.s_xs.at[k, j],
                    r.s_xr.at[k, slot],
                    dev(core, chip),
                ).wait_send()

    def tokens_out(src, dst, k):
        for p in range(PH):
            chip, core, slot = c * PH + p, q // S, q % S
            here = jnp.logical_and(chip == q, core == c)

            @pl.when(here)
            def _():
                pltpu.make_async_copy(token_rows(src, p), dst.at[slot], r.s_xr.at[k, slot]).start()

            @pl.when(jnp.logical_not(here))
            def _():
                remote(
                    token_rows(src, p),
                    dst.at[slot],
                    r.s_xs.at[k, p],
                    r.s_xr.at[k, slot],
                    dev(core, chip),
                ).start()

    def tokens_out_done(src, dst, k):
        for j in range(S):
            pltpu.make_async_copy(dst.at[j], dst.at[j], r.s_xr.at[k, j]).wait()
        for p in range(PH):
            chip, core, slot = c * PH + p, q // S, q % S
            here = jnp.logical_and(chip == q, core == c)

            @pl.when(jnp.logical_not(here))
            def _():
                remote(
                    token_rows(src, p),
                    dst.at[slot],
                    r.s_xs.at[k, p],
                    r.s_xr.at[k, slot],
                    dev(core, chip),
                ).wait_send()

    def seg_send():
        for j in range(S):
            for core in range(2):
                chip = S * c + j
                here = jnp.logical_and(chip == q, c == core)
                i = 2 * j + core

                @pl.when(here)
                def _():
                    pltpu.make_async_copy(r.seg.at[j], r.segbuf.at[q], r.s_gr.at[q]).start()

                @pl.when(jnp.logical_not(here))
                def _():
                    remote(
                        r.seg.at[j],
                        r.segbuf.at[q],
                        r.s_gs.at[i],
                        r.s_gr.at[q],
                        dev(core, chip),
                    ).start()

    def seg_sent():
        for j in range(S):
            for core in range(2):
                chip = S * c + j
                here = jnp.logical_and(chip == q, c == core)

                @pl.when(jnp.logical_not(here))
                def _():
                    remote(
                        r.seg.at[j],
                        r.segbuf.at[q],
                        r.s_gs.at[2 * j + core],
                        r.s_gr.at[q],
                        dev(core, chip),
                    ).wait_send()

    def small_copy(t):
        return remote(
            r.small,
            r.smallbuf.at[q],
            r.s_ms.at[t],
            r.s_mr.at[t],
            dev(c, (q + t) % n),
        )

    def small_arrived(t):
        blk = r.smallbuf.at[(q + n - t) % n]
        return remote(blk, blk, r.s_ms.at[t], r.s_mr.at[t], sibling)

    def edge_copy(i):
        return remote(r.es[i], r.er[i], r.s_es.at[i], r.s_er.at[i], sibling)

    def edge_send(i, last, first):
        r.es[i][...] = jnp.where(c == 0, last, first)
        edge_copy(i).start()

    def edge_take(i):
        edge_copy(i).wait()
        got = r.er[i][...]
        none = jnp.zeros_like(got)
        return jnp.where(c == 1, got, none), jnp.where(c == 0, got, none)

    def columns(u):
        w, half = UNIT_WEIGHT[u], UNIT_PART[u]
        size = plan.gcols(w)
        return (0, size) if half is None else (half * (size // 2), size // 2)

    def urows(ref, u, row0, rows, shift=0):
        col0, size = columns(u)
        return ref.at[pl.ds(aligned(row0), rows), pl.ds(col0 + shift, size)]

    grad_home = {GLU: (r.hid, 2 * D), CONV: (r.dkvr, 0), LEFT: (r.sep, 0), QKV: (r.dg, 0)}

    def gpiece(u, shard, half):
        if u == SMALL:
            return r.gsm.at[pl.ds(pl.multiple_of(half * 16, 16), 16)]
        w = UNIT_WEIGHT[u]
        ref, shift = grad_home.get(w, (r.w[w] if w < WEIGHTS else None, 0))
        return urows(ref, u, shard * plan.kr(w) + half * plan.hr(w), plan.hr(w), shift)

    def rpiece(u, shard):
        w = UNIT_WEIGHT[u]
        if u == SMALL:
            return r.r[w]
        return urows(r.r[w], u, shard * plan.hr(w), plan.hr(w))

    def slots(u, first, count):
        buf = r.p[UNIT_WEIGHT[u]]
        if u == SMALL:
            return buf.at[pl.ds(first, count)]
        col0, size = columns(u)
        return buf.at[pl.ds(first, count), :, pl.ds(col0, size)]

    def ppiece(u, slot):
        buf = r.p[UNIT_WEIGHT[u]]
        if u == SMALL:
            return buf.at[slot]
        col0, size = columns(u)
        return buf.at[slot, :, pl.ds(col0, size)]

    def zpiece(u, way):
        buf = (r.u, r.d)[way][UNIT_WEIGHT[u]]
        if u == SMALL:
            return buf
        col0, size = columns(u)
        return buf.at[:, pl.ds(col0, size)]

    def copy_r(u, s):
        return remote(gpiece(u, s, oc), rpiece(u, s), r.s_rs.at[u], r.s_rr.at[u], sibling)

    def all_r(u, semaphore):
        w = UNIT_WEIGHT[u]
        view = r.r[w] if u == SMALL else urows(r.r[w], u, 0, n * plan.hr(w))
        return bytes_of(view, semaphore.at[u])

    def shards(u):
        return 1 if u == SMALL else n

    def red0(u):
        for s in range(shards(u)):
            copy_r(u, s).start()

    def plus(a, b):
        return a[...].astype(F32) + b[...].astype(F32)

    def add_core(u, s):
        mine = gpiece(u, s, c)
        mine[...] = plus(mine, rpiece(u, s)).astype(mine.dtype)

    def slot1(u, t):
        return (u - 1) * B + t

    def slot2(t):
        return (A - 1) * B + t - 1

    def copy_p1(u, k, t):
        return remote(
            gpiece(u, qof(c, f_ + t, g_ + k), c),
            ppiece(u, slot1(k, t)),
            r.s_ps.at[u, 0],
            r.s_pr.at[u, 0],
            dev(c, qof(c, f_, g_ + k)),
        )

    def copy_p2(u, t):
        to = qof(c, f_ + t, g_)
        return remote(
            r.r[WEIGHTS] if u == SMALL else gpiece(u, to, c),
            ppiece(u, slot2(t)),
            r.s_ps.at[u, 1],
            r.s_pr.at[u, 1],
            dev(c, to),
        )

    def all_p(u, step, semaphore):
        count = B - 1 if step else A - 1 if u == SMALL else (A - 1) * B
        return bytes_of(slots(u, 0, count), semaphore.at[u, step])

    def red1(u):
        all_r(u, r.s_rr).wait()
        if u == SMALL:
            add_core(u, 0)
            for k in range(1, A):
                copy_p1(u, k, 0).start()
            return

        def send(i, _):
            k, t = i // B + 1, i % B
            add_core(u, qof(c, f_ + t, g_ + k))
            copy_p1(u, k, t).start()
            return 0

        lax.fori_loop(0, (A - 1) * B, send, 0)
        lax.fori_loop(0, B, lambda t, _: (add_core(u, qof(c, f_ + t, g_)), 0)[1], 0)

    def red1b(u):
        all_p(u, 0, r.s_pr).wait()

        def send(t, _):
            if u == SMALL:
                total, to = gpiece(u, 0, c)[...].astype(F32), r.r[WEIGHTS]
            else:
                to = gpiece(u, qof(c, f_ + t, g_), c)
                total = to[...].astype(F32)
            for k in range(1, A):
                total = total + ppiece(u, slot1(k, 0 if u == SMALL else t))[...].astype(F32)
            to[...] = total.astype(to.dtype)
            if u != SMALL:
                copy_p2(u, t).start()
            return 0

        if u == SMALL:
            send(0, 0)
            for t in range(1, B):
                copy_p2(u, t).start()
        else:
            lax.fori_loop(1, B, send, 0)

    def red2(u):
        all_p(u, 1, r.s_pr).wait()
        total = (r.r[WEIGHTS] if u == SMALL else gpiece(u, q, c))[...].astype(F32)
        if u != SMALL:
            for k in range(1, A):
                total = total + ppiece(u, slot1(k, 0))[...].astype(F32)
        for t in range(1, B):
            total = total + ppiece(u, slot2(t))[...].astype(F32)
        mine = ppiece(u, 0)
        mine[...] = total.astype(mine.dtype)

    def copy_z(u, way):
        return remote(
            ppiece(u, 1 + way),
            zpiece(u, way),
            r.s_zs.at[u, way],
            r.s_zr.at[u, way],
            dev(c, q, z + 1 if way == 0 else z - 1),
        )

    def red_hop(u, h):
        own, up, down = ppiece(u, 0), ppiece(u, 1), ppiece(u, 2)

        @pl.when(z == h)
        def _():
            if h == 0:
                up[...] = own[...]
            else:
                copy_z(u, 0).wait_recv()
                up[...] = plus(own, zpiece(u, 0)).astype(up.dtype)
            if h < Z - 1:
                copy_z(u, 0).start()

        @pl.when(z == Z - 1 - h)
        def _():
            if h == 0:
                down[...] = own[...]
            else:
                copy_z(u, 1).wait_recv()
                if h < Z - 1:
                    down[...] = plus(own, zpiece(u, 1)).astype(down.dtype)
            if h < Z - 1:
                copy_z(u, 1).start()

    def final_rows(u):
        w = UNIT_WEIGHT[u]
        if u == SMALL:
            return r.o[w].at[pl.ds(pl.multiple_of(c * 16, 16), 16)]
        return urows(r.o[w], u, c * plan.hr(w), plan.hr(w))

    def final_local(u):
        return pltpu.make_async_copy(ppiece(u, 0), final_rows(u), r.s_fl.at[u])

    def final_remote(u):
        return remote(ppiece(u, 0), final_rows(u), r.s_fs.at[u], r.s_fr.at[u], sibling)

    def red_final(u):
        if Z > 1:
            own, up = ppiece(u, 0), ppiece(u, 1)

            @pl.when(z == Z - 1)
            def _():
                own[...] = up[...]

            @pl.when(z < Z - 1)
            def _():
                own[...] = plus(up, zpiece(u, 1)).astype(own.dtype)

        final_local(u).start()
        final_remote(u).start()

    def red_end(u):
        final_local(u).wait()
        final_remote(u).wait()
        all_r(u, r.s_rs).wait()
        all_p(u, 0, r.s_ps).wait()
        all_p(u, 1, r.s_ps).wait()
        if Z > 1:

            @pl.when(z < Z - 1)
            def _():
                copy_z(u, 0).wait_send()

            @pl.when(z > 0)
            def _():
                copy_z(u, 1).wait_send()

    def red2_hop(u):
        red2(u)
        red_hop(u, 0)

    def last_hop(u):
        red_hop(u, Z - 1)
        red_final(u)

    ahead = {}
    turns = iter(SCHEDULE)

    def reduce_start(*units):
        for u in units:
            red0(u)
            if Z > 1:
                ahead[u] = [red1, red1b, red2_hop]
                ahead[u] += [lambda k, h=h: red_hop(k, h) for h in range(1, Z - 1)]
                ahead[u].append(last_hop)
            else:
                ahead[u] = [red1, red1b, red2, red_final]

    def steps_of(units):
        return [(ahead[u].pop(0), u) for u in units if ahead[u]]

    def move(units):
        for step, u in steps_of(units):
            step(u)

    def turn():
        move(next(turns))

    def turns_of(count):
        acts = []
        for k in range(count):
            steps = steps_of(next(turns))
            if steps:
                acts.append((k, lambda steps=steps: [step(u) for step, u in steps][:0]))
        return acts

    def loop(count, body, after=()):
        def step(i, _):
            body(i)
            for k, act in after:
                pl.when(i == k)(lambda act=act: (act(), None)[1])
            return 0

        lax.fori_loop(0, count, step, 0)

    RB = 256
    NB = T // RB

    def rows_of(i, size=RB, base=0):
        return pl.ds(pl.multiple_of(i * size + base, base or size), size)

    seg_send()
    small_local = pltpu.make_async_copy(r.small, r.smallbuf.at[q], r.s_mr.at[0])
    small_local.start()
    for what in START:
        if what == SMALLS:
            for t in range(1, n):
                small_copy(t).start()
        elif what == TOKENS:
            tokens_in(r.x, r.xin, 0)
        else:
            g0(what)
    r.g8[...] = jnp.zeros((16, FF), F32)
    pass_turn()

    for s in range(n):
        blk = r.segbuf.at[s]
        pltpu.make_async_copy(blk, blk, r.s_gr.at[s]).wait()
    for grp in range(n // plan.sr):
        got = r.segbuf[grp * plan.sr]
        for k in range(1, plan.sr):
            got = got + r.segbuf[grp * plan.sr + k]
        r.segrow[:, grp * plan.sw : (grp + 1) * plan.sw] = got
    r.segcol[0:8] = jnp.full((8, 128), -1.0, F32)
    r.segcol[plan.LEN + 8 : plan.LEN + 16] = jnp.full((8, 128), -1.0, F32)
    for k in range(plan.LEN // 128):
        row = r.segrow[0:1, k * 128 : (k + 1) * 128]
        r.segcol[8 + k * 128 : 8 + (k + 1) * 128] = jnp.broadcast_to(row, (128, 128)).T
    r.segloc[...] = r.segcol[pl.ds(pl.multiple_of(c * T, 8), T + 16)]
    r.mext[0 : T + 8] = jnp.where(r.segloc[0 : T + 8] == r.segloc[1 : T + 9], 1.0, 0.0)

    def mask(o, start, rows):
        first = 8 + start + (0 if o > 0 else o)
        return r.mext[first : first + rows]

    small_local.wait()
    for t in range(1, n):
        small_arrived(t).wait_recv()
    for grp in range(n // plan.nr):
        got = r.smallbuf[grp * plan.nr].astype(F32)[0:8, 0 : plan.nw]
        for k in range(1, plan.nr):
            got = got + r.smallbuf[grp * plan.nr + k].astype(F32)[0:8, 0 : plan.nw]
        r.nrm[:, grp * plan.nw : (grp + 1) * plan.nw] = got
    for s in range(n):
        r.midp[:, s * plan.FFn : (s + 1) * plan.FFn] = r.smallbuf[s].astype(F32)[8:24]

    def ln_out(k, v):
        unit, _ = normed(v)
        return (unit * r.nrm[k : k + 1] + r.nrm[4 + k : 5 + k]).astype(BF16)

    def ln_back(k, e, v):
        unit, rs = normed(v)
        eg = e * r.nrm[k : k + 1]
        m1 = jnp.mean(eg, axis=-1, keepdims=True)
        m2 = jnp.mean(eg * unit, axis=-1, keepdims=True)
        cols = slice(k * D, (k + 1) * D)
        r.g8[11:12, cols] += jnp.sum(e * unit, axis=0, keepdims=True)
        r.g8[12:13, cols] += jnp.sum(e, axis=0, keepdims=True)
        return rs * (eg - m1 - unit * m2)

    pass_turn()

    def window(b):
        return min(max(b * MB - (MW - MB) // 2 + 16, 0), T + 32 - MW)

    ahead_of = lax.broadcasted_iota(jnp.int32, (MB, MW), 1) - lax.broadcasted_iota(
        jnp.int32, (MB, MW), 0
    )
    for b in range(T // MB):
        home = r.segloc[8 + b * MB : 8 + (b + 1) * MB]
        for o in range(-4, 5):
            there = r.segloc[8 + b * MB + o : 8 + (b + 1) * MB + o]
            same = jnp.where(home == there, 1.0, 0.0)
            hit = ahead_of == b * MB + 16 - window(b) + o
            tap = jnp.where(hit, jnp.concatenate([same] * (MW // 128), axis=1), 0.0)
            r.ms[b, (o + 4) * MB : (o + 5) * MB] = tap.astype(BF16)

    lane = lax.broadcasted_iota(jnp.int32, (1, 128), 1)
    lane_f = lane.astype(F32)
    own_doc = r.segloc[8 : T + 8] == lane_f
    r.qenc[...] = jnp.where(jnp.logical_and(lane < 4, jnp.logical_not(own_doc)), FAR, 0.0).astype(BF16)
    ones = jnp.logical_and(lane >= 4, lane < 7)
    r.kenc[...] = jnp.where(
        jnp.logical_or(r.segcol[8 : plan.LEN + 8] == lane_f, ones), 1.0, 0.0
    ).astype(BF16)

    pass_turn()
    pass_turn()
    g3(GLU)
    pass_turn()
    tokens_in_done(r.xin, 0)

    def glu(i):
        rows = rows_of(i)
        x = r.xin[rows].astype(F32)
        a1 = ln_out(0, x)
        r.a1[rows] = a1
        value = mm(a1, r.w[GLU][:, 0:D])
        gate = sigmoid(mm(a1, r.w[GLU][:, D : 2 * D]))
        r.sg[rows, 0:D] = gate.astype(BF16)
        r.sg[rows, D : 2 * D] = (value * gate * (1.0 - gate)).astype(BF16)
        y1 = x + value * gate
        r.y1[rows] = y1
        r.a2[rows] = ln_out(1, y1)

    loop(NB, glu, pass_turns(NB))
    pass_turn()
    g3(CONV)

    def conv(i):
        a2 = r.a2[rows_of(i)]
        for o in range(3):
            r.pext[o, rows_of(i, RB, 8)] = mm(a2, r.w[CONV][o])

    loop(NB, conv)
    edge_send(0, r.pext[0, T : T + 8], r.pext[2, 8:16])
    pass_turn()
    top, bottom = edge_take(0)
    r.pext[0, 0:8] = top
    r.pext[2, T + 8 : T + 16] = bottom
    pass_turn()
    for k in range(T // 128):
        lo = k * 128
        before = mask(-1, lo, 128)
        after = mask(1, lo, 128)
        pre = (
            r.pext[0, lo + 7 : lo + 135] * jnp.concatenate([before] * (H // 128), axis=1)
            + r.pext[1, lo + 8 : lo + 136]
            + r.pext[2, lo + 9 : lo + 137] * jnp.concatenate([after] * (H // 128), axis=1)
        )
        value, slope = gelu_both(pre)
        r.pext[1, lo + 8 : lo + 136] = value
        r.dgr[lo : lo + 128] = slope.astype(BF16)
    pass_turn()
    pass_turn()
    g3(LEFT)

    CH = 512
    RM = 128

    def left(i):
        rows, erows = rows_of(i, RM), rows_of(i, RM, 8)
        a2 = r.a2[rows]
        for k in range(FF // CH):
            value, slope = gelu_both(mm(a2, r.w[LEFT][:, k * CH : (k + 1) * CH]))
            r.dgl[rows, k * CH : (k + 1) * CH] = slope.astype(BF16)
            r.big[erows, k * CH : (k + 1) * CH] = value
        r.big[erows, 0:H] += r.pext[1, erows]
        unit, rs = normed(r.big[erows])
        r.nm[rows] = unit.astype(BF16)
        r.rm[rows] = rs
        r.hid[rows_of(i, RM, 16)] = (unit * r.midp[0:1] + r.midp[1:2]).astype(BF16)

    loop(T // RM, left, pass_turns(T // RM))
    edge_send(1, r.hid[T : T + 16], r.hid[16:32])
    r.hid[0:16], r.hid[T + 16 : T + 32] = edge_take(1)
    pass_turn()

    def depthwise(j):
        cols = pl.ds(pl.multiple_of(j * 256, 256), 256)
        for b in range(T // MB):
            near = r.hid[window(b) : window(b) + MW, cols]
            taps = mm(r.ms[b], near)
            total = taps[0:MB] * r.midp[2:3, cols]
            for o in range(1, 9):
                total = total + taps[o * MB : (o + 1) * MB] * r.midp[2 + o : 3 + o, cols]
            r.sep[b * MB : (b + 1) * MB, cols] = total.astype(BF16)

    loop(FF // 256, depthwise, pass_turns(FF // 256))
    pass_turn()
    g3(POINT)

    def point(i):
        rows = rows_of(i)
        y2 = r.y1[rows] + mm(r.sep[rows], r.w[POINT][...])
        r.y2[rows] = y2
        r.a4[rows] = ln_out(2, y2)

    loop(NB, point)
    pass_turn()
    pass_turn()
    g3(QKV)
    scale = 1.0 / math.sqrt(D // HEADS)

    def qkv(i):
        rows = rows_of(i)
        a4 = r.a4[rows]
        r.qb[rows] = (mm(a4, r.w[QKV][:, 0:D]) * scale).astype(BF16)
        here = pl.ds(pl.multiple_of(c * T + i * RB, RB), RB)
        r.kvb[here, 0:D] = mm(a4, r.w[QKV][:, D : 2 * D]).astype(BF16)
        r.kvb[here, D : 2 * D] = mm(a4, r.w[QKV][:, 2 * D : 3 * D]).astype(BF16)

    loop(NB, qkv)

    def kv_copy():
        blk = r.kvb.at[pl.ds(aligned(c * T), T)]
        return remote(blk, blk, r.s_ks.at[0], r.s_kr.at[0], sibling)

    kv_copy().start()
    pass_turn()
    heads_lanes = [lane < 64, lane >= 64]
    kv_copy().wait()
    pass_turn()

    def pair_cols(j, base=0):
        return pl.ds(pl.multiple_of(j * 128 + base, 128), 128)

    def head_lanes(e, v):
        return jnp.where(heads_lanes[e], v, jnp.zeros_like(v))

    def attend(j):
        cols, vcols = pair_cols(j), pair_cols(j, D)
        keys = jnp.concatenate([r.kvb[:, cols], r.kenc[...]], axis=1)
        for k in range(T // RB):
            rows = slice(k * RB, (k + 1) * RB)
            q2 = r.qb[rows, cols]
            got = []
            for e in range(2):
                score = mm_t(jnp.concatenate([head_lanes(e, q2), r.qenc[rows]], axis=1), keys)
                most = jnp.max(score, axis=-1, keepdims=True)
                power = jnp.exp(score - most)
                total = jnp.sum(power, axis=-1, keepdims=True)
                got.append(mm(power.astype(BF16), r.kvb[:, vcols]) / total)
                lse = most + jnp.log(total)
                r.lse[rows] = jnp.where(lane == 2 * j + e, lse, r.lse[rows])
            r.ctx[rows, cols] = jnp.where(heads_lanes[0], got[0], got[1]).astype(BF16)

    r.lse[...] = jnp.zeros((T, 128), F32)

    loop(HEADS // 2, attend, pass_turns(HEADS // 2))
    pass_turn()
    g3(OUT)

    def out(i):
        rows = rows_of(i)
        y3 = r.y2[rows] + mm(r.ctx[rows], r.w[OUT][...])
        r.y3[rows] = y3
        r.a5[rows] = ln_out(3, y3)

    loop(NB, out)
    pass_turn()
    pass_turn()
    g3(FIN)

    def ffn_in(i):
        rows = rows_of(i)
        a5 = r.a5[rows]
        for k in range(FF // CH):
            value, slope = gelu_both(mm(a5, r.w[FIN][:, k * CH : (k + 1) * CH]))
            r.hid[rows, k * CH : (k + 1) * CH] = value.astype(BF16)
            r.dg[rows, k * CH : (k + 1) * CH] = slope.astype(BF16)

    loop(NB, ffn_in, pass_turns(NB))
    pass_turn()
    g3(FOUT)

    def ffn_out(i):
        rows = rows_of(i)
        r.osend[rows] = (r.y3[rows] + mm(r.hid[rows], r.w[FOUT][...])).astype(BF16)

    loop(NB, ffn_out)
    pass_turn()
    tokens_out(r.osend, r.o_out, 2)
    for w in range(WEIGHTS):
        gather_sent(w)

    tokens_in_done(r.cot, 1)

    def ffn_back(i):
        rows = rows_of(i)
        f4 = r.cot[rows]
        for k in range(FF // CH):
            cols = slice(k * CH, (k + 1) * CH)
            up = mm_t(f4, r.w[FOUT][cols])
            r.dg[rows, cols] = (up * r.dg[rows, cols].astype(F32)).astype(BF16)
        e = mm_t(r.dg[rows], r.w[FIN][...])
        r.gs[rows] = f4.astype(F32) + ln_back(3, e, r.y3[rows])

    loop(NB, ffn_back)
    GC = 1024

    def grad_outer(k):
        cols = rows_of(k, GC)
        r.w[FOUT][cols] = mm_tn(r.hid[0:T, cols], r.cot[...]).astype(BF16)

    loop(FF // GC, grad_outer)
    reduce_start(U_FOUT)
    turn()
    r.tr[...] = r.a5[...].T

    def grad_inner(k):
        cols = rows_of(k, GC)
        r.w[FIN][:, cols] = mm(r.tr[...], r.dg[:, cols]).astype(BF16)

    loop(FF // GC, grad_inner)
    reduce_start(U_FIN)
    turn()

    def out_back(i):
        rows = rows_of(i)
        f3 = r.gs[rows].astype(BF16)
        r.a5[rows] = f3
        r.hid[rows, 3 * D : 4 * D] = mm_t(f3, r.w[OUT][...]).astype(BF16)

    loop(NB, out_back)
    r.w[OUT][...] = mm_tn(r.ctx[...], r.a5[...]).astype(BF16)
    reduce_start(U_OUT)
    turn()
    r.tr[...] = r.a4[...].T

    QB = 256

    def with_terms(extra, v):
        high = v.astype(BF16).astype(F32)
        mid = (v - high).astype(BF16).astype(F32)
        low = v - high - mid
        terms = jnp.where(lane == 4, high, jnp.where(lane == 5, mid, jnp.where(lane == 6, low, 0.0)))
        return extra - terms.astype(BF16)

    def attend_back(j):
        cols, vcols = pair_cols(j), pair_cols(j, D)
        k2 = r.kvb[:, cols]
        keys = jnp.concatenate([k2, r.kenc[...]], axis=1)
        values = jnp.concatenate([r.kvb[:, vcols], r.kenc[...]], axis=1)
        for k in range(T // QB):
            rows = slice(k * QB, (k + 1) * QB)
            q2 = r.qb[rows, cols]
            d2 = r.hid[rows, pair_cols(j, 3 * D)]
            inner = d2.astype(F32) * r.ctx[rows, cols].astype(F32)
            dq = jnp.zeros((QB, 128), F32)
            for e in range(2):
                qe, de = head_lanes(e, q2), head_lanes(e, d2)
                lse = jnp.sum(
                    jnp.where(lane == 2 * j + e, r.lse[rows], 0.0), axis=-1, keepdims=True
                )
                delta = jnp.sum(head_lanes(e, inner), axis=-1, keepdims=True)
                shifted = mm_t(keys, jnp.concatenate([qe, with_terms(r.qenc[rows], lse)], axis=1))
                probs = jnp.exp(shifted)
                none = jnp.zeros((QB, 128), BF16)
                moved = mm_t(values, jnp.concatenate([de, with_terms(none, delta)], axis=1))
                ds = (probs * moved).astype(BF16)
                dk = mm(ds, qe)
                dv = mm(probs.astype(BF16), de)
                for kk in range(2):
                    half = slice(kk * T, (kk + 1) * T)
                    at = 2 * D + kk * 128
                    if k == 0 and e == 0:
                        r.big[0:T, at : at + 128] = dk[half]
                        r.big[0:T, at + 256 : at + 384] = dv[half]
                    else:
                        r.big[0:T, at : at + 128] += dk[half]
                        r.big[0:T, at + 256 : at + 384] += dv[half]
                dq = dq + mm_tn(ds, head_lanes(e, k2))
            r.hid[rows, cols] = (dq * scale).astype(BF16)

        def part(core, what):
            at = pl.multiple_of(2 * D + core * 128 + what * 256, 128)
            return r.big[0:T, pl.ds(at, 128)]

        for what in range(2):
            mine = pl.ds(pl.multiple_of(j * 256 + what * 128, 128), 128)
            r.big[0:T, mine] = part(c, what)
            r.cot[:, pl.ds(pl.multiple_of(lax.rem(j, 2) * 256 + what * 128, 128), 128)] = part(
                oc, what
            ).astype(BF16)
        dkv_copy(j).start()

        @pl.when(j > 0)
        def _():
            pair_back(j - 1)

    def dkv_copy(j):
        slot = lax.rem(j, 2)
        return remote(
            r.cot.at[:, pl.ds(pl.multiple_of(slot * 256, 128), 256)],
            r.dkvr.at[:, pl.ds(pl.multiple_of(j * 256, 128), 256)],
            r.s_js.at[j],
            r.s_jr.at[j],
            sibling,
        )

    def pair_back(j):
        dkv_copy(j).wait()
        both = pl.ds(pl.multiple_of(j * 256, 256), 256)
        dkv = (r.big[0:T, both] + r.dkvr[:, both].astype(F32)).astype(BF16)
        pair = jnp.concatenate([r.hid[0:T, pair_cols(j)], dkv], axis=1)
        weight = jnp.concatenate([r.w[QKV][:, pair_cols(j, base)] for base in (0, D, 2 * D)], axis=1)
        share = mm_t(pair, weight)

        @pl.when(j == 0)
        def _():
            r.big[0:T, 3 * D : 4 * D] = share

        @pl.when(j > 0)
        def _():
            r.big[0:T, 3 * D : 4 * D] += share

        grad = mm(r.tr[...], pair)
        r.dg[:, pl.ds(pl.multiple_of(j * 384, 128), 384)] = grad.astype(BF16)

    loop(3, attend_back, turns_of(3))
    reduce_start(U_QKV0)
    attend_back(3)
    turn()
    pair_back(3)
    reduce_start(U_QKV1)
    turn()

    def qkv_back(i):
        rows = rows_of(i)
        r.gs[rows] += ln_back(2, r.big[rows, 3 * D : 4 * D], r.y2[rows])

    loop(NB, qkv_back)

    def point_back(i):
        rows = rows_of(i)
        f2 = r.gs[rows].astype(BF16)
        r.a4[rows] = f2
        for k in range(FF // CH):
            cols = slice(k * CH, (k + 1) * CH)
            d = mm_t(f2, r.w[POINT][cols])
            r.hid[rows_of(i, RB, 16), cols] = d.astype(BF16)

    loop(NB, point_back)
    edge_send(2, r.hid[T : T + 16], r.hid[16:32])
    turn()

    def grad_point(k):
        cols = rows_of(k, GC)
        r.w[POINT][cols] = mm_tn(r.sep[:, cols], r.a4[...]).astype(BF16)

    loop(FF // GC, grad_point)
    reduce_start(U_POINT0, U_POINT1)
    turn()
    r.hid[0:16], r.hid[T + 16 : T + 32] = edge_take(2)

    def depth_back(j):
        cols = pl.ds(pl.multiple_of(j * 256, 256), 256)
        gain, shift = r.midp[0:1, cols], r.midp[1:2, cols]
        sums = [jnp.zeros((8, 256), F32) for _ in range(9)]
        for b in range(T // MB):
            lo = b * MB
            taps = mm(r.ms[b], r.hid[window(b) : window(b) + MW, cols])
            a3 = r.nm[lo : lo + MB, cols].astype(F32) * gain + shift
            total = jnp.zeros((MB, 256), F32)
            for o in range(9):
                moved = taps[(8 - o) * MB : (9 - o) * MB]
                total = total + moved * r.midp[2 + o : 3 + o, cols]
                part = moved * a3
                for g in range(MB // 8):
                    sums[o] = sums[o] + part[g * 8 : (g + 1) * 8]
            r.big[lo + 8 : lo + 8 + MB, cols] = total
        for o in range(9):
            r.g8[2 + o : 3 + o, cols] = jnp.sum(sums[o], axis=0, keepdims=True)

    loop(FF // 256, depth_back, turns_of(FF // 256))

    def mid_back(i):
        rows, erows = rows_of(i, RM), rows_of(i, RM, 8)
        e = r.big[erows]
        unit = r.nm[rows].astype(F32)
        eg = e * r.midp[0:1]
        m1 = jnp.mean(eg, axis=-1, keepdims=True)
        m2 = jnp.mean(eg * unit, axis=-1, keepdims=True)
        r.g8[0:1] += jnp.sum(e * unit, axis=0, keepdims=True)
        r.g8[1:2] += jnp.sum(e, axis=0, keepdims=True)
        dmid = r.rm[rows] * (eg - m1 - unit * m2)
        r.dgl[rows] = (dmid * r.dgl[rows].astype(F32)).astype(BF16)
        right = dmid[:, 0:H] * r.dgr[rows].astype(F32)
        r.pext[0, erows] = right.astype(BF16).astype(F32)

    loop(T // RM, mid_back, turns_of(T // RM))
    edge_send(3, r.pext[0, T : T + 8], r.pext[0, 8:16])
    r.tr[...] = r.a2[...].T

    def grad_left(k):
        cols = rows_of(k, GC)
        r.sep[:, cols] = mm(r.tr[...], r.dgl[:, cols]).astype(BF16)

    half = FF // GC // 2
    lax.fori_loop(0, half, lambda k, _: (grad_left(k), 0)[1], 0)
    reduce_start(U_LEFT0)
    turn()
    lax.fori_loop(half, 2 * half, lambda k, _: (grad_left(k), 0)[1], 0)
    reduce_start(U_LEFT1)
    turn()
    top, bottom = edge_take(3)
    r.pext[0, 0:8] = top
    r.pext[0, T + 8 : T + 16] = bottom
    for k in range(T // 128):
        lo = k * 128
        for o in (-1, 0, 1):
            moved = r.pext[0, lo + 8 - o : lo + 136 - o]
            if o:
                moved = moved * jnp.concatenate([mask(-o, lo, 128)] * (H // 128), axis=1)
            r.hid[lo : lo + 128, (o + 1) * H : (o + 2) * H] = moved.astype(BF16)
    for o in range(3):
        cols = slice(o * H, (o + 1) * H)
        r.dkvr[:, cols] = mm(r.tr[...], r.hid[0:T, cols]).astype(BF16)
    reduce_start(U_CONV)
    turn()

    def branch_back(i):
        rows = rows_of(i)
        e = mm_t(r.dgl[rows], r.w[LEFT][...])
        for o in range(3):
            e = e + mm_t(r.hid[rows, o * H : (o + 1) * H], r.w[CONV][o])
        r.gs[rows] += ln_back(1, e, r.y1[rows])

    loop(NB, branch_back, turns_of(NB))

    def gate_back(i):
        rows = rows_of(i)
        g = r.gs[rows]
        r.sg[rows, 0:D] = (g * r.sg[rows, 0:D].astype(F32)).astype(BF16)
        r.sg[rows, D : 2 * D] = (g * r.sg[rows, D : 2 * D].astype(F32)).astype(BF16)

    loop(NB, gate_back)
    r.tr[...] = r.a1[...].T

    def grad_glu(k):
        cols = rows_of(k, D)
        to = pl.ds(pl.multiple_of(k * D + 2 * D, D), D)
        r.hid[0:T, to] = mm(r.tr[...], r.sg[:, cols]).astype(BF16)

    grad_glu(0)
    reduce_start(U_GLU0)
    turn()
    grad_glu(1)
    reduce_start(U_GLU1)
    turn()

    def glu_back(i):
        rows = rows_of(i)
        e = mm_t(r.sg[rows], r.w[GLU][...])
        total = r.gs[rows] + ln_back(0, e, r.xin[rows].astype(F32))
        r.a5[rows] = total.astype(BF16)

    loop(NB, glu_back, turns_of(NB))
    r.gsm[0:16] = r.g8[:, 0 : FF // 2].astype(BF16)
    r.gsm[16:32] = r.g8[:, FF // 2 : FF].astype(BF16)
    reduce_start(SMALL)
    move(TAIL[0])
    tokens_out(r.a5, r.o_ig, 3)
    move(TAIL[1])
    while any(ahead.values()):
        move(range(UNITS))

    for u in range(UNITS):
        red_end(u)
    tokens_out_done(r.osend, r.o_out, 2)
    tokens_out_done(r.a5, r.o_ig, 3)
    tokens_in_sent(r.x, r.xin, 0)
    tokens_in_sent(r.ct, r.cot, 1)
    seg_sent()
    for t in range(1, n):
        small_copy(t).wait_send()


def local(
    inputs,
    segment_ids,
    cotangent,
    norm_gain,
    norm_bias,
    glu_weight,
    left_weight,
    conv_weight,
    mid_gain,
    mid_bias,
    depth_weight,
    point_weight,
    qkv_weight,
    out_weight,
    ffn_in,
    ffn_out,
):
    seqs, span, width = inputs.shape
    n = lax.axis_size("seq")
    plan = Plan(
        lax.axis_size("dp"), n, seqs, span, width, ffn_in.shape[1], conv_weight.shape[2]
    )
    q = lax.axis_index("seq")

    def placed(piece, repeats):
        if repeats == 1:
            return piece
        size = piece.shape[-1]
        tiled = jnp.tile(piece, (1,) * (piece.ndim - 1) + (repeats,))
        at = lax.broadcasted_iota(jnp.int32, tiled.shape, tiled.ndim - 1) // size
        return jnp.where(at == q % repeats, tiled, jnp.zeros_like(tiled))

    segs = placed(segment_ids.astype(F32), plan.sr)
    segs = jnp.broadcast_to(segs[:, None, :], (seqs, 8, plan.sw))
    norms = placed(jnp.concatenate([norm_gain, norm_bias], 0), plan.nr)
    norms = jnp.pad(norms, ((0, 0), (0, plan.FFn - plan.nw)))
    small = jnp.concatenate([norms, mid_gain[None], mid_bias[None], depth_weight], 0)
    small = jnp.pad(small, ((0, 32 - small.shape[0]), (0, 0)))
    weights = [None] * WEIGHTS
    weights[GLU], weights[CONV], weights[LEFT] = glu_weight, conv_weight, left_weight
    weights[POINT], weights[QKV], weights[OUT] = point_weight, qkv_weight, out_weight
    weights[FIN], weights[FOUT] = ffn_in, ffn_out

    shapes = []
    plan.buffers(shapes.append)
    out_shape = [jax.ShapeDtypeStruct(inputs.shape, BF16)] * 2
    out_shape += [jax.ShapeDtypeStruct(plan.piece(w, plan.kr(w)), BF16) for w in range(WEIGHTS)]
    out_shape += [jax.ShapeDtypeStruct((32, plan.FF // 2), BF16)]
    hbm = pl.BlockSpec(memory_space=pl.ANY)
    got = pl.pallas_call(
        lambda *refs: kernel(plan, *refs),
        out_shape=out_shape,
        in_specs=[hbm] * INPUTS,
        out_specs=[hbm] * OUTPUTS,
        scratch_shapes=shapes,
        compiler_params=pltpu.CompilerParams(
            collective_id=0, has_side_effects=True, vmem_limit_bytes=64 << 20
        ),
        name="cell",
    )(inputs, segs, cotangent, small, *weights)
    out = unpacked(plan, got)
    return (
        out[0],
        out[1],
        out[2 + WEIGHTS],
        out[3 + WEIGHTS],
        out[2 + GLU],
        out[2 + LEFT],
        out[2 + CONV],
        out[4 + WEIGHTS].reshape(-1),
        out[5 + WEIGHTS].reshape(-1),
        out[6 + WEIGHTS],
        out[2 + POINT],
        out[2 + QKV],
        out[2 + OUT],
        out[2 + FIN],
        out[2 + FOUT],
    )


def unpacked(plan, parts):
    count = 2 + WEIGHTS
    dn = plan.D // plan.n
    wide = [jax.ShapeDtypeStruct(p.shape, F32) for p in parts[:count]]
    conv, qkv, H = 2 + CONV, 2 + QKV, plan.HALF
    wide[conv] = jax.ShapeDtypeStruct((3, plan.kr(CONV), H), F32)
    tiny = [(4, dn), (4, dn), (1, plan.FFn), (1, plan.FFn), (9, plan.FFn)]
    out_shape = wide + [jax.ShapeDtypeStruct(shape, F32) for shape in tiny]

    def body(*refs):
        ins, outs = refs[:count], refs[count + 1 : 2 * count + 1]
        sums, tinies = refs[count], refs[2 * count + 1 : 2 * count + 6]
        near, far = refs[2 * count + 6 : 3 * count + 6], refs[3 * count + 6 : 4 * count + 6]
        came, went = refs[4 * count + 6], refs[4 * count + 7]

        def arrive(i):
            return pltpu.make_async_copy(ins[i], near[i], came.at[i])

        def leave(i):
            return pltpu.make_async_copy(far[i], outs[i], went.at[i])

        for i in range(count):
            arrive(i).start()
        q = lax.axis_index("seq")
        whole = jnp.concatenate([sums[0:16].astype(F32), sums[16:32].astype(F32)], axis=1)
        rolled = pltpu.roll(whole, (plan.FF - q * plan.FFn) % plan.FF, 1)[:, 0 : plan.FFn]
        tinies[2][...] = rolled[0:1]
        tinies[3][...] = rolled[1:2]
        tinies[4][...] = rolled[2:11]
        for k in range(2):
            row = whole[11 + k : 12 + k]
            rows = [row[:, i * plan.D : (i + 1) * plan.D] for i in range(4)]
            both = jnp.concatenate(rows + rows, axis=0)
            tinies[k][...] = pltpu.roll(both, (plan.D - q * dn) % plan.D, 1)[0:4, 0:dn]
        for i in range(count):
            arrive(i).wait()
            if i == conv:
                for k in range(3):
                    far[i][k] = near[i][:, k * H : (k + 1) * H].astype(F32)
            elif i == qkv:
                for k in range(12):
                    to = (k % 3) * plan.D + k // 3 * 128
                    far[i][:, to : to + 128] = near[i][:, k * 128 : (k + 1) * 128].astype(F32)
            else:
                far[i][...] = near[i][...].astype(F32)
            leave(i).start()
        for i in range(count):
            leave(i).wait()

    hbm = pl.BlockSpec(memory_space=pl.ANY)
    vmem = pl.BlockSpec(memory_space=pltpu.VMEM)
    return pl.pallas_call(
        body,
        out_shape=out_shape,
        in_specs=[hbm] * count + [vmem],
        out_specs=[hbm] * count + [vmem] * len(tiny),
        scratch_shapes=[pltpu.VMEM(p.shape, BF16) for p in parts[:count]]
        + [pltpu.VMEM(shape.shape, F32) for shape in wide]
        + [pltpu.SemaphoreType.DMA((count,))] * 2,
        compiler_params=pltpu.CompilerParams(vmem_limit_bytes=64 << 20),
    )(*parts)


def solution(mesh):
    in_specs = (
        P("dp", "seq", None),
        P("dp", "seq"),
        P("dp", "seq", None),
        P(None, "seq"),
        P(None, "seq"),
        P("seq", None),
        P("seq", None),
        P(None, "seq", None),
        P("seq"),
        P("seq"),
        P(None, "seq"),
        P("seq", None),
        P("seq", None),
        P("seq", None),
        P("seq", None),
        P("seq", None),
    )
    out_specs = (
        P("dp", "seq", None),
        P("dp", "seq", None),
        P(None, "seq"),
        P(None, "seq"),
        P("seq", None),
        P("seq", None),
        P(None, "seq", None),
        P("seq"),
        P("seq"),
        P(None, "seq"),
        P("seq", None),
        P("seq", None),
        P("seq", None),
        P("seq", None),
        P("seq", None),
    )
    return jax.shard_map(local, mesh=mesh, in_specs=in_specs, out_specs=out_specs, check_vma=False)
```

```python
import math

import jax
import jax.numpy as jnp
from jax import lax
from jax.experimental import pallas as pl
from jax.experimental.pallas import tpu as pltpu
from jax.sharding import PartitionSpec as P

HEADS = 8
EPS = 1e-06
MESH = pl.DeviceIdType.MESH
F32 = jnp.float32
BF16 = jnp.bfloat16

GLU, CONV, LEFT, POINT, QKV, OUT, FIN, FOUT = range(8)
WEIGHTS = 8
(U_GLU0, U_GLU1, U_CONV, U_LEFT0, U_LEFT1, U_POINT0, U_POINT1, U_QKV0, U_QKV1, U_OUT, U_FIN, U_FOUT, SMALL) = range(13)
UNITS = 13
UNIT_WEIGHT = (GLU, GLU, CONV, LEFT, LEFT, POINT, POINT, QKV, QKV, OUT, FIN, FOUT, WEIGHTS)
UNIT_PART = (0, 1, None, 0, 1, 0, 1, 0, 1, None, None, None, None)

SHARED = (GLU, LEFT, POINT, FIN,)
SMALLS, TOKENS = 8, 9
START = (GLU, SMALLS, LEFT, TOKENS)
FORWARD = (
    ((1, GLU),),
    (),
    (),
    ((1, LEFT), (2, GLU), (0, CONV), (2, LEFT), (0, POINT), (1, CONV), (0, QKV), (3, GLU)),
    (),
    ((1, POINT),),
    (),
    ((2, CONV), (3, LEFT), (0, OUT)),
    ((1, QKV),),
    (),
    (),
    (),
    ((0, FIN),),
    ((1, OUT), (2, POINT)),
    (),
    ((0, FOUT),),
    ((2, QKV),),
    ((1, FIN),),
    (),
    (),
    ((2, OUT),),
    (),
    ((3, POINT),),
    ((0, TOKENS),),
    (),
    (),
    ((1, FOUT),),
    (),
    ((2, FIN),),
    (),
    (),
    (),
    ((2, FOUT), (3, FIN)),
    (),
    (),
    (),
    (),
    (),
    (),
    (),
    (),
)
SCHEDULE = (
    (),
    (),
    (),
    (U_FOUT, U_FIN, U_OUT),
    (),
    (U_FOUT,),
    (),
    (U_FIN,),
    (U_FOUT, U_OUT, U_QKV0, U_QKV1),
    (),
    (U_FIN,),
    (U_OUT, U_POINT0),
    (U_QKV0, U_POINT1),
    (),
    (U_QKV1, U_FOUT),
    (),
    (),
    (U_QKV0,),
    (U_POINT0,),
    (U_QKV1,),
    (U_FIN,),
    (),
    (U_OUT, U_POINT1),
    (U_FOUT, U_POINT0),
    (U_QKV0,),
    (U_LEFT0, U_LEFT1, U_QKV1),
    (U_POINT1, U_CONV),
    (),
    (U_POINT0, U_FIN),
    (),
    (U_OUT, U_GLU0),
)
TAIL = (
    (U_GLU1, U_LEFT0, SMALL, U_QKV0, U_POINT1, U_LEFT1, U_QKV1, U_LEFT0, U_POINT0, U_CONV, U_LEFT1, U_POINT1, U_GLU0, U_LEFT0, U_GLU1, U_CONV, SMALL),
    (U_GLU0, U_LEFT1, U_GLU1, SMALL, U_LEFT0, U_CONV, U_GLU0, U_LEFT1, U_GLU1, SMALL, U_CONV, U_GLU0, U_GLU1, SMALL, U_FOUT, U_FIN, U_OUT, U_QKV0, U_QKV1, U_POINT0, U_POINT1, U_LEFT0, U_LEFT1, U_CONV, U_GLU0, U_GLU1, SMALL),
)

MB, MW = 128, 256
FAR = -(2.0**30)


def mm(a, b):
    return lax.dot_general(a, b, (((1,), (0,)), ((), ())), preferred_element_type=F32)


def mm_t(a, b):
    return lax.dot_general(a, b, (((1,), (1,)), ((), ())), preferred_element_type=F32)


def mm_tn(a, b):
    return lax.dot_general(a, b, (((0,), (0,)), ((), ())), preferred_element_type=F32)


def normed(v):
    centred = v - jnp.mean(v, axis=-1, keepdims=True)
    r = lax.rsqrt(jnp.mean(centred * centred, axis=-1, keepdims=True) + EPS)
    return centred * r, r


def gelu_both(v):
    c = math.sqrt(2.0 / math.pi)
    sq = v * v
    t = jnp.tanh(v * (c + (c * 0.044715) * sq))
    half = 0.5 * t + 0.5
    value = v * half
    slope = half + (0.5 * v) * (1.0 - t * t) * (c + (3.0 * c * 0.044715) * sq)
    return value, slope


def sigmoid(v):
    return 0.5 * jnp.tanh(0.5 * v) + 0.5


class Buffers:
    pass


class Plan:
    def __init__(self, dp, n, seqs, span, width, hidden, half):
        self.n, self.Z = n, dp // 2
        self.S, self.span = seqs, span
        self.D, self.FF, self.HALF = width, hidden, half
        self.LEN = span * n
        self.T = self.LEN // 2
        self.PH = n // 2
        self.B = math.isqrt(n)
        self.A = n // self.B
        assert self.A == self.B and n == 2 * seqs and dp % 2 == 0
        self.shared = SHARED if self.Z % 2 == 0 else ()
        self.sw = max(span, 128)
        self.sr = self.sw // span
        dn = width // n
        self.nw = max(dn, 128)
        self.nr = self.nw // dn
        self.FFn = hidden // n
        self.dims = [
            (width, 2 * width),
            (width, half),
            (width, hidden),
            (hidden, width),
            (width, 3 * width),
            (width, width),
            (width, hidden),
            (hidden, width),
        ]

    def whole(self, w):
        k, cols = self.dims[w]
        return (3, k, cols) if w == CONV else (k, cols)

    def kr(self, w):
        return self.dims[w][0] // self.n

    def hr(self, w):
        return self.kr(w) // 2

    def gcols(self, w):
        return self.dims[w][1] * (3 if w == CONV else 1)

    def piece(self, w, rows):
        return (rows, self.gcols(w))

    def buffers(self, take):
        T, D, FF, H, n = self.T, self.D, self.FF, self.HALF, self.n
        r = Buffers()

        def vm(shape, dtype):
            return take(pltpu.VMEM(shape, dtype))

        def sem(*shape):
            return take(pltpu.SemaphoreType.DMA(shape))

        every = range(WEIGHTS)
        parts = [(self.piece(w, self.hr(w)), BF16) for w in every] + [((16, FF // 2), BF16)]
        r.w = [vm(self.whole(w), BF16) for w in every]
        r.g8 = vm((16, FF), F32)
        r.gsm = vm((32, FF // 2), BF16)
        r.r = [None] * WEIGHTS + [vm((16, FF // 2), BF16)]
        for w in (CONV, QKV, OUT, FIN, FOUT):
            r.r[w] = vm(self.piece(w, n * self.hr(w)), BF16)
        r.r[LEFT], r.r[POINT], r.r[GLU] = r.r[FIN], r.r[FOUT], r.r[QKV]
        r.p = [vm((n - 1,) + shape, dtype) for shape, dtype in parts]
        if self.Z > 1:
            r.u = [vm(shape, dtype) for shape, dtype in parts]
            r.d = [vm(shape, dtype) for shape, dtype in parts]
        r.segbuf = vm((n, 8, self.sw), F32)
        r.segrow = vm((8, self.LEN), F32)
        r.segcol = vm((self.LEN + 16, 128), F32)
        r.segloc = vm((T + 16, 128), F32)
        r.mext = vm((T + 16, 128), F32)
        r.ms = vm((T // MB, 9 * MB, MW), BF16)
        r.qenc = vm((T, 128), BF16)
        r.kenc = vm((self.LEN, 128), BF16)
        r.smallbuf = vm((n, 32, self.FFn), BF16)
        r.nrm = vm((8, D), F32)
        r.midp = vm((16, FF), F32)
        r.xin = vm((T, D), BF16)
        r.cot = vm((T, D), BF16)
        r.a1 = vm((T, D), BF16)
        r.sg = vm((T, 2 * D), BF16)
        r.y1 = vm((T, D), F32)
        r.a2 = vm((T, D), BF16)
        r.pext = vm((3, T + 16, H), F32)
        r.dgl = vm((T, FF), BF16)
        r.dgr = vm((T, H), BF16)
        r.nm = vm((T, FF), BF16)
        r.rm = vm((T, 1), F32)
        r.big = vm((T + 16, FF), F32)
        r.sep = vm((T, FF), BF16)
        r.y2 = vm((T, D), F32)
        r.a4 = vm((T, D), BF16)
        r.qb = vm((T, D), BF16)
        r.kvb = vm((self.LEN, 2 * D), BF16)
        r.lse = vm((T, 128), F32)
        r.ctx = vm((T, D), BF16)
        r.y3 = vm((T, D), F32)
        r.a5 = vm((T, D), BF16)
        r.hid = vm((T + 32, FF), BF16)
        r.dg = vm((T, FF), BF16)
        r.osend = vm((T, D), BF16)
        r.gs = r.y3
        r.dkvr = vm((T, 2 * D), BF16)
        r.tr = vm((D, T), BF16)
        edges = (((8, H), F32), ((16, FF), BF16), ((16, FF), BF16), ((8, H), F32))
        r.es = [vm(shape, dtype) for shape, dtype in edges]
        r.er = [vm(shape, dtype) for shape, dtype in edges]
        r.s_loc = sem(WEIGHTS)
        r.s_as = sem(WEIGHTS)
        r.s_ar = sem(WEIGHTS, self.B - 1)
        r.s_br = sem(WEIGHTS, (self.A - 1) * self.B)
        r.s_ds = sem(WEIGHTS)
        r.s_dr = sem(WEIGHTS)
        if self.shared:
            r.s_hs = sem(WEIGHTS)
            r.s_hr = sem(WEIGHTS)
        r.s_rs = sem(UNITS)
        r.s_rr = sem(UNITS)
        r.s_ps = sem(UNITS, 2)
        r.s_pr = sem(UNITS, 2)
        if self.Z > 1:
            r.s_zs = sem(UNITS, 2)
            r.s_zr = sem(UNITS, 2)
        r.s_fs = sem(UNITS)
        r.s_fr = sem(UNITS)
        r.s_fl = sem(UNITS)
        r.s_xs = sem(4, self.S)
        r.s_xr = sem(4, max(self.PH, self.S))
        r.s_gs = sem(2 * self.S)
        r.s_gr = sem(n)
        r.s_ms = sem(n)
        r.s_mr = sem(n)
        r.s_es = sem(4)
        r.s_er = sem(4)
        r.s_ks = sem(1)
        r.s_kr = sem(1)
        r.s_js = sem(HEADS // 2)
        r.s_jr = sem(HEADS // 2)
        return r


INPUTS = 4 + WEIGHTS
OUTPUTS = 2 + WEIGHTS + 1


def kernel(plan, *refs):
    ins, outs = refs[:INPUTS], refs[INPUTS : INPUTS + OUTPUTS]
    scratch = iter(refs[INPUTS + OUTPUTS :])
    r = plan.buffers(lambda shape: next(scratch))
    r.x, r.seg, r.ct, r.small = ins[:4]
    r.h = ins[4:]
    r.o_out, r.o_ig = outs[:2]
    r.o = outs[2:]
    n, Z, S, span = plan.n, plan.Z, plan.S, plan.span
    T, D, FF, H, PH = plan.T, plan.D, plan.FF, plan.HALF, plan.PH
    A, B = plan.A, plan.B
    dp, q = lax.axis_index("dp"), lax.axis_index("seq")
    z, c = dp // 2, dp % 2
    oc = 1 - c

    def aligned(v, m=16):
        return pl.multiple_of(v, m)

    def dev(core, chip, plane=None):
        return ((z if plane is None else plane) * 2 + core, chip)

    sibling = dev(oc, q)

    def remote(src, dst, ss, rs, to):
        return pltpu.make_async_remote_copy(
            src_ref=src, dst_ref=dst, send_sem=ss, recv_sem=rs, device_id=to, device_id_type=MESH
        )

    barrier = pltpu.get_barrier_semaphore()
    for core in range(2):

        def greet(t, _, core=core):
            chip = lax.rem(q + t, n)
            to = (z * 2 + (c + core) % 2, chip)
            pl.semaphore_signal(barrier, inc=1, device_id=to, device_id_type=MESH)
            return 0

        lax.fori_loop(1 - core, n, greet, 0)
    if Z > 1:

        @pl.when(z > 0)
        def _():
            pl.semaphore_signal(barrier, inc=1, device_id=dev(c, q, z - 1), device_id_type=MESH)

        @pl.when(z < Z - 1)
        def _():
            pl.semaphore_signal(barrier, inc=1, device_id=dev(c, q, z + 1), device_id_type=MESH)

    pl.semaphore_wait(barrier, 2 * n - 1 + (z + Z - 1) // Z + (2 * Z - 2 - z) // Z)

    def vrows(ref, w, row0, rows):
        ds = pl.ds(aligned(row0), rows)
        return ref.at[:, ds] if w == CONV else ref.at[ds]

    def bytes_of(view, semaphore):
        return pltpu.make_async_copy(view, view, semaphore)

    def qof(core, f, g):
        f, g = f % B, g % B
        return core * (f * B + g) + (1 - core) * (g * B + f)

    b_, a_ = q % B, q // B
    f_, g_ = c * a_ + oc * b_, c * b_ + oc * a_
    par = z % 2
    partner = dev(c, q, z + 1 - 2 * par)

    def wrows(ref, w, row0, rows, side):
        if w not in plan.shared:
            return vrows(ref, w, row0, rows)
        size = plan.dims[w][1] // 2
        cols = pl.ds(pl.multiple_of(side * size, 128), size)
        if w == CONV:
            return ref.at[:, pl.ds(aligned(row0), rows), cols]
        return ref.at[pl.ds(aligned(row0), rows), cols]

    def wblock(w, shard, side=par):
        return wrows(r.w[w], w, shard * plan.kr(w) + c * plan.hr(w), plan.hr(w), side)

    def own_block(w):
        return wrows(r.h[w], w, c * plan.hr(w), plan.hr(w), par)

    def copy_a(w, t):
        to = dev(c, qof(c, f_ + t, g_))
        return remote(own_block(w), wblock(w, q), r.s_as.at[w], r.s_ar.at[w, t - 1], to)

    def copy_b(w, u, t):
        blk = wblock(w, qof(c, f_ + B - t, g_))
        src = own_block(w) if t == 0 else blk
        to = dev(c, qof(c, f_, g_ + u))
        return remote(src, blk, r.s_as.at[w], r.s_br.at[w, (u - 1) * B + t], to)

    def shard_from(u, t):
        return qof(c, f_ + B - t, g_ + B - u)

    def pass_on(w, u, t):
        blk = wblock(w, shard_from(u, t))
        remote(blk, blk, r.s_ds.at[w], r.s_dr.at[w], sibling).start()
        if w in plan.shared:
            remote(blk, blk, r.s_hs.at[w], r.s_hr.at[w], partner).start()

    def local_shard(w):
        dst = vrows(r.w[w], w, q * plan.kr(w), plan.kr(w))
        return pltpu.make_async_copy(r.h[w], dst, r.s_loc.at[w])

    def g0(w):
        local_shard(w).start()
        for t in range(1, B):
            copy_a(w, t).start()
        for u in range(1, A):
            copy_b(w, u, 0).start()

    def g1(w):
        for t in range(1, B):
            bytes_of(wblock(w, shard_from(0, t)), r.s_ar.at[w, t - 1]).wait()
            for u in range(1, A):
                copy_b(w, u, t).start()
            pass_on(w, 0, t)

    def g2(w):
        for u in range(1, A):
            for t in range(B):
                bytes_of(wblock(w, shard_from(u, t)), r.s_br.at[w, (u - 1) * B + t]).wait()
                pass_on(w, u, t)

    def others(w):
        return wrows(r.w[w], w, 0, (n - 1) * plan.hr(w), 0)

    def gz(w):
        if w not in plan.shared:
            return
        bytes_of(others(w), r.s_hr.at[w]).wait()
        for u in range(A):
            for t in range(B):
                if (u, t) != (0, 0):
                    blk = wblock(w, shard_from(u, t), 1 - par)
                    remote(blk, blk, r.s_ds.at[w], r.s_dr.at[w], sibling).start()

    def g3(w):
        local_shard(w).wait()
        bytes_of(vrows(r.w[w], w, 0, (n - 1) * plan.hr(w)), r.s_dr.at[w]).wait()

    gather_steps = (g0, g1, g2, gz)
    forward_turns = iter(FORWARD)

    def gather(steps):
        for k, w in steps:
            if w == TOKENS:
                tokens_in(r.ct, r.cot, 1)
            else:
                gather_steps[k](w)

    def pass_turn():
        gather(next(forward_turns))

    def pass_turns(count):
        every = [(k, next(forward_turns)) for k in range(count)]
        return [(k, lambda steps=steps: gather(steps)) for k, steps in every if steps]

    def gather_sent(w):
        bytes_of(others(w), r.s_as.at[w]).wait()
        bytes_of(vrows(r.w[w], w, 0, (n - 1) * plan.hr(w)), r.s_ds.at[w]).wait()
        if w in plan.shared:
            bytes_of(others(w), r.s_hs.at[w]).wait()

    def token_rows(ref, slot):
        return ref.at[pl.ds(aligned(slot * span), span)]

    def tokens_in(src, dst, k):
        for j in range(S):
            chip, core, slot = S * c + j, q // PH, q % PH
            here = jnp.logical_and(chip == q, core == c)
            there = token_rows(dst, slot)

            @pl.when(here)
            def _():
                pltpu.make_async_copy(src.at[j], there, r.s_xr.at[k, slot]).start()

            @pl.when(jnp.logical_not(here))
            def _():
                remote(
                    src.at[j], there, r.s_xs.at[k, j], r.s_xr.at[k, slot], dev(core, chip)
                ).start()

    def tokens_in_done(dst, k):
        for slot in range(PH):
            blk = token_rows(dst, slot)
            pltpu.make_async_copy(blk, blk, r.s_xr.at[k, slot]).wait()

    def tokens_in_sent(src, dst, k):
        for j in range(S):
            chip, core, slot = S * c + j, q // PH, q % PH
            here = jnp.logical_and(chip == q, core == c)

            @pl.when(jnp.logical_not(here))
            def _():
                remote(
                    src.at[j],
                    token_rows(dst, slot),
                    r.s_xs.at[k, j],
                    r.s_xr.at[k, slot],
                    dev(core, chip),
                ).wait_send()

    def tokens_out(src, dst, k):
        for p in range(PH):
            chip, core, slot = c * PH + p, q // S, q % S
            here = jnp.logical_and(chip == q, core == c)

            @pl.when(here)
            def _():
                pltpu.make_async_copy(token_rows(src, p), dst.at[slot], r.s_xr.at[k, slot]).start()

            @pl.when(jnp.logical_not(here))
            def _():
                remote(
                    token_rows(src, p),
                    dst.at[slot],
                    r.s_xs.at[k, p],
                    r.s_xr.at[k, slot],
                    dev(core, chip),
                ).start()

    def tokens_out_done(src, dst, k):
        for j in range(S):
            pltpu.make_async_copy(dst.at[j], dst.at[j], r.s_xr.at[k, j]).wait()
        for p in range(PH):
            chip, core, slot = c * PH + p, q // S, q % S
            here = jnp.logical_and(chip == q, core == c)

            @pl.when(jnp.logical_not(here))
            def _():
                remote(
                    token_rows(src, p),
                    dst.at[slot],
                    r.s_xs.at[k, p],
                    r.s_xr.at[k, slot],
                    dev(core, chip),
                ).wait_send()

    def seg_send():
        for j in range(S):
            for core in range(2):
                chip = S * c + j
                here = jnp.logical_and(chip == q, c == core)
                i = 2 * j + core

                @pl.when(here)
                def _():
                    pltpu.make_async_copy(r.seg.at[j], r.segbuf.at[q], r.s_gr.at[q]).start()

                @pl.when(jnp.logical_not(here))
                def _():
                    remote(
                        r.seg.at[j],
                        r.segbuf.at[q],
                        r.s_gs.at[i],
                        r.s_gr.at[q],
                        dev(core, chip),
                    ).start()

    def seg_sent():
        for j in range(S):
            for core in range(2):
                chip = S * c + j
                here = jnp.logical_and(chip == q, c == core)

                @pl.when(jnp.logical_not(here))
                def _():
                    remote(
                        r.seg.at[j],
                        r.segbuf.at[q],
                        r.s_gs.at[2 * j + core],
                        r.s_gr.at[q],
                        dev(core, chip),
                    ).wait_send()

    def small_copy(t):
        return remote(
            r.small,
            r.smallbuf.at[q],
            r.s_ms.at[t],
            r.s_mr.at[t],
            dev(c, (q + t) % n),
        )

    def small_arrived(t):
        blk = r.smallbuf.at[(q + n - t) % n]
        return remote(blk, blk, r.s_ms.at[t], r.s_mr.at[t], sibling)

    def edge_copy(i):
        return remote(r.es[i], r.er[i], r.s_es.at[i], r.s_er.at[i], sibling)

    def edge_send(i, last, first):
        r.es[i][...] = jnp.where(c == 0, last, first)
        edge_copy(i).start()

    def edge_take(i):
        edge_copy(i).wait()
        got = r.er[i][...]
        none = jnp.zeros_like(got)
        return jnp.where(c == 1, got, none), jnp.where(c == 0, got, none)

    def columns(u):
        w, half = UNIT_WEIGHT[u], UNIT_PART[u]
        size = plan.gcols(w)
        return (0, size) if half is None else (half * (size // 2), size // 2)

    def urows(ref, u, row0, rows, shift=0):
        col0, size = columns(u)
        return ref.at[pl.ds(aligned(row0), rows), pl.ds(col0 + shift, size)]

    grad_home = {GLU: (r.hid, 2 * D), CONV: (r.dkvr, 0), LEFT: (r.sep, 0), QKV: (r.dg, 0)}

    def gpiece(u, shard, half):
        if u == SMALL:
            return r.gsm.at[pl.ds(pl.multiple_of(half * 16, 16), 16)]
        w = UNIT_WEIGHT[u]
        ref, shift = grad_home.get(w, (r.w[w] if w < WEIGHTS else None, 0))
        return urows(ref, u, shard * plan.kr(w) + half * plan.hr(w), plan.hr(w), shift)

    def rpiece(u, shard):
        w = UNIT_WEIGHT[u]
        if u == SMALL:
            return r.r[w]
        return urows(r.r[w], u, shard * plan.hr(w), plan.hr(w))

    def slots(u, first, count):
        buf = r.p[UNIT_WEIGHT[u]]
        if u == SMALL:
            return buf.at[pl.ds(first, count)]
        col0, size = columns(u)
        return buf.at[pl.ds(first, count), :, pl.ds(col0, size)]

    def ppiece(u, slot):
        buf = r.p[UNIT_WEIGHT[u]]
        if u == SMALL:
            return buf.at[slot]
        col0, size = columns(u)
        return buf.at[slot, :, pl.ds(col0, size)]

    def zpiece(u, way):
        buf = (r.u, r.d)[way][UNIT_WEIGHT[u]]
        if u == SMALL:
            return buf
        col0, size = columns(u)
        return buf.at[:, pl.ds(col0, size)]

    def copy_r(u, s):
        return remote(gpiece(u, s, oc), rpiece(u, s), r.s_rs.at[u], r.s_rr.at[u], sibling)

    def all_r(u, semaphore):
        w = UNIT_WEIGHT[u]
        view = r.r[w] if u == SMALL else urows(r.r[w], u, 0, n * plan.hr(w))
        return bytes_of(view, semaphore.at[u])

    def shards(u):
        return 1 if u == SMALL else n

    def red0(u):
        for s in range(shards(u)):
            copy_r(u, s).start()

    def plus(a, b):
        return a[...].astype(F32) + b[...].astype(F32)

    def add_core(u, s):
        mine = gpiece(u, s, c)
        mine[...] = plus(mine, rpiece(u, s)).astype(mine.dtype)

    def slot1(u, t):
        return (u - 1) * B + t

    def slot2(t):
        return (A - 1) * B + t - 1

    def copy_p1(u, k, t):
        return remote(
            gpiece(u, qof(c, f_ + t, g_ + k), c),
            ppiece(u, slot1(k, t)),
            r.s_ps.at[u, 0],
            r.s_pr.at[u, 0],
            dev(c, qof(c, f_, g_ + k)),
        )

    def copy_p2(u, t):
        to = qof(c, f_ + t, g_)
        return remote(
            r.r[WEIGHTS] if u == SMALL else gpiece(u, to, c),
            ppiece(u, slot2(t)),
            r.s_ps.at[u, 1],
            r.s_pr.at[u, 1],
            dev(c, to),
        )

    def all_p(u, step, semaphore):
        count = B - 1 if step else A - 1 if u == SMALL else (A - 1) * B
        return bytes_of(slots(u, 0, count), semaphore.at[u, step])

    def red1(u):
        all_r(u, r.s_rr).wait()
        if u == SMALL:
            add_core(u, 0)
            for k in range(1, A):
                copy_p1(u, k, 0).start()
            return

        def send(i, _):
            k, t = i // B + 1, i % B
            add_core(u, qof(c, f_ + t, g_ + k))
            copy_p1(u, k, t).start()
            return 0

        lax.fori_loop(0, (A - 1) * B, send, 0)
        lax.fori_loop(0, B, lambda t, _: (add_core(u, qof(c, f_ + t, g_)), 0)[1], 0)

    def red1b(u):
        all_p(u, 0, r.s_pr).wait()

        def send(t, _):
            if u == SMALL:
                total, to = gpiece(u, 0, c)[...].astype(F32), r.r[WEIGHTS]
            else:
                to = gpiece(u, qof(c, f_ + t, g_), c)
                total = to[...].astype(F32)
            for k in range(1, A):
                total = total + ppiece(u, slot1(k, 0 if u == SMALL else t))[...].astype(F32)
            to[...] = total.astype(to.dtype)
            if u != SMALL:
                copy_p2(u, t).start()
            return 0

        if u == SMALL:
            send(0, 0)
            for t in range(1, B):
                copy_p2(u, t).start()
        else:
            lax.fori_loop(1, B, send, 0)

    def red2(u):
        all_p(u, 1, r.s_pr).wait()
        total = (r.r[WEIGHTS] if u == SMALL else gpiece(u, q, c))[...].astype(F32)
        if u != SMALL:
            for k in range(1, A):
                total = total + ppiece(u, slot1(k, 0))[...].astype(F32)
        for t in range(1, B):
            total = total + ppiece(u, slot2(t))[...].astype(F32)
        mine = ppiece(u, 0)
        mine[...] = total.astype(mine.dtype)

    def copy_z(u, way):
        return remote(
            ppiece(u, 1 + way),
            zpiece(u, way),
            r.s_zs.at[u, way],
            r.s_zr.at[u, way],
            dev(c, q, z + 1 if way == 0 else z - 1),
        )

    def red_hop(u, h):
        own, up, down = ppiece(u, 0), ppiece(u, 1), ppiece(u, 2)

        @pl.when(z == h)
        def _():
            if h == 0:
                up[...] = own[...]
            else:
                copy_z(u, 0).wait_recv()
                up[...] = plus(own, zpiece(u, 0)).astype(up.dtype)
            if h < Z - 1:
                copy_z(u, 0).start()

        @pl.when(z == Z - 1 - h)
        def _():
            if h == 0:
                down[...] = own[...]
            else:
                copy_z(u, 1).wait_recv()
                if h < Z - 1:
                    down[...] = plus(own, zpiece(u, 1)).astype(down.dtype)
            if h < Z - 1:
                copy_z(u, 1).start()

    def final_rows(u):
        w = UNIT_WEIGHT[u]
        if u == SMALL:
            return r.o[w].at[pl.ds(pl.multiple_of(c * 16, 16), 16)]
        return urows(r.o[w], u, c * plan.hr(w), plan.hr(w))

    def final_local(u):
        return pltpu.make_async_copy(ppiece(u, 0), final_rows(u), r.s_fl.at[u])

    def final_remote(u):
        return remote(ppiece(u, 0), final_rows(u), r.s_fs.at[u], r.s_fr.at[u], sibling)

    def red_final(u):
        if Z > 1:
            own, up = ppiece(u, 0), ppiece(u, 1)

            @pl.when(z == Z - 1)
            def _():
                own[...] = up[...]

            @pl.when(z < Z - 1)
            def _():
                own[...] = plus(up, zpiece(u, 1)).astype(own.dtype)

        final_local(u).start()
        final_remote(u).start()

    def red_end(u):
        final_local(u).wait()
        final_remote(u).wait()
        all_r(u, r.s_rs).wait()
        all_p(u, 0, r.s_ps).wait()
        all_p(u, 1, r.s_ps).wait()
        if Z > 1:

            @pl.when(z < Z - 1)
            def _():
                copy_z(u, 0).wait_send()

            @pl.when(z > 0)
            def _():
                copy_z(u, 1).wait_send()

    def red2_hop(u):
        red2(u)
        red_hop(u, 0)

    def last_hop(u):
        red_hop(u, Z - 1)
        red_final(u)

    ahead = {}
    turns = iter(SCHEDULE)

    def enlist(u):
        if Z > 1:
            ahead[u] = [red1, red1b, red2_hop]
            ahead[u] += [lambda k, h=h: red_hop(k, h) for h in range(1, Z - 1)]
            ahead[u].append(last_hop)
        else:
            ahead[u] = [red1, red1b, red2, red_final]

    def reduce_start(*units):
        for u in units:
            red0(u)
            enlist(u)

    def steps_of(units):
        return [(ahead[u].pop(0), u) for u in units if ahead[u]]

    def move(units):
        for step, u in steps_of(units):
            step(u)

    def turn():
        move(next(turns))

    def turns_of(count):
        acts = []
        for k in range(count):
            steps = steps_of(next(turns))
            if steps:
                acts.append((k, lambda steps=steps: [step(u) for step, u in steps][:0]))
        return acts

    def loop(count, body, after=()):
        def step(i, _):
            body(i)
            for k, act in after:
                pl.when(i == k)(lambda act=act: (act(), None)[1])
            return 0

        lax.fori_loop(0, count, step, 0)

    RB = 256
    NB = T // RB

    def rows_of(i, size=RB, base=0):
        return pl.ds(pl.multiple_of(i * size + base, base or size), size)

    seg_send()
    small_local = pltpu.make_async_copy(r.small, r.smallbuf.at[q], r.s_mr.at[0])
    small_local.start()
    for what in START:
        if what == SMALLS:
            for t in range(1, n):
                small_copy(t).start()
        elif what == TOKENS:
            tokens_in(r.x, r.xin, 0)
        else:
            g0(what)
    r.g8[...] = jnp.zeros((16, FF), F32)
    pass_turn()

    for s in range(n):
        blk = r.segbuf.at[s]
        pltpu.make_async_copy(blk, blk, r.s_gr.at[s]).wait()
    for grp in range(n // plan.sr):
        got = r.segbuf[grp * plan.sr]
        for k in range(1, plan.sr):
            got = got + r.segbuf[grp * plan.sr + k]
        r.segrow[:, grp * plan.sw : (grp + 1) * plan.sw] = got
    r.segcol[0:8] = jnp.full((8, 128), -1.0, F32)
    r.segcol[plan.LEN + 8 : plan.LEN + 16] = jnp.full((8, 128), -1.0, F32)
    for k in range(plan.LEN // 128):
        row = r.segrow[0:1, k * 128 : (k + 1) * 128]
        r.segcol[8 + k * 128 : 8 + (k + 1) * 128] = jnp.broadcast_to(row, (128, 128)).T
    r.segloc[...] = r.segcol[pl.ds(pl.multiple_of(c * T, 8), T + 16)]
    r.mext[0 : T + 8] = jnp.where(r.segloc[0 : T + 8] == r.segloc[1 : T + 9], 1.0, 0.0)

    def mask(o, start, rows):
        first = 8 + start + (0 if o > 0 else o)
        return r.mext[first : first + rows]

    small_local.wait()
    for t in range(1, n):
        small_arrived(t).wait_recv()
    for grp in range(n // plan.nr):
        got = r.smallbuf[grp * plan.nr].astype(F32)[0:8, 0 : plan.nw]
        for k in range(1, plan.nr):
            got = got + r.smallbuf[grp * plan.nr + k].astype(F32)[0:8, 0 : plan.nw]
        r.nrm[:, grp * plan.nw : (grp + 1) * plan.nw] = got
    for s in range(n):
        r.midp[:, s * plan.FFn : (s + 1) * plan.FFn] = r.smallbuf[s].astype(F32)[8:24]

    def ln_out(k, v):
        unit, _ = normed(v)
        return (unit * r.nrm[k : k + 1] + r.nrm[4 + k : 5 + k]).astype(BF16)

    def ln_back(k, e, v):
        unit, rs = normed(v)
        eg = e * r.nrm[k : k + 1]
        m1 = jnp.mean(eg, axis=-1, keepdims=True)
        m2 = jnp.mean(eg * unit, axis=-1, keepdims=True)
        cols = slice(k * D, (k + 1) * D)
        r.g8[11:12, cols] += jnp.sum(e * unit, axis=0, keepdims=True)
        r.g8[12:13, cols] += jnp.sum(e, axis=0, keepdims=True)
        return rs * (eg - m1 - unit * m2)

    pass_turn()

    def window(b):
        return min(max(b * MB - (MW - MB) // 2 + 16, 0), T + 32 - MW)

    ahead_of = lax.broadcasted_iota(jnp.int32, (MB, MW), 1) - lax.broadcasted_iota(
        jnp.int32, (MB, MW), 0
    )
    for b in range(T // MB):
        home = r.segloc[8 + b * MB : 8 + (b + 1) * MB]
        for o in range(-4, 5):
            there = r.segloc[8 + b * MB + o : 8 + (b + 1) * MB + o]
            same = jnp.where(home == there, 1.0, 0.0)
            hit = ahead_of == b * MB + 16 - window(b) + o
            tap = jnp.where(hit, jnp.concatenate([same] * (MW // 128), axis=1), 0.0)
            r.ms[b, (o + 4) * MB : (o + 5) * MB] = tap.astype(BF16)

    lane = lax.broadcasted_iota(jnp.int32, (1, 128), 1)
    lane_f = lane.astype(F32)
    own_doc = r.segloc[8 : T + 8] == lane_f
    r.qenc[...] = jnp.where(jnp.logical_and(lane < 4, jnp.logical_not(own_doc)), FAR, 0.0).astype(BF16)
    ones = jnp.logical_and(lane >= 4, lane < 7)
    r.kenc[...] = jnp.where(
        jnp.logical_or(r.segcol[8 : plan.LEN + 8] == lane_f, ones), 1.0, 0.0
    ).astype(BF16)

    pass_turn()
    pass_turn()
    g3(GLU)
    pass_turn()
    tokens_in_done(r.xin, 0)

    def glu(i):
        rows = rows_of(i)
        x = r.xin[rows].astype(F32)
        a1 = ln_out(0, x)
        r.a1[rows] = a1
        value = mm(a1, r.w[GLU][:, 0:D])
        gate = sigmoid(mm(a1, r.w[GLU][:, D : 2 * D]))
        r.sg[rows, 0:D] = gate.astype(BF16)
        r.sg[rows, D : 2 * D] = (value * gate * (1.0 - gate)).astype(BF16)
        y1 = x + value * gate
        r.y1[rows] = y1
        r.a2[rows] = ln_out(1, y1)

    loop(NB, glu, pass_turns(NB))
    pass_turn()
    g3(CONV)

    def conv(i):
        a2 = r.a2[rows_of(i)]
        for o in range(3):
            r.pext[o, rows_of(i, RB, 8)] = mm(a2, r.w[CONV][o])

    loop(NB, conv)
    edge_send(0, r.pext[0, T : T + 8], r.pext[2, 8:16])
    pass_turn()
    top, bottom = edge_take(0)
    r.pext[0, 0:8] = top
    r.pext[2, T + 8 : T + 16] = bottom
    pass_turn()
    for k in range(T // 128):
        lo = k * 128
        before = mask(-1, lo, 128)
        after = mask(1, lo, 128)
        pre = (
            r.pext[0, lo + 7 : lo + 135] * jnp.concatenate([before] * (H // 128), axis=1)
            + r.pext[1, lo + 8 : lo + 136]
            + r.pext[2, lo + 9 : lo + 137] * jnp.concatenate([after] * (H // 128), axis=1)
        )
        value, slope = gelu_both(pre)
        r.pext[1, lo + 8 : lo + 136] = value
        r.dgr[lo : lo + 128] = slope.astype(BF16)
    pass_turn()
    pass_turn()
    g3(LEFT)

    CH = 512
    RM = 128

    def left(i):
        rows, erows = rows_of(i, RM), rows_of(i, RM, 8)
        a2 = r.a2[rows]
        for k in range(FF // CH):
            value, slope = gelu_both(mm(a2, r.w[LEFT][:, k * CH : (k + 1) * CH]))
            r.dgl[rows, k * CH : (k + 1) * CH] = slope.astype(BF16)
            r.big[erows, k * CH : (k + 1) * CH] = value
        r.big[erows, 0:H] += r.pext[1, erows]
        unit, rs = normed(r.big[erows])
        r.nm[rows] = unit.astype(BF16)
        r.rm[rows] = rs
        r.hid[rows_of(i, RM, 16)] = (unit * r.midp[0:1] + r.midp[1:2]).astype(BF16)

    loop(T // RM, left, pass_turns(T // RM))
    edge_send(1, r.hid[T : T + 16], r.hid[16:32])
    r.hid[0:16], r.hid[T + 16 : T + 32] = edge_take(1)
    pass_turn()

    def depthwise(j):
        cols = pl.ds(pl.multiple_of(j * 256, 256), 256)
        for b in range(T // MB):
            near = r.hid[window(b) : window(b) + MW, cols]
            taps = mm(r.ms[b], near)
            total = taps[0:MB] * r.midp[2:3, cols]
            for o in range(1, 9):
                total = total + taps[o * MB : (o + 1) * MB] * r.midp[2 + o : 3 + o, cols]
            r.sep[b * MB : (b + 1) * MB, cols] = total.astype(BF16)

    loop(FF // 256, depthwise, pass_turns(FF // 256))
    pass_turn()
    g3(POINT)

    def point(i):
        rows = rows_of(i)
        y2 = r.y1[rows] + mm(r.sep[rows], r.w[POINT][...])
        r.y2[rows] = y2
        r.a4[rows] = ln_out(2, y2)

    loop(NB, point)
    pass_turn()
    pass_turn()
    g3(QKV)
    scale = 1.0 / math.sqrt(D // HEADS)

    def qkv(i):
        rows = rows_of(i)
        a4 = r.a4[rows]
        r.qb[rows] = (mm(a4, r.w[QKV][:, 0:D]) * scale).astype(BF16)
        here = pl.ds(pl.multiple_of(c * T + i * RB, RB), RB)
        r.kvb[here, 0:D] = mm(a4, r.w[QKV][:, D : 2 * D]).astype(BF16)
        r.kvb[here, D : 2 * D] = mm(a4, r.w[QKV][:, 2 * D : 3 * D]).astype(BF16)

    loop(NB, qkv)

    def kv_copy():
        blk = r.kvb.at[pl.ds(aligned(c * T), T)]
        return remote(blk, blk, r.s_ks.at[0], r.s_kr.at[0], sibling)

    kv_copy().start()
    pass_turn()
    heads_lanes = [lane < 64, lane >= 64]
    kv_copy().wait()
    pass_turn()

    def pair_cols(j, base=0):
        return pl.ds(pl.multiple_of(j * 128 + base, 128), 128)

    def head_lanes(e, v):
        return jnp.where(heads_lanes[e], v, jnp.zeros_like(v))

    def attend(j):
        cols, vcols = pair_cols(j), pair_cols(j, D)
        keys = jnp.concatenate([r.kvb[:, cols], r.kenc[...]], axis=1)
        for k in range(T // RB):
            rows = slice(k * RB, (k + 1) * RB)
            q2 = r.qb[rows, cols]
            got = []
            for e in range(2):
                score = mm_t(jnp.concatenate([head_lanes(e, q2), r.qenc[rows]], axis=1), keys)
                most = jnp.max(score, axis=-1, keepdims=True)
                power = jnp.exp(score - most)
                total = jnp.sum(power, axis=-1, keepdims=True)
                got.append(mm(power.astype(BF16), r.kvb[:, vcols]) / total)
                lse = most + jnp.log(total)
                r.lse[rows] = jnp.where(lane == 2 * j + e, lse, r.lse[rows])
            r.ctx[rows, cols] = jnp.where(heads_lanes[0], got[0], got[1]).astype(BF16)

    r.lse[...] = jnp.zeros((T, 128), F32)

    loop(HEADS // 2, attend, pass_turns(HEADS // 2))
    pass_turn()
    g3(OUT)

    def out(i):
        rows = rows_of(i)
        y3 = r.y2[rows] + mm(r.ctx[rows], r.w[OUT][...])
        r.y3[rows] = y3
        r.a5[rows] = ln_out(3, y3)

    loop(NB, out)
    pass_turn()
    pass_turn()
    g3(FIN)

    def ffn_in(i):
        rows = rows_of(i)
        a5 = r.a5[rows]
        for k in range(FF // CH):
            value, slope = gelu_both(mm(a5, r.w[FIN][:, k * CH : (k + 1) * CH]))
            r.hid[rows, k * CH : (k + 1) * CH] = value.astype(BF16)
            r.dg[rows, k * CH : (k + 1) * CH] = slope.astype(BF16)

    loop(NB, ffn_in, pass_turns(NB))
    pass_turn()
    g3(FOUT)

    def ffn_out(i):
        rows = rows_of(i)
        r.osend[rows] = (r.y3[rows] + mm(r.hid[rows], r.w[FOUT][...])).astype(BF16)

    loop(NB, ffn_out)
    pass_turn()
    tokens_out(r.osend, r.o_out, 2)
    for w in range(WEIGHTS):
        gather_sent(w)

    tokens_in_done(r.cot, 1)

    def ffn_back(i):
        rows = rows_of(i)
        f4 = r.cot[rows]
        for k in range(FF // CH):
            cols = slice(k * CH, (k + 1) * CH)
            up = mm_t(f4, r.w[FOUT][cols])
            r.dg[rows, cols] = (up * r.dg[rows, cols].astype(F32)).astype(BF16)
        e = mm_t(r.dg[rows], r.w[FIN][...])
        r.gs[rows] = f4.astype(F32) + ln_back(3, e, r.y3[rows])

    loop(NB, ffn_back)
    GC = 1024

    def grad_outer(k):
        cols = rows_of(k, GC)
        r.w[FOUT][cols] = mm_tn(r.hid[0:T, cols], r.cot[...]).astype(BF16)

    loop(FF // GC, grad_outer)
    reduce_start(U_FOUT)
    turn()
    r.tr[...] = r.a5[...].T

    def grad_inner(k):
        cols = rows_of(k, GC)
        r.w[FIN][:, cols] = mm(r.tr[...], r.dg[:, cols]).astype(BF16)

    loop(FF // GC, grad_inner)
    reduce_start(U_FIN)
    turn()

    def out_back(i):
        rows = rows_of(i)
        f3 = r.gs[rows].astype(BF16)
        r.a5[rows] = f3
        r.hid[rows, 3 * D : 4 * D] = mm_t(f3, r.w[OUT][...]).astype(BF16)

    loop(NB, out_back)
    r.w[OUT][...] = mm_tn(r.ctx[...], r.a5[...]).astype(BF16)
    reduce_start(U_OUT)
    turn()
    r.tr[...] = r.a4[...].T

    QB = 256

    def with_terms(extra, v):
        high = v.astype(BF16).astype(F32)
        mid = (v - high).astype(BF16).astype(F32)
        low = v - high - mid
        terms = jnp.where(lane == 4, high, jnp.where(lane == 5, mid, jnp.where(lane == 6, low, 0.0)))
        return extra - terms.astype(BF16)

    def attend_back(j):
        cols, vcols = pair_cols(j), pair_cols(j, D)
        k2 = r.kvb[:, cols]
        keys = jnp.concatenate([k2, r.kenc[...]], axis=1)
        values = jnp.concatenate([r.kvb[:, vcols], r.kenc[...]], axis=1)
        for k in range(T // QB):
            rows = slice(k * QB, (k + 1) * QB)
            q2 = r.qb[rows, cols]
            d2 = r.hid[rows, pair_cols(j, 3 * D)]
            inner = d2.astype(F32) * r.ctx[rows, cols].astype(F32)
            dq = jnp.zeros((QB, 128), F32)
            for e in range(2):
                qe, de = head_lanes(e, q2), head_lanes(e, d2)
                lse = jnp.sum(
                    jnp.where(lane == 2 * j + e, r.lse[rows], 0.0), axis=-1, keepdims=True
                )
                delta = jnp.sum(head_lanes(e, inner), axis=-1, keepdims=True)
                shifted = mm_t(keys, jnp.concatenate([qe, with_terms(r.qenc[rows], lse)], axis=1))
                probs = jnp.exp(shifted)
                none = jnp.zeros((QB, 128), BF16)
                moved = mm_t(values, jnp.concatenate([de, with_terms(none, delta)], axis=1))
                ds = (probs * moved).astype(BF16)
                dk = mm(ds, qe)
                dv = mm(probs.astype(BF16), de)
                for kk in range(2):
                    half = slice(kk * T, (kk + 1) * T)
                    at = 2 * D + kk * 128
                    if k == 0 and e == 0:
                        r.big[0:T, at : at + 128] = dk[half]
                        r.big[0:T, at + 256 : at + 384] = dv[half]
                    else:
                        r.big[0:T, at : at + 128] += dk[half]
                        r.big[0:T, at + 256 : at + 384] += dv[half]
                dq = dq + mm_tn(ds, head_lanes(e, k2))
            r.hid[rows, cols] = (dq * scale).astype(BF16)

        def part(core, what):
            at = pl.multiple_of(2 * D + core * 128 + what * 256, 128)
            return r.big[0:T, pl.ds(at, 128)]

        for what in range(2):
            mine = pl.ds(pl.multiple_of(j * 256 + what * 128, 128), 128)
            r.big[0:T, mine] = part(c, what)
            r.cot[:, pl.ds(pl.multiple_of(lax.rem(j, 2) * 256 + what * 128, 128), 128)] = part(
                oc, what
            ).astype(BF16)
        dkv_copy(j).start()

        @pl.when(j > 0)
        def _():
            pair_back(j - 1)

    def dkv_copy(j):
        slot = lax.rem(j, 2)
        return remote(
            r.cot.at[:, pl.ds(pl.multiple_of(slot * 256, 128), 256)],
            r.dkvr.at[:, pl.ds(pl.multiple_of(j * 256, 128), 256)],
            r.s_js.at[j],
            r.s_jr.at[j],
            sibling,
        )

    def pair_back(j):
        dkv_copy(j).wait()
        both = pl.ds(pl.multiple_of(j * 256, 256), 256)
        dkv = (r.big[0:T, both] + r.dkvr[:, both].astype(F32)).astype(BF16)
        pair = jnp.concatenate([r.hid[0:T, pair_cols(j)], dkv], axis=1)
        weight = jnp.concatenate([r.w[QKV][:, pair_cols(j, base)] for base in (0, D, 2 * D)], axis=1)
        share = mm_t(pair, weight)

        @pl.when(j == 0)
        def _():
            r.big[0:T, 3 * D : 4 * D] = share

        @pl.when(j > 0)
        def _():
            r.big[0:T, 3 * D : 4 * D] += share

        grad = mm(r.tr[...], pair)
        r.dg[:, pl.ds(pl.multiple_of(j * 384, 128), 384)] = grad.astype(BF16)

    acts = turns_of(3)
    enlist(U_QKV0)
    acts += [(2, lambda: red0(U_QKV0))] + [(k + 3, act) for k, act in turns_of(1)]
    loop(HEADS // 2, attend_back, acts)
    pair_back(HEADS // 2 - 1)
    reduce_start(U_QKV1)
    turn()

    def qkv_back(i):
        rows = rows_of(i)
        r.gs[rows] += ln_back(2, r.big[rows, 3 * D : 4 * D], r.y2[rows])

    loop(NB, qkv_back)

    def point_back(i):
        rows = rows_of(i)
        f2 = r.gs[rows].astype(BF16)
        r.a4[rows] = f2
        for k in range(FF // CH):
            cols = slice(k * CH, (k + 1) * CH)
            d = mm_t(f2, r.w[POINT][cols])
            r.hid[rows_of(i, RB, 16), cols] = d.astype(BF16)

    loop(NB, point_back)
    edge_send(2, r.hid[T : T + 16], r.hid[16:32])
    turn()

    def grad_point(k):
        cols = rows_of(k, GC)
        r.w[POINT][cols] = mm_tn(r.sep[:, cols], r.a4[...]).astype(BF16)

    loop(FF // GC, grad_point)
    reduce_start(U_POINT0, U_POINT1)
    turn()
    r.hid[0:16], r.hid[T + 16 : T + 32] = edge_take(2)

    def depth_back(j):
        cols = pl.ds(pl.multiple_of(j * 256, 256), 256)
        gain, shift = r.midp[0:1, cols], r.midp[1:2, cols]
        sums = [jnp.zeros((8, 256), F32) for _ in range(9)]
        for b in range(T // MB):
            lo = b * MB
            taps = mm(r.ms[b], r.hid[window(b) : window(b) + MW, cols])
            a3 = r.nm[lo : lo + MB, cols].astype(F32) * gain + shift
            total = jnp.zeros((MB, 256), F32)
            for o in range(9):
                moved = taps[(8 - o) * MB : (9 - o) * MB]
                total = total + moved * r.midp[2 + o : 3 + o, cols]
                part = moved * a3
                for g in range(MB // 8):
                    sums[o] = sums[o] + part[g * 8 : (g + 1) * 8]
            r.big[lo + 8 : lo + 8 + MB, cols] = total
        for o in range(9):
            r.g8[2 + o : 3 + o, cols] = jnp.sum(sums[o], axis=0, keepdims=True)

    loop(FF // 256, depth_back, turns_of(FF // 256))

    def mid_back(i):
        rows, erows = rows_of(i, RM), rows_of(i, RM, 8)
        e = r.big[erows]
        unit = r.nm[rows].astype(F32)
        eg = e * r.midp[0:1]
        m1 = jnp.mean(eg, axis=-1, keepdims=True)
        m2 = jnp.mean(eg * unit, axis=-1, keepdims=True)
        r.g8[0:1] += jnp.sum(e * unit, axis=0, keepdims=True)
        r.g8[1:2] += jnp.sum(e, axis=0, keepdims=True)
        dmid = r.rm[rows] * (eg - m1 - unit * m2)
        r.dgl[rows] = (dmid * r.dgl[rows].astype(F32)).astype(BF16)
        right = dmid[:, 0:H] * r.dgr[rows].astype(F32)
        r.pext[0, erows] = right.astype(BF16).astype(F32)

    loop(T // RM, mid_back, turns_of(T // RM))
    edge_send(3, r.pext[0, T : T + 8], r.pext[0, 8:16])
    r.tr[...] = r.a2[...].T

    def grad_left(k):
        cols = rows_of(k, GC)
        r.sep[:, cols] = mm(r.tr[...], r.dgl[:, cols]).astype(BF16)

    half = FF // GC // 2
    lax.fori_loop(0, half, lambda k, _: (grad_left(k), 0)[1], 0)
    reduce_start(U_LEFT0)
    turn()
    lax.fori_loop(half, 2 * half, lambda k, _: (grad_left(k), 0)[1], 0)
    reduce_start(U_LEFT1)
    turn()
    top, bottom = edge_take(3)
    r.pext[0, 0:8] = top
    r.pext[0, T + 8 : T + 16] = bottom
    for k in range(T // 128):
        lo = k * 128
        for o in (-1, 0, 1):
            moved = r.pext[0, lo + 8 - o : lo + 136 - o]
            if o:
                moved = moved * jnp.concatenate([mask(-o, lo, 128)] * (H // 128), axis=1)
            r.hid[lo : lo + 128, (o + 1) * H : (o + 2) * H] = moved.astype(BF16)
    for o in range(3):
        cols = slice(o * H, (o + 1) * H)
        r.dkvr[:, cols] = mm(r.tr[...], r.hid[0:T, cols]).astype(BF16)
    reduce_start(U_CONV)
    turn()

    def branch_back(i):
        rows = rows_of(i)
        e = mm_t(r.dgl[rows], r.w[LEFT][...])
        for o in range(3):
            e = e + mm_t(r.hid[rows, o * H : (o + 1) * H], r.w[CONV][o])
        r.gs[rows] += ln_back(1, e, r.y1[rows])

    loop(NB, branch_back, turns_of(NB))

    def gate_back(i):
        rows = rows_of(i)
        g = r.gs[rows]
        r.sg[rows, 0:D] = (g * r.sg[rows, 0:D].astype(F32)).astype(BF16)
        r.sg[rows, D : 2 * D] = (g * r.sg[rows, D : 2 * D].astype(F32)).astype(BF16)

    loop(NB, gate_back)
    r.tr[...] = r.a1[...].T

    def grad_glu(k):
        cols = rows_of(k, D)
        to = pl.ds(pl.multiple_of(k * D + 2 * D, D), D)
        r.hid[0:T, to] = mm(r.tr[...], r.sg[:, cols]).astype(BF16)

    grad_glu(0)
    reduce_start(U_GLU0)
    turn()
    grad_glu(1)
    reduce_start(U_GLU1)
    turn()

    def glu_back(i):
        rows = rows_of(i)
        e = mm_t(r.sg[rows], r.w[GLU][...])
        total = r.gs[rows] + ln_back(0, e, r.xin[rows].astype(F32))
        r.a5[rows] = total.astype(BF16)

    loop(NB, glu_back, turns_of(NB))
    r.gsm[0:16] = r.g8[:, 0 : FF // 2].astype(BF16)
    r.gsm[16:32] = r.g8[:, FF // 2 : FF].astype(BF16)
    reduce_start(SMALL)
    move(TAIL[0])
    tokens_out(r.a5, r.o_ig, 3)
    move(TAIL[1])
    while any(ahead.values()):
        move(range(UNITS))

    for u in range(UNITS):
        red_end(u)
    tokens_out_done(r.osend, r.o_out, 2)
    tokens_out_done(r.a5, r.o_ig, 3)
    tokens_in_sent(r.x, r.xin, 0)
    tokens_in_sent(r.ct, r.cot, 1)
    seg_sent()
    for t in range(1, n):
        small_copy(t).wait_send()


def local(
    inputs,
    segment_ids,
    cotangent,
    norm_gain,
    norm_bias,
    glu_weight,
    left_weight,
    conv_weight,
    mid_gain,
    mid_bias,
    depth_weight,
    point_weight,
    qkv_weight,
    out_weight,
    ffn_in,
    ffn_out,
):
    seqs, span, width = inputs.shape
    n = lax.axis_size("seq")
    plan = Plan(
        lax.axis_size("dp"), n, seqs, span, width, ffn_in.shape[1], conv_weight.shape[2]
    )
    q = lax.axis_index("seq")

    def placed(piece, repeats):
        if repeats == 1:
            return piece
        size = piece.shape[-1]
        tiled = jnp.tile(piece, (1,) * (piece.ndim - 1) + (repeats,))
        at = lax.broadcasted_iota(jnp.int32, tiled.shape, tiled.ndim - 1) // size
        return jnp.where(at == q % repeats, tiled, jnp.zeros_like(tiled))

    segs = placed(segment_ids.astype(F32), plan.sr)
    segs = jnp.broadcast_to(segs[:, None, :], (seqs, 8, plan.sw))
    norms = placed(jnp.concatenate([norm_gain, norm_bias], 0), plan.nr)
    norms = jnp.pad(norms, ((0, 0), (0, plan.FFn - plan.nw)))
    small = jnp.concatenate([norms, mid_gain[None], mid_bias[None], depth_weight], 0)
    small = jnp.pad(small, ((0, 32 - small.shape[0]), (0, 0)))
    weights = [None] * WEIGHTS
    weights[GLU], weights[CONV], weights[LEFT] = glu_weight, conv_weight, left_weight
    weights[POINT], weights[QKV], weights[OUT] = point_weight, qkv_weight, out_weight
    weights[FIN], weights[FOUT] = ffn_in, ffn_out

    shapes = []
    plan.buffers(shapes.append)
    out_shape = [jax.ShapeDtypeStruct(inputs.shape, BF16)] * 2
    out_shape += [jax.ShapeDtypeStruct(plan.piece(w, plan.kr(w)), BF16) for w in range(WEIGHTS)]
    out_shape += [jax.ShapeDtypeStruct((32, plan.FF // 2), BF16)]
    hbm = pl.BlockSpec(memory_space=pl.ANY)
    got = pl.pallas_call(
        lambda *refs: kernel(plan, *refs),
        out_shape=out_shape,
        in_specs=[hbm] * INPUTS,
        out_specs=[hbm] * OUTPUTS,
        scratch_shapes=shapes,
        compiler_params=pltpu.CompilerParams(
            collective_id=0, has_side_effects=True, vmem_limit_bytes=64 << 20
        ),
        name="cell",
    )(inputs, segs, cotangent, small, *weights)
    out = unpacked(plan, got)
    return (
        out[0],
        out[1],
        out[2 + WEIGHTS],
        out[3 + WEIGHTS],
        out[2 + GLU],
        out[2 + LEFT],
        out[2 + CONV],
        out[4 + WEIGHTS].reshape(-1),
        out[5 + WEIGHTS].reshape(-1),
        out[6 + WEIGHTS],
        out[2 + POINT],
        out[2 + QKV],
        out[2 + OUT],
        out[2 + FIN],
        out[2 + FOUT],
    )


def unpacked(plan, parts):
    count = 2 + WEIGHTS
    dn = plan.D // plan.n
    wide = [jax.ShapeDtypeStruct(p.shape, F32) for p in parts[:count]]
    conv, qkv, H = 2 + CONV, 2 + QKV, plan.HALF
    wide[conv] = jax.ShapeDtypeStruct((3, plan.kr(CONV), H), F32)
    tiny = [(4, dn), (4, dn), (1, plan.FFn), (1, plan.FFn), (9, plan.FFn)]
    out_shape = wide + [jax.ShapeDtypeStruct(shape, F32) for shape in tiny]

    def body(*refs):
        ins, outs = refs[:count], refs[count + 1 : 2 * count + 1]
        sums, tinies = refs[count], refs[2 * count + 1 : 2 * count + 6]
        near, far = refs[2 * count + 6 : 3 * count + 6], refs[3 * count + 6 : 4 * count + 6]
        came, went = refs[4 * count + 6], refs[4 * count + 7]

        def arrive(i):
            return pltpu.make_async_copy(ins[i], near[i], came.at[i])

        def leave(i):
            return pltpu.make_async_copy(far[i], outs[i], went.at[i])

        for i in range(count):
            arrive(i).start()
        q = lax.axis_index("seq")
        whole = jnp.concatenate([sums[0:16].astype(F32), sums[16:32].astype(F32)], axis=1)
        rolled = pltpu.roll(whole, (plan.FF - q * plan.FFn) % plan.FF, 1)[:, 0 : plan.FFn]
        tinies[2][...] = rolled[0:1]
        tinies[3][...] = rolled[1:2]
        tinies[4][...] = rolled[2:11]
        for k in range(2):
            row = whole[11 + k : 12 + k]
            rows = [row[:, i * plan.D : (i + 1) * plan.D] for i in range(4)]
            both = jnp.concatenate(rows + rows, axis=0)
            tinies[k][...] = pltpu.roll(both, (plan.D - q * dn) % plan.D, 1)[0:4, 0:dn]
        for i in range(count):
            arrive(i).wait()
            if i == conv:
                for k in range(3):
                    far[i][k] = near[i][:, k * H : (k + 1) * H].astype(F32)
            elif i == qkv:
                for k in range(12):
                    to = (k % 3) * plan.D + k // 3 * 128
                    far[i][:, to : to + 128] = near[i][:, k * 128 : (k + 1) * 128].astype(F32)
            else:
                far[i][...] = near[i][...].astype(F32)
            leave(i).start()
        for i in range(count):
            leave(i).wait()

    hbm = pl.BlockSpec(memory_space=pl.ANY)
    vmem = pl.BlockSpec(memory_space=pltpu.VMEM)
    return pl.pallas_call(
        body,
        out_shape=out_shape,
        in_specs=[hbm] * count + [vmem],
        out_specs=[hbm] * count + [vmem] * len(tiny),
        scratch_shapes=[pltpu.VMEM(p.shape, BF16) for p in parts[:count]]
        + [pltpu.VMEM(shape.shape, F32) for shape in wide]
        + [pltpu.SemaphoreType.DMA((count,))] * 2,
        compiler_params=pltpu.CompilerParams(vmem_limit_bytes=64 << 20),
    )(*parts)


def solution(mesh):
    in_specs = (
        P("dp", "seq", None),
        P("dp", "seq"),
        P("dp", "seq", None),
        P(None, "seq"),
        P(None, "seq"),
        P("seq", None),
        P("seq", None),
        P(None, "seq", None),
        P("seq"),
        P("seq"),
        P(None, "seq"),
        P("seq", None),
        P("seq", None),
        P("seq", None),
        P("seq", None),
        P("seq", None),
    )
    out_specs = (
        P("dp", "seq", None),
        P("dp", "seq", None),
        P(None, "seq"),
        P(None, "seq"),
        P("seq", None),
        P("seq", None),
        P(None, "seq", None),
        P("seq"),
        P("seq"),
        P(None, "seq"),
        P("seq", None),
        P("seq", None),
        P("seq", None),
        P("seq", None),
        P("seq", None),
    )
    return jax.shard_map(local, mesh=mesh, in_specs=in_specs, out_specs=out_specs, check_vma=False)
```

```python
import math

import jax
import jax.numpy as jnp
from jax import lax
from jax.experimental import pallas as pl
from jax.experimental.pallas import tpu as pltpu
from jax.sharding import PartitionSpec as P

HEADS = 8
EPS = 1e-06
MESH = pl.DeviceIdType.MESH
F32 = jnp.float32
BF16 = jnp.bfloat16

GLU, CONV, LEFT, POINT, QKV, OUT, FIN, FOUT = range(8)
WEIGHTS = 8
(U_GLU0, U_GLU1, U_CONV, U_LEFT0, U_LEFT1, U_POINT0, U_POINT1, U_QKV0, U_QKV1, U_OUT, U_FIN, U_FOUT, SMALL) = range(13)
UNITS = 13
UNIT_WEIGHT = (GLU, GLU, CONV, LEFT, LEFT, POINT, POINT, QKV, QKV, OUT, FIN, FOUT, WEIGHTS)
UNIT_PART = (0, 1, None, 0, 1, 0, 1, 0, 1, None, None, None, None)

SHARED = (GLU, CONV, POINT,)
SMALLS, TOKENS = 8, 9
START = (GLU, CONV, SMALLS, TOKENS)
FORWARD = (
    ((1, GLU), (1, CONV)),
    (),
    ((0, LEFT),),
    ((2, GLU), (2, CONV), (0, POINT), (1, LEFT), (3, GLU)),
    (),
    ((1, POINT), (3, CONV)),
    ((0, QKV),),
    (),
    (),
    (),
    ((2, LEFT),),
    ((2, POINT), (0, OUT), (0, FIN)),
    (),
    ((1, QKV),),
    (),
    ((1, OUT),),
    (),
    (),
    ((3, POINT), (0, FOUT)),
    ((1, FIN),),
    (),
    (),
    (),
    ((2, QKV), (2, OUT)),
    (),
    (),
    ((1, FOUT),),
    ((0, TOKENS),),
    ((2, FIN),),
    ((2, FOUT),),
    (),
    (),
    (),
    (),
    (),
    (),
    (),
)
SCHEDULE = (
    (),
    (),
    (),
    (U_FOUT,),
    (U_FIN,),
    (),
    (),
    (U_OUT,),
    (U_FOUT,),
    (),
    (U_FIN, U_QKV0),
    (U_OUT,),
    (U_FOUT, U_QKV1),
    (U_QKV0,),
    (),
    (U_FIN,),
    (U_POINT0, U_POINT1),
    (U_QKV0, U_QKV1),
    (U_FOUT,),
    (),
    (),
    (),
    (U_QKV1, U_POINT0),
    (),
    (),
    (U_OUT, U_FIN),
    (U_POINT1,),
    (U_POINT0, U_FOUT),
    (U_LEFT0, U_QKV1),
    (U_QKV0, U_OUT, U_POINT1, U_LEFT1),
    (),
    (U_POINT0, U_FIN),
    (),
    (U_LEFT0,),
    (U_QKV1, U_CONV, U_GLU0, U_GLU1, U_LEFT1),
)
TAIL = (
    (SMALL, U_POINT1, U_QKV0, U_LEFT0, U_OUT, U_CONV, U_POINT0, U_LEFT1, U_GLU0, U_LEFT0, U_POINT1, U_GLU1, SMALL),
    (U_CONV, U_GLU0, U_LEFT1, U_GLU1, U_LEFT0, SMALL, U_CONV, U_GLU0, U_LEFT1, U_GLU1, SMALL, U_CONV, U_GLU0, U_GLU1, SMALL, U_FOUT, U_FIN, U_OUT, U_QKV0, U_QKV1, U_POINT0, U_POINT1, U_LEFT0, U_LEFT1, U_CONV, U_GLU0, U_GLU1, SMALL),
)

MB, MW = 128, 256
TAPS = (-4, -3, -2, -1, 1, 2, 3, 4)
FAR = -(2.0**30)


def mm(a, b):
    return lax.dot_general(a, b, (((1,), (0,)), ((), ())), preferred_element_type=F32)


def mm_t(a, b):
    return lax.dot_general(a, b, (((1,), (1,)), ((), ())), preferred_element_type=F32)


def mm_tn(a, b):
    return lax.dot_general(a, b, (((0,), (0,)), ((), ())), preferred_element_type=F32)


def normed(v):
    centred = v - jnp.mean(v, axis=-1, keepdims=True)
    r = lax.rsqrt(jnp.mean(centred * centred, axis=-1, keepdims=True) + EPS)
    return centred * r, r


def gelu_both(v):
    c = math.sqrt(2.0 / math.pi)
    sq = v * v
    t = jnp.tanh(v * (c + (c * 0.044715) * sq))
    half = 0.5 * t + 0.5
    value = v * half
    slope = half + (0.5 * v) * (1.0 - t * t) * (c + (3.0 * c * 0.044715) * sq)
    return value, slope


def sigmoid(v):
    return 0.5 * jnp.tanh(0.5 * v) + 0.5


class Buffers:
    pass


class Plan:
    def __init__(self, dp, n, seqs, span, width, hidden, half):
        self.n, self.Z = n, dp // 2
        self.S, self.span = seqs, span
        self.D, self.FF, self.HALF = width, hidden, half
        self.LEN = span * n
        self.T = self.LEN // 2
        self.PH = n // 2
        self.B = math.isqrt(n)
        self.A = n // self.B
        assert self.A == self.B and n == 2 * seqs and dp % 2 == 0
        self.shared = SHARED if self.Z % 2 == 0 else ()
        self.sw = max(span, 128)
        self.sr = self.sw // span
        dn = width // n
        self.nw = max(dn, 128)
        self.nr = self.nw // dn
        self.FFn = hidden // n
        self.srows = 8 * self.nw // self.FFn
        self.spack = -(-(self.srows + 11) // 16) * 16
        self.dims = [
            (width, 2 * width),
            (width, half),
            (width, hidden),
            (hidden, width),
            (width, 3 * width),
            (width, width),
            (width, hidden),
            (hidden, width),
        ]

    def whole(self, w):
        k, cols = self.dims[w]
        return (3, k, cols) if w == CONV else (k, cols)

    def kr(self, w):
        return self.dims[w][0] // self.n

    def hr(self, w):
        return self.kr(w) // 2

    def gcols(self, w):
        return self.dims[w][1] * (3 if w == CONV else 1)

    def piece(self, w, rows):
        return (rows, self.gcols(w))

    def buffers(self, take):
        T, D, FF, H, n = self.T, self.D, self.FF, self.HALF, self.n
        r = Buffers()

        def vm(shape, dtype):
            return take(pltpu.VMEM(shape, dtype))

        def sem(*shape):
            return take(pltpu.SemaphoreType.DMA(shape))

        every = range(WEIGHTS)
        parts = [(self.piece(w, self.hr(w)), BF16) for w in every] + [((16, FF // 2), BF16)]
        r.w = [vm(self.whole(w), BF16) for w in every]
        r.g8 = vm((16, FF), F32)
        r.gsm = vm((32, FF // 2), BF16)
        r.r = [None] * WEIGHTS + [vm((16, FF // 2), BF16)]
        for w in (CONV, QKV, OUT, FIN, FOUT):
            r.r[w] = vm(self.piece(w, n * self.hr(w)), BF16)
        r.r[LEFT], r.r[POINT], r.r[GLU] = r.r[FIN], r.r[FOUT], r.r[QKV]
        r.p = [vm((n - 1,) + shape, dtype) for shape, dtype in parts]
        if self.Z > 1:
            r.u = [vm(shape, dtype) for shape, dtype in parts]
            r.d = [vm(shape, dtype) for shape, dtype in parts]
        r.segbuf = vm((n, 8, self.sw), jnp.int32)
        r.segrow = vm((8, self.LEN), F32)
        r.segcol = vm((self.LEN + 16, 128), F32)
        r.segloc = vm((T + 16, 128), F32)
        r.mext = vm((T + 16, 128), F32)
        r.ms = vm((T // MB, 8 * MB, MW), BF16)
        r.qenc = vm((T, 128), BF16)
        r.kenc = vm((self.LEN, 128), BF16)
        r.smallbuf = vm((n, self.spack, self.FFn), BF16)
        r.nrm = vm((8, D), F32)
        r.midp = vm((16, FF), F32)
        r.xin = vm((T, D), BF16)
        r.cot = vm((T, D), BF16)
        r.a1 = vm((T, D), BF16)
        r.sg = vm((T, 2 * D), BF16)
        r.y1 = vm((T, D), F32)
        r.a2 = vm((T, D), BF16)
        r.pext = vm((3, T + 16, H), F32)
        r.dgl = vm((T, FF), BF16)
        r.dgr = vm((T, H), BF16)
        r.nm = vm((T, FF), BF16)
        r.rm = vm((T, 1), F32)
        r.big = vm((T + 16, FF), F32)
        r.sep = vm((T, FF), BF16)
        r.y2 = vm((T, D), F32)
        r.a4 = vm((T, D), BF16)
        r.qb = vm((T, D), BF16)
        r.kvb = vm((self.LEN, 2 * D), BF16)
        r.lse = vm((T, 128), F32)
        r.ctx = vm((T, D), BF16)
        r.y3 = vm((T, D), F32)
        r.a5 = vm((T, D), BF16)
        r.hid = vm((T + 32, FF), BF16)
        r.dg = vm((T, FF), BF16)
        r.osend = vm((T, D), BF16)
        r.gs = r.y3
        r.dkvr = vm((T, 2 * D), BF16)
        r.tr = vm((D, T), BF16)
        edges = (((8, H), F32), ((16, FF), BF16), ((16, FF), BF16), ((8, H), F32))
        r.es = [vm(shape, dtype) for shape, dtype in edges]
        r.er = [vm(shape, dtype) for shape, dtype in edges]
        r.s_loc = sem(WEIGHTS)
        r.s_as = sem(WEIGHTS)
        r.s_ar = sem(WEIGHTS, self.B - 1)
        r.s_br = sem(WEIGHTS, (self.A - 1) * self.B)
        r.s_dr = sem(WEIGHTS)
        if self.shared:
            r.s_hr = sem(WEIGHTS)
        r.s_rs = sem(UNITS)
        r.s_rr = sem(UNITS)
        r.s_ps = sem(UNITS)
        r.s_pr = sem(UNITS, 2)
        if self.Z > 1:
            r.s_zs = sem(UNITS)
            r.s_zr = sem(UNITS, 2)
        r.s_fs = sem(UNITS)
        r.s_fr = sem(UNITS)
        r.s_xs = sem(4, self.S)
        r.s_xr = sem(4, max(self.PH, self.S))
        r.s_gs = sem(2 * self.S)
        r.s_gr = sem(n)
        r.s_ms = sem(n)
        r.s_mr = sem(n)
        r.s_es = sem(4)
        r.s_er = sem(4)
        r.s_ks = sem(HEADS // 2)
        r.s_kr = sem(HEADS // 2)
        r.s_js = sem(HEADS // 2)
        r.s_jr = sem(HEADS // 2)
        return r


INPUTS = 4 + WEIGHTS
OUTPUTS = 2 + WEIGHTS + 1


def kernel(plan, *refs):
    ins, outs = refs[:INPUTS], refs[INPUTS : INPUTS + OUTPUTS]
    scratch = iter(refs[INPUTS + OUTPUTS :])
    r = plan.buffers(lambda shape: next(scratch))
    r.x, r.seg, r.ct, r.small = ins[:4]
    r.h = ins[4:]
    r.o_out, r.o_ig = outs[:2]
    r.o = outs[2:]
    n, Z, S, span = plan.n, plan.Z, plan.S, plan.span
    T, D, FF, H, PH = plan.T, plan.D, plan.FF, plan.HALF, plan.PH
    A, B = plan.A, plan.B
    dp, q = lax.axis_index("dp"), lax.axis_index("seq")
    z, c = dp // 2, dp % 2
    oc = 1 - c

    def aligned(v, m=16):
        return pl.multiple_of(v, m)

    def dev(core, chip, plane=None):
        return ((z if plane is None else plane) * 2 + core, chip)

    sibling = dev(oc, q)

    def remote(src, dst, ss, rs, to):
        return pltpu.make_async_remote_copy(
            src_ref=src, dst_ref=dst, send_sem=ss, recv_sem=rs, device_id=to, device_id_type=MESH
        )

    barrier = pltpu.get_barrier_semaphore()
    for core in range(2):

        def greet(t, _, core=core):
            chip = lax.rem(q + t, n)
            to = (z * 2 + (c + core) % 2, chip)
            pl.semaphore_signal(barrier, inc=1, device_id=to, device_id_type=MESH)
            return 0

        lax.fori_loop(1 - core, n, greet, 0)
    if Z > 1:

        @pl.when(z > 0)
        def _():
            pl.semaphore_signal(barrier, inc=1, device_id=dev(c, q, z - 1), device_id_type=MESH)

        @pl.when(z < Z - 1)
        def _():
            pl.semaphore_signal(barrier, inc=1, device_id=dev(c, q, z + 1), device_id_type=MESH)

    pl.semaphore_wait(barrier, 2 * n - 1 + (z + Z - 1) // Z + (2 * Z - 2 - z) // Z)

    def vrows(ref, w, row0, rows):
        ds = pl.ds(aligned(row0), rows)
        return ref.at[:, ds] if w == CONV else ref.at[ds]

    def bytes_of(view, semaphore):
        return pltpu.make_async_copy(view, view, semaphore)

    def qof(core, f, g):
        f, g = f % B, g % B
        return core * (f * B + g) + (1 - core) * (g * B + f)

    b_, a_ = q % B, q // B
    f_, g_ = c * a_ + oc * b_, c * b_ + oc * a_
    par = z % 2
    partner = dev(c, q, z + 1 - 2 * par)

    def wrows(ref, w, row0, rows, side):
        if w not in plan.shared:
            return vrows(ref, w, row0, rows)
        size = plan.dims[w][1] // 2
        cols = pl.ds(pl.multiple_of(side * size, 128), size)
        if w == CONV:
            return ref.at[:, pl.ds(aligned(row0), rows), cols]
        return ref.at[pl.ds(aligned(row0), rows), cols]

    def wblock(w, shard, side=par):
        return wrows(r.w[w], w, shard * plan.kr(w) + c * plan.hr(w), plan.hr(w), side)

    def own_block(w):
        return wrows(r.h[w], w, c * plan.hr(w), plan.hr(w), par)

    def copy_a(w, t):
        to = dev(c, qof(c, f_ + t, g_))
        return remote(own_block(w), wblock(w, q), r.s_as.at[w], r.s_ar.at[w, t - 1], to)

    def copy_b(w, u, t):
        blk = wblock(w, qof(c, f_ + B - t, g_))
        src = own_block(w) if t == 0 else blk
        to = dev(c, qof(c, f_, g_ + u))
        return remote(src, blk, r.s_as.at[w], r.s_br.at[w, (u - 1) * B + t], to)

    def shard_from(u, t):
        return qof(c, f_ + B - t, g_ + B - u)

    def pass_on(w, u, t):
        blk = wblock(w, shard_from(u, t))
        remote(blk, blk, r.s_as.at[w], r.s_dr.at[w], sibling).start()
        if w in plan.shared:
            remote(blk, blk, r.s_as.at[w], r.s_hr.at[w], partner).start()

    def local_shard(w):
        dst = vrows(r.w[w], w, q * plan.kr(w), plan.kr(w))
        return pltpu.make_async_copy(r.h[w], dst, r.s_loc.at[w])

    def g0(w):
        local_shard(w).start()
        for t in range(1, B):
            copy_a(w, t).start()
        for u in range(1, A):
            copy_b(w, u, 0).start()

    def g1(w):
        for t in range(1, B):
            bytes_of(wblock(w, shard_from(0, t)), r.s_ar.at[w, t - 1]).wait()
            for u in range(1, A):
                copy_b(w, u, t).start()
            pass_on(w, 0, t)

    def g2(w):
        for u in range(1, A):
            for t in range(B):
                bytes_of(wblock(w, shard_from(u, t)), r.s_br.at[w, (u - 1) * B + t]).wait()
                pass_on(w, u, t)

    def others(w):
        return wrows(r.w[w], w, 0, (n - 1) * plan.hr(w), 0)

    def gz(w):
        if w not in plan.shared:
            return
        bytes_of(others(w), r.s_hr.at[w]).wait()
        for u in range(A):
            for t in range(B):
                if (u, t) != (0, 0):
                    blk = wblock(w, shard_from(u, t), 1 - par)
                    remote(blk, blk, r.s_as.at[w], r.s_dr.at[w], sibling).start()

    def g3(w):
        local_shard(w).wait()
        bytes_of(vrows(r.w[w], w, 0, (n - 1) * plan.hr(w)), r.s_dr.at[w]).wait()

    gather_steps = (g0, g1, g2, gz)
    forward_turns = iter(FORWARD)

    def gather(steps):
        for k, w in steps:
            if w == TOKENS:
                tokens_in(r.ct, r.cot, 1)
            else:
                gather_steps[k](w)

    def pass_turn():
        gather(next(forward_turns))

    def pass_turns(count):
        every = [(k, next(forward_turns)) for k in range(count)]
        return [(k, lambda steps=steps: gather(steps)) for k, steps in every if steps]

    def gather_sent(w):
        bytes_of(vrows(r.w[w], w, 0, 2 * (n - 1) * plan.hr(w)), r.s_as.at[w]).wait()

    def token_rows(ref, slot):
        return ref.at[pl.ds(aligned(slot * span), span)]

    def tokens_in(src, dst, k):
        for j in range(S):
            chip, core, slot = S * c + j, q // PH, q % PH
            here = jnp.logical_and(chip == q, core == c)
            there = token_rows(dst, slot)

            @pl.when(here)
            def _():
                pltpu.make_async_copy(src.at[j], there, r.s_xr.at[k, slot]).start()

            @pl.when(jnp.logical_not(here))
            def _():
                remote(
                    src.at[j], there, r.s_xs.at[k, j], r.s_xr.at[k, slot], dev(core, chip)
                ).start()

    def tokens_in_done(dst, k):
        for slot in range(PH):
            blk = token_rows(dst, slot)
            pltpu.make_async_copy(blk, blk, r.s_xr.at[k, slot]).wait()

    def tokens_in_sent(src, dst, k):
        for j in range(S):
            chip, core, slot = S * c + j, q // PH, q % PH
            here = jnp.logical_and(chip == q, core == c)

            @pl.when(jnp.logical_not(here))
            def _():
                remote(
                    src.at[j],
                    token_rows(dst, slot),
                    r.s_xs.at[k, j],
                    r.s_xr.at[k, slot],
                    dev(core, chip),
                ).wait_send()

    def tokens_out(src, dst, k):
        for p in range(PH):
            chip, core, slot = c * PH + p, q // S, q % S
            here = jnp.logical_and(chip == q, core == c)

            @pl.when(here)
            def _():
                pltpu.make_async_copy(token_rows(src, p), dst.at[slot], r.s_xr.at[k, slot]).start()

            @pl.when(jnp.logical_not(here))
            def _():
                remote(
                    token_rows(src, p),
                    dst.at[slot],
                    r.s_xs.at[k, p],
                    r.s_xr.at[k, slot],
                    dev(core, chip),
                ).start()

    def tokens_out_done(src, dst, k):
        for j in range(S):
            pltpu.make_async_copy(dst.at[j], dst.at[j], r.s_xr.at[k, j]).wait()
        for p in range(PH):
            chip, core, slot = c * PH + p, q // S, q % S
            here = jnp.logical_and(chip == q, core == c)

            @pl.when(jnp.logical_not(here))
            def _():
                remote(
                    token_rows(src, p),
                    dst.at[slot],
                    r.s_xs.at[k, p],
                    r.s_xr.at[k, slot],
                    dev(core, chip),
                ).wait_send()

    def seg_send():
        for j in range(S):
            for core in range(2):
                chip = S * c + j
                here = jnp.logical_and(chip == q, c == core)
                i = 2 * j + core

                @pl.when(here)
                def _():
                    pltpu.make_async_copy(r.seg.at[j], r.segbuf.at[q], r.s_gr.at[q]).start()

                @pl.when(jnp.logical_not(here))
                def _():
                    remote(
                        r.seg.at[j],
                        r.segbuf.at[q],
                        r.s_gs.at[i],
                        r.s_gr.at[q],
                        dev(core, chip),
                    ).start()

    def seg_sent():
        for j in range(S):
            for core in range(2):
                chip = S * c + j
                here = jnp.logical_and(chip == q, c == core)

                @pl.when(jnp.logical_not(here))
                def _():
                    remote(
                        r.seg.at[j],
                        r.segbuf.at[q],
                        r.s_gs.at[2 * j + core],
                        r.s_gr.at[q],
                        dev(core, chip),
                    ).wait_send()

    def small_copy(t):
        return remote(
            r.small,
            r.smallbuf.at[q],
            r.s_ms.at[t],
            r.s_mr.at[t],
            dev(c, (q + t) % n),
        )

    def small_arrived(t):
        blk = r.smallbuf.at[(q + n - t) % n]
        return remote(blk, blk, r.s_ms.at[t], r.s_mr.at[t], sibling)

    def edge_copy(i):
        return remote(r.es[i], r.er[i], r.s_es.at[i], r.s_er.at[i], sibling)

    def edge_send(i, last, first):
        r.es[i][...] = jnp.where(c == 0, last, first)
        edge_copy(i).start()

    def edge_take(i):
        edge_copy(i).wait()
        got = r.er[i][...]
        none = jnp.zeros_like(got)
        return jnp.where(c == 1, got, none), jnp.where(c == 0, got, none)

    def columns(u):
        w, half = UNIT_WEIGHT[u], UNIT_PART[u]
        size = plan.gcols(w)
        return (0, size) if half is None else (half * (size // 2), size // 2)

    def urows(ref, u, row0, rows, shift=0):
        col0, size = columns(u)
        return ref.at[pl.ds(aligned(row0), rows), pl.ds(col0 + shift, size)]

    grad_home = {GLU: (r.hid, 2 * D), CONV: (r.dkvr, 0), LEFT: (r.sep, 0), QKV: (r.dg, 0)}

    def gpiece(u, shard, half):
        if u == SMALL:
            return r.gsm.at[pl.ds(pl.multiple_of(half * 16, 16), 16)]
        w = UNIT_WEIGHT[u]
        ref, shift = grad_home.get(w, (r.w[w] if w < WEIGHTS else None, 0))
        return urows(ref, u, shard * plan.kr(w) + half * plan.hr(w), plan.hr(w), shift)

    def rpiece(u, shard):
        w = UNIT_WEIGHT[u]
        if u == SMALL:
            return r.r[w]
        return urows(r.r[w], u, shard * plan.hr(w), plan.hr(w))

    def slots(u, first, count):
        buf = r.p[UNIT_WEIGHT[u]]
        if u == SMALL:
            return buf.at[pl.ds(first, count)]
        col0, size = columns(u)
        return buf.at[pl.ds(first, count), :, pl.ds(col0, size)]

    def ppiece(u, slot):
        buf = r.p[UNIT_WEIGHT[u]]
        if u == SMALL:
            return buf.at[slot]
        col0, size = columns(u)
        return buf.at[slot, :, pl.ds(col0, size)]

    def zpiece(u, way):
        buf = (r.u, r.d)[way][UNIT_WEIGHT[u]]
        if u == SMALL:
            return buf
        col0, size = columns(u)
        return buf.at[:, pl.ds(col0, size)]

    def copy_r(u, s):
        return remote(gpiece(u, s, oc), rpiece(u, s), r.s_rs.at[u], r.s_rr.at[u], sibling)

    def all_r(u, semaphore):
        w = UNIT_WEIGHT[u]
        view = r.r[w] if u == SMALL else urows(r.r[w], u, 0, n * plan.hr(w))
        return bytes_of(view, semaphore.at[u])

    def shards(u):
        return 1 if u == SMALL else n

    def red0(u):
        for s in range(shards(u)):
            copy_r(u, s).start()

    def put(to, *terms):
        size = to.shape[0]
        rows = min(size, 32)

        def some(i, _):
            at = pl.ds(pl.multiple_of(i * rows, rows), rows)
            total = terms[0][at].astype(F32)
            for term in terms[1:]:
                total = total + term[at].astype(F32)
            to[at] = total.astype(to.dtype)
            return 0

        lax.fori_loop(0, size // rows, some, 0)

    def add_core(u, s):
        mine = gpiece(u, s, c)
        put(mine, mine, rpiece(u, s))

    def slot1(u, t):
        return (u - 1) * B + t

    def slot2(t):
        return (A - 1) * B + t - 1

    def copy_p1(u, k, t):
        return remote(
            gpiece(u, qof(c, f_ + t, g_ + k), c),
            ppiece(u, slot1(k, t)),
            r.s_ps.at[u],
            r.s_pr.at[u, 0],
            dev(c, qof(c, f_, g_ + k)),
        )

    def copy_p2(u, t):
        to = qof(c, f_ + t, g_)
        return remote(
            r.r[WEIGHTS] if u == SMALL else gpiece(u, to, c),
            ppiece(u, slot2(t)),
            r.s_ps.at[u],
            r.s_pr.at[u, 1],
            dev(c, to),
        )

    def all_p(u, step, semaphore):
        count = B - 1 if step else A - 1 if u == SMALL else (A - 1) * B
        return bytes_of(slots(u, 0, count), semaphore.at[u, step])

    def red1(u):
        all_r(u, r.s_rr).wait()
        if u == SMALL:
            add_core(u, 0)
            for k in range(1, A):
                copy_p1(u, k, 0).start()
            return

        def send(i, _):
            k, t = i // B + 1, i % B
            add_core(u, qof(c, f_ + t, g_ + k))
            copy_p1(u, k, t).start()
            return 0

        lax.fori_loop(0, (A - 1) * B, send, 0)
        lax.fori_loop(0, B, lambda t, _: (add_core(u, qof(c, f_ + t, g_)), 0)[1], 0)

    def red1b(u):
        all_p(u, 0, r.s_pr).wait()

        def send(t, _):
            mine = gpiece(u, 0 if u == SMALL else qof(c, f_ + t, g_), c)
            came = [ppiece(u, slot1(k, 0 if u == SMALL else t)) for k in range(1, A)]
            put(r.r[WEIGHTS] if u == SMALL else mine, mine, *came)
            if u != SMALL:
                copy_p2(u, t).start()
            return 0

        if u == SMALL:
            send(0, 0)
            for t in range(1, B):
                copy_p2(u, t).start()
        else:
            lax.fori_loop(1, B, send, 0)

    def red2(u):
        all_p(u, 1, r.s_pr).wait()
        came = [] if u == SMALL else [ppiece(u, slot1(k, 0)) for k in range(1, A)]
        came += [ppiece(u, slot2(t)) for t in range(1, B)]
        put(ppiece(u, 0), r.r[WEIGHTS] if u == SMALL else gpiece(u, q, c), *came)

    def copy_z(u, way):
        return remote(
            ppiece(u, 1 + way),
            zpiece(u, way),
            r.s_zs.at[u],
            r.s_zr.at[u, way],
            dev(c, q, z + 1 if way == 0 else z - 1),
        )

    def red_hop(u, h):
        own, up, down = ppiece(u, 0), ppiece(u, 1), ppiece(u, 2)

        @pl.when(z == h)
        def _():
            if h == 0:
                put(up, own)
            else:
                copy_z(u, 0).wait_recv()
                put(up, own, zpiece(u, 0))
            if h < Z - 1:
                copy_z(u, 0).start()

        @pl.when(z == Z - 1 - h)
        def _():
            if h == 0:
                put(down, own)
            else:
                copy_z(u, 1).wait_recv()
                if h < Z - 1:
                    put(down, own, zpiece(u, 1))
            if h < Z - 1:
                copy_z(u, 1).start()

    def final_rows(u):
        w = UNIT_WEIGHT[u]
        if u == SMALL:
            return r.o[w].at[pl.ds(pl.multiple_of(c * 16, 16), 16)]
        return urows(r.o[w], u, c * plan.hr(w), plan.hr(w))

    def final_local(u):
        return pltpu.make_async_copy(ppiece(u, 0), final_rows(u), r.s_fs.at[u])

    def final_remote(u):
        return remote(ppiece(u, 0), final_rows(u), r.s_fs.at[u], r.s_fr.at[u], sibling)

    def red_final(u):
        if Z > 1:
            own, up = ppiece(u, 0), ppiece(u, 1)

            @pl.when(z == Z - 1)
            def _():
                put(own, up)

            @pl.when(z < Z - 1)
            def _():
                put(own, up, zpiece(u, 1))

        final_local(u).start()
        final_remote(u).start()

    def red_end(u):
        final_remote(u).wait_recv()
        bytes_of(slots(u, 0, 2), r.s_fs.at[u]).wait()
        all_r(u, r.s_rs).wait()
        bytes_of(slots(u, 0, A + B - 2 if u == SMALL else n - 1), r.s_ps.at[u]).wait()
        if Z > 1:
            ends = jnp.logical_or(z == 0, z == Z - 1)

            @pl.when(ends)
            def _():
                bytes_of(slots(u, 0, 1), r.s_zs.at[u]).wait()

            @pl.when(jnp.logical_not(ends))
            def _():
                bytes_of(slots(u, 0, 2), r.s_zs.at[u]).wait()

    def red2_hop(u):
        red2(u)
        red_hop(u, 0)

    def last_hop(u):
        red_hop(u, Z - 1)
        red_final(u)

    ahead = {}
    turns = iter(SCHEDULE)

    def enlist(u):
        if Z > 1:
            ahead[u] = [red1, red1b, red2_hop]
            ahead[u] += [lambda k, h=h: red_hop(k, h) for h in range(1, Z - 1)]
            ahead[u].append(last_hop)
        else:
            ahead[u] = [red1, red1b, red2, red_final]

    def reduce_start(*units):
        for u in units:
            red0(u)
            enlist(u)

    def steps_of(units):
        return [(ahead[u].pop(0), u) for u in units if ahead[u]]

    def move(units):
        for step, u in steps_of(units):
            step(u)

    def turn():
        move(next(turns))

    def turns_of(count):
        acts = []
        for k in range(count):
            steps = steps_of(next(turns))
            if steps:
                acts.append((k, lambda steps=steps: [step(u) for step, u in steps][:0]))
        return acts

    def loop(count, body, after=()):
        def step(i, _):
            body(i)
            for k, act in after:
                pl.when(i == k)(lambda act=act: (act(), None)[1])
            return 0

        lax.fori_loop(0, count, step, 0)

    RB = 256
    NB = T // RB

    def rows_of(i, size=RB, base=0):
        return pl.ds(pl.multiple_of(i * size + base, base or size), size)

    seg_send()
    small_local = pltpu.make_async_copy(r.small, r.smallbuf.at[q], r.s_mr.at[0])
    small_local.start()
    for what in START:
        if what == SMALLS:
            for t in range(1, n):
                small_copy(t).start()
        elif what == TOKENS:
            tokens_in(r.x, r.xin, 0)
        else:
            g0(what)
    r.g8[...] = jnp.zeros((16, FF), F32)
    pass_turn()

    for s in range(n):
        blk = r.segbuf.at[s]
        pltpu.make_async_copy(blk, blk, r.s_gr.at[s]).wait()
    for grp in range(n // plan.sr):
        got = r.segbuf[grp * plan.sr]
        for k in range(1, plan.sr):
            got = got + r.segbuf[grp * plan.sr + k]
        r.segrow[:, grp * plan.sw : (grp + 1) * plan.sw] = got.astype(F32)
    r.segcol[0:8] = jnp.full((8, 128), -1.0, F32)
    r.segcol[plan.LEN + 8 : plan.LEN + 16] = jnp.full((8, 128), -1.0, F32)
    for k in range(plan.LEN // 128):
        row = r.segrow[0:1, k * 128 : (k + 1) * 128]
        r.segcol[8 + k * 128 : 8 + (k + 1) * 128] = jnp.broadcast_to(row, (128, 128)).T
    r.segloc[...] = r.segcol[pl.ds(pl.multiple_of(c * T, 8), T + 16)]
    r.mext[0 : T + 8] = jnp.where(r.segloc[0 : T + 8] == r.segloc[1 : T + 9], 1.0, 0.0)

    def mask(o, start, rows):
        first = 8 + start + (0 if o > 0 else o)
        return r.mext[first : first + rows]

    small_local.wait()
    for t in range(1, n):
        small_arrived(t).wait_recv()
    for grp in range(n // plan.nr):
        got = r.smallbuf[grp * plan.nr].astype(F32)
        for k in range(1, plan.nr):
            got = got + r.smallbuf[grp * plan.nr + k].astype(F32)
        for k in range(8):
            row, first = divmod(k * plan.nw, plan.FFn)
            r.nrm[k : k + 1, grp * plan.nw : (grp + 1) * plan.nw] = got[
                row : row + 1, first : first + plan.nw
            ]
    for s in range(n):
        rows = r.smallbuf[s].astype(F32)[plan.srows : plan.srows + 11]
        r.midp[0:11, s * plan.FFn : (s + 1) * plan.FFn] = rows

    def ln_out(k, v):
        unit, _ = normed(v)
        return (unit * r.nrm[k : k + 1] + r.nrm[4 + k : 5 + k]).astype(BF16)

    def ln_back(k, e, v):
        unit, rs = normed(v)
        eg = e * r.nrm[k : k + 1]
        m1 = jnp.mean(eg, axis=-1, keepdims=True)
        m2 = jnp.mean(eg * unit, axis=-1, keepdims=True)
        cols = slice(k * D, (k + 1) * D)
        r.g8[11:12, cols] += jnp.sum(e * unit, axis=0, keepdims=True)
        r.g8[12:13, cols] += jnp.sum(e, axis=0, keepdims=True)
        return rs * (eg - m1 - unit * m2)

    pass_turn()

    def window(b):
        return min(max(b * MB - (MW - MB) // 2 + 16, 0), T + 32 - MW)

    ahead_of = lax.broadcasted_iota(jnp.int32, (MB, MW), 1) - lax.broadcasted_iota(
        jnp.int32, (MB, MW), 0
    )
    for b in range(T // MB):
        home = r.segloc[8 + b * MB : 8 + (b + 1) * MB]
        for i, o in enumerate(TAPS):
            there = r.segloc[8 + b * MB + o : 8 + (b + 1) * MB + o]
            same = jnp.where(home == there, 1.0, 0.0)
            hit = ahead_of == b * MB + 16 - window(b) + o
            tap = jnp.where(hit, jnp.concatenate([same] * (MW // 128), axis=1), 0.0)
            r.ms[b, i * MB : (i + 1) * MB] = tap.astype(BF16)

    lane = lax.broadcasted_iota(jnp.int32, (1, 128), 1)
    lane_f = lane.astype(F32)
    own_doc = r.segloc[8 : T + 8] == lane_f
    r.qenc[...] = jnp.where(jnp.logical_and(lane < 4, jnp.logical_not(own_doc)), FAR, 0.0).astype(BF16)
    ones = jnp.logical_and(lane >= 4, lane < 7)
    r.kenc[...] = jnp.where(
        jnp.logical_or(r.segcol[8 : plan.LEN + 8] == lane_f, ones), 1.0, 0.0
    ).astype(BF16)

    pass_turn()
    pass_turn()
    g3(GLU)
    pass_turn()
    tokens_in_done(r.xin, 0)

    def glu(i):
        rows = rows_of(i)
        x = r.xin[rows].astype(F32)
        a1 = ln_out(0, x)
        r.a1[rows] = a1
        value = mm(a1, r.w[GLU][:, 0:D])
        gate = sigmoid(mm(a1, r.w[GLU][:, D : 2 * D]))
        r.sg[rows, 0:D] = gate.astype(BF16)
        r.sg[rows, D : 2 * D] = (value * gate * (1.0 - gate)).astype(BF16)
        y1 = x + value * gate
        r.y1[rows] = y1
        r.a2[rows] = ln_out(1, y1)

    loop(NB, glu, pass_turns(NB))
    pass_turn()
    g3(CONV)

    def conv(i):
        a2 = r.a2[rows_of(i)]
        for o in range(3):
            r.pext[o, rows_of(i, RB, 8)] = mm(a2, r.w[CONV][o])

    loop(NB, conv)
    edge_send(0, r.pext[0, T : T + 8], r.pext[2, 8:16])
    pass_turn()
    top, bottom = edge_take(0)
    r.pext[0, 0:8] = top
    r.pext[2, T + 8 : T + 16] = bottom
    pass_turn()
    for k in range(T // 128):
        lo = k * 128
        before = mask(-1, lo, 128)
        after = mask(1, lo, 128)
        pre = (
            r.pext[0, lo + 7 : lo + 135] * jnp.concatenate([before] * (H // 128), axis=1)
            + r.pext[1, lo + 8 : lo + 136]
            + r.pext[2, lo + 9 : lo + 137] * jnp.concatenate([after] * (H // 128), axis=1)
        )
        value, slope = gelu_both(pre)
        r.pext[1, lo + 8 : lo + 136] = value
        r.dgr[lo : lo + 128] = slope.astype(BF16)
    pass_turn()
    pass_turn()
    g3(LEFT)

    CH = 512
    RM = 128

    def left(i):
        rows, erows = rows_of(i, RM), rows_of(i, RM, 8)
        a2 = r.a2[rows]
        for k in range(FF // CH):
            value, slope = gelu_both(mm(a2, r.w[LEFT][:, k * CH : (k + 1) * CH]))
            r.dgl[rows, k * CH : (k + 1) * CH] = slope.astype(BF16)
            r.big[erows, k * CH : (k + 1) * CH] = value
        r.big[erows, 0:H] += r.pext[1, erows]
        unit, rs = normed(r.big[erows])
        r.nm[rows] = unit.astype(BF16)
        r.rm[rows] = rs
        r.hid[rows_of(i, RM, 16)] = (unit * r.midp[0:1] + r.midp[1:2]).astype(BF16)

    loop(T // RM, left, pass_turns(T // RM))
    edge_send(1, r.hid[T : T + 16], r.hid[16:32])
    r.hid[0:16], r.hid[T + 16 : T + 32] = edge_take(1)
    pass_turn()

    def depthwise(j):
        cols = pl.ds(pl.multiple_of(j * 512, 512), 512)
        for b in range(T // MB):
            near = r.hid[window(b) : window(b) + MW, cols]
            taps = mm(r.ms[b], near)
            total = r.hid[16 + b * MB : 16 + (b + 1) * MB, cols].astype(F32) * r.midp[6:7, cols]
            for i, o in enumerate(TAPS):
                total = total + taps[i * MB : (i + 1) * MB] * r.midp[6 + o : 7 + o, cols]
            r.sep[b * MB : (b + 1) * MB, cols] = total.astype(BF16)

    loop(FF // 512, depthwise, pass_turns(FF // 512))
    pass_turn()
    g3(POINT)

    def point(i):
        rows = rows_of(i, T)
        y2 = r.y1[rows] + mm(r.sep[rows], r.w[POINT][...])
        r.y2[rows] = y2
        r.a4[rows] = ln_out(2, y2)

    loop(1, point)
    pass_turn()
    pass_turn()
    g3(QKV)
    scale = 1.0 / math.sqrt(D // HEADS)

    def keys_values(i):
        rows = rows_of(i)
        a4 = r.a4[rows]
        here = pl.ds(pl.multiple_of(c * T + i * RB, RB), RB)
        r.kvb[here, 0:D] = mm(a4, r.w[QKV][:, D : 2 * D]).astype(BF16)
        r.kvb[here, D : 2 * D] = mm(a4, r.w[QKV][:, 2 * D : 3 * D]).astype(BF16)

    def queries(i):
        rows = rows_of(i)
        r.qb[rows] = (mm(r.a4[rows], r.w[QKV][:, 0:D]) * scale).astype(BF16)

    def kv_copy(j, base):
        blk = r.kvb.at[pl.ds(aligned(c * T), T), pair_cols(j, base)]
        return remote(blk, blk, r.s_ks.at[j], r.s_kr.at[j], sibling)

    def pair_cols(j, base=0):
        return pl.ds(pl.multiple_of(j * 128 + base, 128), 128)

    def pair_bytes(j, semaphore):
        return bytes_of(r.kvb.at[pl.ds(0, T), pl.ds(0, 256)], semaphore.at[j])

    loop(NB, keys_values)
    for j in range(HEADS // 2):
        kv_copy(j, 0).start()
        kv_copy(j, D).start()
    loop(NB, queries)
    pass_turn()
    pass_turn()
    heads_lanes = [lane < 64, lane >= 64]
    def head_lanes(e, v):
        return jnp.where(heads_lanes[e], v, jnp.zeros_like(v))

    def attend(j):
        pair_bytes(j, r.s_kr).wait()
        cols, vcols = pair_cols(j), pair_cols(j, D)
        keys = jnp.concatenate([r.kvb[:, cols], r.kenc[...]], axis=1)
        for k in range(T // RB):
            rows = slice(k * RB, (k + 1) * RB)
            q2 = r.qb[rows, cols]
            got = []
            for e in range(2):
                score = mm_t(jnp.concatenate([head_lanes(e, q2), r.qenc[rows]], axis=1), keys)
                most = jnp.max(score, axis=-1, keepdims=True)
                power = jnp.exp(score - most)
                total = jnp.sum(power, axis=-1, keepdims=True)
                got.append(mm(power.astype(BF16), r.kvb[:, vcols]) / total)
                lse = most + jnp.log(total)
                r.lse[rows] = jnp.where(lane == 2 * j + e, lse, r.lse[rows])
            r.ctx[rows, cols] = jnp.where(heads_lanes[0], got[0], got[1]).astype(BF16)

    r.lse[...] = jnp.zeros((T, 128), F32)

    loop(HEADS // 2, attend, pass_turns(HEADS // 2))
    pass_turn()
    g3(OUT)

    def out(i):
        rows = rows_of(i, T)
        y3 = r.y2[rows] + mm(r.ctx[rows], r.w[OUT][...])
        r.y3[rows] = y3
        r.a5[rows] = ln_out(3, y3)

    loop(1, out)
    pass_turn()
    pass_turn()
    g3(FIN)

    def ffn_in(i):
        rows = rows_of(i)
        a5 = r.a5[rows]
        for k in range(FF // CH):
            value, slope = gelu_both(mm(a5, r.w[FIN][:, k * CH : (k + 1) * CH]))
            r.hid[rows, k * CH : (k + 1) * CH] = value.astype(BF16)
            r.dg[rows, k * CH : (k + 1) * CH] = slope.astype(BF16)

    loop(NB, ffn_in, pass_turns(NB))
    pass_turn()
    g3(FOUT)

    def ffn_out(i):
        rows = rows_of(i, T)
        r.osend[rows] = (r.y3[rows] + mm(r.hid[rows], r.w[FOUT][...])).astype(BF16)

    loop(1, ffn_out)
    pass_turn()
    tokens_out(r.osend, r.o_out, 2)
    for w in range(WEIGHTS):
        gather_sent(w)
    for j in range(HEADS // 2):
        pair_bytes(j, r.s_ks).wait()

    tokens_in_done(r.cot, 1)

    def ffn_back(i):
        rows = rows_of(i, T)
        f4 = r.cot[rows]
        for k in range(FF // CH):
            cols = slice(k * CH, (k + 1) * CH)
            up = mm_t(f4, r.w[FOUT][cols])
            r.dg[rows, cols] = (up * r.dg[rows, cols].astype(F32)).astype(BF16)
        e = mm_t(r.dg[rows], r.w[FIN][...])
        r.gs[rows] = f4.astype(F32) + ln_back(3, e, r.y3[rows])

    loop(1, ffn_back)
    GC = 1024

    def grad_outer(k):
        cols = rows_of(k, GC)
        r.w[FOUT][cols] = mm_tn(r.hid[0:T, cols], r.cot[...]).astype(BF16)

    loop(FF // GC, grad_outer)
    reduce_start(U_FOUT)
    turn()
    r.tr[...] = r.a5[...].T

    def grad_inner(k):
        cols = rows_of(k, GC)
        r.w[FIN][:, cols] = mm(r.tr[...], r.dg[:, cols]).astype(BF16)

    loop(FF // GC, grad_inner)
    reduce_start(U_FIN)
    turn()

    def out_back(i):
        rows = rows_of(i, T)
        f3 = r.gs[rows].astype(BF16)
        r.a5[rows] = f3
        r.hid[rows, 3 * D : 4 * D] = mm_t(f3, r.w[OUT][...]).astype(BF16)

    loop(1, out_back)
    r.w[OUT][...] = mm_tn(r.ctx[...], r.a5[...]).astype(BF16)
    reduce_start(U_OUT)
    turn()
    r.tr[...] = r.a4[...].T

    QB = 256

    def with_terms(extra, v):
        high = v.astype(BF16).astype(F32)
        mid = (v - high).astype(BF16).astype(F32)
        low = v - high - mid
        terms = jnp.where(lane == 4, high, jnp.where(lane == 5, mid, jnp.where(lane == 6, low, 0.0)))
        return extra - terms.astype(BF16)

    halfway = []

    def attend_back(j):
        cols, vcols = pair_cols(j), pair_cols(j, D)
        k2 = r.kvb[:, cols]
        keys = jnp.concatenate([k2, r.kenc[...]], axis=1)
        turned = [head_lanes(e, k2).T for e in range(2)]
        values = jnp.concatenate([r.kvb[:, vcols], r.kenc[...]], axis=1)
        for k in range(T // QB):
            rows = slice(k * QB, (k + 1) * QB)
            q2 = r.qb[rows, cols]
            d2 = r.hid[rows, pair_cols(j, 3 * D)]
            inner = d2.astype(F32) * r.ctx[rows, cols].astype(F32)
            dq = jnp.zeros((128, QB), F32)
            for e in range(2):
                qe, de = head_lanes(e, q2), head_lanes(e, d2)
                lse = jnp.sum(
                    jnp.where(lane == 2 * j + e, r.lse[rows], 0.0), axis=-1, keepdims=True
                )
                delta = jnp.sum(head_lanes(e, inner), axis=-1, keepdims=True)
                shifted = mm_t(keys, jnp.concatenate([qe, with_terms(r.qenc[rows], lse)], axis=1))
                probs = jnp.exp(shifted)
                none = jnp.zeros((QB, 128), BF16)
                moved = mm_t(values, jnp.concatenate([de, with_terms(none, delta)], axis=1))
                ds = (probs * moved).astype(BF16)
                dk = mm(ds, qe)
                dv = mm(probs.astype(BF16), de)
                for kk in range(2):
                    half = slice(kk * T, (kk + 1) * T)
                    at = 2 * D + kk * 128
                    if k == 0 and e == 0:
                        r.big[0:T, at : at + 128] = dk[half]
                        r.big[0:T, at + 256 : at + 384] = dv[half]
                    else:
                        r.big[0:T, at : at + 128] += dk[half]
                        r.big[0:T, at + 256 : at + 384] += dv[half]
                dq = dq + mm(turned[e], ds)
            r.hid[rows, cols] = (dq.T * scale).astype(BF16)
            if k == 0:
                for step, act in halfway:
                    pl.when(j == step)(lambda act=act: (act(), None)[1])

        def part(core, what):
            at = pl.multiple_of(2 * D + core * 128 + what * 256, 128)
            return r.big[0:T, pl.ds(at, 128)]

        @pl.when(j >= 2)
        def _():
            dkv_copy(j - 2).wait_send()

        for what in range(2):
            mine = pl.ds(pl.multiple_of(j * 256 + what * 128, 128), 128)
            r.big[0:T, mine] = part(c, what)
            r.cot[:, pl.ds(pl.multiple_of(lax.rem(j, 2) * 256 + what * 128, 128), 128)] = part(
                oc, what
            ).astype(BF16)
        dkv_copy(j).start()

        @pl.when(j == 2)
        def _():
            pairs_back(0)

    def dkv_copy(j):
        slot = lax.rem(j, 2)
        return remote(
            r.cot.at[:, pl.ds(pl.multiple_of(slot * 256, 128), 256)],
            r.dkvr.at[:, pl.ds(pl.multiple_of(j * 256, 128), 256)],
            r.s_js.at[j],
            r.s_jr.at[j],
            sibling,
        )

    def pairs_back(m):
        parts, weights = [], []
        for j in (2 * m, 2 * m + 1):
            dkv_copy(j).wait_recv()
            if m == 1:
                dkv_copy(j).wait_send()
            both = slice(j * 256, (j + 1) * 256)
            dkv = r.big[0:T, both] + r.dkvr[:, both].astype(F32)
            own = slice(j * 128, (j + 1) * 128)
            parts += [r.hid[0:T, own], dkv.astype(BF16)]
            for base in (0, D, 2 * D):
                weights.append(r.w[QKV][:, base + j * 128 : base + (j + 1) * 128])
        pairs = jnp.concatenate(parts, axis=1)
        share = mm_t(pairs, jnp.concatenate(weights, axis=1))
        if m == 0:
            r.big[0:T, 3 * D : 4 * D] = share
        else:
            r.big[0:T, 3 * D : 4 * D] += share
        r.dg[:, m * 768 : (m + 1) * 768] = mm(r.tr[...], pairs).astype(BF16)

    acts = []
    for k in range(HEADS // 2):
        halfway += [(k, act) for _, act in turns_of(1)]
        if k == 2:
            enlist(U_QKV0)
            acts.append((2, lambda: red0(U_QKV0)))
        acts += [(k, act) for _, act in turns_of(1)]
    loop(HEADS // 2, attend_back, acts)
    pairs_back(1)
    reduce_start(U_QKV1)
    turn()

    def qkv_back(i):
        rows = rows_of(i)
        r.gs[rows] += ln_back(2, r.big[rows, 3 * D : 4 * D], r.y2[rows])

    loop(NB, qkv_back)

    def point_back(i):
        rows = rows_of(i, T)
        f2 = r.gs[rows].astype(BF16)
        r.a4[rows] = f2
        for k in range(FF // CH):
            cols = slice(k * CH, (k + 1) * CH)
            d = mm_t(f2, r.w[POINT][cols])
            r.hid[rows_of(i, T, 16), cols] = d.astype(BF16)

    loop(1, point_back)
    edge_send(2, r.hid[T : T + 16], r.hid[16:32])
    turn()

    def grad_point(k):
        cols = rows_of(k, GC)
        r.w[POINT][cols] = mm_tn(r.sep[:, cols], r.a4[...]).astype(BF16)

    loop(FF // GC, grad_point)
    reduce_start(U_POINT0, U_POINT1)
    turn()
    r.hid[0:16], r.hid[T + 16 : T + 32] = edge_take(2)

    def depth_back(j):
        cols = pl.ds(pl.multiple_of(j * 256, 256), 256)
        gain, shift = r.midp[0:1, cols], r.midp[1:2, cols]
        sums = [jnp.zeros((8, 256), F32) for _ in range(9)]
        for b in range(T // MB):
            lo = b * MB
            taps = mm(r.ms[b], r.hid[window(b) : window(b) + MW, cols])
            a3 = r.nm[lo : lo + MB, cols].astype(F32) * gain + shift
            total = jnp.zeros((MB, 256), F32)
            here = r.hid[16 + lo : 16 + lo + MB, cols].astype(F32)
            for o in range(-4, 5):
                i = TAPS.index(-o) if o else 0
                moved = taps[i * MB : (i + 1) * MB] if o else here
                total = total + moved * r.midp[6 + o : 7 + o, cols]
                part = moved * a3
                for g in range(MB // 8):
                    sums[o + 4] = sums[o + 4] + part[g * 8 : (g + 1) * 8]
            r.big[lo + 8 : lo + 8 + MB, cols] = total
        for o in range(9):
            r.g8[2 + o : 3 + o, cols] = jnp.sum(sums[o], axis=0, keepdims=True)

    loop(FF // 256, depth_back, turns_of(FF // 256))

    def mid_back(i):
        rows, erows = rows_of(i, RM), rows_of(i, RM, 8)
        e = r.big[erows]
        unit = r.nm[rows].astype(F32)
        eg = e * r.midp[0:1]
        m1 = jnp.mean(eg, axis=-1, keepdims=True)
        m2 = jnp.mean(eg * unit, axis=-1, keepdims=True)
        r.g8[0:1] += jnp.sum(e * unit, axis=0, keepdims=True)
        r.g8[1:2] += jnp.sum(e, axis=0, keepdims=True)
        dmid = r.rm[rows] * (eg - m1 - unit * m2)
        r.dgl[rows] = (dmid * r.dgl[rows].astype(F32)).astype(BF16)
        right = dmid[:, 0:H] * r.dgr[rows].astype(F32)
        r.pext[0, erows] = right.astype(BF16).astype(F32)

    loop(T // RM, mid_back, turns_of(T // RM))
    edge_send(3, r.pext[0, T : T + 8], r.pext[0, 8:16])
    r.tr[...] = r.a2[...].T

    def grad_left(k):
        cols = rows_of(k, GC)
        r.sep[:, cols] = mm(r.tr[...], r.dgl[:, cols]).astype(BF16)

    half = FF // GC // 2
    lax.fori_loop(0, half, lambda k, _: (grad_left(k), 0)[1], 0)
    reduce_start(U_LEFT0)
    turn()
    lax.fori_loop(half, 2 * half, lambda k, _: (grad_left(k), 0)[1], 0)
    reduce_start(U_LEFT1)
    turn()
    top, bottom = edge_take(3)
    r.pext[0, 0:8] = top
    r.pext[0, T + 8 : T + 16] = bottom
    for k in range(T // 128):
        lo = k * 128
        for o in (-1, 0, 1):
            moved = r.pext[0, lo + 8 - o : lo + 136 - o]
            if o:
                moved = moved * jnp.concatenate([mask(-o, lo, 128)] * (H // 128), axis=1)
            r.hid[lo : lo + 128, (o + 1) * H : (o + 2) * H] = moved.astype(BF16)
    for o in range(3):
        cols = slice(o * H, (o + 1) * H)
        r.dkvr[:, cols] = mm(r.tr[...], r.hid[0:T, cols]).astype(BF16)
    reduce_start(U_CONV)
    turn()

    def branch_back(i):
        rows = rows_of(i)
        e = mm_t(r.dgl[rows], r.w[LEFT][...])
        for o in range(3):
            e = e + mm_t(r.hid[rows, o * H : (o + 1) * H], r.w[CONV][o])
        r.gs[rows] += ln_back(1, e, r.y1[rows])

    loop(NB, branch_back, turns_of(NB))

    def gate_back(i):
        rows = rows_of(i)
        g = r.gs[rows]
        r.sg[rows, 0:D] = (g * r.sg[rows, 0:D].astype(F32)).astype(BF16)
        r.sg[rows, D : 2 * D] = (g * r.sg[rows, D : 2 * D].astype(F32)).astype(BF16)

    loop(NB, gate_back)
    r.tr[...] = r.a1[...].T

    def grad_glu(k):
        cols = rows_of(k, D)
        to = pl.ds(pl.multiple_of(k * D + 2 * D, D), D)
        r.hid[0:T, to] = mm(r.tr[...], r.sg[:, cols]).astype(BF16)

    grad_glu(0)
    reduce_start(U_GLU0)
    turn()
    grad_glu(1)
    reduce_start(U_GLU1)
    turn()

    def glu_back(i):
        rows = rows_of(i)
        e = mm_t(r.sg[rows], r.w[GLU][...])
        total = r.gs[rows] + ln_back(0, e, r.xin[rows].astype(F32))
        r.a5[rows] = total.astype(BF16)

    loop(NB, glu_back, turns_of(NB))
    r.gsm[0:16] = r.g8[:, 0 : FF // 2].astype(BF16)
    r.gsm[16:32] = r.g8[:, FF // 2 : FF].astype(BF16)
    reduce_start(SMALL)
    move(TAIL[0])
    tokens_out(r.a5, r.o_ig, 3)
    move(TAIL[1])
    while any(ahead.values()):
        move(range(UNITS))

    for u in range(UNITS):
        red_end(u)
    tokens_out_done(r.osend, r.o_out, 2)
    tokens_out_done(r.a5, r.o_ig, 3)
    tokens_in_sent(r.x, r.xin, 0)
    tokens_in_sent(r.ct, r.cot, 1)
    seg_sent()
    for t in range(1, n):
        small_copy(t).wait_send()


def local(
    inputs,
    segment_ids,
    cotangent,
    norm_gain,
    norm_bias,
    glu_weight,
    left_weight,
    conv_weight,
    mid_gain,
    mid_bias,
    depth_weight,
    point_weight,
    qkv_weight,
    out_weight,
    ffn_in,
    ffn_out,
):
    seqs, span, width = inputs.shape
    n = lax.axis_size("seq")
    plan = Plan(
        lax.axis_size("dp"), n, seqs, span, width, ffn_in.shape[1], conv_weight.shape[2]
    )
    q = lax.axis_index("seq")

    def placed(piece, repeats):
        if repeats == 1:
            return piece
        size = piece.shape[-1]
        tiled = jnp.tile(piece, (1,) * (piece.ndim - 1) + (repeats,))
        at = lax.broadcasted_iota(jnp.int32, tiled.shape, tiled.ndim - 1) // size
        return jnp.where(at == q % repeats, tiled, jnp.zeros_like(tiled))

    segs = placed(segment_ids, plan.sr)
    segs = jnp.broadcast_to(segs[:, None, :], (seqs, 8, plan.sw))
    norms = placed(jnp.concatenate([norm_gain, norm_bias], 0), plan.nr)
    norms = norms.reshape(plan.srows, plan.FFn)
    small = jnp.concatenate([norms, mid_gain[None], mid_bias[None], depth_weight], 0)
    small = jnp.pad(small, ((0, plan.spack - small.shape[0]), (0, 0)))
    weights = [None] * WEIGHTS
    weights[GLU], weights[CONV], weights[LEFT] = glu_weight, conv_weight, left_weight
    weights[POINT], weights[QKV], weights[OUT] = point_weight, qkv_weight, out_weight
    weights[FIN], weights[FOUT] = ffn_in, ffn_out

    shapes = []
    plan.buffers(shapes.append)
    out_shape = [jax.ShapeDtypeStruct(inputs.shape, BF16)] * 2
    out_shape += [jax.ShapeDtypeStruct(plan.piece(w, plan.kr(w)), BF16) for w in range(WEIGHTS)]
    out_shape += [jax.ShapeDtypeStruct((32, plan.FF // 2), BF16)]
    hbm = pl.BlockSpec(memory_space=pl.ANY)
    got = pl.pallas_call(
        lambda *refs: kernel(plan, *refs),
        out_shape=out_shape,
        in_specs=[hbm] * INPUTS,
        out_specs=[hbm] * OUTPUTS,
        scratch_shapes=shapes,
        compiler_params=pltpu.CompilerParams(
            collective_id=0, has_side_effects=True, vmem_limit_bytes=64 << 20
        ),
        name="cell",
    )(inputs, segs, cotangent, small, *weights)
    out = unpacked(plan, got)
    return (
        out[0],
        out[1],
        out[2 + WEIGHTS],
        out[3 + WEIGHTS],
        out[2 + GLU],
        out[2 + LEFT],
        out[2 + CONV],
        out[4 + WEIGHTS].reshape(-1),
        out[5 + WEIGHTS].reshape(-1),
        out[6 + WEIGHTS],
        out[2 + POINT],
        out[2 + QKV],
        out[2 + OUT],
        out[2 + FIN],
        out[2 + FOUT],
    )


def unpacked(plan, parts):
    count = 2 + WEIGHTS
    dn = plan.D // plan.n
    wide = [jax.ShapeDtypeStruct(p.shape, F32) for p in parts[:count]]
    conv, qkv, H = 2 + CONV, 2 + QKV, plan.HALF
    wide[conv] = jax.ShapeDtypeStruct((3, plan.kr(CONV), H), F32)
    tiny = [(4, dn), (4, dn), (1, plan.FFn), (1, plan.FFn), (9, plan.FFn)]
    out_shape = wide + [jax.ShapeDtypeStruct(shape, F32) for shape in tiny]

    def body(*refs):
        ins, outs = refs[:count], refs[count + 1 : 2 * count + 1]
        sums, tinies = refs[count], refs[2 * count + 1 : 2 * count + 6]
        near, far = refs[2 * count + 6 : 3 * count + 6], refs[3 * count + 6 : 4 * count + 6]
        came, went = refs[4 * count + 6], refs[4 * count + 7]

        def arrive(i):
            return pltpu.make_async_copy(ins[i], near[i], came.at[i])

        def leave(i):
            return pltpu.make_async_copy(far[i], outs[i], went.at[i])

        for i in range(count):
            arrive(i).start()
        q = lax.axis_index("seq")
        whole = jnp.concatenate([sums[0:16].astype(F32), sums[16:32].astype(F32)], axis=1)
        rolled = pltpu.roll(whole, (plan.FF - q * plan.FFn) % plan.FF, 1)[:, 0 : plan.FFn]
        tinies[2][...] = rolled[0:1]
        tinies[3][...] = rolled[1:2]
        tinies[4][...] = rolled[2:11]
        for k in range(2):
            row = whole[11 + k : 12 + k]
            rows = [row[:, i * plan.D : (i + 1) * plan.D] for i in range(4)]
            both = jnp.concatenate(rows + rows, axis=0)
            tinies[k][...] = pltpu.roll(both, (plan.D - q * dn) % plan.D, 1)[0:4, 0:dn]
        for i in range(count):
            arrive(i).wait()
            if i == conv:
                for k in range(3):
                    far[i][k] = near[i][:, k * H : (k + 1) * H].astype(F32)
            elif i == qkv:
                for k in range(12):
                    to = (k % 3) * plan.D + k // 3 * 128
                    far[i][:, to : to + 128] = near[i][:, k * 128 : (k + 1) * 128].astype(F32)
            else:
                far[i][...] = near[i][...].astype(F32)
            leave(i).start()
        for i in range(count):
            leave(i).wait()

    hbm = pl.BlockSpec(memory_space=pl.ANY)
    vmem = pl.BlockSpec(memory_space=pltpu.VMEM)
    return pl.pallas_call(
        body,
        out_shape=out_shape,
        in_specs=[hbm] * count + [vmem],
        out_specs=[hbm] * count + [vmem] * len(tiny),
        scratch_shapes=[pltpu.VMEM(p.shape, BF16) for p in parts[:count]]
        + [pltpu.VMEM(shape.shape, F32) for shape in wide]
        + [pltpu.SemaphoreType.DMA((count,))] * 2,
        compiler_params=pltpu.CompilerParams(vmem_limit_bytes=64 << 20),
    )(*parts)


def solution(mesh):
    in_specs = (
        P("dp", "seq", None),
        P("dp", "seq"),
        P("dp", "seq", None),
        P(None, "seq"),
        P(None, "seq"),
        P("seq", None),
        P("seq", None),
        P(None, "seq", None),
        P("seq"),
        P("seq"),
        P(None, "seq"),
        P("seq", None),
        P("seq", None),
        P("seq", None),
        P("seq", None),
        P("seq", None),
    )
    out_specs = (
        P("dp", "seq", None),
        P("dp", "seq", None),
        P(None, "seq"),
        P(None, "seq"),
        P("seq", None),
        P("seq", None),
        P(None, "seq", None),
        P("seq"),
        P("seq"),
        P(None, "seq"),
        P("seq", None),
        P("seq", None),
        P("seq", None),
        P("seq", None),
        P("seq", None),
    )
    return jax.shard_map(local, mesh=mesh, in_specs=in_specs, out_specs=out_specs, check_vma=False)
```

```python
import math

import jax
import jax.numpy as jnp
from jax import lax
from jax.experimental import pallas as pl
from jax.experimental.pallas import tpu as pltpu
from jax.sharding import PartitionSpec as P

HEADS = 8
EPS = 1e-06
MESH = pl.DeviceIdType.MESH
F32 = jnp.float32
BF16 = jnp.bfloat16

GLU, CONV, LEFT, POINT, QKV, OUT, FIN, FOUT = range(8)
WEIGHTS = 8
(U_GLU0, U_GLU1, U_CONV, U_LEFT0, U_LEFT1, U_POINT0, U_POINT1, U_QKV0, U_QKV1, U_OUT, U_FIN, U_FOUT, SMALL) = range(13)
UNITS = 13
UNIT_WEIGHT = (GLU, GLU, CONV, LEFT, LEFT, POINT, POINT, QKV, QKV, OUT, FIN, FOUT, WEIGHTS)
UNIT_PART = (0, 1, None, 0, 1, 0, 1, 0, 1, None, None, None, None)

SHARED = (GLU, CONV, POINT,)
SMALLS, TOKENS = 8, 9
START = (GLU, CONV, SMALLS, TOKENS)
FORWARD = (
    ((1, GLU), (1, CONV)),
    (),
    ((0, LEFT),),
    ((2, GLU), (2, CONV), (0, POINT), (3, GLU)),
    ((1, LEFT),),
    ((1, POINT), (3, CONV)),
    ((0, QKV),),
    (),
    (),
    (),
    ((2, LEFT),),
    ((2, POINT), (0, OUT), (0, FIN)),
    (),
    ((1, QKV),),
    (),
    ((1, OUT),),
    (),
    (),
    ((3, POINT), (0, FOUT)),
    ((1, FIN),),
    (),
    (),
    (),
    ((2, QKV), (2, OUT)),
    (),
    (),
    ((1, FOUT),),
    ((0, TOKENS),),
    ((2, FIN),),
    ((2, FOUT),),
    (),
    (),
    (),
    (),
    (),
    (),
    (),
)
SCHEDULE = (
    (),
    (),
    (),
    (U_FOUT,),
    (U_FIN,),
    (),
    (),
    (U_OUT,),
    (U_FOUT,),
    (),
    (U_FIN, U_QKV0),
    (U_OUT,),
    (U_FOUT, U_QKV1),
    (U_QKV0,),
    (),
    (U_FIN,),
    (U_POINT0, U_POINT1),
    (U_QKV0, U_QKV1),
    (U_FOUT,),
    (),
    (),
    (),
    (U_QKV1, U_POINT0),
    (),
    (),
    (U_OUT, U_FIN),
    (U_POINT1,),
    (U_POINT0, U_FOUT),
    (U_LEFT0, U_QKV1),
    (U_QKV0, U_OUT, U_POINT1, U_LEFT1),
    (),
    (U_POINT0, U_FIN),
    (),
    (U_LEFT0,),
    (U_QKV1, U_CONV, U_GLU0, U_GLU1, U_LEFT1),
)
TAIL = (
    (SMALL, U_POINT1, U_QKV0, U_LEFT0, U_OUT, U_CONV, U_POINT0, U_LEFT1, U_GLU0, U_LEFT0, U_POINT1, U_GLU1, SMALL),
    (U_CONV, U_GLU0, U_LEFT1, U_GLU1, U_LEFT0, SMALL, U_CONV, U_GLU0, U_LEFT1, U_GLU1, SMALL, U_CONV, U_GLU0, U_GLU1, SMALL, U_FOUT, U_FIN, U_OUT, U_QKV0, U_QKV1, U_POINT0, U_POINT1, U_LEFT0, U_LEFT1, U_CONV, U_GLU0, U_GLU1, SMALL),
)

MB, MW = 128, 256
TAPS = (-4, -3, -2, -1, 1, 2, 3, 4)
FAR = -(2.0**30)


def mm(a, b):
    return lax.dot_general(a, b, (((1,), (0,)), ((), ())), preferred_element_type=F32)


def mm_t(a, b):
    return lax.dot_general(a, b, (((1,), (1,)), ((), ())), preferred_element_type=F32)


def mm_tn(a, b):
    return lax.dot_general(a, b, (((0,), (0,)), ((), ())), preferred_element_type=F32)


def normed(v):
    centred = v - jnp.mean(v, axis=-1, keepdims=True)
    r = lax.rsqrt(jnp.mean(centred * centred, axis=-1, keepdims=True) + EPS)
    return centred * r, r


def gelu_both(v):
    c = math.sqrt(2.0 / math.pi)
    sq = v * v
    t = jnp.tanh(v * (c + (c * 0.044715) * sq))
    half = 0.5 * t + 0.5
    value = v * half
    slope = half + (0.5 * v) * (1.0 - t * t) * (c + (3.0 * c * 0.044715) * sq)
    return value, slope


def sigmoid(v):
    return 0.5 * jnp.tanh(0.5 * v) + 0.5


class Buffers:
    pass


class Plan:
    def __init__(self, dp, n, seqs, span, width, hidden, half):
        self.n, self.Z = n, dp // 2
        self.S, self.span = seqs, span
        self.D, self.FF, self.HALF = width, hidden, half
        self.LEN = span * n
        self.T = self.LEN // 2
        self.PH = n // 2
        self.B = math.isqrt(n)
        self.A = n // self.B
        assert self.A == self.B and n == 2 * seqs and dp % 2 == 0
        self.shared = SHARED if self.Z % 2 == 0 else ()
        self.sw = max(span, 128)
        self.sr = self.sw // span
        dn = width // n
        self.nw = max(dn, 128)
        self.nr = self.nw // dn
        self.FFn = hidden // n
        self.spack = 32
        self.dims = [
            (width, 2 * width),
            (width, half),
            (width, hidden),
            (hidden, width),
            (width, 3 * width),
            (width, width),
            (width, hidden),
            (hidden, width),
        ]

    def whole(self, w):
        k, cols = self.dims[w]
        return (3, k, cols) if w == CONV else (k, cols)

    def kr(self, w):
        return self.dims[w][0] // self.n

    def hr(self, w):
        return self.kr(w) // 2

    def gcols(self, w):
        return self.dims[w][1] * (3 if w == CONV else 1)

    def piece(self, w, rows):
        return (rows, self.gcols(w))

    def buffers(self, take):
        T, D, FF, H, n = self.T, self.D, self.FF, self.HALF, self.n
        r = Buffers()

        def vm(shape, dtype):
            return take(pltpu.VMEM(shape, dtype))

        def sem(*shape):
            return take(pltpu.SemaphoreType.DMA(shape))

        every = range(WEIGHTS)
        parts = [(self.piece(w, self.hr(w)), BF16) for w in every] + [((16, FF // 2), BF16)]
        r.w = [vm(self.whole(w), BF16) for w in every]
        r.g8 = vm((16, FF), F32)
        r.gsm = vm((32, FF // 2), BF16)
        r.r = [None] * WEIGHTS + [vm((16, FF // 2), BF16)]
        for w in (CONV, QKV, OUT, FIN, FOUT):
            r.r[w] = vm(self.piece(w, n * self.hr(w)), BF16)
        r.r[LEFT], r.r[POINT], r.r[GLU] = r.r[FIN], r.r[FOUT], r.r[QKV]
        r.p = [vm((n - 1,) + shape, dtype) for shape, dtype in parts]
        if self.Z > 1:
            r.u = [vm(shape, dtype) for shape, dtype in parts]
            r.d = [vm(shape, dtype) for shape, dtype in parts]
        r.segbuf = vm((n, self.S, self.sw), jnp.int32)
        r.segrow = vm((8, self.LEN), F32)
        r.segcol = vm((self.LEN + 16, 128), F32)
        r.segloc = vm((T + 16, 128), F32)
        r.mext = vm((T + 16, 128), F32)
        r.ms = vm((T // MB, 8 * MB, MW), BF16)
        r.qenc = vm((T, 128), BF16)
        r.kenc = vm((self.LEN, 128), BF16)
        r.smallbuf = vm((n, self.spack, self.FFn), BF16)
        r.nrm = vm((8, D), F32)
        r.midp = vm((16, FF), F32)
        r.xin = vm((T, D), BF16)
        r.cot = vm((T, D), BF16)
        r.a1 = vm((T, D), BF16)
        r.sg = vm((T, 2 * D), BF16)
        r.y1 = vm((T, D), F32)
        r.a2 = vm((T, D), BF16)
        r.pext = vm((3, T + 16, H), F32)
        r.dgl = vm((T, FF), BF16)
        r.dgr = vm((T, H), BF16)
        r.nm = vm((T, FF), BF16)
        r.rm = vm((T, 1), F32)
        r.big = vm((T + 16, FF), F32)
        r.sep = vm((T, FF), BF16)
        r.y2 = vm((T, D), F32)
        r.a4 = vm((T, D), BF16)
        r.qb = vm((T, D), BF16)
        r.kvb = vm((self.LEN, 2 * D), BF16)
        r.lse = vm((T, 128), F32)
        r.ctx = vm((T, D), BF16)
        r.y3 = vm((T, D), F32)
        r.a5 = vm((T, D), BF16)
        r.hid = vm((T + 32, FF), BF16)
        r.dg = vm((T, FF), BF16)
        r.osend = vm((T, D), BF16)
        r.gs = r.y3
        r.dkvr = vm((T, 2 * D), BF16)
        r.tr = vm((D, T), BF16)
        edges = (((8, H), F32), ((16, FF), BF16), ((16, FF), BF16), ((8, H), F32))
        r.es = [vm(shape, dtype) for shape, dtype in edges]
        r.er = [vm(shape, dtype) for shape, dtype in edges]
        r.s_loc = sem(WEIGHTS)
        r.s_as = sem(WEIGHTS)
        r.s_ar = sem(WEIGHTS, self.B - 1)
        r.s_br = sem(WEIGHTS, (self.A - 1) * self.B)
        r.s_dr = sem(WEIGHTS)
        if self.shared:
            r.s_hr = sem(WEIGHTS)
        r.s_rs = sem(UNITS)
        r.s_rr = sem(UNITS)
        r.s_ps = sem(UNITS)
        r.s_pr = sem(UNITS, 2)
        if self.Z > 1:
            r.s_zs = sem(UNITS)
            r.s_zr = sem(UNITS, 2)
        r.s_fs = sem(UNITS)
        r.s_fr = sem(UNITS)
        r.s_xs = sem(4, self.S)
        r.s_xr = sem(4, max(self.PH, self.S))
        r.s_gs = sem(2 * self.S)
        r.s_gr = sem(n)
        r.s_ms = sem(n)
        r.s_mr = sem(n)
        r.s_es = sem(4)
        r.s_er = sem(4)
        r.s_ks = sem(HEADS // 2)
        r.s_kr = sem(HEADS // 2)
        r.s_js = sem(HEADS // 2)
        r.s_jr = sem(HEADS // 2)
        return r


INPUTS = 4 + WEIGHTS
OUTPUTS = 2 + WEIGHTS + 1


def kernel(plan, *refs):
    ins, outs = refs[:INPUTS], refs[INPUTS : INPUTS + OUTPUTS]
    scratch = iter(refs[INPUTS + OUTPUTS :])
    r = plan.buffers(lambda shape: next(scratch))
    r.x, r.seg, r.ct, r.small = ins[:4]
    r.h = ins[4:]
    r.o_out, r.o_ig = outs[:2]
    r.o = outs[2:]
    n, Z, S, span = plan.n, plan.Z, plan.S, plan.span
    T, D, FF, H, PH = plan.T, plan.D, plan.FF, plan.HALF, plan.PH
    A, B = plan.A, plan.B
    dp, q = lax.axis_index("dp"), lax.axis_index("seq")
    z, c = dp // 2, dp % 2
    oc = 1 - c

    def aligned(v, m=16):
        return pl.multiple_of(v, m)

    def dev(core, chip, plane=None):
        return ((z if plane is None else plane) * 2 + core, chip)

    sibling = dev(oc, q)

    def remote(src, dst, ss, rs, to):
        return pltpu.make_async_remote_copy(
            src_ref=src, dst_ref=dst, send_sem=ss, recv_sem=rs, device_id=to, device_id_type=MESH
        )

    barrier = pltpu.get_barrier_semaphore()
    for core in range(2):

        def greet(t, _, core=core):
            chip = lax.rem(q + t, n)
            to = (z * 2 + (c + core) % 2, chip)
            pl.semaphore_signal(barrier, inc=1, device_id=to, device_id_type=MESH)
            return 0

        lax.fori_loop(1 - core, n, greet, 0)
    if Z > 1:

        @pl.when(z > 0)
        def _():
            pl.semaphore_signal(barrier, inc=1, device_id=dev(c, q, z - 1), device_id_type=MESH)

        @pl.when(z < Z - 1)
        def _():
            pl.semaphore_signal(barrier, inc=1, device_id=dev(c, q, z + 1), device_id_type=MESH)

    pl.semaphore_wait(barrier, 2 * n - 1 + (z + Z - 1) // Z + (2 * Z - 2 - z) // Z)

    def vrows(ref, w, row0, rows):
        ds = pl.ds(aligned(row0), rows)
        return ref.at[:, ds] if w == CONV else ref.at[ds]

    def bytes_of(view, semaphore):
        return pltpu.make_async_copy(view, view, semaphore)

    def qof(core, f, g):
        f, g = f % B, g % B
        return core * (f * B + g) + (1 - core) * (g * B + f)

    b_, a_ = q % B, q // B
    f_, g_ = c * a_ + oc * b_, c * b_ + oc * a_
    par = z % 2
    partner = dev(c, q, z + 1 - 2 * par)

    def wrows(ref, w, row0, rows, side):
        if w not in plan.shared:
            return vrows(ref, w, row0, rows)
        size = plan.dims[w][1] // 2
        cols = pl.ds(pl.multiple_of(side * size, 128), size)
        if w == CONV:
            return ref.at[:, pl.ds(aligned(row0), rows), cols]
        return ref.at[pl.ds(aligned(row0), rows), cols]

    def wblock(w, shard, side=par):
        return wrows(r.w[w], w, shard * plan.kr(w) + c * plan.hr(w), plan.hr(w), side)

    def own_block(w):
        return wrows(r.h[w], w, c * plan.hr(w), plan.hr(w), par)

    def copy_a(w, t):
        to = dev(c, qof(c, f_ + t, g_))
        return remote(own_block(w), wblock(w, q), r.s_as.at[w], r.s_ar.at[w, t - 1], to)

    def copy_b(w, u, t):
        blk = wblock(w, qof(c, f_ + B - t, g_))
        src = own_block(w) if t == 0 else blk
        to = dev(c, qof(c, f_, g_ + u))
        return remote(src, blk, r.s_as.at[w], r.s_br.at[w, (u - 1) * B + t], to)

    def shard_from(u, t):
        return qof(c, f_ + B - t, g_ + B - u)

    def pass_on(w, u, t):
        blk = wblock(w, shard_from(u, t))
        remote(blk, blk, r.s_as.at[w], r.s_dr.at[w], sibling).start()
        if w in plan.shared:
            remote(blk, blk, r.s_as.at[w], r.s_hr.at[w], partner).start()

    def local_shard(w):
        dst = vrows(r.w[w], w, q * plan.kr(w), plan.kr(w))
        return pltpu.make_async_copy(r.h[w], dst, r.s_loc.at[w])

    def g0(w):
        local_shard(w).start()
        for t in range(1, B):
            copy_a(w, t).start()
        for u in range(1, A):
            copy_b(w, u, 0).start()

    def g1(w):
        for t in range(1, B):
            bytes_of(wblock(w, shard_from(0, t)), r.s_ar.at[w, t - 1]).wait()
            for u in range(1, A):
                copy_b(w, u, t).start()
            pass_on(w, 0, t)

    def g2(w):
        for u in range(1, A):
            for t in range(B):
                bytes_of(wblock(w, shard_from(u, t)), r.s_br.at[w, (u - 1) * B + t]).wait()
                pass_on(w, u, t)

    def others(w):
        return wrows(r.w[w], w, 0, (n - 1) * plan.hr(w), 0)

    def gz(w):
        if w not in plan.shared:
            return
        bytes_of(others(w), r.s_hr.at[w]).wait()
        for u in range(A):
            for t in range(B):
                if (u, t) != (0, 0):
                    blk = wblock(w, shard_from(u, t), 1 - par)
                    remote(blk, blk, r.s_as.at[w], r.s_dr.at[w], sibling).start()

    def g3(w):
        local_shard(w).wait()
        bytes_of(vrows(r.w[w], w, 0, (n - 1) * plan.hr(w)), r.s_dr.at[w]).wait()

    gather_steps = (g0, g1, g2, gz)
    forward_turns = iter(FORWARD)

    def gather(steps):
        for k, w in steps:
            if w == TOKENS:
                tokens_in(r.ct, r.cot, 1)
            else:
                gather_steps[k](w)

    def pass_turn():
        gather(next(forward_turns))

    def pass_turns(count):
        every = [(k, next(forward_turns)) for k in range(count)]
        return [(k, lambda steps=steps: gather(steps)) for k, steps in every if steps]

    def gather_sent(w):
        bytes_of(vrows(r.w[w], w, 0, 2 * (n - 1) * plan.hr(w)), r.s_as.at[w]).wait()

    def token_rows(ref, slot):
        return ref.at[pl.ds(aligned(slot * span), span)]

    def tokens_in(src, dst, k):
        for j in range(S):
            chip, core, slot = S * c + j, q // PH, q % PH
            here = jnp.logical_and(chip == q, core == c)
            there = token_rows(dst, slot)

            @pl.when(here)
            def _():
                pltpu.make_async_copy(src.at[j], there, r.s_xr.at[k, slot]).start()

            @pl.when(jnp.logical_not(here))
            def _():
                remote(
                    src.at[j], there, r.s_xs.at[k, j], r.s_xr.at[k, slot], dev(core, chip)
                ).start()

    def tokens_in_done(dst, k):
        for slot in range(PH):
            blk = token_rows(dst, slot)
            pltpu.make_async_copy(blk, blk, r.s_xr.at[k, slot]).wait()

    def tokens_in_sent(src, dst, k):
        for j in range(S):
            chip, core, slot = S * c + j, q // PH, q % PH
            here = jnp.logical_and(chip == q, core == c)

            @pl.when(jnp.logical_not(here))
            def _():
                remote(
                    src.at[j],
                    token_rows(dst, slot),
                    r.s_xs.at[k, j],
                    r.s_xr.at[k, slot],
                    dev(core, chip),
                ).wait_send()

    def tokens_out(src, dst, k):
        for p in range(PH):
            chip, core, slot = c * PH + p, q // S, q % S
            here = jnp.logical_and(chip == q, core == c)

            @pl.when(here)
            def _():
                pltpu.make_async_copy(token_rows(src, p), dst.at[slot], r.s_xr.at[k, slot]).start()

            @pl.when(jnp.logical_not(here))
            def _():
                remote(
                    token_rows(src, p),
                    dst.at[slot],
                    r.s_xs.at[k, p],
                    r.s_xr.at[k, slot],
                    dev(core, chip),
                ).start()

    def tokens_out_done(src, dst, k):
        for j in range(S):
            pltpu.make_async_copy(dst.at[j], dst.at[j], r.s_xr.at[k, j]).wait()
        for p in range(PH):
            chip, core, slot = c * PH + p, q // S, q % S
            here = jnp.logical_and(chip == q, core == c)

            @pl.when(jnp.logical_not(here))
            def _():
                remote(
                    token_rows(src, p),
                    dst.at[slot],
                    r.s_xs.at[k, p],
                    r.s_xr.at[k, slot],
                    dev(core, chip),
                ).wait_send()

    def seg_send():
        for j in range(S):
            for core in range(2):
                chip = S * c + j
                here = jnp.logical_and(chip == q, c == core)
                i = 2 * j + core

                @pl.when(here)
                def _():
                    pltpu.make_async_copy(r.seg, r.segbuf.at[q], r.s_gr.at[q]).start()

                @pl.when(jnp.logical_not(here))
                def _():
                    remote(
                        r.seg,
                        r.segbuf.at[q],
                        r.s_gs.at[i],
                        r.s_gr.at[q],
                        dev(core, chip),
                    ).start()

    def seg_sent():
        for j in range(S):
            for core in range(2):
                chip = S * c + j
                here = jnp.logical_and(chip == q, c == core)

                @pl.when(jnp.logical_not(here))
                def _():
                    remote(
                        r.seg,
                        r.segbuf.at[q],
                        r.s_gs.at[2 * j + core],
                        r.s_gr.at[q],
                        dev(core, chip),
                    ).wait_send()

    def small_copy(t):
        return remote(
            r.small,
            r.smallbuf.at[q],
            r.s_ms.at[t],
            r.s_mr.at[t],
            dev(c, (q + t) % n),
        )

    def small_arrived(t):
        blk = r.smallbuf.at[(q + n - t) % n]
        return remote(blk, blk, r.s_ms.at[t], r.s_mr.at[t], sibling)

    def edge_copy(i):
        return remote(r.es[i], r.er[i], r.s_es.at[i], r.s_er.at[i], sibling)

    def edge_send(i, last, first):
        r.es[i][...] = jnp.where(c == 0, last, first)
        edge_copy(i).start()

    def edge_take(i):
        edge_copy(i).wait()
        got = r.er[i][...]
        none = jnp.zeros_like(got)
        return jnp.where(c == 1, got, none), jnp.where(c == 0, got, none)

    def columns(u):
        w, half = UNIT_WEIGHT[u], UNIT_PART[u]
        size = plan.gcols(w)
        return (0, size) if half is None else (half * (size // 2), size // 2)

    def urows(ref, u, row0, rows, shift=0):
        col0, size = columns(u)
        return ref.at[pl.ds(aligned(row0), rows), pl.ds(col0 + shift, size)]

    grad_home = {GLU: (r.hid, 2 * D), CONV: (r.dkvr, 0), LEFT: (r.sep, 0), QKV: (r.dg, 0)}

    def gpiece(u, shard, half):
        if u == SMALL:
            return r.gsm.at[pl.ds(pl.multiple_of(half * 16, 16), 16)]
        w = UNIT_WEIGHT[u]
        ref, shift = grad_home.get(w, (r.w[w] if w < WEIGHTS else None, 0))
        return urows(ref, u, shard * plan.kr(w) + half * plan.hr(w), plan.hr(w), shift)

    def rpiece(u, shard):
        w = UNIT_WEIGHT[u]
        if u == SMALL:
            return r.r[w]
        return urows(r.r[w], u, shard * plan.hr(w), plan.hr(w))

    def slots(u, first, count):
        buf = r.p[UNIT_WEIGHT[u]]
        if u == SMALL:
            return buf.at[pl.ds(first, count)]
        col0, size = columns(u)
        return buf.at[pl.ds(first, count), :, pl.ds(col0, size)]

    def ppiece(u, slot):
        buf = r.p[UNIT_WEIGHT[u]]
        if u == SMALL:
            return buf.at[slot]
        col0, size = columns(u)
        return buf.at[slot, :, pl.ds(col0, size)]

    def zpiece(u, way):
        buf = (r.u, r.d)[way][UNIT_WEIGHT[u]]
        if u == SMALL:
            return buf
        col0, size = columns(u)
        return buf.at[:, pl.ds(col0, size)]

    def copy_r(u, s):
        return remote(gpiece(u, s, oc), rpiece(u, s), r.s_rs.at[u], r.s_rr.at[u], sibling)

    def all_r(u, semaphore):
        w = UNIT_WEIGHT[u]
        view = r.r[w] if u == SMALL else urows(r.r[w], u, 0, n * plan.hr(w))
        return bytes_of(view, semaphore.at[u])

    def shards(u):
        return 1 if u == SMALL else n

    def red0(u):
        for s in range(shards(u)):
            copy_r(u, s).start()

    def put(to, *terms):
        size = to.shape[0]
        rows = min(size, 64)

        def some(i, _):
            at = pl.ds(pl.multiple_of(i * rows, rows), rows)
            total = terms[0][at].astype(F32)
            for term in terms[1:]:
                total = total + term[at].astype(F32)
            to[at] = total.astype(to.dtype)
            return 0

        lax.fori_loop(0, size // rows, some, 0)

    def add_core(u, s):
        mine = gpiece(u, s, c)
        put(mine, mine, rpiece(u, s))

    def slot1(u, t):
        return (u - 1) * B + t

    def slot2(t):
        return (A - 1) * B + t - 1

    def copy_p1(u, k, t):
        return remote(
            gpiece(u, qof(c, f_ + t, g_ + k), c),
            ppiece(u, slot1(k, t)),
            r.s_ps.at[u],
            r.s_pr.at[u, 0],
            dev(c, qof(c, f_, g_ + k)),
        )

    def copy_p2(u, t):
        to = qof(c, f_ + t, g_)
        return remote(
            r.r[WEIGHTS] if u == SMALL else gpiece(u, to, c),
            ppiece(u, slot2(t)),
            r.s_ps.at[u],
            r.s_pr.at[u, 1],
            dev(c, to),
        )

    def all_p(u, step, semaphore):
        count = B - 1 if step else A - 1 if u == SMALL else (A - 1) * B
        return bytes_of(slots(u, 0, count), semaphore.at[u, step])

    def red1(u):
        all_r(u, r.s_rr).wait()
        if u == SMALL:
            add_core(u, 0)
            for k in range(1, A):
                copy_p1(u, k, 0).start()
            return

        def send(i, _):
            k, t = i // B + 1, i % B
            add_core(u, qof(c, f_ + t, g_ + k))
            copy_p1(u, k, t).start()
            return 0

        lax.fori_loop(0, (A - 1) * B, send, 0)
        lax.fori_loop(0, B, lambda t, _: (add_core(u, qof(c, f_ + t, g_)), 0)[1], 0)

    def red1b(u):
        all_p(u, 0, r.s_pr).wait()

        def send(t, _):
            mine = gpiece(u, 0 if u == SMALL else qof(c, f_ + t, g_), c)
            came = [ppiece(u, slot1(k, 0 if u == SMALL else t)) for k in range(1, A)]
            put(r.r[WEIGHTS] if u == SMALL else mine, mine, *came)
            if u != SMALL:
                copy_p2(u, t).start()
            return 0

        if u == SMALL:
            send(0, 0)
            for t in range(1, B):
                copy_p2(u, t).start()
        else:
            lax.fori_loop(1, B, send, 0)

    def red2(u):
        all_p(u, 1, r.s_pr).wait()
        came = [] if u == SMALL else [ppiece(u, slot1(k, 0)) for k in range(1, A)]
        came += [ppiece(u, slot2(t)) for t in range(1, B)]
        put(ppiece(u, 0), r.r[WEIGHTS] if u == SMALL else gpiece(u, q, c), *came)

    def copy_z(u, way):
        return remote(
            ppiece(u, 1 + way),
            zpiece(u, way),
            r.s_zs.at[u],
            r.s_zr.at[u, way],
            dev(c, q, z + 1 if way == 0 else z - 1),
        )

    def red_hop(u, h):
        own, up, down = ppiece(u, 0), ppiece(u, 1), ppiece(u, 2)

        @pl.when(z == h)
        def _():
            if h == 0:
                put(up, own)
            else:
                copy_z(u, 0).wait_recv()
                put(up, own, zpiece(u, 0))
            if h < Z - 1:
                copy_z(u, 0).start()

        @pl.when(z == Z - 1 - h)
        def _():
            if h == 0:
                put(down, own)
            else:
                copy_z(u, 1).wait_recv()
                if h < Z - 1:
                    put(down, own, zpiece(u, 1))
            if h < Z - 1:
                copy_z(u, 1).start()

    def final_rows(u):
        w = UNIT_WEIGHT[u]
        if u == SMALL:
            return r.o[w].at[pl.ds(pl.multiple_of(c * 16, 16), 16)]
        return urows(r.o[w], u, c * plan.hr(w), plan.hr(w))

    def final_local(u):
        return pltpu.make_async_copy(ppiece(u, 0), final_rows(u), r.s_fs.at[u])

    def final_remote(u):
        return remote(ppiece(u, 0), final_rows(u), r.s_fs.at[u], r.s_fr.at[u], sibling)

    def red_final(u):
        if Z > 1:
            own, up = ppiece(u, 0), ppiece(u, 1)

            @pl.when(z == Z - 1)
            def _():
                put(own, up)

            @pl.when(z < Z - 1)
            def _():
                put(own, up, zpiece(u, 1))

        final_local(u).start()
        final_remote(u).start()

    def red_end(u):
        final_remote(u).wait_recv()
        bytes_of(slots(u, 0, 2), r.s_fs.at[u]).wait()
        all_r(u, r.s_rs).wait()
        bytes_of(slots(u, 0, A + B - 2 if u == SMALL else n - 1), r.s_ps.at[u]).wait()
        if Z > 1:
            ends = jnp.logical_or(z == 0, z == Z - 1)

            @pl.when(ends)
            def _():
                bytes_of(slots(u, 0, 1), r.s_zs.at[u]).wait()

            @pl.when(jnp.logical_not(ends))
            def _():
                bytes_of(slots(u, 0, 2), r.s_zs.at[u]).wait()

    def red2_hop(u):
        red2(u)
        red_hop(u, 0)

    def last_hop(u):
        red_hop(u, Z - 1)
        red_final(u)

    ahead = {}
    turns = iter(SCHEDULE)

    def enlist(u):
        if Z > 1:
            ahead[u] = [red1, red1b, red2_hop]
            ahead[u] += [lambda k, h=h: red_hop(k, h) for h in range(1, Z - 1)]
            ahead[u].append(last_hop)
        else:
            ahead[u] = [red1, red1b, red2, red_final]

    def reduce_start(*units):
        for u in units:
            red0(u)
            enlist(u)

    def steps_of(units):
        return [(ahead[u].pop(0), u) for u in units if ahead[u]]

    def move(units):
        for step, u in steps_of(units):
            step(u)

    def turn():
        move(next(turns))

    def turns_of(count):
        acts = []
        for k in range(count):
            steps = steps_of(next(turns))
            if steps:
                acts.append((k, lambda steps=steps: [step(u) for step, u in steps][:0]))
        return acts

    def loop(count, body, after=()):
        def step(i, _):
            body(i)
            for k, act in after:
                pl.when(i == k)(lambda act=act: (act(), None)[1])
            return 0

        lax.fori_loop(0, count, step, 0)

    RB = 256
    NB = T // RB

    def rows_of(i, size=RB, base=0):
        return pl.ds(pl.multiple_of(i * size + base, base or size), size)

    seg_send()
    small_local = pltpu.make_async_copy(r.small, r.smallbuf.at[q], r.s_mr.at[0])
    small_local.start()
    for what in START:
        if what == SMALLS:
            for t in range(1, n):
                small_copy(t).start()
        elif what == TOKENS:
            tokens_in(r.x, r.xin, 0)
        else:
            g0(what)
    r.g8[...] = jnp.zeros((16, FF), F32)
    pass_turn()

    for s in range(n):
        blk = r.segbuf.at[s]
        pltpu.make_async_copy(blk, blk, r.s_gr.at[s]).wait()
    mine = lax.broadcasted_iota(jnp.int32, (S, plan.sw), 0) == lax.rem(q, S)
    for grp in range(n // plan.sr):
        got = r.segbuf[grp * plan.sr]
        for k in range(1, plan.sr):
            got = got + r.segbuf[grp * plan.sr + k]
        row = jnp.sum(jnp.where(mine, got.astype(F32), 0.0), axis=0, keepdims=True)
        r.segrow[0:1, grp * plan.sw : (grp + 1) * plan.sw] = row
    r.segcol[0:8] = jnp.full((8, 128), -1.0, F32)
    r.segcol[plan.LEN + 8 : plan.LEN + 16] = jnp.full((8, 128), -1.0, F32)
    for k in range(plan.LEN // 128):
        row = r.segrow[0:1, k * 128 : (k + 1) * 128]
        r.segcol[8 + k * 128 : 8 + (k + 1) * 128] = jnp.broadcast_to(row, (128, 128)).T
    r.segloc[...] = r.segcol[pl.ds(pl.multiple_of(c * T, 8), T + 16)]
    r.mext[0 : T + 8] = jnp.where(r.segloc[0 : T + 8] == r.segloc[1 : T + 9], 1.0, 0.0)

    def mask(o, start, rows):
        first = 8 + start + (0 if o > 0 else o)
        return r.mext[first : first + rows]

    small_local.wait()
    for t in range(1, n):
        small_arrived(t).wait_recv()
    for grp in range(n // plan.nr):
        got = r.smallbuf[grp * plan.nr].astype(F32)
        for k in range(1, plan.nr):
            got = got + r.smallbuf[grp * plan.nr + k].astype(F32)
        r.nrm[:, grp * plan.nw : (grp + 1) * plan.nw] = got[0:8, 0 : plan.nw]
    for s in range(n):
        rows = r.smallbuf[s].astype(F32)[8:19]
        r.midp[0:11, s * plan.FFn : (s + 1) * plan.FFn] = rows

    def ln_out(k, v):
        unit, _ = normed(v)
        return (unit * r.nrm[k : k + 1] + r.nrm[4 + k : 5 + k]).astype(BF16)

    def ln_back(k, e, v):
        unit, rs = normed(v)
        eg = e * r.nrm[k : k + 1]
        m1 = jnp.mean(eg, axis=-1, keepdims=True)
        m2 = jnp.mean(eg * unit, axis=-1, keepdims=True)
        cols = slice(k * D, (k + 1) * D)
        r.g8[11:12, cols] += jnp.sum(e * unit, axis=0, keepdims=True)
        r.g8[12:13, cols] += jnp.sum(e, axis=0, keepdims=True)
        return rs * (eg - m1 - unit * m2)

    pass_turn()

    def window(b):
        return min(max(b * MB - (MW - MB) // 2 + 16, 0), T + 32 - MW)

    ahead_of = lax.broadcasted_iota(jnp.int32, (MB, MW), 1) - lax.broadcasted_iota(
        jnp.int32, (MB, MW), 0
    )
    def shift_matrices(b):
        near = r.segloc[pl.ds(pl.multiple_of(b * MB, MB), MB + 16)]
        home = near[8 : MB + 8]
        first = jnp.where(b == 0, 16, jnp.where(b == T // MB - 1, MW - MB - 16, (MW - MB) // 2))
        for i, o in enumerate(TAPS):
            same = jnp.where(home == near[8 + o : MB + 8 + o], 1.0, 0.0)
            tap = jnp.where(
                ahead_of == first + o, jnp.concatenate([same] * (MW // 128), axis=1), 0.0
            )
            r.ms[b, i * MB : (i + 1) * MB] = tap.astype(BF16)

    loop(T // MB, shift_matrices)

    lane = lax.broadcasted_iota(jnp.int32, (1, 128), 1)
    lane_f = lane.astype(F32)
    own_doc = r.segloc[8 : T + 8] == lane_f
    r.qenc[...] = jnp.where(jnp.logical_and(lane < 4, jnp.logical_not(own_doc)), FAR, 0.0).astype(BF16)
    ones = jnp.logical_and(lane >= 4, lane < 7)
    r.kenc[...] = jnp.where(
        jnp.logical_or(r.segcol[8 : plan.LEN + 8] == lane_f, ones), 1.0, 0.0
    ).astype(BF16)

    pass_turn()
    pass_turn()
    g3(GLU)
    pass_turn()
    tokens_in_done(r.xin, 0)

    def glu(i):
        rows = rows_of(i)
        x = r.xin[rows].astype(F32)
        a1 = ln_out(0, x)
        r.a1[rows] = a1
        value = mm(a1, r.w[GLU][:, 0:D])
        gate = sigmoid(mm(a1, r.w[GLU][:, D : 2 * D]))
        r.sg[rows, 0:D] = gate.astype(BF16)
        r.sg[rows, D : 2 * D] = (value * gate * (1.0 - gate)).astype(BF16)
        y1 = x + value * gate
        r.y1[rows] = y1
        r.a2[rows] = ln_out(1, y1)

    loop(NB, glu, pass_turns(NB))
    pass_turn()
    g3(CONV)

    def conv(i):
        a2 = r.a2[rows_of(i)]
        for o in range(3):
            r.pext[o, rows_of(i, RB, 8)] = mm(a2, r.w[CONV][o])

    loop(NB, conv)
    edge_send(0, r.pext[0, T : T + 8], r.pext[2, 8:16])
    pass_turn()
    top, bottom = edge_take(0)
    r.pext[0, 0:8] = top
    r.pext[2, T + 8 : T + 16] = bottom
    pass_turn()
    for k in range(T // 128):
        lo = k * 128
        before = mask(-1, lo, 128)
        after = mask(1, lo, 128)
        pre = (
            r.pext[0, lo + 7 : lo + 135] * jnp.concatenate([before] * (H // 128), axis=1)
            + r.pext[1, lo + 8 : lo + 136]
            + r.pext[2, lo + 9 : lo + 137] * jnp.concatenate([after] * (H // 128), axis=1)
        )
        value, slope = gelu_both(pre)
        r.pext[1, lo + 8 : lo + 136] = value
        r.dgr[lo : lo + 128] = slope.astype(BF16)
    pass_turn()
    pass_turn()
    g3(LEFT)

    CH = 512
    RM = 128

    def left(i):
        rows, erows = rows_of(i, RM), rows_of(i, RM, 8)
        a2 = r.a2[rows]
        for k in range(FF // CH):
            value, slope = gelu_both(mm(a2, r.w[LEFT][:, k * CH : (k + 1) * CH]))
            r.dgl[rows, k * CH : (k + 1) * CH] = slope.astype(BF16)
            r.big[erows, k * CH : (k + 1) * CH] = value
        r.big[erows, 0:H] += r.pext[1, erows]
        unit, rs = normed(r.big[erows])
        r.nm[rows] = unit.astype(BF16)
        r.rm[rows] = rs
        r.hid[rows_of(i, RM, 16)] = (unit * r.midp[0:1] + r.midp[1:2]).astype(BF16)

    loop(T // RM, left, pass_turns(T // RM))
    edge_send(1, r.hid[T : T + 16], r.hid[16:32])
    r.hid[0:16], r.hid[T + 16 : T + 32] = edge_take(1)
    pass_turn()

    def depthwise(j):
        cols = pl.ds(pl.multiple_of(j * 512, 512), 512)
        for b in range(T // MB):
            near = r.hid[window(b) : window(b) + MW, cols]
            taps = mm(r.ms[b], near)
            total = r.hid[16 + b * MB : 16 + (b + 1) * MB, cols].astype(F32) * r.midp[6:7, cols]
            for i, o in enumerate(TAPS):
                total = total + taps[i * MB : (i + 1) * MB] * r.midp[6 + o : 7 + o, cols]
            r.sep[b * MB : (b + 1) * MB, cols] = total.astype(BF16)

    loop(FF // 512, depthwise, pass_turns(FF // 512))
    pass_turn()
    g3(POINT)

    def point(i):
        rows = rows_of(i, T)
        y2 = r.y1[rows] + mm(r.sep[rows], r.w[POINT][...])
        r.y2[rows] = y2
        r.a4[rows] = ln_out(2, y2)

    loop(1, point)
    pass_turn()
    pass_turn()
    g3(QKV)
    scale = 1.0 / math.sqrt(D // HEADS)

    def keys_values(i):
        rows = rows_of(i)
        a4 = r.a4[rows]
        here = pl.ds(pl.multiple_of(c * T + i * RB, RB), RB)
        r.kvb[here, 0:D] = mm(a4, r.w[QKV][:, D : 2 * D]).astype(BF16)
        r.kvb[here, D : 2 * D] = mm(a4, r.w[QKV][:, 2 * D : 3 * D]).astype(BF16)

    def queries(i):
        rows = rows_of(i)
        r.qb[rows] = (mm(r.a4[rows], r.w[QKV][:, 0:D]) * scale).astype(BF16)

    def kv_copy(j, base):
        blk = r.kvb.at[pl.ds(aligned(c * T), T), pair_cols(j, base)]
        return remote(blk, blk, r.s_ks.at[j], r.s_kr.at[j], sibling)

    def pair_cols(j, base=0):
        return pl.ds(pl.multiple_of(j * 128 + base, 128), 128)

    def pair_bytes(j, semaphore):
        return bytes_of(r.kvb.at[pl.ds(0, T), pl.ds(0, 256)], semaphore.at[j])

    loop(NB, keys_values)
    for j in range(HEADS // 2):
        kv_copy(j, 0).start()
        kv_copy(j, D).start()
    loop(NB, queries)
    pass_turn()
    pass_turn()
    heads_lanes = [lane < 64, lane >= 64]
    def head_lanes(e, v):
        return jnp.where(heads_lanes[e], v, jnp.zeros_like(v))

    def attend(j):
        pair_bytes(j, r.s_kr).wait()
        cols, vcols = pair_cols(j), pair_cols(j, D)
        keys = jnp.concatenate([r.kvb[:, cols], r.kenc[...]], axis=1)
        for k in range(T // RB):
            rows = slice(k * RB, (k + 1) * RB)
            q2 = r.qb[rows, cols]
            got = []
            for e in range(2):
                score = mm_t(jnp.concatenate([head_lanes(e, q2), r.qenc[rows]], axis=1), keys)
                most = jnp.max(score, axis=-1, keepdims=True)
                power = jnp.exp(score - most)
                total = jnp.sum(power, axis=-1, keepdims=True)
                got.append(mm(power.astype(BF16), r.kvb[:, vcols]) / total)
                lse = most + jnp.log(total)
                r.lse[rows] = jnp.where(lane == 2 * j + e, lse, r.lse[rows])
            r.ctx[rows, cols] = jnp.where(heads_lanes[0], got[0], got[1]).astype(BF16)

    r.lse[...] = jnp.zeros((T, 128), F32)

    loop(HEADS // 2, attend, pass_turns(HEADS // 2))
    pass_turn()
    g3(OUT)

    def out(i):
        rows = rows_of(i, T)
        y3 = r.y2[rows] + mm(r.ctx[rows], r.w[OUT][...])
        r.y3[rows] = y3
        r.a5[rows] = ln_out(3, y3)

    loop(1, out)
    pass_turn()
    pass_turn()
    g3(FIN)

    def ffn_in(i):
        rows = rows_of(i)
        a5 = r.a5[rows]
        for k in range(FF // CH):
            value, slope = gelu_both(mm(a5, r.w[FIN][:, k * CH : (k + 1) * CH]))
            r.hid[rows, k * CH : (k + 1) * CH] = value.astype(BF16)
            r.dg[rows, k * CH : (k + 1) * CH] = slope.astype(BF16)

    loop(NB, ffn_in, pass_turns(NB))
    pass_turn()
    g3(FOUT)

    def ffn_out(i):
        rows = rows_of(i, T)
        r.osend[rows] = (r.y3[rows] + mm(r.hid[rows], r.w[FOUT][...])).astype(BF16)

    loop(1, ffn_out)
    pass_turn()
    tokens_out(r.osend, r.o_out, 2)
    for w in range(WEIGHTS):
        gather_sent(w)
    for j in range(HEADS // 2):
        pair_bytes(j, r.s_ks).wait()

    tokens_in_done(r.cot, 1)

    def ffn_back(i):
        rows = rows_of(i, T)
        f4 = r.cot[rows]
        for k in range(FF // CH):
            cols = slice(k * CH, (k + 1) * CH)
            up = mm_t(f4, r.w[FOUT][cols])
            r.dg[rows, cols] = (up * r.dg[rows, cols].astype(F32)).astype(BF16)
        e = mm_t(r.dg[rows], r.w[FIN][...])
        r.gs[rows] = f4.astype(F32) + ln_back(3, e, r.y3[rows])

    loop(1, ffn_back)
    GC = 1024

    def grad_outer(k):
        cols = rows_of(k, GC)
        r.w[FOUT][cols] = mm_tn(r.hid[0:T, cols], r.cot[...]).astype(BF16)

    loop(FF // GC, grad_outer)
    reduce_start(U_FOUT)
    turn()
    r.tr[...] = r.a5[...].T

    def grad_inner(k):
        cols = rows_of(k, GC)
        r.w[FIN][:, cols] = mm(r.tr[...], r.dg[:, cols]).astype(BF16)

    loop(FF // GC, grad_inner)
    reduce_start(U_FIN)
    turn()

    def out_back(i):
        rows = rows_of(i, T)
        f3 = r.gs[rows].astype(BF16)
        r.a5[rows] = f3
        r.hid[rows, 3 * D : 4 * D] = mm_t(f3, r.w[OUT][...]).astype(BF16)

    loop(1, out_back)
    r.w[OUT][...] = mm_tn(r.ctx[...], r.a5[...]).astype(BF16)
    reduce_start(U_OUT)
    turn()
    r.tr[...] = r.a4[...].T

    QB = 256

    def with_terms(extra, v):
        high = v.astype(BF16).astype(F32)
        mid = (v - high).astype(BF16).astype(F32)
        low = v - high - mid
        terms = jnp.where(lane == 4, high, jnp.where(lane == 5, mid, jnp.where(lane == 6, low, 0.0)))
        return extra - terms.astype(BF16)

    halfway = []

    def attend_back(j):
        cols, vcols = pair_cols(j), pair_cols(j, D)
        k2 = r.kvb[:, cols]
        keys = jnp.concatenate([k2, r.kenc[...]], axis=1)
        turned = [head_lanes(e, k2).T for e in range(2)]
        values = jnp.concatenate([r.kvb[:, vcols], r.kenc[...]], axis=1)
        for k in range(T // QB):
            rows = slice(k * QB, (k + 1) * QB)
            q2 = r.qb[rows, cols]
            d2 = r.hid[rows, pair_cols(j, 3 * D)]
            inner = d2.astype(F32) * r.ctx[rows, cols].astype(F32)
            dq = jnp.zeros((128, QB), F32)
            for e in range(2):
                qe, de = head_lanes(e, q2), head_lanes(e, d2)
                lse = jnp.sum(
                    jnp.where(lane == 2 * j + e, r.lse[rows], 0.0), axis=-1, keepdims=True
                )
                delta = jnp.sum(head_lanes(e, inner), axis=-1, keepdims=True)
                shifted = mm_t(keys, jnp.concatenate([qe, with_terms(r.qenc[rows], lse)], axis=1))
                probs = jnp.exp(shifted)
                none = jnp.zeros((QB, 128), BF16)
                moved = mm_t(values, jnp.concatenate([de, with_terms(none, delta)], axis=1))
                ds = (probs * moved).astype(BF16)
                dk = mm(ds, qe)
                dv = mm(probs.astype(BF16), de)
                for kk in range(2):
                    half = slice(kk * T, (kk + 1) * T)
                    at = 2 * D + kk * 128
                    if k == 0 and e == 0:
                        r.big[0:T, at : at + 128] = dk[half]
                        r.big[0:T, at + 256 : at + 384] = dv[half]
                    else:
                        r.big[0:T, at : at + 128] += dk[half]
                        r.big[0:T, at + 256 : at + 384] += dv[half]
                dq = dq + mm(turned[e], ds)
            r.hid[rows, cols] = (dq.T * scale).astype(BF16)
            if k == 0:
                for step, act in halfway:
                    pl.when(j == step)(lambda act=act: (act(), None)[1])

        def part(core, what):
            at = pl.multiple_of(2 * D + core * 128 + what * 256, 128)
            return r.big[0:T, pl.ds(at, 128)]

        @pl.when(j >= 2)
        def _():
            dkv_copy(j - 2).wait_send()

        for what in range(2):
            mine = pl.ds(pl.multiple_of(j * 256 + what * 128, 128), 128)
            r.big[0:T, mine] = part(c, what)
            r.cot[:, pl.ds(pl.multiple_of(lax.rem(j, 2) * 256 + what * 128, 128), 128)] = part(
                oc, what
            ).astype(BF16)
        dkv_copy(j).start()

        @pl.when(j == 2)
        def _():
            pairs_back(0)

    def dkv_copy(j):
        slot = lax.rem(j, 2)
        return remote(
            r.cot.at[:, pl.ds(pl.multiple_of(slot * 256, 128), 256)],
            r.dkvr.at[:, pl.ds(pl.multiple_of(j * 256, 128), 256)],
            r.s_js.at[j],
            r.s_jr.at[j],
            sibling,
        )

    def pairs_back(m):
        parts, weights = [], []
        for j in (2 * m, 2 * m + 1):
            dkv_copy(j).wait_recv()
            if m == 1:
                dkv_copy(j).wait_send()
            both = slice(j * 256, (j + 1) * 256)
            dkv = r.big[0:T, both] + r.dkvr[:, both].astype(F32)
            own = slice(j * 128, (j + 1) * 128)
            parts += [r.hid[0:T, own], dkv.astype(BF16)]
            for base in (0, D, 2 * D):
                weights.append(r.w[QKV][:, base + j * 128 : base + (j + 1) * 128])
        pairs = jnp.concatenate(parts, axis=1)
        share = mm_t(pairs, jnp.concatenate(weights, axis=1))
        if m == 0:
            r.big[0:T, 3 * D : 4 * D] = share
        else:
            r.big[0:T, 3 * D : 4 * D] += share
        r.dg[:, m * 768 : (m + 1) * 768] = mm(r.tr[...], pairs).astype(BF16)

    acts = []
    for k in range(HEADS // 2):
        halfway += [(k, act) for _, act in turns_of(1)]
        if k == 2:
            enlist(U_QKV0)
            acts.append((2, lambda: red0(U_QKV0)))
        acts += [(k, act) for _, act in turns_of(1)]
    loop(HEADS // 2, attend_back, acts)
    pairs_back(1)
    reduce_start(U_QKV1)
    turn()

    def qkv_back(i):
        rows = rows_of(i)
        r.gs[rows] += ln_back(2, r.big[rows, 3 * D : 4 * D], r.y2[rows])

    loop(NB, qkv_back)

    def point_back(i):
        rows = rows_of(i, T)
        f2 = r.gs[rows].astype(BF16)
        r.a4[rows] = f2
        for k in range(FF // CH):
            cols = slice(k * CH, (k + 1) * CH)
            d = mm_t(f2, r.w[POINT][cols])
            r.hid[rows_of(i, T, 16), cols] = d.astype(BF16)

    loop(1, point_back)
    edge_send(2, r.hid[T : T + 16], r.hid[16:32])
    turn()

    def grad_point(k):
        cols = rows_of(k, GC)
        r.w[POINT][cols] = mm_tn(r.sep[:, cols], r.a4[...]).astype(BF16)

    loop(FF // GC, grad_point)
    reduce_start(U_POINT0, U_POINT1)
    turn()
    r.hid[0:16], r.hid[T + 16 : T + 32] = edge_take(2)

    def depth_back(j):
        cols = pl.ds(pl.multiple_of(j * 256, 256), 256)
        gain, shift = r.midp[0:1, cols], r.midp[1:2, cols]
        sums = [jnp.zeros((8, 256), F32) for _ in range(9)]
        for b in range(T // MB):
            lo = b * MB
            taps = mm(r.ms[b], r.hid[window(b) : window(b) + MW, cols])
            a3 = r.nm[lo : lo + MB, cols].astype(F32) * gain + shift
            total = jnp.zeros((MB, 256), F32)
            here = r.hid[16 + lo : 16 + lo + MB, cols].astype(F32)
            for o in range(-4, 5):
                i = TAPS.index(-o) if o else 0
                moved = taps[i * MB : (i + 1) * MB] if o else here
                total = total + moved * r.midp[6 + o : 7 + o, cols]
                part = moved * a3
                for g in range(MB // 8):
                    sums[o + 4] = sums[o + 4] + part[g * 8 : (g + 1) * 8]
            r.big[lo + 8 : lo + 8 + MB, cols] = total
        for o in range(9):
            r.g8[2 + o : 3 + o, cols] = jnp.sum(sums[o], axis=0, keepdims=True)

    loop(FF // 256, depth_back, turns_of(FF // 256))

    def mid_back(i):
        rows, erows = rows_of(i, RM), rows_of(i, RM, 8)
        e = r.big[erows]
        unit = r.nm[rows].astype(F32)
        eg = e * r.midp[0:1]
        m1 = jnp.mean(eg, axis=-1, keepdims=True)
        m2 = jnp.mean(eg * unit, axis=-1, keepdims=True)
        r.g8[0:1] += jnp.sum(e * unit, axis=0, keepdims=True)
        r.g8[1:2] += jnp.sum(e, axis=0, keepdims=True)
        dmid = r.rm[rows] * (eg - m1 - unit * m2)
        r.dgl[rows] = (dmid * r.dgl[rows].astype(F32)).astype(BF16)
        right = dmid[:, 0:H] * r.dgr[rows].astype(F32)
        r.pext[0, erows] = right.astype(BF16).astype(F32)

    loop(T // RM, mid_back, turns_of(T // RM))
    edge_send(3, r.pext[0, T : T + 8], r.pext[0, 8:16])
    r.tr[...] = r.a2[...].T

    def grad_left(k):
        cols = rows_of(k, GC)
        r.sep[:, cols] = mm(r.tr[...], r.dgl[:, cols]).astype(BF16)

    half = FF // GC // 2
    lax.fori_loop(0, half, lambda k, _: (grad_left(k), 0)[1], 0)
    reduce_start(U_LEFT0)
    turn()
    lax.fori_loop(half, 2 * half, lambda k, _: (grad_left(k), 0)[1], 0)
    reduce_start(U_LEFT1)
    turn()
    top, bottom = edge_take(3)
    r.pext[0, 0:8] = top
    r.pext[0, T + 8 : T + 16] = bottom
    for k in range(T // 128):
        lo = k * 128
        for o in (-1, 0, 1):
            moved = r.pext[0, lo + 8 - o : lo + 136 - o]
            if o:
                moved = moved * jnp.concatenate([mask(-o, lo, 128)] * (H // 128), axis=1)
            r.hid[lo : lo + 128, (o + 1) * H : (o + 2) * H] = moved.astype(BF16)
    for o in range(3):
        cols = slice(o * H, (o + 1) * H)
        r.dkvr[:, cols] = mm(r.tr[...], r.hid[0:T, cols]).astype(BF16)
    reduce_start(U_CONV)
    turn()

    def branch_back(i):
        rows = rows_of(i)
        e = mm_t(r.dgl[rows], r.w[LEFT][...])
        for o in range(3):
            e = e + mm_t(r.hid[rows, o * H : (o + 1) * H], r.w[CONV][o])
        r.gs[rows] += ln_back(1, e, r.y1[rows])

    loop(NB, branch_back, turns_of(NB))

    def gate_back(i):
        rows = rows_of(i)
        g = r.gs[rows]
        r.sg[rows, 0:D] = (g * r.sg[rows, 0:D].astype(F32)).astype(BF16)
        r.sg[rows, D : 2 * D] = (g * r.sg[rows, D : 2 * D].astype(F32)).astype(BF16)

    loop(NB, gate_back)
    r.tr[...] = r.a1[...].T

    def grad_glu(k):
        cols = rows_of(k, D)
        to = pl.ds(pl.multiple_of(k * D + 2 * D, D), D)
        r.hid[0:T, to] = mm(r.tr[...], r.sg[:, cols]).astype(BF16)

    grad_glu(0)
    reduce_start(U_GLU0)
    turn()
    grad_glu(1)
    reduce_start(U_GLU1)
    turn()

    def glu_back(i):
        rows = rows_of(i)
        e = mm_t(r.sg[rows], r.w[GLU][...])
        total = r.gs[rows] + ln_back(0, e, r.xin[rows].astype(F32))
        r.a5[rows] = total.astype(BF16)

    loop(NB, glu_back, turns_of(NB))
    r.gsm[0:16] = r.g8[:, 0 : FF // 2].astype(BF16)
    r.gsm[16:32] = r.g8[:, FF // 2 : FF].astype(BF16)
    reduce_start(SMALL)
    move(TAIL[0])
    tokens_out(r.a5, r.o_ig, 3)
    move(TAIL[1])
    while any(ahead.values()):
        move(range(UNITS))

    for u in range(UNITS):
        red_end(u)
    tokens_out_done(r.osend, r.o_out, 2)
    tokens_out_done(r.a5, r.o_ig, 3)
    tokens_in_sent(r.x, r.xin, 0)
    tokens_in_sent(r.ct, r.cot, 1)
    seg_sent()
    for t in range(1, n):
        small_copy(t).wait_send()


def local(
    inputs,
    segment_ids,
    cotangent,
    norm_gain,
    norm_bias,
    glu_weight,
    left_weight,
    conv_weight,
    mid_gain,
    mid_bias,
    depth_weight,
    point_weight,
    qkv_weight,
    out_weight,
    ffn_in,
    ffn_out,
):
    seqs, span, width = inputs.shape
    n = lax.axis_size("seq")
    plan = Plan(
        lax.axis_size("dp"), n, seqs, span, width, ffn_in.shape[1], conv_weight.shape[2]
    )
    q = lax.axis_index("seq")

    def placed(piece, repeats):
        if repeats == 1:
            return piece
        size = piece.shape[-1]
        tiled = jnp.tile(piece, (1,) * (piece.ndim - 1) + (repeats,))
        at = lax.broadcasted_iota(jnp.int32, tiled.shape, tiled.ndim - 1) // size
        return jnp.where(at == q % repeats, tiled, jnp.zeros_like(tiled))

    segs = placed(segment_ids, plan.sr)
    norms = placed(jnp.concatenate([norm_gain, norm_bias], 0), plan.nr)
    rows = plan.spack
    at = lax.broadcasted_iota(jnp.int32, (rows, plan.FFn), 0)
    small = jnp.pad(norms, ((0, rows - 8), (0, plan.FFn - plan.nw)))
    small = jnp.where(at == 8, mid_gain[None], jnp.where(at == 9, mid_bias[None], small))
    taps = jnp.pad(depth_weight, ((10, rows - 10 - depth_weight.shape[0]), (0, 0)))
    small = jnp.where(at >= 10, taps, small)
    weights = [None] * WEIGHTS
    weights[GLU], weights[CONV], weights[LEFT] = glu_weight, conv_weight, left_weight
    weights[POINT], weights[QKV], weights[OUT] = point_weight, qkv_weight, out_weight
    weights[FIN], weights[FOUT] = ffn_in, ffn_out

    shapes = []
    plan.buffers(shapes.append)
    out_shape = [jax.ShapeDtypeStruct(inputs.shape, BF16)] * 2
    out_shape += [jax.ShapeDtypeStruct(plan.piece(w, plan.kr(w)), BF16) for w in range(WEIGHTS)]
    out_shape += [jax.ShapeDtypeStruct((32, plan.FF // 2), BF16)]
    hbm = pl.BlockSpec(memory_space=pl.ANY)
    got = pl.pallas_call(
        lambda *refs: kernel(plan, *refs),
        out_shape=out_shape,
        in_specs=[hbm] * INPUTS,
        out_specs=[hbm] * OUTPUTS,
        scratch_shapes=shapes,
        compiler_params=pltpu.CompilerParams(
            collective_id=0, has_side_effects=True, vmem_limit_bytes=64 << 20
        ),
        name="cell",
    )(inputs, segs, cotangent, small, *weights)
    out = unpacked(plan, got)
    return (
        out[0],
        out[1],
        out[2 + WEIGHTS],
        out[3 + WEIGHTS],
        out[2 + GLU],
        out[2 + LEFT],
        out[2 + CONV],
        out[4 + WEIGHTS].reshape(-1),
        out[5 + WEIGHTS].reshape(-1),
        out[6 + WEIGHTS],
        out[2 + POINT],
        out[2 + QKV],
        out[2 + OUT],
        out[2 + FIN],
        out[2 + FOUT],
    )


def unpacked(plan, parts):
    count = 2 + WEIGHTS
    dn = plan.D // plan.n
    wide = [jax.ShapeDtypeStruct(p.shape, F32) for p in parts[:count]]
    conv, qkv, H = 2 + CONV, 2 + QKV, plan.HALF
    wide[conv] = jax.ShapeDtypeStruct((3, plan.kr(CONV), H), F32)
    tiny = [(4, dn), (4, dn), (1, plan.FFn), (1, plan.FFn), (9, plan.FFn)]
    out_shape = wide + [jax.ShapeDtypeStruct(shape, F32) for shape in tiny]

    def body(*refs):
        ins, outs = refs[:count], refs[count + 1 : 2 * count + 1]
        sums, tinies = refs[count], refs[2 * count + 1 : 2 * count + 6]
        near, far = refs[2 * count + 6 : 3 * count + 6], refs[3 * count + 6 : 4 * count + 6]
        came, went = refs[4 * count + 6], refs[4 * count + 7]

        def arrive(i):
            return pltpu.make_async_copy(ins[i], near[i], came.at[i])

        def leave(i):
            return pltpu.make_async_copy(far[i], outs[i], went.at[i])

        for i in range(count):
            arrive(i).start()
        q = lax.axis_index("seq")
        whole = jnp.concatenate([sums[0:16].astype(F32), sums[16:32].astype(F32)], axis=1)
        rolled = pltpu.roll(whole, (plan.FF - q * plan.FFn) % plan.FF, 1)[:, 0 : plan.FFn]
        tinies[2][...] = rolled[0:1]
        tinies[3][...] = rolled[1:2]
        tinies[4][...] = rolled[2:11]
        for k in range(2):
            row = whole[11 + k : 12 + k]
            rows = [row[:, i * plan.D : (i + 1) * plan.D] for i in range(4)]
            both = jnp.concatenate(rows + rows, axis=0)
            tinies[k][...] = pltpu.roll(both, (plan.D - q * dn) % plan.D, 1)[0:4, 0:dn]
        for i in range(count):
            arrive(i).wait()
            if i == conv:
                for k in range(3):
                    far[i][k] = near[i][:, k * H : (k + 1) * H].astype(F32)
            elif i == qkv:
                for k in range(12):
                    to = (k % 3) * plan.D + k // 3 * 128
                    far[i][:, to : to + 128] = near[i][:, k * 128 : (k + 1) * 128].astype(F32)
            else:
                far[i][...] = near[i][...].astype(F32)
            leave(i).start()
        for i in range(count):
            leave(i).wait()

    hbm = pl.BlockSpec(memory_space=pl.ANY)
    vmem = pl.BlockSpec(memory_space=pltpu.VMEM)
    return pl.pallas_call(
        body,
        out_shape=out_shape,
        in_specs=[hbm] * count + [vmem],
        out_specs=[hbm] * count + [vmem] * len(tiny),
        scratch_shapes=[pltpu.VMEM(p.shape, BF16) for p in parts[:count]]
        + [pltpu.VMEM(shape.shape, F32) for shape in wide]
        + [pltpu.SemaphoreType.DMA((count,))] * 2,
        compiler_params=pltpu.CompilerParams(vmem_limit_bytes=64 << 20),
    )(*parts)


def solution(mesh):
    in_specs = (
        P("dp", "seq", None),
        P("dp", "seq"),
        P("dp", "seq", None),
        P(None, "seq"),
        P(None, "seq"),
        P("seq", None),
        P("seq", None),
        P(None, "seq", None),
        P("seq"),
        P("seq"),
        P(None, "seq"),
        P("seq", None),
        P("seq", None),
        P("seq", None),
        P("seq", None),
        P("seq", None),
    )
    out_specs = (
        P("dp", "seq", None),
        P("dp", "seq", None),
        P(None, "seq"),
        P(None, "seq"),
        P("seq", None),
        P("seq", None),
        P(None, "seq", None),
        P("seq"),
        P("seq"),
        P(None, "seq"),
        P("seq", None),
        P("seq", None),
        P("seq", None),
        P("seq", None),
        P("seq", None),
    )
    return jax.shard_map(local, mesh=mesh, in_specs=in_specs, out_specs=out_specs, check_vma=False)
```

```python
import math

import jax
import jax.numpy as jnp
from jax import lax
from jax.experimental import pallas as pl
from jax.experimental.pallas import tpu as pltpu
from jax.sharding import PartitionSpec as P

HEADS = 8
EPS = 1e-06
MESH = pl.DeviceIdType.MESH
F32 = jnp.float32
BF16 = jnp.bfloat16

GLU, CONV, LEFT, POINT, QKV, OUT, FIN, FOUT = range(8)
WEIGHTS = 8
(U_GLU0, U_GLU1, U_CONV, U_LEFT0, U_LEFT1, U_POINT0, U_POINT1, U_QKV0, U_QKV1, U_OUT, U_FIN, U_FOUT, SMALL) = range(13)
UNITS = 13
UNIT_WEIGHT = (GLU, GLU, CONV, LEFT, LEFT, POINT, POINT, QKV, QKV, OUT, FIN, FOUT, WEIGHTS)
UNIT_PART = (0, 1, None, 0, 1, 0, 1, 0, 1, None, None, None, None)

SHARED = (GLU, LEFT, POINT, FIN,)
SMALLS, TOKENS = 8, 9
START = (GLU, SMALLS, CONV, LEFT, TOKENS)
FORWARD = (
    ((1, GLU),),
    (),
    ((1, CONV),),
    ((1, LEFT), (2, GLU), (0, POINT), (2, CONV), (2, LEFT), (0, QKV), (3, GLU), (1, POINT)),
    (),
    ((0, OUT),),
    ((0, FIN),),
    (),
    (),
    ((1, QKV),),
    (),
    ((3, LEFT), (2, POINT), (1, OUT)),
    (),
    ((1, FIN),),
    ((0, FOUT),),
    ((2, QKV),),
    (),
    ((2, OUT),),
    ((3, POINT), (2, FIN)),
    ((0, TOKENS),),
    (),
    (),
    (),
    (),
    ((1, FOUT),),
    (),
    (),
    ((3, FIN),),
    (),
    ((2, FOUT),),
    (),
    (),
    (),
    (),
    (),
    (),
    (),
)
SCHEDULE = (
    (),
    (),
    (),
    (U_FOUT,),
    (U_FIN,),
    (),
    (),
    (U_OUT,),
    (U_FOUT,),
    (),
    (U_FIN, U_QKV0),
    (U_OUT,),
    (U_FOUT, U_QKV1),
    (U_QKV0,),
    (),
    (U_FIN,),
    (U_POINT0, U_POINT1),
    (U_QKV0, U_QKV1),
    (U_FOUT,),
    (),
    (),
    (),
    (U_QKV1, U_POINT0),
    (),
    (),
    (U_OUT, U_FIN),
    (U_POINT1,),
    (U_POINT0, U_FOUT),
    (U_LEFT0, U_QKV1),
    (U_QKV0, U_OUT, U_POINT1, U_LEFT1),
    (),
    (U_POINT0, U_FIN),
    (),
    (U_LEFT0,),
    (U_QKV1, U_CONV, U_GLU0, U_GLU1, U_LEFT1),
)
TAIL = (
    (SMALL, U_POINT1, U_QKV0, U_LEFT0, U_OUT, U_CONV, U_POINT0, U_LEFT1, U_GLU0, U_LEFT0, U_POINT1, U_GLU1, SMALL),
    (U_CONV, U_GLU0, U_LEFT1, U_GLU1, U_LEFT0, SMALL, U_CONV, U_GLU0, U_LEFT1, U_GLU1, SMALL, U_CONV, U_GLU0, U_GLU1, SMALL, U_FOUT, U_FIN, U_OUT, U_QKV0, U_QKV1, U_POINT0, U_POINT1, U_LEFT0, U_LEFT1, U_CONV, U_GLU0, U_GLU1, SMALL),
)

MB, MW = 128, 256
TAPS = (-4, -3, -2, -1, 1, 2, 3, 4)
FAR = -(2.0**30)


def mm(a, b):
    return lax.dot_general(a, b, (((1,), (0,)), ((), ())), preferred_element_type=F32)


def mm_t(a, b):
    return lax.dot_general(a, b, (((1,), (1,)), ((), ())), preferred_element_type=F32)


def mm_tn(a, b):
    return lax.dot_general(a, b, (((0,), (0,)), ((), ())), preferred_element_type=F32)


def normed(v):
    centred = v - jnp.mean(v, axis=-1, keepdims=True)
    r = lax.rsqrt(jnp.mean(centred * centred, axis=-1, keepdims=True) + EPS)
    return centred * r, r


def gelu_both(v):
    c = math.sqrt(2.0 / math.pi)
    sq = v * v
    t = jnp.tanh(v * (c + (c * 0.044715) * sq))
    half = 0.5 * t + 0.5
    value = v * half
    slope = half + (0.5 * v) * (1.0 - t * t) * (c + (3.0 * c * 0.044715) * sq)
    return value, slope


def sigmoid(v):
    return 0.5 * jnp.tanh(0.5 * v) + 0.5


class Buffers:
    pass


class Plan:
    def __init__(self, dp, n, seqs, span, width, hidden, half):
        self.n, self.Z = n, dp // 2
        self.S, self.span = seqs, span
        self.D, self.FF, self.HALF = width, hidden, half
        self.LEN = span * n
        self.T = self.LEN // 2
        self.PH = n // 2
        self.B = math.isqrt(n)
        self.A = n // self.B
        assert self.A == self.B and n == 2 * seqs and dp % 2 == 0
        self.shared = SHARED if self.Z % 2 == 0 else ()
        self.sw = max(span, 128)
        self.sr = self.sw // span
        dn = width // n
        self.nw = max(dn, 128)
        self.nr = self.nw // dn
        self.FFn = hidden // n
        self.spack = 32
        self.dims = [
            (width, 2 * width),
            (width, half),
            (width, hidden),
            (hidden, width),
            (width, 3 * width),
            (width, width),
            (width, hidden),
            (hidden, width),
        ]

    def whole(self, w):
        k, cols = self.dims[w]
        return (3, k, cols) if w == CONV else (k, cols)

    def kr(self, w):
        return self.dims[w][0] // self.n

    def hr(self, w):
        return self.kr(w) // 2

    def gcols(self, w):
        return self.dims[w][1] * (3 if w == CONV else 1)

    def piece(self, w, rows):
        return (rows, self.gcols(w))

    def buffers(self, take):
        T, D, FF, H, n = self.T, self.D, self.FF, self.HALF, self.n
        r = Buffers()

        def vm(shape, dtype):
            return take(pltpu.VMEM(shape, dtype))

        def sem(*shape):
            return take(pltpu.SemaphoreType.DMA(shape))

        every = range(WEIGHTS)
        parts = [(self.piece(w, self.hr(w)), BF16) for w in every] + [((16, FF // 2), BF16)]
        r.w = [vm(self.whole(w), BF16) for w in every]
        r.g8 = vm((16, FF), F32)
        r.gsm = vm((32, FF // 2), BF16)
        r.r = [None] * WEIGHTS + [vm((16, FF // 2), BF16)]
        for w in (CONV, QKV, OUT, FIN, FOUT):
            r.r[w] = vm(self.piece(w, n * self.hr(w)), BF16)
        r.r[LEFT], r.r[POINT], r.r[GLU] = r.r[FIN], r.r[FOUT], r.r[QKV]
        r.p = [vm((n - 1,) + shape, dtype) for shape, dtype in parts]
        if self.Z > 1:
            r.u = [vm(shape, dtype) for shape, dtype in parts]
            r.d = [vm(shape, dtype) for shape, dtype in parts]
        r.segbuf = vm((n, self.S, self.sw), jnp.int32)
        r.segrow = vm((8, self.LEN), F32)
        r.segcol = vm((self.LEN + 16, 128), F32)
        r.segloc = vm((T + 16, 128), F32)
        r.mext = vm((T + 16, 128), F32)
        r.ms = vm((T // MB, 8 * MB, MW), BF16)
        r.qenc = vm((T, 128), BF16)
        r.kenc = vm((self.LEN, 128), BF16)
        r.smallbuf = vm((n, self.spack, self.FFn), BF16)
        r.nrm = vm((8, D), F32)
        r.midp = vm((16, FF), F32)
        r.xin = vm((T, D), BF16)
        r.cot = vm((T, D), BF16)
        r.a1 = vm((T, D), BF16)
        r.sg = vm((T, 2 * D), BF16)
        r.y1 = vm((T, D), F32)
        r.a2 = vm((T, D), BF16)
        r.pext = vm((3, T + 16, H), F32)
        r.rgl = vm((T, H), F32)
        r.dgl = vm((T, FF), BF16)
        r.dgr = vm((T, H), BF16)
        r.nm = vm((T, FF), BF16)
        r.rm = vm((T, 1), F32)
        r.big = vm((T + 16, FF), F32)
        r.sep = vm((T, FF), BF16)
        r.y2 = vm((T, D), F32)
        r.a4 = vm((T, D), BF16)
        r.qb = vm((T, D), BF16)
        r.kvb = vm((self.LEN, 2 * D), BF16)
        r.lse = vm((T, 128), F32)
        r.ctx = vm((T, D), BF16)
        r.y3 = vm((T, D), F32)
        r.a5 = vm((T, D), BF16)
        r.hid = vm((T + 32, FF), BF16)
        r.dg = vm((T, FF), BF16)
        r.osend = vm((T, D), BF16)
        r.gs = r.y3
        r.dkvr = vm((T, 2 * D), BF16)
        r.tr = vm((D, T), BF16)
        edges = (((8, H), F32), ((16, FF), BF16), ((16, FF), BF16), ((8, H), F32))
        r.es = [vm(shape, dtype) for shape, dtype in edges]
        r.er = [vm(shape, dtype) for shape, dtype in edges]
        r.s_loc = sem(WEIGHTS)
        r.s_as = sem(WEIGHTS)
        r.s_ar = sem(WEIGHTS, self.B - 1)
        r.s_br = sem(WEIGHTS, (self.A - 1) * self.B)
        r.s_dr = sem(WEIGHTS)
        if self.shared:
            r.s_hr = sem(WEIGHTS)
        r.s_rs = sem(UNITS)
        r.s_rr = sem(UNITS)
        r.s_ps = sem(UNITS)
        r.s_pr = sem(UNITS, 2)
        if self.Z > 1:
            r.s_zs = sem(UNITS)
            r.s_zr = sem(UNITS, 2)
        r.s_fs = sem(UNITS)
        r.s_fr = sem(UNITS)
        r.s_xs = sem(4, self.S)
        r.s_xr = sem(4, max(self.PH, self.S))
        r.s_gs = sem(2 * self.S)
        r.s_gr = sem(n)
        r.s_ms = sem(n)
        r.s_mr = sem(n)
        r.s_es = sem(4)
        r.s_er = sem(4)
        r.s_ks = sem(HEADS // 2)
        r.s_kr = sem(HEADS // 2)
        r.s_js = sem(HEADS // 2)
        r.s_jr = sem(HEADS // 2)
        return r


INPUTS = 4 + WEIGHTS
OUTPUTS = 2 + WEIGHTS + 1


def kernel(plan, *refs):
    ins, outs = refs[:INPUTS], refs[INPUTS : INPUTS + OUTPUTS]
    scratch = iter(refs[INPUTS + OUTPUTS :])
    r = plan.buffers(lambda shape: next(scratch))
    r.x, r.seg, r.ct, r.small = ins[:4]
    r.h = ins[4:]
    r.o_out, r.o_ig = outs[:2]
    r.o = outs[2:]
    n, Z, S, span = plan.n, plan.Z, plan.S, plan.span
    T, D, FF, H, PH = plan.T, plan.D, plan.FF, plan.HALF, plan.PH
    A, B = plan.A, plan.B
    dp, q = lax.axis_index("dp"), lax.axis_index("seq")
    z, c = dp // 2, dp % 2
    oc = 1 - c

    def aligned(v, m=16):
        return pl.multiple_of(v, m)

    def dev(core, chip, plane=None):
        return ((z if plane is None else plane) * 2 + core, chip)

    sibling = dev(oc, q)

    def remote(src, dst, ss, rs, to):
        return pltpu.make_async_remote_copy(
            src_ref=src, dst_ref=dst, send_sem=ss, recv_sem=rs, device_id=to, device_id_type=MESH
        )

    barrier = pltpu.get_barrier_semaphore()
    for core in range(2):

        def greet(t, _, core=core):
            chip = lax.rem(q + t, n)
            to = (z * 2 + (c + core) % 2, chip)
            pl.semaphore_signal(barrier, inc=1, device_id=to, device_id_type=MESH)
            return 0

        lax.fori_loop(1 - core, n, greet, 0)
    if Z > 1:

        @pl.when(z > 0)
        def _():
            pl.semaphore_signal(barrier, inc=1, device_id=dev(c, q, z - 1), device_id_type=MESH)

        @pl.when(z < Z - 1)
        def _():
            pl.semaphore_signal(barrier, inc=1, device_id=dev(c, q, z + 1), device_id_type=MESH)

    pl.semaphore_wait(barrier, 2 * n - 1 + (z + Z - 1) // Z + (2 * Z - 2 - z) // Z)

    def vrows(ref, w, row0, rows):
        ds = pl.ds(aligned(row0), rows)
        return ref.at[:, ds] if w == CONV else ref.at[ds]

    def bytes_of(view, semaphore):
        return pltpu.make_async_copy(view, view, semaphore)

    def qof(core, f, g):
        f, g = f % B, g % B
        return core * (f * B + g) + (1 - core) * (g * B + f)

    b_, a_ = q % B, q // B
    f_, g_ = c * a_ + oc * b_, c * b_ + oc * a_
    par = z % 2
    partner = dev(c, q, z + 1 - 2 * par)

    def wrows(ref, w, row0, rows, side):
        if w not in plan.shared:
            return vrows(ref, w, row0, rows)
        size = plan.dims[w][1] // 2
        cols = pl.ds(pl.multiple_of(side * size, 128), size)
        if w == CONV:
            return ref.at[:, pl.ds(aligned(row0), rows), cols]
        return ref.at[pl.ds(aligned(row0), rows), cols]

    def wblock(w, shard, side=par):
        return wrows(r.w[w], w, shard * plan.kr(w) + c * plan.hr(w), plan.hr(w), side)

    def own_block(w):
        return wrows(r.h[w], w, c * plan.hr(w), plan.hr(w), par)

    def copy_a(w, t):
        to = dev(c, qof(c, f_ + t, g_))
        return remote(own_block(w), wblock(w, q), r.s_as.at[w], r.s_ar.at[w, t - 1], to)

    def copy_b(w, u, t):
        blk = wblock(w, qof(c, f_ + B - t, g_))
        src = own_block(w) if t == 0 else blk
        to = dev(c, qof(c, f_, g_ + u))
        return remote(src, blk, r.s_as.at[w], r.s_br.at[w, (u - 1) * B + t], to)

    def shard_from(u, t):
        return qof(c, f_ + B - t, g_ + B - u)

    def pass_on(w, u, t):
        blk = wblock(w, shard_from(u, t))
        remote(blk, blk, r.s_as.at[w], r.s_dr.at[w], sibling).start()
        if w in plan.shared:
            remote(blk, blk, r.s_as.at[w], r.s_hr.at[w], partner).start()

    def local_shard(w):
        dst = vrows(r.w[w], w, q * plan.kr(w), plan.kr(w))
        return pltpu.make_async_copy(r.h[w], dst, r.s_loc.at[w])

    def g0(w):
        local_shard(w).start()
        for t in range(1, B):
            copy_a(w, t).start()
        for u in range(1, A):
            copy_b(w, u, 0).start()

    def g1(w):
        for t in range(1, B):
            bytes_of(wblock(w, shard_from(0, t)), r.s_ar.at[w, t - 1]).wait()
            for u in range(1, A):
                copy_b(w, u, t).start()
            pass_on(w, 0, t)

    def g2(w):
        for u in range(1, A):
            for t in range(B):
                bytes_of(wblock(w, shard_from(u, t)), r.s_br.at[w, (u - 1) * B + t]).wait()
                pass_on(w, u, t)

    def others(w):
        return wrows(r.w[w], w, 0, (n - 1) * plan.hr(w), 0)

    def gz(w):
        if w not in plan.shared:
            return
        bytes_of(others(w), r.s_hr.at[w]).wait()
        for u in range(A):
            for t in range(B):
                if (u, t) != (0, 0):
                    blk = wblock(w, shard_from(u, t), 1 - par)
                    remote(blk, blk, r.s_as.at[w], r.s_dr.at[w], sibling).start()

    def g3(w):
        local_shard(w).wait()
        bytes_of(vrows(r.w[w], w, 0, (n - 1) * plan.hr(w)), r.s_dr.at[w]).wait()

    gather_steps = (g0, g1, g2, gz)
    forward_turns = iter(FORWARD)

    def gather(steps):
        for k, w in steps:
            if w == TOKENS:
                tokens_in(r.ct, r.cot, 1)
            else:
                gather_steps[k](w)

    def pass_turn():
        gather(next(forward_turns))

    def pass_turns(count):
        every = [(k, next(forward_turns)) for k in range(count)]
        return [(k, lambda steps=steps: gather(steps)) for k, steps in every if steps]

    def gather_sent(w):
        bytes_of(vrows(r.w[w], w, 0, 2 * (n - 1) * plan.hr(w)), r.s_as.at[w]).wait()

    def token_rows(ref, slot):
        return ref.at[pl.ds(aligned(slot * span), span)]

    def tokens_in(src, dst, k):
        for j in range(S):
            chip, core, slot = S * c + j, q // PH, q % PH
            here = jnp.logical_and(chip == q, core == c)
            there = token_rows(dst, slot)

            @pl.when(here)
            def _():
                pltpu.make_async_copy(src.at[j], there, r.s_xr.at[k, slot]).start()

            @pl.when(jnp.logical_not(here))
            def _():
                remote(
                    src.at[j], there, r.s_xs.at[k, j], r.s_xr.at[k, slot], dev(core, chip)
                ).start()

    def tokens_in_done(dst, k):
        for slot in range(PH):
            blk = token_rows(dst, slot)
            pltpu.make_async_copy(blk, blk, r.s_xr.at[k, slot]).wait()

    def tokens_in_sent(src, dst, k):
        for j in range(S):
            chip, core, slot = S * c + j, q // PH, q % PH
            here = jnp.logical_and(chip == q, core == c)

            @pl.when(jnp.logical_not(here))
            def _():
                remote(
                    src.at[j],
                    token_rows(dst, slot),
                    r.s_xs.at[k, j],
                    r.s_xr.at[k, slot],
                    dev(core, chip),
                ).wait_send()

    def tokens_out(src, dst, k):
        for p in range(PH):
            chip, core, slot = c * PH + p, q // S, q % S
            here = jnp.logical_and(chip == q, core == c)

            @pl.when(here)
            def _():
                pltpu.make_async_copy(token_rows(src, p), dst.at[slot], r.s_xr.at[k, slot]).start()

            @pl.when(jnp.logical_not(here))
            def _():
                remote(
                    token_rows(src, p),
                    dst.at[slot],
                    r.s_xs.at[k, p],
                    r.s_xr.at[k, slot],
                    dev(core, chip),
                ).start()

    def tokens_out_done(src, dst, k):
        for j in range(S):
            pltpu.make_async_copy(dst.at[j], dst.at[j], r.s_xr.at[k, j]).wait()
        for p in range(PH):
            chip, core, slot = c * PH + p, q // S, q % S
            here = jnp.logical_and(chip == q, core == c)

            @pl.when(jnp.logical_not(here))
            def _():
                remote(
                    token_rows(src, p),
                    dst.at[slot],
                    r.s_xs.at[k, p],
                    r.s_xr.at[k, slot],
                    dev(core, chip),
                ).wait_send()

    def seg_send():
        for j in range(S):
            for core in range(2):
                chip = S * c + j
                here = jnp.logical_and(chip == q, c == core)
                i = 2 * j + core

                @pl.when(here)
                def _():
                    pltpu.make_async_copy(r.seg, r.segbuf.at[q], r.s_gr.at[q]).start()

                @pl.when(jnp.logical_not(here))
                def _():
                    remote(
                        r.seg,
                        r.segbuf.at[q],
                        r.s_gs.at[i],
                        r.s_gr.at[q],
                        dev(core, chip),
                    ).start()

    def seg_sent():
        for j in range(S):
            for core in range(2):
                chip = S * c + j
                here = jnp.logical_and(chip == q, c == core)

                @pl.when(jnp.logical_not(here))
                def _():
                    remote(
                        r.seg,
                        r.segbuf.at[q],
                        r.s_gs.at[2 * j + core],
                        r.s_gr.at[q],
                        dev(core, chip),
                    ).wait_send()

    def small_copy(t):
        return remote(
            r.small,
            r.smallbuf.at[q],
            r.s_ms.at[t],
            r.s_mr.at[t],
            dev(c, (q + t) % n),
        )

    def small_arrived(t):
        blk = r.smallbuf.at[(q + n - t) % n]
        return remote(blk, blk, r.s_ms.at[t], r.s_mr.at[t], sibling)

    def edge_copy(i):
        return remote(r.es[i], r.er[i], r.s_es.at[i], r.s_er.at[i], sibling)

    def edge_send(i, last, first):
        r.es[i][...] = jnp.where(c == 0, last, first)
        edge_copy(i).start()

    def edge_take(i):
        edge_copy(i).wait()
        got = r.er[i][...]
        none = jnp.zeros_like(got)
        return jnp.where(c == 1, got, none), jnp.where(c == 0, got, none)

    def columns(u):
        w, half = UNIT_WEIGHT[u], UNIT_PART[u]
        size = plan.gcols(w)
        return (0, size) if half is None else (half * (size // 2), size // 2)

    def urows(ref, u, row0, rows, shift=0):
        col0, size = columns(u)
        return ref.at[pl.ds(aligned(row0), rows), pl.ds(col0 + shift, size)]

    grad_home = {GLU: (r.hid, 2 * D), CONV: (r.dkvr, 0), LEFT: (r.sep, 0), QKV: (r.dg, 0)}

    def gpiece(u, shard, half):
        if u == SMALL:
            return r.gsm.at[pl.ds(pl.multiple_of(half * 16, 16), 16)]
        w = UNIT_WEIGHT[u]
        ref, shift = grad_home.get(w, (r.w[w] if w < WEIGHTS else None, 0))
        return urows(ref, u, shard * plan.kr(w) + half * plan.hr(w), plan.hr(w), shift)

    def rpiece(u, shard):
        w = UNIT_WEIGHT[u]
        if u == SMALL:
            return r.r[w]
        return urows(r.r[w], u, shard * plan.hr(w), plan.hr(w))

    def slots(u, first, count):
        buf = r.p[UNIT_WEIGHT[u]]
        if u == SMALL:
            return buf.at[pl.ds(first, count)]
        col0, size = columns(u)
        return buf.at[pl.ds(first, count), :, pl.ds(col0, size)]

    def ppiece(u, slot):
        buf = r.p[UNIT_WEIGHT[u]]
        if u == SMALL:
            return buf.at[slot]
        col0, size = columns(u)
        return buf.at[slot, :, pl.ds(col0, size)]

    def zpiece(u, way):
        buf = (r.u, r.d)[way][UNIT_WEIGHT[u]]
        if u == SMALL:
            return buf
        col0, size = columns(u)
        return buf.at[:, pl.ds(col0, size)]

    def copy_r(u, s):
        return remote(gpiece(u, s, oc), rpiece(u, s), r.s_rs.at[u], r.s_rr.at[u], sibling)

    def all_r(u, semaphore):
        w = UNIT_WEIGHT[u]
        view = r.r[w] if u == SMALL else urows(r.r[w], u, 0, n * plan.hr(w))
        return bytes_of(view, semaphore.at[u])

    def shards(u):
        return 1 if u == SMALL else n

    def red0(u):
        for s in range(shards(u)):
            copy_r(u, s).start()

    def put(to, *terms):
        size = to.shape[0]
        rows = min(size, 64)

        def some(i, _):
            at = pl.ds(pl.multiple_of(i * rows, rows), rows)
            total = terms[0][at].astype(F32)
            for term in terms[1:]:
                total = total + term[at].astype(F32)
            to[at] = total.astype(to.dtype)
            return 0

        lax.fori_loop(0, size // rows, some, 0)

    def add_core(u, s):
        mine = gpiece(u, s, c)
        put(mine, mine, rpiece(u, s))

    def slot1(u, t):
        return (u - 1) * B + t

    def slot2(t):
        return (A - 1) * B + t - 1

    def copy_p1(u, k, t):
        return remote(
            gpiece(u, qof(c, f_ + t, g_ + k), c),
            ppiece(u, slot1(k, t)),
            r.s_ps.at[u],
            r.s_pr.at[u, 0],
            dev(c, qof(c, f_, g_ + k)),
        )

    def copy_p2(u, t):
        to = qof(c, f_ + t, g_)
        return remote(
            r.r[WEIGHTS] if u == SMALL else gpiece(u, to, c),
            ppiece(u, slot2(t)),
            r.s_ps.at[u],
            r.s_pr.at[u, 1],
            dev(c, to),
        )

    def all_p(u, step, semaphore):
        count = B - 1 if step else A - 1 if u == SMALL else (A - 1) * B
        return bytes_of(slots(u, 0, count), semaphore.at[u, step])

    def red1(u):
        all_r(u, r.s_rr).wait()
        if u == SMALL:
            add_core(u, 0)
            for k in range(1, A):
                copy_p1(u, k, 0).start()
            return

        def send(i, _):
            k, t = i // B + 1, i % B
            add_core(u, qof(c, f_ + t, g_ + k))
            copy_p1(u, k, t).start()
            return 0

        lax.fori_loop(0, (A - 1) * B, send, 0)
        lax.fori_loop(0, B, lambda t, _: (add_core(u, qof(c, f_ + t, g_)), 0)[1], 0)

    def red1b(u):
        all_p(u, 0, r.s_pr).wait()

        def send(t, _):
            mine = gpiece(u, 0 if u == SMALL else qof(c, f_ + t, g_), c)
            came = [ppiece(u, slot1(k, 0 if u == SMALL else t)) for k in range(1, A)]
            put(r.r[WEIGHTS] if u == SMALL else mine, mine, *came)
            if u != SMALL:
                copy_p2(u, t).start()
            return 0

        if u == SMALL:
            send(0, 0)
            for t in range(1, B):
                copy_p2(u, t).start()
        else:
            lax.fori_loop(1, B, send, 0)

    def red2(u):
        all_p(u, 1, r.s_pr).wait()
        came = [] if u == SMALL else [ppiece(u, slot1(k, 0)) for k in range(1, A)]
        came += [ppiece(u, slot2(t)) for t in range(1, B)]
        put(ppiece(u, 0), r.r[WEIGHTS] if u == SMALL else gpiece(u, q, c), *came)

    def copy_z(u, way):
        return remote(
            ppiece(u, 1 + way),
            zpiece(u, way),
            r.s_zs.at[u],
            r.s_zr.at[u, way],
            dev(c, q, z + 1 if way == 0 else z - 1),
        )

    def red_hop(u, h):
        own, up, down = ppiece(u, 0), ppiece(u, 1), ppiece(u, 2)

        @pl.when(z == h)
        def _():
            if h == 0:
                put(up, own)
            else:
                copy_z(u, 0).wait_recv()
                put(up, own, zpiece(u, 0))
            if h < Z - 1:
                copy_z(u, 0).start()

        @pl.when(z == Z - 1 - h)
        def _():
            if h == 0:
                put(down, own)
            else:
                copy_z(u, 1).wait_recv()
                if h < Z - 1:
                    put(down, own, zpiece(u, 1))
            if h < Z - 1:
                copy_z(u, 1).start()

    def final_rows(u):
        w = UNIT_WEIGHT[u]
        if u == SMALL:
            return r.o[w].at[pl.ds(pl.multiple_of(c * 16, 16), 16)]
        return urows(r.o[w], u, c * plan.hr(w), plan.hr(w))

    def final_local(u):
        return pltpu.make_async_copy(ppiece(u, 0), final_rows(u), r.s_fs.at[u])

    def final_remote(u):
        return remote(ppiece(u, 0), final_rows(u), r.s_fs.at[u], r.s_fr.at[u], sibling)

    def red_final(u):
        if Z > 1:
            own, up = ppiece(u, 0), ppiece(u, 1)

            @pl.when(z == Z - 1)
            def _():
                put(own, up)

            @pl.when(z < Z - 1)
            def _():
                put(own, up, zpiece(u, 1))

        final_local(u).start()
        final_remote(u).start()

    def red_end(u):
        final_remote(u).wait_recv()
        bytes_of(slots(u, 0, 2), r.s_fs.at[u]).wait()
        all_r(u, r.s_rs).wait()
        bytes_of(slots(u, 0, A + B - 2 if u == SMALL else n - 1), r.s_ps.at[u]).wait()
        if Z > 1:
            ends = jnp.logical_or(z == 0, z == Z - 1)

            @pl.when(ends)
            def _():
                bytes_of(slots(u, 0, 1), r.s_zs.at[u]).wait()

            @pl.when(jnp.logical_not(ends))
            def _():
                bytes_of(slots(u, 0, 2), r.s_zs.at[u]).wait()

    def red2_hop(u):
        red2(u)
        red_hop(u, 0)

    def last_hop(u):
        red_hop(u, Z - 1)
        red_final(u)

    ahead = {}
    turns = iter(SCHEDULE)

    def enlist(u):
        if Z > 1:
            ahead[u] = [red1, red1b, red2_hop]
            ahead[u] += [lambda k, h=h: red_hop(k, h) for h in range(1, Z - 1)]
            ahead[u].append(last_hop)
        else:
            ahead[u] = [red1, red1b, red2, red_final]

    def reduce_start(*units):
        for u in units:
            red0(u)
            enlist(u)

    def steps_of(units):
        return [(ahead[u].pop(0), u) for u in units if ahead[u]]

    def move(units):
        for step, u in steps_of(units):
            step(u)

    def turn():
        move(next(turns))

    def turns_of(count):
        acts = []
        for k in range(count):
            steps = steps_of(next(turns))
            if steps:
                acts.append((k, lambda steps=steps: [step(u) for step, u in steps][:0]))
        return acts

    def loop(count, body, after=()):
        def step(i, _):
            body(i)
            for k, act in after:
                pl.when(i == k)(lambda act=act: (act(), None)[1])
            return 0

        lax.fori_loop(0, count, step, 0)

    RB = 256
    NB = T // RB

    def rows_of(i, size=RB, base=0):
        return pl.ds(pl.multiple_of(i * size + base, base or size), size)

    seg_send()
    small_local = pltpu.make_async_copy(r.small, r.smallbuf.at[q], r.s_mr.at[0])
    small_local.start()
    for what in START:
        if what == SMALLS:
            for t in range(1, n):
                small_copy(t).start()
        elif what == TOKENS:
            tokens_in(r.x, r.xin, 0)
        else:
            g0(what)
    r.g8[...] = jnp.zeros((16, FF), F32)
    pass_turn()

    for s in range(n):
        blk = r.segbuf.at[s]
        pltpu.make_async_copy(blk, blk, r.s_gr.at[s]).wait()
    mine = lax.broadcasted_iota(jnp.int32, (S, plan.sw), 0) == lax.rem(q, S)
    for grp in range(n // plan.sr):
        got = r.segbuf[grp * plan.sr]
        for k in range(1, plan.sr):
            got = got + r.segbuf[grp * plan.sr + k]
        row = jnp.sum(jnp.where(mine, got.astype(F32), 0.0), axis=0, keepdims=True)
        r.segrow[0:1, grp * plan.sw : (grp + 1) * plan.sw] = row
    r.segcol[0:8] = jnp.full((8, 128), -1.0, F32)
    r.segcol[plan.LEN + 8 : plan.LEN + 16] = jnp.full((8, 128), -1.0, F32)
    for k in range(plan.LEN // 128):
        row = r.segrow[0:1, k * 128 : (k + 1) * 128]
        r.segcol[8 + k * 128 : 8 + (k + 1) * 128] = jnp.broadcast_to(row, (128, 128)).T
    r.segloc[...] = r.segcol[pl.ds(pl.multiple_of(c * T, 8), T + 16)]
    r.mext[0 : T + 8] = jnp.where(r.segloc[0 : T + 8] == r.segloc[1 : T + 9], 1.0, 0.0)

    def mask(o, start, rows):
        first = 8 + start + (0 if o > 0 else o)
        return r.mext[first : first + rows]

    small_local.wait()
    for t in range(1, n):
        small_arrived(t).wait_recv()
    for grp in range(n // plan.nr):
        got = r.smallbuf[grp * plan.nr].astype(F32)
        for k in range(1, plan.nr):
            got = got + r.smallbuf[grp * plan.nr + k].astype(F32)
        r.nrm[:, grp * plan.nw : (grp + 1) * plan.nw] = got[0:8, 0 : plan.nw]
    for s in range(n):
        rows = r.smallbuf[s].astype(F32)[8:19]
        r.midp[0:11, s * plan.FFn : (s + 1) * plan.FFn] = rows

    def ln_out(k, v):
        unit, _ = normed(v)
        return (unit * r.nrm[k : k + 1] + r.nrm[4 + k : 5 + k]).astype(BF16)

    def ln_back(k, e, v):
        unit, rs = normed(v)
        eg = e * r.nrm[k : k + 1]
        m1 = jnp.mean(eg, axis=-1, keepdims=True)
        m2 = jnp.mean(eg * unit, axis=-1, keepdims=True)
        cols = slice(k * D, (k + 1) * D)
        r.g8[11:12, cols] += jnp.sum(e * unit, axis=0, keepdims=True)
        r.g8[12:13, cols] += jnp.sum(e, axis=0, keepdims=True)
        return rs * (eg - m1 - unit * m2)

    pass_turn()

    def window(b):
        return min(max(b * MB - (MW - MB) // 2 + 16, 0), T + 32 - MW)

    ahead_of = lax.broadcasted_iota(jnp.int32, (MB, MW), 1) - lax.broadcasted_iota(
        jnp.int32, (MB, MW), 0
    )
    def shift_matrices(b):
        near = r.segloc[pl.ds(pl.multiple_of(b * MB, MB), MB + 16)]
        home = near[8 : MB + 8]
        first = jnp.where(b == 0, 16, jnp.where(b == T // MB - 1, MW - MB - 16, (MW - MB) // 2))
        for i, o in enumerate(TAPS):
            same = jnp.where(home == near[8 + o : MB + 8 + o], 1.0, 0.0)
            tap = jnp.where(
                ahead_of == first + o, jnp.concatenate([same] * (MW // 128), axis=1), 0.0
            )
            r.ms[b, i * MB : (i + 1) * MB] = tap.astype(BF16)

    loop(T // MB, shift_matrices)

    lane = lax.broadcasted_iota(jnp.int32, (1, 128), 1)
    lane_f = lane.astype(F32)
    own_doc = r.segloc[8 : T + 8] == lane_f
    r.qenc[...] = jnp.where(jnp.logical_and(lane < 4, jnp.logical_not(own_doc)), FAR, 0.0).astype(BF16)
    ones = jnp.logical_and(lane >= 4, lane < 7)
    r.kenc[...] = jnp.where(
        jnp.logical_or(r.segcol[8 : plan.LEN + 8] == lane_f, ones), 1.0, 0.0
    ).astype(BF16)

    pass_turn()
    pass_turn()
    g3(GLU)
    pass_turn()
    tokens_in_done(r.xin, 0)

    def glu(i):
        rows = rows_of(i)
        x = r.xin[rows].astype(F32)
        a1 = ln_out(0, x)
        r.a1[rows] = a1
        value = mm(a1, r.w[GLU][:, 0:D])
        gate = sigmoid(mm(a1, r.w[GLU][:, D : 2 * D]))
        r.sg[rows, 0:D] = gate.astype(BF16)
        r.sg[rows, D : 2 * D] = (value * gate * (1.0 - gate)).astype(BF16)
        y1 = x + value * gate
        r.y1[rows] = y1
        r.a2[rows] = ln_out(1, y1)

    loop(NB, glu, pass_turns(NB))
    pass_turn()
    g3(CONV)

    def conv(i):
        i = c * i + oc * (NB - 1 - i)
        a2 = r.a2[rows_of(i)]
        for o in range(3):
            r.pext[o, rows_of(i, RB, 8)] = mm(a2, r.w[CONV][o])

    def right(k):
        lo = k * 128
        before = mask(-1, lo, 128)
        after = mask(1, lo, 128)
        pre = (
            r.pext[0, lo + 7 : lo + 135] * jnp.concatenate([before] * (H // 128), axis=1)
            + r.pext[1, lo + 8 : lo + 136]
            + r.pext[2, lo + 9 : lo + 137] * jnp.concatenate([after] * (H // 128), axis=1)
        )
        value, slope = gelu_both(pre)
        r.rgl[lo : lo + 128] = value
        r.dgr[lo : lo + 128] = slope.astype(BF16)

    edge = (0, lambda: edge_send(0, r.pext[0, T : T + 8], r.pext[2, 8:16]))
    loop(NB, conv, [edge])
    pass_turn()
    blocks = range(T // 128)
    for k in blocks[1:-1]:
        right(k)
    pass_turn()
    top, bottom = edge_take(0)
    r.pext[0, 0:8] = top
    r.pext[2, T + 8 : T + 16] = bottom
    right(blocks[0])
    right(blocks[-1])
    pass_turn()
    pass_turn()
    g3(LEFT)

    CH = 512
    RM = 128

    def inner_first(i, count):
        return c * i + oc * (count - 1 - i)

    def left(i):
        i = inner_first(i, T // RM)
        rows, erows = rows_of(i, RM), rows_of(i, RM, 8)
        a2 = r.a2[rows]
        for k in range(FF // CH):
            value, slope = gelu_both(mm(a2, r.w[LEFT][:, k * CH : (k + 1) * CH]))
            r.dgl[rows, k * CH : (k + 1) * CH] = slope.astype(BF16)
            r.big[erows, k * CH : (k + 1) * CH] = value
        r.big[erows, 0:H] += r.rgl[rows]
        unit, rs = normed(r.big[erows])
        r.nm[rows] = unit.astype(BF16)
        r.rm[rows] = rs
        r.hid[rows_of(i, RM, 16)] = (unit * r.midp[0:1] + r.midp[1:2]).astype(BF16)

    edge = (0, lambda: edge_send(1, r.hid[T : T + 16], r.hid[16:32]))
    loop(T // RM, left, [edge] + pass_turns(T // RM))
    r.hid[0:16], r.hid[T + 16 : T + 32] = edge_take(1)
    pass_turn()

    def depthwise(j):
        cols = pl.ds(pl.multiple_of(j * 512, 512), 512)
        for b in range(T // MB):
            near = r.hid[window(b) : window(b) + MW, cols]
            taps = mm(r.ms[b], near)
            total = r.hid[16 + b * MB : 16 + (b + 1) * MB, cols].astype(F32) * r.midp[6:7, cols]
            for i, o in enumerate(TAPS):
                total = total + taps[i * MB : (i + 1) * MB] * r.midp[6 + o : 7 + o, cols]
            r.sep[b * MB : (b + 1) * MB, cols] = total.astype(BF16)

    loop(FF // 512, depthwise, pass_turns(FF // 512))
    pass_turn()
    g3(POINT)

    def point(i):
        rows = rows_of(i, T)
        y2 = r.y1[rows] + mm(r.sep[rows], r.w[POINT][...])
        r.y2[rows] = y2
        r.a4[rows] = ln_out(2, y2)

    loop(1, point)
    pass_turn()
    pass_turn()
    g3(QKV)
    scale = 1.0 / math.sqrt(D // HEADS)

    def keys_values(i):
        rows = rows_of(i)
        a4 = r.a4[rows]
        here = pl.ds(pl.multiple_of(c * T + i * RB, RB), RB)
        r.kvb[here, 0:D] = mm(a4, r.w[QKV][:, D : 2 * D]).astype(BF16)
        r.kvb[here, D : 2 * D] = mm(a4, r.w[QKV][:, 2 * D : 3 * D]).astype(BF16)

    def queries(i):
        rows = rows_of(i)
        r.qb[rows] = (mm(r.a4[rows], r.w[QKV][:, 0:D]) * scale).astype(BF16)

    def kv_copy(j, base):
        blk = r.kvb.at[pl.ds(aligned(c * T), T), pair_cols(j, base)]
        return remote(blk, blk, r.s_ks.at[j], r.s_kr.at[j], sibling)

    def pair_cols(j, base=0):
        return pl.ds(pl.multiple_of(j * 128 + base, 128), 128)

    def pair_bytes(j, semaphore):
        return bytes_of(r.kvb.at[pl.ds(0, T), pl.ds(0, 256)], semaphore.at[j])

    loop(NB, keys_values)
    for j in range(HEADS // 2):
        kv_copy(j, 0).start()
        kv_copy(j, D).start()
    loop(NB, queries)
    pass_turn()
    pass_turn()
    heads_lanes = [lane < 64, lane >= 64]
    def head_lanes(e, v):
        return jnp.where(heads_lanes[e], v, jnp.zeros_like(v))

    def attend(j):
        pair_bytes(j, r.s_kr).wait()
        cols, vcols = pair_cols(j), pair_cols(j, D)
        keys = jnp.concatenate([r.kvb[:, cols], r.kenc[...]], axis=1)
        for k in range(T // RB):
            rows = slice(k * RB, (k + 1) * RB)
            q2 = r.qb[rows, cols]
            got = []
            for e in range(2):
                score = mm_t(jnp.concatenate([head_lanes(e, q2), r.qenc[rows]], axis=1), keys)
                most = jnp.max(score, axis=-1, keepdims=True)
                power = jnp.exp(score - most)
                total = jnp.sum(power, axis=-1, keepdims=True)
                got.append(mm(power.astype(BF16), r.kvb[:, vcols]) / total)
                lse = most + jnp.log(total)
                r.lse[rows] = jnp.where(lane == 2 * j + e, lse, r.lse[rows])
            r.ctx[rows, cols] = jnp.where(heads_lanes[0], got[0], got[1]).astype(BF16)

    r.lse[...] = jnp.zeros((T, 128), F32)

    loop(HEADS // 2, attend, pass_turns(HEADS // 2))
    pass_turn()
    g3(OUT)

    def out(i):
        rows = rows_of(i, T)
        y3 = r.y2[rows] + mm(r.ctx[rows], r.w[OUT][...])
        r.y3[rows] = y3
        r.a5[rows] = ln_out(3, y3)

    loop(1, out)
    pass_turn()
    pass_turn()
    g3(FIN)

    def ffn_in(i):
        rows = rows_of(i)
        a5 = r.a5[rows]
        for k in range(FF // CH):
            value, slope = gelu_both(mm(a5, r.w[FIN][:, k * CH : (k + 1) * CH]))
            r.hid[rows, k * CH : (k + 1) * CH] = value.astype(BF16)
            r.dg[rows, k * CH : (k + 1) * CH] = slope.astype(BF16)

    loop(NB, ffn_in, pass_turns(NB))
    pass_turn()
    g3(FOUT)

    def ffn_out(i):
        rows = rows_of(i, T)
        r.osend[rows] = (r.y3[rows] + mm(r.hid[rows], r.w[FOUT][...])).astype(BF16)

    loop(1, ffn_out)
    pass_turn()
    tokens_out(r.osend, r.o_out, 2)
    for w in range(WEIGHTS):
        gather_sent(w)
    for j in range(HEADS // 2):
        pair_bytes(j, r.s_ks).wait()

    tokens_in_done(r.cot, 1)

    def ffn_back(i):
        rows = rows_of(i, T)
        f4 = r.cot[rows]
        for k in range(FF // CH):
            cols = slice(k * CH, (k + 1) * CH)
            up = mm_t(f4, r.w[FOUT][cols])
            r.dg[rows, cols] = (up * r.dg[rows, cols].astype(F32)).astype(BF16)
        e = mm_t(r.dg[rows], r.w[FIN][...])
        r.gs[rows] = f4.astype(F32) + ln_back(3, e, r.y3[rows])

    loop(1, ffn_back)
    GC = 1024

    def grad_outer(k):
        cols = rows_of(k, GC)
        r.w[FOUT][cols] = mm_tn(r.hid[0:T, cols], r.cot[...]).astype(BF16)

    loop(FF // GC, grad_outer)
    reduce_start(U_FOUT)
    turn()
    r.tr[...] = r.a5[...].T

    def grad_inner(k):
        cols = rows_of(k, GC)
        r.w[FIN][:, cols] = mm(r.tr[...], r.dg[:, cols]).astype(BF16)

    loop(FF // GC, grad_inner)
    reduce_start(U_FIN)
    turn()

    def out_back(i):
        rows = rows_of(i, T)
        f3 = r.gs[rows].astype(BF16)
        r.a5[rows] = f3
        r.hid[rows, 3 * D : 4 * D] = mm_t(f3, r.w[OUT][...]).astype(BF16)

    loop(1, out_back)
    r.w[OUT][...] = mm_tn(r.ctx[...], r.a5[...]).astype(BF16)
    reduce_start(U_OUT)
    turn()
    r.tr[...] = r.a4[...].T

    QB = 256

    def with_terms(extra, v):
        high = v.astype(BF16).astype(F32)
        mid = (v - high).astype(BF16).astype(F32)
        low = v - high - mid
        terms = jnp.where(lane == 4, high, jnp.where(lane == 5, mid, jnp.where(lane == 6, low, 0.0)))
        return extra - terms.astype(BF16)

    halfway = []

    def attend_back(j):
        cols, vcols = pair_cols(j), pair_cols(j, D)
        k2 = r.kvb[:, cols]
        keys = jnp.concatenate([k2, r.kenc[...]], axis=1)
        turned = [head_lanes(e, k2).T for e in range(2)]
        values = jnp.concatenate([r.kvb[:, vcols], r.kenc[...]], axis=1)
        for k in range(T // QB):
            rows = slice(k * QB, (k + 1) * QB)
            q2 = r.qb[rows, cols]
            d2 = r.hid[rows, pair_cols(j, 3 * D)]
            inner = d2.astype(F32) * r.ctx[rows, cols].astype(F32)
            dq = jnp.zeros((128, QB), F32)
            for e in range(2):
                qe, de = head_lanes(e, q2), head_lanes(e, d2)
                lse = jnp.sum(
                    jnp.where(lane == 2 * j + e, r.lse[rows], 0.0), axis=-1, keepdims=True
                )
                delta = jnp.sum(head_lanes(e, inner), axis=-1, keepdims=True)
                shifted = mm_t(keys, jnp.concatenate([qe, with_terms(r.qenc[rows], lse)], axis=1))
                probs = jnp.exp(shifted)
                none = jnp.zeros((QB, 128), BF16)
                moved = mm_t(values, jnp.concatenate([de, with_terms(none, delta)], axis=1))
                ds = (probs * moved).astype(BF16)
                dk = mm(ds, qe)
                dv = mm(probs.astype(BF16), de)
                for kk in range(2):
                    half = slice(kk * T, (kk + 1) * T)
                    at = 2 * D + kk * 128
                    if k == 0 and e == 0:
                        r.big[0:T, at : at + 128] = dk[half]
                        r.big[0:T, at + 256 : at + 384] = dv[half]
                    else:
                        r.big[0:T, at : at + 128] += dk[half]
                        r.big[0:T, at + 256 : at + 384] += dv[half]
                dq = dq + mm(turned[e], ds)
            r.hid[rows, cols] = (dq.T * scale).astype(BF16)
            if k == 0:
                for step, act in halfway:
                    pl.when(j == step)(lambda act=act: (act(), None)[1])

        def part(core, what):
            at = pl.multiple_of(2 * D + core * 128 + what * 256, 128)
            return r.big[0:T, pl.ds(at, 128)]

        @pl.when(j >= 2)
        def _():
            dkv_copy(j - 2).wait_send()

        for what in range(2):
            mine = pl.ds(pl.multiple_of(j * 256 + what * 128, 128), 128)
            r.big[0:T, mine] = part(c, what)
            r.cot[:, pl.ds(pl.multiple_of(lax.rem(j, 2) * 256 + what * 128, 128), 128)] = part(
                oc, what
            ).astype(BF16)
        dkv_copy(j).start()

        @pl.when(j == 2)
        def _():
            pairs_back(0)

    def dkv_copy(j):
        slot = lax.rem(j, 2)
        return remote(
            r.cot.at[:, pl.ds(pl.multiple_of(slot * 256, 128), 256)],
            r.dkvr.at[:, pl.ds(pl.multiple_of(j * 256, 128), 256)],
            r.s_js.at[j],
            r.s_jr.at[j],
            sibling,
        )

    def pairs_back(m):
        parts, weights = [], []
        for j in (2 * m, 2 * m + 1):
            dkv_copy(j).wait_recv()
            if m == 1:
                dkv_copy(j).wait_send()
            both = slice(j * 256, (j + 1) * 256)
            dkv = r.big[0:T, both] + r.dkvr[:, both].astype(F32)
            own = slice(j * 128, (j + 1) * 128)
            parts += [r.hid[0:T, own], dkv.astype(BF16)]
            for base in (0, D, 2 * D):
                weights.append(r.w[QKV][:, base + j * 128 : base + (j + 1) * 128])
        pairs = jnp.concatenate(parts, axis=1)
        share = mm_t(pairs, jnp.concatenate(weights, axis=1))
        if m == 0:
            r.big[0:T, 3 * D : 4 * D] = share
        else:
            r.big[0:T, 3 * D : 4 * D] += share
        r.dg[:, m * 768 : (m + 1) * 768] = mm(r.tr[...], pairs).astype(BF16)

    acts = []
    for k in range(HEADS // 2):
        halfway += [(k, act) for _, act in turns_of(1)]
        if k == 2:
            enlist(U_QKV0)
            acts.append((2, lambda: red0(U_QKV0)))
        acts += [(k, act) for _, act in turns_of(1)]
    loop(HEADS // 2, attend_back, acts)
    pairs_back(1)
    reduce_start(U_QKV1)
    turn()

    def qkv_back(i):
        rows = rows_of(i)
        r.gs[rows] += ln_back(2, r.big[rows, 3 * D : 4 * D], r.y2[rows])

    loop(NB, qkv_back)

    def point_back(i):
        rows = rows_of(i, T)
        f2 = r.gs[rows].astype(BF16)
        r.a4[rows] = f2
        for k in range(FF // CH):
            cols = slice(k * CH, (k + 1) * CH)
            d = mm_t(f2, r.w[POINT][cols])
            r.hid[rows_of(i, T, 16), cols] = d.astype(BF16)

    loop(1, point_back)
    edge_send(2, r.hid[T : T + 16], r.hid[16:32])
    turn()

    def grad_point(k):
        cols = rows_of(k, GC)
        r.w[POINT][cols] = mm_tn(r.sep[:, cols], r.a4[...]).astype(BF16)

    loop(FF // GC, grad_point)
    reduce_start(U_POINT0, U_POINT1)
    turn()
    r.hid[0:16], r.hid[T + 16 : T + 32] = edge_take(2)

    def depth_back(j):
        cols = pl.ds(pl.multiple_of(j * 256, 256), 256)
        gain, shift = r.midp[0:1, cols], r.midp[1:2, cols]
        sums = [jnp.zeros((8, 256), F32) for _ in range(9)]
        for b in range(T // MB):
            lo = b * MB
            taps = mm(r.ms[b], r.hid[window(b) : window(b) + MW, cols])
            a3 = r.nm[lo : lo + MB, cols].astype(F32) * gain + shift
            total = jnp.zeros((MB, 256), F32)
            here = r.hid[16 + lo : 16 + lo + MB, cols].astype(F32)
            for o in range(-4, 5):
                i = TAPS.index(-o) if o else 0
                moved = taps[i * MB : (i + 1) * MB] if o else here
                total = total + moved * r.midp[6 + o : 7 + o, cols]
                part = moved * a3
                for g in range(MB // 8):
                    sums[o + 4] = sums[o + 4] + part[g * 8 : (g + 1) * 8]
            r.big[lo + 8 : lo + 8 + MB, cols] = total
        for o in range(9):
            r.g8[2 + o : 3 + o, cols] = jnp.sum(sums[o], axis=0, keepdims=True)

    loop(FF // 256, depth_back, turns_of(FF // 256))

    def mid_back(i):
        rows, erows = rows_of(i, RM), rows_of(i, RM, 8)
        e = r.big[erows]
        unit = r.nm[rows].astype(F32)
        eg = e * r.midp[0:1]
        m1 = jnp.mean(eg, axis=-1, keepdims=True)
        m2 = jnp.mean(eg * unit, axis=-1, keepdims=True)
        r.g8[0:1] += jnp.sum(e * unit, axis=0, keepdims=True)
        r.g8[1:2] += jnp.sum(e, axis=0, keepdims=True)
        dmid = r.rm[rows] * (eg - m1 - unit * m2)
        r.dgl[rows] = (dmid * r.dgl[rows].astype(F32)).astype(BF16)
        right = dmid[:, 0:H] * r.dgr[rows].astype(F32)
        r.pext[0, erows] = right.astype(BF16).astype(F32)

    loop(T // RM, mid_back, turns_of(T // RM))
    edge_send(3, r.pext[0, T : T + 8], r.pext[0, 8:16])
    r.tr[...] = r.a2[...].T

    def grad_left(k):
        cols = rows_of(k, GC)
        r.sep[:, cols] = mm(r.tr[...], r.dgl[:, cols]).astype(BF16)

    half = FF // GC // 2
    lax.fori_loop(0, half, lambda k, _: (grad_left(k), 0)[1], 0)
    reduce_start(U_LEFT0)
    turn()
    lax.fori_loop(half, 2 * half, lambda k, _: (grad_left(k), 0)[1], 0)
    reduce_start(U_LEFT1)
    turn()
    top, bottom = edge_take(3)
    r.pext[0, 0:8] = top
    r.pext[0, T + 8 : T + 16] = bottom
    for k in range(T // 128):
        lo = k * 128
        for o in (-1, 0, 1):
            moved = r.pext[0, lo + 8 - o : lo + 136 - o]
            if o:
                moved = moved * jnp.concatenate([mask(-o, lo, 128)] * (H // 128), axis=1)
            r.hid[lo : lo + 128, (o + 1) * H : (o + 2) * H] = moved.astype(BF16)
    for o in range(3):
        cols = slice(o * H, (o + 1) * H)
        r.dkvr[:, cols] = mm(r.tr[...], r.hid[0:T, cols]).astype(BF16)
    reduce_start(U_CONV)
    turn()

    def branch_back(i):
        rows = rows_of(i)
        e = mm_t(r.dgl[rows], r.w[LEFT][...])
        for o in range(3):
            e = e + mm_t(r.hid[rows, o * H : (o + 1) * H], r.w[CONV][o])
        r.gs[rows] += ln_back(1, e, r.y1[rows])

    loop(NB, branch_back, turns_of(NB))

    def gate_back(i):
        rows = rows_of(i)
        g = r.gs[rows]
        r.sg[rows, 0:D] = (g * r.sg[rows, 0:D].astype(F32)).astype(BF16)
        r.sg[rows, D : 2 * D] = (g * r.sg[rows, D : 2 * D].astype(F32)).astype(BF16)

    loop(NB, gate_back)
    r.tr[...] = r.a1[...].T

    def grad_glu(k):
        cols = rows_of(k, D)
        to = pl.ds(pl.multiple_of(k * D + 2 * D, D), D)
        r.hid[0:T, to] = mm(r.tr[...], r.sg[:, cols]).astype(BF16)

    grad_glu(0)
    reduce_start(U_GLU0)
    turn()
    grad_glu(1)
    reduce_start(U_GLU1)
    turn()

    def glu_back(i):
        rows = rows_of(i)
        e = mm_t(r.sg[rows], r.w[GLU][...])
        total = r.gs[rows] + ln_back(0, e, r.xin[rows].astype(F32))
        r.a5[rows] = total.astype(BF16)

    loop(NB, glu_back, turns_of(NB))
    r.gsm[0:16] = r.g8[:, 0 : FF // 2].astype(BF16)
    r.gsm[16:32] = r.g8[:, FF // 2 : FF].astype(BF16)
    reduce_start(SMALL)
    move(TAIL[0])
    tokens_out(r.a5, r.o_ig, 3)
    move(TAIL[1])
    while any(ahead.values()):
        move(range(UNITS))

    for u in range(UNITS):
        red_end(u)
    tokens_out_done(r.osend, r.o_out, 2)
    tokens_out_done(r.a5, r.o_ig, 3)
    tokens_in_sent(r.x, r.xin, 0)
    tokens_in_sent(r.ct, r.cot, 1)
    seg_sent()
    for t in range(1, n):
        small_copy(t).wait_send()


def local(
    inputs,
    segment_ids,
    cotangent,
    norm_gain,
    norm_bias,
    glu_weight,
    left_weight,
    conv_weight,
    mid_gain,
    mid_bias,
    depth_weight,
    point_weight,
    qkv_weight,
    out_weight,
    ffn_in,
    ffn_out,
):
    seqs, span, width = inputs.shape
    n = lax.axis_size("seq")
    plan = Plan(
        lax.axis_size("dp"), n, seqs, span, width, ffn_in.shape[1], conv_weight.shape[2]
    )
    q = lax.axis_index("seq")

    def placed(piece, repeats):
        if repeats == 1:
            return piece
        size = piece.shape[-1]
        tiled = jnp.tile(piece, (1,) * (piece.ndim - 1) + (repeats,))
        at = lax.broadcasted_iota(jnp.int32, tiled.shape, tiled.ndim - 1) // size
        return jnp.where(at == q % repeats, tiled, jnp.zeros_like(tiled))

    segs = placed(segment_ids, plan.sr)
    norms = placed(jnp.concatenate([norm_gain, norm_bias], 0), plan.nr)
    rows = plan.spack
    at = lax.broadcasted_iota(jnp.int32, (rows, plan.FFn), 0)
    small = jnp.pad(norms, ((0, rows - 8), (0, plan.FFn - plan.nw)))
    small = jnp.where(at == 8, mid_gain[None], jnp.where(at == 9, mid_bias[None], small))
    taps = jnp.pad(depth_weight, ((10, rows - 10 - depth_weight.shape[0]), (0, 0)))
    small = jnp.where(at >= 10, taps, small)
    weights = [None] * WEIGHTS
    weights[GLU], weights[CONV], weights[LEFT] = glu_weight, conv_weight, left_weight
    weights[POINT], weights[QKV], weights[OUT] = point_weight, qkv_weight, out_weight
    weights[FIN], weights[FOUT] = ffn_in, ffn_out

    shapes = []
    plan.buffers(shapes.append)
    out_shape = [jax.ShapeDtypeStruct(inputs.shape, BF16)] * 2
    out_shape += [jax.ShapeDtypeStruct(plan.piece(w, plan.kr(w)), BF16) for w in range(WEIGHTS)]
    out_shape += [jax.ShapeDtypeStruct((32, plan.FF // 2), BF16)]
    hbm = pl.BlockSpec(memory_space=pl.ANY)
    got = pl.pallas_call(
        lambda *refs: kernel(plan, *refs),
        out_shape=out_shape,
        in_specs=[hbm] * INPUTS,
        out_specs=[hbm] * OUTPUTS,
        scratch_shapes=shapes,
        compiler_params=pltpu.CompilerParams(
            collective_id=0, has_side_effects=True, vmem_limit_bytes=64 << 20
        ),
        name="cell",
    )(inputs, segs, cotangent, small, *weights)
    out = unpacked(plan, got)
    return (
        out[0],
        out[1],
        out[2 + WEIGHTS],
        out[3 + WEIGHTS],
        out[2 + GLU],
        out[2 + LEFT],
        out[2 + CONV],
        out[4 + WEIGHTS].reshape(-1),
        out[5 + WEIGHTS].reshape(-1),
        out[6 + WEIGHTS],
        out[2 + POINT],
        out[2 + QKV],
        out[2 + OUT],
        out[2 + FIN],
        out[2 + FOUT],
    )


def unpacked(plan, parts):
    count = 2 + WEIGHTS
    dn = plan.D // plan.n
    wide = [jax.ShapeDtypeStruct(p.shape, F32) for p in parts[:count]]
    conv, qkv, H = 2 + CONV, 2 + QKV, plan.HALF
    wide[conv] = jax.ShapeDtypeStruct((3, plan.kr(CONV), H), F32)
    tiny = [(4, dn), (4, dn), (1, plan.FFn), (1, plan.FFn), (9, plan.FFn)]
    out_shape = wide + [jax.ShapeDtypeStruct(shape, F32) for shape in tiny]

    def body(*refs):
        ins, outs = refs[:count], refs[count + 1 : 2 * count + 1]
        sums, tinies = refs[count], refs[2 * count + 1 : 2 * count + 6]
        near, far = refs[2 * count + 6 : 3 * count + 6], refs[3 * count + 6 : 4 * count + 6]
        came, went = refs[4 * count + 6], refs[4 * count + 7]

        def arrive(i):
            return pltpu.make_async_copy(ins[i], near[i], came.at[i])

        def leave(i):
            return pltpu.make_async_copy(far[i], outs[i], went.at[i])

        for i in range(count):
            arrive(i).start()
        q = lax.axis_index("seq")
        whole = jnp.concatenate([sums[0:16].astype(F32), sums[16:32].astype(F32)], axis=1)
        rolled = pltpu.roll(whole, (plan.FF - q * plan.FFn) % plan.FF, 1)[:, 0 : plan.FFn]
        tinies[2][...] = rolled[0:1]
        tinies[3][...] = rolled[1:2]
        tinies[4][...] = rolled[2:11]
        for k in range(2):
            row = whole[11 + k : 12 + k]
            rows = [row[:, i * plan.D : (i + 1) * plan.D] for i in range(4)]
            both = jnp.concatenate(rows + rows, axis=0)
            tinies[k][...] = pltpu.roll(both, (plan.D - q * dn) % plan.D, 1)[0:4, 0:dn]
        for i in range(count):
            arrive(i).wait()
            if i == conv:
                for k in range(3):
                    far[i][k] = near[i][:, k * H : (k + 1) * H].astype(F32)
            elif i == qkv:
                for k in range(12):
                    to = (k % 3) * plan.D + k // 3 * 128
                    far[i][:, to : to + 128] = near[i][:, k * 128 : (k + 1) * 128].astype(F32)
            else:
                far[i][...] = near[i][...].astype(F32)
            leave(i).start()
        for i in range(count):
            leave(i).wait()

    hbm = pl.BlockSpec(memory_space=pl.ANY)
    vmem = pl.BlockSpec(memory_space=pltpu.VMEM)
    return pl.pallas_call(
        body,
        out_shape=out_shape,
        in_specs=[hbm] * count + [vmem],
        out_specs=[hbm] * count + [vmem] * len(tiny),
        scratch_shapes=[pltpu.VMEM(p.shape, BF16) for p in parts[:count]]
        + [pltpu.VMEM(shape.shape, F32) for shape in wide]
        + [pltpu.SemaphoreType.DMA((count,))] * 2,
        compiler_params=pltpu.CompilerParams(vmem_limit_bytes=64 << 20),
    )(*parts)


def solution(mesh):
    in_specs = (
        P("dp", "seq", None),
        P("dp", "seq"),
        P("dp", "seq", None),
        P(None, "seq"),
        P(None, "seq"),
        P("seq", None),
        P("seq", None),
        P(None, "seq", None),
        P("seq"),
        P("seq"),
        P(None, "seq"),
        P("seq", None),
        P("seq", None),
        P("seq", None),
        P("seq", None),
        P("seq", None),
    )
    out_specs = (
        P("dp", "seq", None),
        P("dp", "seq", None),
        P(None, "seq"),
        P(None, "seq"),
        P("seq", None),
        P("seq", None),
        P(None, "seq", None),
        P("seq"),
        P("seq"),
        P(None, "seq"),
        P("seq", None),
        P("seq", None),
        P("seq", None),
        P("seq", None),
        P("seq", None),
    )
    return jax.shard_map(local, mesh=mesh, in_specs=in_specs, out_specs=out_specs, check_vma=False)
```

```python
import math

import jax
import jax.numpy as jnp
from jax import lax
from jax.experimental import pallas as pl
from jax.experimental.pallas import tpu as pltpu
from jax.sharding import PartitionSpec as P

HEADS = 8
EPS = 1e-06
MESH = pl.DeviceIdType.MESH
F32 = jnp.float32
BF16 = jnp.bfloat16

GLU, CONV, LEFT, POINT, QKV, OUT, FIN, FOUT = range(8)
WEIGHTS = 8
(U_GLU0, U_GLU1, U_CONV, U_LEFT0, U_LEFT1, U_POINT0, U_POINT1, U_QKV0, U_QKV1, U_OUT, U_FIN, U_FOUT, SMALL) = range(13)
UNITS = 13
UNIT_WEIGHT = (GLU, GLU, CONV, LEFT, LEFT, POINT, POINT, QKV, QKV, OUT, FIN, FOUT, WEIGHTS)
UNIT_PART = (0, 1, None, 0, 1, 0, 1, 0, 1, None, None, None, None)

SHARED = (GLU, LEFT, POINT, FIN,)
SMALLS, TOKENS = 8, 9
START = (GLU, SMALLS, CONV, LEFT, TOKENS)
FORWARD = (
    ((1, GLU),),
    (),
    ((1, CONV),),
    ((1, LEFT), (2, GLU), (0, POINT), (2, CONV), (2, LEFT), (0, QKV), (3, GLU), (1, POINT)),
    (),
    ((0, OUT),),
    ((0, FIN),),
    (),
    (),
    ((1, QKV),),
    (),
    ((3, LEFT), (2, POINT), (1, OUT)),
    (),
    ((1, FIN),),
    ((0, FOUT),),
    ((2, QKV),),
    (),
    ((2, OUT),),
    ((3, POINT), (2, FIN)),
    ((0, TOKENS),),
    (),
    (),
    (),
    (),
    ((1, FOUT),),
    (),
    (),
    ((3, FIN),),
    (),
    ((2, FOUT),),
    (),
    (),
    (),
    (),
    (),
    (),
    (),
)
SCHEDULE = (
    (),
    (),
    (),
    (U_FOUT,),
    (U_FIN,),
    (),
    (),
    (U_OUT,),
    (U_FOUT,),
    (),
    (U_FIN, U_QKV0),
    (U_OUT,),
    (U_FOUT, U_QKV1),
    (U_QKV0,),
    (),
    (U_FIN,),
    (U_POINT0, U_POINT1),
    (U_QKV0, U_QKV1),
    (U_FOUT,),
    (),
    (),
    (),
    (U_QKV1, U_POINT0),
    (),
    (),
    (U_OUT, U_FIN),
    (U_POINT1,),
    (U_POINT0, U_FOUT),
    (U_LEFT0, U_QKV1),
    (U_QKV0, U_OUT, U_POINT1, U_LEFT1),
    (),
    (U_POINT0, U_FIN),
    (),
    (U_LEFT0,),
    (U_QKV1, U_CONV, U_GLU0, U_GLU1, U_LEFT1),
)
TAIL = (
    (SMALL, U_POINT1, U_QKV0, U_LEFT0, U_OUT, U_CONV, U_POINT0, U_LEFT1, U_GLU0, U_LEFT0, U_POINT1, U_GLU1, SMALL),
    (U_CONV, U_GLU0, U_LEFT1, U_GLU1, U_LEFT0, SMALL, U_CONV, U_GLU0, U_LEFT1, U_GLU1, SMALL, U_CONV, U_GLU0, U_GLU1, SMALL, U_FOUT, U_FIN, U_OUT, U_QKV0, U_QKV1, U_POINT0, U_POINT1, U_LEFT0, U_LEFT1, U_CONV, U_GLU0, U_GLU1, SMALL),
)

MB, MW = 128, 256
TAPS = (-4, -3, -2, -1, 1, 2, 3, 4)
FAR = -(2.0**30)


def mm(a, b):
    return lax.dot_general(a, b, (((1,), (0,)), ((), ())), preferred_element_type=F32)


def mm_t(a, b):
    return lax.dot_general(a, b, (((1,), (1,)), ((), ())), preferred_element_type=F32)


def mm_tn(a, b):
    return lax.dot_general(a, b, (((0,), (0,)), ((), ())), preferred_element_type=F32)


def normed(v):
    centred = v - jnp.mean(v, axis=-1, keepdims=True)
    r = lax.rsqrt(jnp.mean(centred * centred, axis=-1, keepdims=True) + EPS)
    return centred * r, r


def gelu_both(v):
    c = math.sqrt(2.0 / math.pi)
    sq = v * v
    t = jnp.tanh(v * (c + (c * 0.044715) * sq))
    half = 0.5 * t + 0.5
    value = v * half
    slope = half + (value * (1.0 - half)) * (2.0 * c + (6.0 * c * 0.044715) * sq)
    return value, slope


def sigmoid(v):
    return 0.5 * jnp.tanh(0.5 * v) + 0.5


class Buffers:
    pass


class Plan:
    def __init__(self, dp, n, seqs, span, width, hidden, half):
        self.n, self.Z = n, dp // 2
        self.S, self.span = seqs, span
        self.D, self.FF, self.HALF = width, hidden, half
        self.LEN = span * n
        self.T = self.LEN // 2
        self.PH = n // 2
        self.B = math.isqrt(n)
        self.A = n // self.B
        assert self.A == self.B and n == 2 * seqs and dp % 2 == 0
        self.shared = SHARED if self.Z % 2 == 0 else ()
        self.sw = max(span, 128)
        self.sr = self.sw // span
        dn = width // n
        self.nw = max(dn, 128)
        self.nr = self.nw // dn
        self.FFn = hidden // n
        self.spack = 32
        self.dims = [
            (width, 2 * width),
            (width, half),
            (width, hidden),
            (hidden, width),
            (width, 3 * width),
            (width, width),
            (width, hidden),
            (hidden, width),
        ]

    def whole(self, w):
        k, cols = self.dims[w]
        return (3, k, cols) if w == CONV else (k, cols)

    def kr(self, w):
        return self.dims[w][0] // self.n

    def hr(self, w):
        return self.kr(w) // 2

    def gcols(self, w):
        return self.dims[w][1] * (3 if w == CONV else 1)

    def piece(self, w, rows):
        return (rows, self.gcols(w))

    def buffers(self, take):
        T, D, FF, H, n = self.T, self.D, self.FF, self.HALF, self.n
        r = Buffers()

        def vm(shape, dtype):
            return take(pltpu.VMEM(shape, dtype))

        def sem(*shape):
            return take(pltpu.SemaphoreType.DMA(shape))

        every = range(WEIGHTS)
        parts = [(self.piece(w, self.hr(w)), BF16) for w in every] + [((16, FF // 2), BF16)]
        r.w = [vm(self.whole(w), BF16) for w in every]
        r.g8 = vm((16, FF), F32)
        r.gsm = vm((32, FF // 2), BF16)
        r.r = [None] * WEIGHTS + [vm((16, FF // 2), BF16)]
        for w in (CONV, QKV, OUT, FIN, FOUT):
            r.r[w] = vm(self.piece(w, n * self.hr(w)), BF16)
        r.r[LEFT], r.r[POINT], r.r[GLU] = r.r[FIN], r.r[FOUT], r.r[QKV]
        r.p = [vm((n - 1,) + shape, dtype) for shape, dtype in parts]
        if self.Z > 1:
            r.u = [vm(shape, dtype) for shape, dtype in parts]
            r.d = [vm(shape, dtype) for shape, dtype in parts]
        r.segbuf = vm((n, self.S, self.sw), jnp.int32)
        r.segrow = vm((8, self.LEN), F32)
        r.segcol = vm((self.LEN + 16, 128), F32)
        r.segloc = vm((T + 16, 128), F32)
        r.mext = vm((T + 16, 128), F32)
        r.ms = vm((T // MB, 8 * MB, MW), BF16)
        r.qenc = vm((T, 128), BF16)
        r.kenc = vm((self.LEN, 128), BF16)
        r.smallbuf = vm((n, self.spack, self.FFn), BF16)
        r.nrm = vm((8, D), F32)
        r.midp = vm((16, FF), F32)
        r.xin = vm((T, D), BF16)
        r.cot = vm((T, D), BF16)
        r.a1 = vm((T, D), BF16)
        r.sg = vm((T, 2 * D), BF16)
        r.y1 = vm((T, D), F32)
        r.a2 = vm((T, D), BF16)
        r.pext = vm((3, T + 16, H), F32)
        r.rgl = vm((T, H), F32)
        r.dgl = vm((T, FF), BF16)
        r.dgr = vm((T, H), BF16)
        r.nm = vm((T, FF), BF16)
        r.rm = vm((T, 1), F32)
        r.big = vm((T + 16, FF), F32)
        r.sep = vm((T, FF), BF16)
        r.y2 = vm((T, D), F32)
        r.a4 = vm((T, D), BF16)
        r.qb = vm((T, D), BF16)
        r.kvb = vm((self.LEN, 2 * D), BF16)
        r.lse = vm((T, 128), F32)
        r.ctx = vm((T, D), BF16)
        r.y3 = vm((T, D), F32)
        r.a5 = vm((T, D), BF16)
        r.hid = vm((T + 32, FF), BF16)
        r.dg = vm((T, FF), BF16)
        r.osend = vm((T, D), BF16)
        r.gs = r.y3
        r.dkvr = vm((T, 2 * D), BF16)
        r.tr = vm((D, T), BF16)
        edges = (((8, H), F32), ((16, FF), BF16), ((16, FF), BF16), ((8, H), F32))
        r.es = [vm(shape, dtype) for shape, dtype in edges]
        r.er = [vm(shape, dtype) for shape, dtype in edges]
        r.s_loc = sem(WEIGHTS)
        r.s_as = sem(WEIGHTS)
        r.s_ar = sem(WEIGHTS, self.B - 1)
        r.s_br = sem(WEIGHTS, (self.A - 1) * self.B)
        r.s_dr = sem(WEIGHTS)
        if self.shared:
            r.s_hr = sem(WEIGHTS)
        r.s_rs = sem(UNITS)
        r.s_rr = sem(UNITS)
        r.s_ps = sem(UNITS)
        r.s_pr = sem(UNITS, 2)
        if self.Z > 1:
            r.s_zs = sem(UNITS)
            r.s_zr = sem(UNITS, 2)
        r.s_fs = sem(UNITS)
        r.s_fr = sem(UNITS)
        r.s_xs = sem(4, self.S)
        r.s_xr = sem(4, max(self.PH, self.S))
        r.s_gs = sem(2 * self.S)
        r.s_gr = sem(n)
        r.s_ms = sem(n)
        r.s_mr = sem(n)
        r.s_es = sem(4)
        r.s_er = sem(4)
        r.s_ks = sem(HEADS // 2)
        r.s_kr = sem(HEADS // 2)
        r.s_js = sem(HEADS // 2)
        r.s_jr = sem(HEADS // 2)
        return r


INPUTS = 4 + WEIGHTS
OUTPUTS = 2 + WEIGHTS + 1


def kernel(plan, *refs):
    ins, outs = refs[:INPUTS], refs[INPUTS : INPUTS + OUTPUTS]
    scratch = iter(refs[INPUTS + OUTPUTS :])
    r = plan.buffers(lambda shape: next(scratch))
    r.x, r.seg, r.ct, r.small = ins[:4]
    r.h = ins[4:]
    r.o_out, r.o_ig = outs[:2]
    r.o = outs[2:]
    n, Z, S, span = plan.n, plan.Z, plan.S, plan.span
    T, D, FF, H, PH = plan.T, plan.D, plan.FF, plan.HALF, plan.PH
    A, B = plan.A, plan.B
    dp, q = lax.axis_index("dp"), lax.axis_index("seq")
    z, c = dp // 2, dp % 2
    oc = 1 - c

    def aligned(v, m=16):
        return pl.multiple_of(v, m)

    def dev(core, chip, plane=None):
        return ((z if plane is None else plane) * 2 + core, chip)

    sibling = dev(oc, q)

    def remote(src, dst, ss, rs, to):
        return pltpu.make_async_remote_copy(
            src_ref=src, dst_ref=dst, send_sem=ss, recv_sem=rs, device_id=to, device_id_type=MESH
        )

    barrier = pltpu.get_barrier_semaphore()
    for core in range(2):

        def greet(t, _, core=core):
            chip = lax.rem(q + t, n)
            to = (z * 2 + (c + core) % 2, chip)
            pl.semaphore_signal(barrier, inc=1, device_id=to, device_id_type=MESH)
            return 0

        lax.fori_loop(1 - core, n, greet, 0)
    if Z > 1:

        @pl.when(z > 0)
        def _():
            pl.semaphore_signal(barrier, inc=1, device_id=dev(c, q, z - 1), device_id_type=MESH)

        @pl.when(z < Z - 1)
        def _():
            pl.semaphore_signal(barrier, inc=1, device_id=dev(c, q, z + 1), device_id_type=MESH)

    pl.semaphore_wait(barrier, 2 * n - 1 + (z + Z - 1) // Z + (2 * Z - 2 - z) // Z)

    def vrows(ref, w, row0, rows):
        ds = pl.ds(aligned(row0), rows)
        return ref.at[:, ds] if w == CONV else ref.at[ds]

    def bytes_of(view, semaphore):
        return pltpu.make_async_copy(view, view, semaphore)

    def qof(core, f, g):
        f, g = f % B, g % B
        return core * (f * B + g) + (1 - core) * (g * B + f)

    b_, a_ = q % B, q // B
    f_, g_ = c * a_ + oc * b_, c * b_ + oc * a_
    par = z % 2
    partner = dev(c, q, z + 1 - 2 * par)

    def wrows(ref, w, row0, rows, side):
        if w not in plan.shared:
            return vrows(ref, w, row0, rows)
        size = plan.dims[w][1] // 2
        cols = pl.ds(pl.multiple_of(side * size, 128), size)
        if w == CONV:
            return ref.at[:, pl.ds(aligned(row0), rows), cols]
        return ref.at[pl.ds(aligned(row0), rows), cols]

    def wblock(w, shard, side=par):
        return wrows(r.w[w], w, shard * plan.kr(w) + c * plan.hr(w), plan.hr(w), side)

    def own_block(w):
        return wrows(r.h[w], w, c * plan.hr(w), plan.hr(w), par)

    def copy_a(w, t):
        to = dev(c, qof(c, f_ + t, g_))
        return remote(own_block(w), wblock(w, q), r.s_as.at[w], r.s_ar.at[w, t - 1], to)

    def copy_b(w, u, t):
        blk = wblock(w, qof(c, f_ + B - t, g_))
        src = own_block(w) if t == 0 else blk
        to = dev(c, qof(c, f_, g_ + u))
        return remote(src, blk, r.s_as.at[w], r.s_br.at[w, (u - 1) * B + t], to)

    def shard_from(u, t):
        return qof(c, f_ + B - t, g_ + B - u)

    def pass_on(w, u, t):
        blk = wblock(w, shard_from(u, t))
        remote(blk, blk, r.s_as.at[w], r.s_dr.at[w], sibling).start()
        if w in plan.shared:
            remote(blk, blk, r.s_as.at[w], r.s_hr.at[w], partner).start()

    def local_shard(w):
        dst = vrows(r.w[w], w, q * plan.kr(w), plan.kr(w))
        return pltpu.make_async_copy(r.h[w], dst, r.s_loc.at[w])

    def g0(w):
        local_shard(w).start()
        for t in range(1, B):
            copy_a(w, t).start()
        for u in range(1, A):
            copy_b(w, u, 0).start()

    def g1(w):
        for t in range(1, B):
            bytes_of(wblock(w, shard_from(0, t)), r.s_ar.at[w, t - 1]).wait()
            for u in range(1, A):
                copy_b(w, u, t).start()
            pass_on(w, 0, t)

    def g2(w):
        for u in range(1, A):
            for t in range(B):
                bytes_of(wblock(w, shard_from(u, t)), r.s_br.at[w, (u - 1) * B + t]).wait()
                pass_on(w, u, t)

    def others(w):
        return wrows(r.w[w], w, 0, (n - 1) * plan.hr(w), 0)

    def gz(w):
        if w not in plan.shared:
            return
        bytes_of(others(w), r.s_hr.at[w]).wait()
        for u in range(A):
            for t in range(B):
                if (u, t) != (0, 0):
                    blk = wblock(w, shard_from(u, t), 1 - par)
                    remote(blk, blk, r.s_as.at[w], r.s_dr.at[w], sibling).start()

    def g3(w):
        local_shard(w).wait()
        bytes_of(vrows(r.w[w], w, 0, (n - 1) * plan.hr(w)), r.s_dr.at[w]).wait()

    gather_steps = (g0, g1, g2, gz)
    forward_turns = iter(FORWARD)

    def gather(steps):
        for k, w in steps:
            if w == TOKENS:
                tokens_in(r.ct, r.cot, 1)
            else:
                gather_steps[k](w)

    def pass_turn():
        gather(next(forward_turns))

    def pass_turns(count):
        every = [(k, next(forward_turns)) for k in range(count)]
        return [(k, lambda steps=steps: gather(steps)) for k, steps in every if steps]

    def gather_sent(w):
        bytes_of(vrows(r.w[w], w, 0, 2 * (n - 1) * plan.hr(w)), r.s_as.at[w]).wait()

    def token_rows(ref, slot):
        return ref.at[pl.ds(aligned(slot * span), span)]

    def tokens_in(src, dst, k):
        for j in range(S):
            chip, core, slot = S * c + j, q // PH, q % PH
            here = jnp.logical_and(chip == q, core == c)
            there = token_rows(dst, slot)

            @pl.when(here)
            def _():
                pltpu.make_async_copy(src.at[j], there, r.s_xr.at[k, slot]).start()

            @pl.when(jnp.logical_not(here))
            def _():
                remote(
                    src.at[j], there, r.s_xs.at[k, j], r.s_xr.at[k, slot], dev(core, chip)
                ).start()

    def tokens_in_done(dst, k):
        for slot in range(PH):
            blk = token_rows(dst, slot)
            pltpu.make_async_copy(blk, blk, r.s_xr.at[k, slot]).wait()

    def tokens_in_sent(src, dst, k):
        for j in range(S):
            chip, core, slot = S * c + j, q // PH, q % PH
            here = jnp.logical_and(chip == q, core == c)

            @pl.when(jnp.logical_not(here))
            def _():
                remote(
                    src.at[j],
                    token_rows(dst, slot),
                    r.s_xs.at[k, j],
                    r.s_xr.at[k, slot],
                    dev(core, chip),
                ).wait_send()

    def tokens_out(src, dst, k):
        for p in range(PH):
            chip, core, slot = c * PH + p, q // S, q % S
            here = jnp.logical_and(chip == q, core == c)

            @pl.when(here)
            def _():
                pltpu.make_async_copy(token_rows(src, p), dst.at[slot], r.s_xr.at[k, slot]).start()

            @pl.when(jnp.logical_not(here))
            def _():
                remote(
                    token_rows(src, p),
                    dst.at[slot],
                    r.s_xs.at[k, p],
                    r.s_xr.at[k, slot],
                    dev(core, chip),
                ).start()

    def tokens_out_done(src, dst, k):
        for j in range(S):
            pltpu.make_async_copy(dst.at[j], dst.at[j], r.s_xr.at[k, j]).wait()
        for p in range(PH):
            chip, core, slot = c * PH + p, q // S, q % S
            here = jnp.logical_and(chip == q, core == c)

            @pl.when(jnp.logical_not(here))
            def _():
                remote(
                    token_rows(src, p),
                    dst.at[slot],
                    r.s_xs.at[k, p],
                    r.s_xr.at[k, slot],
                    dev(core, chip),
                ).wait_send()

    def seg_send():
        for j in range(S):
            for core in range(2):
                chip = S * c + j
                here = jnp.logical_and(chip == q, c == core)
                i = 2 * j + core

                @pl.when(here)
                def _():
                    pltpu.make_async_copy(r.seg, r.segbuf.at[q], r.s_gr.at[q]).start()

                @pl.when(jnp.logical_not(here))
                def _():
                    remote(
                        r.seg,
                        r.segbuf.at[q],
                        r.s_gs.at[i],
                        r.s_gr.at[q],
                        dev(core, chip),
                    ).start()

    def seg_sent():
        for j in range(S):
            for core in range(2):
                chip = S * c + j
                here = jnp.logical_and(chip == q, c == core)

                @pl.when(jnp.logical_not(here))
                def _():
                    remote(
                        r.seg,
                        r.segbuf.at[q],
                        r.s_gs.at[2 * j + core],
                        r.s_gr.at[q],
                        dev(core, chip),
                    ).wait_send()

    def small_copy(t):
        return remote(
            r.small,
            r.smallbuf.at[q],
            r.s_ms.at[t],
            r.s_mr.at[t],
            dev(c, (q + t) % n),
        )

    def small_arrived(t):
        blk = r.smallbuf.at[(q + n - t) % n]
        return remote(blk, blk, r.s_ms.at[t], r.s_mr.at[t], sibling)

    def edge_copy(i):
        return remote(r.es[i], r.er[i], r.s_es.at[i], r.s_er.at[i], sibling)

    def edge_send(i, last, first):
        r.es[i][...] = jnp.where(c == 0, last, first)
        edge_copy(i).start()

    def edge_take(i):
        edge_copy(i).wait()
        got = r.er[i][...]
        none = jnp.zeros_like(got)
        return jnp.where(c == 1, got, none), jnp.where(c == 0, got, none)

    def columns(u):
        w, half = UNIT_WEIGHT[u], UNIT_PART[u]
        size = plan.gcols(w)
        return (0, size) if half is None else (half * (size // 2), size // 2)

    def urows(ref, u, row0, rows, shift=0):
        col0, size = columns(u)
        return ref.at[pl.ds(aligned(row0), rows), pl.ds(col0 + shift, size)]

    grad_home = {GLU: (r.hid, 2 * D), CONV: (r.dkvr, 0), LEFT: (r.sep, 0), QKV: (r.dg, 0)}

    def gpiece(u, shard, half):
        if u == SMALL:
            return r.gsm.at[pl.ds(pl.multiple_of(half * 16, 16), 16)]
        w = UNIT_WEIGHT[u]
        ref, shift = grad_home.get(w, (r.w[w] if w < WEIGHTS else None, 0))
        return urows(ref, u, shard * plan.kr(w) + half * plan.hr(w), plan.hr(w), shift)

    def rpiece(u, shard):
        w = UNIT_WEIGHT[u]
        if u == SMALL:
            return r.r[w]
        return urows(r.r[w], u, shard * plan.hr(w), plan.hr(w))

    def slots(u, first, count):
        buf = r.p[UNIT_WEIGHT[u]]
        if u == SMALL:
            return buf.at[pl.ds(first, count)]
        col0, size = columns(u)
        return buf.at[pl.ds(first, count), :, pl.ds(col0, size)]

    def ppiece(u, slot):
        buf = r.p[UNIT_WEIGHT[u]]
        if u == SMALL:
            return buf.at[slot]
        col0, size = columns(u)
        return buf.at[slot, :, pl.ds(col0, size)]

    def zpiece(u, way):
        buf = (r.u, r.d)[way][UNIT_WEIGHT[u]]
        if u == SMALL:
            return buf
        col0, size = columns(u)
        return buf.at[:, pl.ds(col0, size)]

    def copy_r(u, s):
        return remote(gpiece(u, s, oc), rpiece(u, s), r.s_rs.at[u], r.s_rr.at[u], sibling)

    def all_r(u, semaphore):
        w = UNIT_WEIGHT[u]
        view = r.r[w] if u == SMALL else urows(r.r[w], u, 0, n * plan.hr(w))
        return bytes_of(view, semaphore.at[u])

    def shards(u):
        return 1 if u == SMALL else n

    def red0(u):
        for s in range(shards(u)):
            copy_r(u, s).start()

    def put(to, *terms):
        size = to.shape[0]
        rows = min(size, 64)

        def some(i, _):
            at = pl.ds(pl.multiple_of(i * rows, rows), rows)
            total = terms[0][at].astype(F32)
            for term in terms[1:]:
                total = total + term[at].astype(F32)
            to[at] = total.astype(to.dtype)
            return 0

        lax.fori_loop(0, size // rows, some, 0)

    def add_core(u, s):
        mine = gpiece(u, s, c)
        put(mine, mine, rpiece(u, s))

    def slot1(u, t):
        return (u - 1) * B + t

    def slot2(t):
        return (A - 1) * B + t - 1

    def copy_p1(u, k, t):
        return remote(
            gpiece(u, qof(c, f_ + t, g_ + k), c),
            ppiece(u, slot1(k, t)),
            r.s_ps.at[u],
            r.s_pr.at[u, 0],
            dev(c, qof(c, f_, g_ + k)),
        )

    def copy_p2(u, t):
        to = qof(c, f_ + t, g_)
        return remote(
            r.r[WEIGHTS] if u == SMALL else gpiece(u, to, c),
            ppiece(u, slot2(t)),
            r.s_ps.at[u],
            r.s_pr.at[u, 1],
            dev(c, to),
        )

    def all_p(u, step, semaphore):
        count = B - 1 if step else A - 1 if u == SMALL else (A - 1) * B
        return bytes_of(slots(u, 0, count), semaphore.at[u, step])

    def red1(u):
        all_r(u, r.s_rr).wait()
        if u == SMALL:
            add_core(u, 0)
            for k in range(1, A):
                copy_p1(u, k, 0).start()
            return

        def send(i, _):
            k, t = i // B + 1, i % B
            add_core(u, qof(c, f_ + t, g_ + k))
            copy_p1(u, k, t).start()
            return 0

        lax.fori_loop(0, (A - 1) * B, send, 0)
        lax.fori_loop(0, B, lambda t, _: (add_core(u, qof(c, f_ + t, g_)), 0)[1], 0)

    def red1b(u):
        all_p(u, 0, r.s_pr).wait()

        def send(t, _):
            mine = gpiece(u, 0 if u == SMALL else qof(c, f_ + t, g_), c)
            came = [ppiece(u, slot1(k, 0 if u == SMALL else t)) for k in range(1, A)]
            put(r.r[WEIGHTS] if u == SMALL else mine, mine, *came)
            if u != SMALL:
                copy_p2(u, t).start()
            return 0

        if u == SMALL:
            send(0, 0)
            for t in range(1, B):
                copy_p2(u, t).start()
        else:
            lax.fori_loop(1, B, send, 0)

    def red2(u):
        all_p(u, 1, r.s_pr).wait()
        came = [] if u == SMALL else [ppiece(u, slot1(k, 0)) for k in range(1, A)]
        came += [ppiece(u, slot2(t)) for t in range(1, B)]
        put(ppiece(u, 0), r.r[WEIGHTS] if u == SMALL else gpiece(u, q, c), *came)

    def copy_z(u, way):
        return remote(
            ppiece(u, 1 + way),
            zpiece(u, way),
            r.s_zs.at[u],
            r.s_zr.at[u, way],
            dev(c, q, z + 1 if way == 0 else z - 1),
        )

    def red_hop(u, h):
        own, up, down = ppiece(u, 0), ppiece(u, 1), ppiece(u, 2)

        @pl.when(z == h)
        def _():
            if h == 0:
                put(up, own)
            else:
                copy_z(u, 0).wait_recv()
                put(up, own, zpiece(u, 0))
            if h < Z - 1:
                copy_z(u, 0).start()

        @pl.when(z == Z - 1 - h)
        def _():
            if h == 0:
                put(down, own)
            else:
                copy_z(u, 1).wait_recv()
                if h < Z - 1:
                    put(down, own, zpiece(u, 1))
            if h < Z - 1:
                copy_z(u, 1).start()

    def final_rows(u):
        w = UNIT_WEIGHT[u]
        if u == SMALL:
            return r.o[w].at[pl.ds(pl.multiple_of(c * 16, 16), 16)]
        return urows(r.o[w], u, c * plan.hr(w), plan.hr(w))

    def final_local(u):
        return pltpu.make_async_copy(ppiece(u, 0), final_rows(u), r.s_fs.at[u])

    def final_remote(u):
        return remote(ppiece(u, 0), final_rows(u), r.s_fs.at[u], r.s_fr.at[u], sibling)

    def red_final(u):
        if Z > 1:
            own, up = ppiece(u, 0), ppiece(u, 1)

            @pl.when(z == Z - 1)
            def _():
                put(own, up)

            @pl.when(z < Z - 1)
            def _():
                put(own, up, zpiece(u, 1))

        final_local(u).start()
        final_remote(u).start()

    def red_end(u):
        final_remote(u).wait_recv()
        bytes_of(slots(u, 0, 2), r.s_fs.at[u]).wait()
        all_r(u, r.s_rs).wait()
        bytes_of(slots(u, 0, A + B - 2 if u == SMALL else n - 1), r.s_ps.at[u]).wait()
        if Z > 1:
            ends = jnp.logical_or(z == 0, z == Z - 1)

            @pl.when(ends)
            def _():
                bytes_of(slots(u, 0, 1), r.s_zs.at[u]).wait()

            @pl.when(jnp.logical_not(ends))
            def _():
                bytes_of(slots(u, 0, 2), r.s_zs.at[u]).wait()

    def red2_hop(u):
        red2(u)
        red_hop(u, 0)

    def last_hop(u):
        red_hop(u, Z - 1)
        red_final(u)

    ahead = {}
    turns = iter(SCHEDULE)

    def enlist(u):
        if Z > 1:
            ahead[u] = [red1, red1b, red2_hop]
            ahead[u] += [lambda k, h=h: red_hop(k, h) for h in range(1, Z - 1)]
            ahead[u].append(last_hop)
        else:
            ahead[u] = [red1, red1b, red2, red_final]

    def reduce_start(*units):
        for u in units:
            red0(u)
            enlist(u)

    def steps_of(units):
        return [(ahead[u].pop(0), u) for u in units if ahead[u]]

    def move(units):
        for step, u in steps_of(units):
            step(u)

    def turn():
        move(next(turns))

    def turns_of(count):
        acts = []
        for k in range(count):
            steps = steps_of(next(turns))
            if steps:
                acts.append((k, lambda steps=steps: [step(u) for step, u in steps][:0]))
        return acts

    def loop(count, body, after=()):
        def step(i, _):
            body(i)
            for k, act in after:
                pl.when(i == k)(lambda act=act: (act(), None)[1])
            return 0

        lax.fori_loop(0, count, step, 0)

    RB = 256
    NB = T // RB

    def rows_of(i, size=RB, base=0):
        return pl.ds(pl.multiple_of(i * size + base, base or size), size)

    seg_send()
    small_local = pltpu.make_async_copy(r.small, r.smallbuf.at[q], r.s_mr.at[0])
    small_local.start()
    for what in START:
        if what == SMALLS:
            for t in range(1, n):
                small_copy(t).start()
        elif what == TOKENS:
            tokens_in(r.x, r.xin, 0)
        else:
            g0(what)
    r.g8[...] = jnp.zeros((16, FF), F32)
    pass_turn()

    for s in range(n):
        blk = r.segbuf.at[s]
        pltpu.make_async_copy(blk, blk, r.s_gr.at[s]).wait()
    mine = lax.broadcasted_iota(jnp.int32, (S, plan.sw), 0) == lax.rem(q, S)
    for grp in range(n // plan.sr):
        got = r.segbuf[grp * plan.sr]
        for k in range(1, plan.sr):
            got = got + r.segbuf[grp * plan.sr + k]
        row = jnp.sum(jnp.where(mine, got.astype(F32), 0.0), axis=0, keepdims=True)
        r.segrow[0:1, grp * plan.sw : (grp + 1) * plan.sw] = row
    r.segcol[0:8] = jnp.full((8, 128), -1.0, F32)
    r.segcol[plan.LEN + 8 : plan.LEN + 16] = jnp.full((8, 128), -1.0, F32)
    for k in range(plan.LEN // 128):
        row = r.segrow[0:1, k * 128 : (k + 1) * 128]
        r.segcol[8 + k * 128 : 8 + (k + 1) * 128] = jnp.broadcast_to(row, (128, 128)).T
    r.segloc[...] = r.segcol[pl.ds(pl.multiple_of(c * T, 8), T + 16)]
    r.mext[0 : T + 8] = jnp.where(r.segloc[0 : T + 8] == r.segloc[1 : T + 9], 1.0, 0.0)

    def mask(o, start, rows):
        first = 8 + start + (0 if o > 0 else o)
        return r.mext[first : first + rows]

    small_local.wait()
    for t in range(1, n):
        small_arrived(t).wait_recv()
    for grp in range(n // plan.nr):
        got = r.smallbuf[grp * plan.nr].astype(F32)
        for k in range(1, plan.nr):
            got = got + r.smallbuf[grp * plan.nr + k].astype(F32)
        r.nrm[:, grp * plan.nw : (grp + 1) * plan.nw] = got[0:8, 0 : plan.nw]
    for s in range(n):
        rows = r.smallbuf[s].astype(F32)[8:19]
        r.midp[0:11, s * plan.FFn : (s + 1) * plan.FFn] = rows

    def ln_out(k, v):
        unit, _ = normed(v)
        return (unit * r.nrm[k : k + 1] + r.nrm[4 + k : 5 + k]).astype(BF16)

    def ln_back(k, e, v):
        unit, rs = normed(v)
        eg = e * r.nrm[k : k + 1]
        m1 = jnp.mean(eg, axis=-1, keepdims=True)
        m2 = jnp.mean(eg * unit, axis=-1, keepdims=True)
        cols = slice(k * D, (k + 1) * D)
        r.g8[11:12, cols] += jnp.sum(e * unit, axis=0, keepdims=True)
        r.g8[12:13, cols] += jnp.sum(e, axis=0, keepdims=True)
        return rs * (eg - m1 - unit * m2)

    pass_turn()

    def window(b):
        return min(max(b * MB - (MW - MB) // 2 + 16, 0), T + 32 - MW)

    ahead_of = lax.broadcasted_iota(jnp.int32, (MB, MW), 1) - lax.broadcasted_iota(
        jnp.int32, (MB, MW), 0
    )
    def shift_matrices(b):
        near = r.segloc[pl.ds(pl.multiple_of(b * MB, MB), MB + 16)]
        home = near[8 : MB + 8]
        first = jnp.where(b == 0, 16, jnp.where(b == T // MB - 1, MW - MB - 16, (MW - MB) // 2))
        for i, o in enumerate(TAPS):
            same = jnp.where(home == near[8 + o : MB + 8 + o], 1.0, 0.0)
            tap = jnp.where(
                ahead_of == first + o, jnp.concatenate([same] * (MW // 128), axis=1), 0.0
            )
            r.ms[b, i * MB : (i + 1) * MB] = tap.astype(BF16)

    loop(T // MB, shift_matrices)

    lane = lax.broadcasted_iota(jnp.int32, (1, 128), 1)
    lane_f = lane.astype(F32)
    own_doc = r.segloc[8 : T + 8] == lane_f
    r.qenc[...] = jnp.where(jnp.logical_and(lane < 4, jnp.logical_not(own_doc)), FAR, 0.0).astype(BF16)
    ones = jnp.logical_and(lane >= 4, lane < 7)
    r.kenc[...] = jnp.where(
        jnp.logical_or(r.segcol[8 : plan.LEN + 8] == lane_f, ones), 1.0, 0.0
    ).astype(BF16)

    pass_turn()
    pass_turn()
    g3(GLU)
    pass_turn()
    tokens_in_done(r.xin, 0)

    def glu(i):
        rows = rows_of(i)
        x = r.xin[rows].astype(F32)
        a1 = ln_out(0, x)
        r.a1[rows] = a1
        value = mm(a1, r.w[GLU][:, 0:D])
        gate = sigmoid(mm(a1, r.w[GLU][:, D : 2 * D]))
        r.sg[rows, 0:D] = gate.astype(BF16)
        r.sg[rows, D : 2 * D] = (value * gate * (1.0 - gate)).astype(BF16)
        y1 = x + value * gate
        r.y1[rows] = y1
        r.a2[rows] = ln_out(1, y1)

    loop(NB, glu, pass_turns(NB))
    pass_turn()
    g3(CONV)

    def conv(i):
        i = c * i + oc * (NB - 1 - i)
        a2 = r.a2[rows_of(i)]
        for o in range(3):
            r.pext[o, rows_of(i, RB, 8)] = mm(a2, r.w[CONV][o])

    def right(k):
        lo = k * 128
        before = mask(-1, lo, 128)
        after = mask(1, lo, 128)
        pre = (
            r.pext[0, lo + 7 : lo + 135] * jnp.concatenate([before] * (H // 128), axis=1)
            + r.pext[1, lo + 8 : lo + 136]
            + r.pext[2, lo + 9 : lo + 137] * jnp.concatenate([after] * (H // 128), axis=1)
        )
        value, slope = gelu_both(pre)
        r.rgl[lo : lo + 128] = value
        r.dgr[lo : lo + 128] = slope.astype(BF16)

    edge = (0, lambda: edge_send(0, r.pext[0, T : T + 8], r.pext[2, 8:16]))
    loop(NB, conv, [edge])
    pass_turn()
    blocks = range(T // 128)
    for k in blocks[1:-1]:
        right(k)
    pass_turn()
    top, bottom = edge_take(0)
    r.pext[0, 0:8] = top
    r.pext[2, T + 8 : T + 16] = bottom
    right(blocks[0])
    right(blocks[-1])
    pass_turn()
    pass_turn()
    g3(LEFT)

    CH = 512
    RM = 128

    def inner_first(i, count):
        return c * i + oc * (count - 1 - i)

    def left(i):
        i = inner_first(i, T // RM)
        rows, erows = rows_of(i, RM), rows_of(i, RM, 8)
        a2 = r.a2[rows]
        for k in range(FF // CH):
            value, slope = gelu_both(mm(a2, r.w[LEFT][:, k * CH : (k + 1) * CH]))
            r.dgl[rows, k * CH : (k + 1) * CH] = slope.astype(BF16)
            r.big[erows, k * CH : (k + 1) * CH] = value
        r.big[erows, 0:H] += r.rgl[rows]
        unit, rs = normed(r.big[erows])
        r.nm[rows] = unit.astype(BF16)
        r.rm[rows] = rs
        r.hid[rows_of(i, RM, 16)] = (unit * r.midp[0:1] + r.midp[1:2]).astype(BF16)

    edge = (0, lambda: edge_send(1, r.hid[T : T + 16], r.hid[16:32]))
    loop(T // RM, left, [edge] + pass_turns(T // RM))
    r.hid[0:16], r.hid[T + 16 : T + 32] = edge_take(1)
    pass_turn()

    def depthwise(j):
        cols = pl.ds(pl.multiple_of(j * 512, 512), 512)
        for b in range(T // MB):
            near = r.hid[window(b) : window(b) + MW, cols]
            taps = mm(r.ms[b], near)
            total = r.hid[16 + b * MB : 16 + (b + 1) * MB, cols].astype(F32) * r.midp[6:7, cols]
            for i, o in enumerate(TAPS):
                total = total + taps[i * MB : (i + 1) * MB] * r.midp[6 + o : 7 + o, cols]
            r.sep[b * MB : (b + 1) * MB, cols] = total.astype(BF16)

    loop(FF // 512, depthwise, pass_turns(FF // 512))
    pass_turn()
    g3(POINT)

    def point(i):
        rows = rows_of(i, T)
        y2 = r.y1[rows] + mm(r.sep[rows], r.w[POINT][...])
        r.y2[rows] = y2
        r.a4[rows] = ln_out(2, y2)

    loop(1, point)
    pass_turn()
    pass_turn()
    g3(QKV)
    scale = 1.0 / math.sqrt(D // HEADS)

    def keys_values(i):
        rows = rows_of(i)
        a4 = r.a4[rows]
        here = pl.ds(pl.multiple_of(c * T + i * RB, RB), RB)
        r.kvb[here, 0:D] = mm(a4, r.w[QKV][:, D : 2 * D]).astype(BF16)
        r.kvb[here, D : 2 * D] = mm(a4, r.w[QKV][:, 2 * D : 3 * D]).astype(BF16)

    def queries(i):
        rows = rows_of(i)
        r.qb[rows] = (mm(r.a4[rows], r.w[QKV][:, 0:D]) * scale).astype(BF16)

    def kv_copy(j, base):
        blk = r.kvb.at[pl.ds(aligned(c * T), T), pair_cols(j, base)]
        return remote(blk, blk, r.s_ks.at[j], r.s_kr.at[j], sibling)

    def pair_cols(j, base=0):
        return pl.ds(pl.multiple_of(j * 128 + base, 128), 128)

    def pair_bytes(j, semaphore):
        return bytes_of(r.kvb.at[pl.ds(0, T), pl.ds(0, 256)], semaphore.at[j])

    loop(NB, keys_values)
    for j in range(HEADS // 2):
        kv_copy(j, 0).start()
        kv_copy(j, D).start()
    loop(NB, queries)
    pass_turn()
    pass_turn()
    heads_lanes = [lane < 64, lane >= 64]
    def head_lanes(e, v):
        return jnp.where(heads_lanes[e], v, jnp.zeros_like(v))

    def attend(j):
        pair_bytes(j, r.s_kr).wait()
        cols, vcols = pair_cols(j), pair_cols(j, D)
        keys = jnp.concatenate([r.kvb[:, cols], r.kenc[...]], axis=1)
        for k in range(T // RB):
            rows = slice(k * RB, (k + 1) * RB)
            q2 = r.qb[rows, cols]
            got = []
            for e in range(2):
                score = mm_t(jnp.concatenate([head_lanes(e, q2), r.qenc[rows]], axis=1), keys)
                most = jnp.max(score, axis=-1, keepdims=True)
                power = jnp.exp(score - most)
                total = jnp.sum(power, axis=-1, keepdims=True)
                got.append(mm(power.astype(BF16), r.kvb[:, vcols]) / total)
                lse = most + jnp.log(total)
                r.lse[rows] = jnp.where(lane == 2 * j + e, lse, r.lse[rows])
            r.ctx[rows, cols] = jnp.where(heads_lanes[0], got[0], got[1]).astype(BF16)

    r.lse[...] = jnp.zeros((T, 128), F32)

    loop(HEADS // 2, attend, pass_turns(HEADS // 2))
    pass_turn()
    g3(OUT)

    def out(i):
        rows = rows_of(i, T)
        y3 = r.y2[rows] + mm(r.ctx[rows], r.w[OUT][...])
        r.y3[rows] = y3
        r.a5[rows] = ln_out(3, y3)

    loop(1, out)
    pass_turn()
    pass_turn()
    g3(FIN)

    def ffn_in(i):
        rows = rows_of(i)
        a5 = r.a5[rows]
        for k in range(FF // CH):
            value, slope = gelu_both(mm(a5, r.w[FIN][:, k * CH : (k + 1) * CH]))
            r.hid[rows, k * CH : (k + 1) * CH] = value.astype(BF16)
            r.dg[rows, k * CH : (k + 1) * CH] = slope.astype(BF16)

    loop(NB, ffn_in, pass_turns(NB))
    pass_turn()
    g3(FOUT)

    def ffn_out(i):
        rows = rows_of(i, T)
        r.osend[rows] = (r.y3[rows] + mm(r.hid[rows], r.w[FOUT][...])).astype(BF16)

    loop(1, ffn_out)
    pass_turn()
    tokens_out(r.osend, r.o_out, 2)
    for w in range(WEIGHTS):
        gather_sent(w)
    for j in range(HEADS // 2):
        pair_bytes(j, r.s_ks).wait()

    tokens_in_done(r.cot, 1)

    def ffn_back(i):
        rows = rows_of(i, T)
        f4 = r.cot[rows]
        for k in range(FF // CH):
            cols = slice(k * CH, (k + 1) * CH)
            up = mm_t(f4, r.w[FOUT][cols])
            r.dg[rows, cols] = (up * r.dg[rows, cols].astype(F32)).astype(BF16)
        e = mm_t(r.dg[rows], r.w[FIN][...])
        r.gs[rows] = f4.astype(F32) + ln_back(3, e, r.y3[rows])

    loop(1, ffn_back)
    GC = 1024

    def grad_outer(k):
        cols = rows_of(k, GC)
        r.w[FOUT][cols] = mm_tn(r.hid[0:T, cols], r.cot[...]).astype(BF16)

    loop(FF // GC, grad_outer)
    reduce_start(U_FOUT)
    turn()
    r.tr[...] = r.a5[...].T

    def grad_inner(k):
        cols = rows_of(k, GC)
        r.w[FIN][:, cols] = mm(r.tr[...], r.dg[:, cols]).astype(BF16)

    loop(FF // GC, grad_inner)
    reduce_start(U_FIN)
    turn()

    def out_back(i):
        rows = rows_of(i, T)
        f3 = r.gs[rows].astype(BF16)
        r.a5[rows] = f3
        r.hid[rows, 3 * D : 4 * D] = mm_t(f3, r.w[OUT][...]).astype(BF16)

    loop(1, out_back)
    r.w[OUT][...] = mm_tn(r.ctx[...], r.a5[...]).astype(BF16)
    reduce_start(U_OUT)
    turn()
    r.tr[...] = r.a4[...].T

    QB = 256

    def with_terms(extra, v):
        high = v.astype(BF16).astype(F32)
        mid = (v - high).astype(BF16).astype(F32)
        low = v - high - mid
        terms = jnp.where(lane == 4, high, jnp.where(lane == 5, mid, jnp.where(lane == 6, low, 0.0)))
        return extra - terms.astype(BF16)

    halfway = []

    def attend_back(j):
        cols, vcols = pair_cols(j), pair_cols(j, D)
        k2 = r.kvb[:, cols]
        keys = jnp.concatenate([k2, r.kenc[...]], axis=1)
        turned = [head_lanes(e, k2).T for e in range(2)]
        values = jnp.concatenate([r.kvb[:, vcols], r.kenc[...]], axis=1)
        for k in range(T // QB):
            rows = slice(k * QB, (k + 1) * QB)
            q2 = r.qb[rows, cols]
            d2 = r.hid[rows, pair_cols(j, 3 * D)]
            inner = d2.astype(F32) * r.ctx[rows, cols].astype(F32)
            dq = jnp.zeros((128, QB), F32)
            for e in range(2):
                qe, de = head_lanes(e, q2), head_lanes(e, d2)
                lse = jnp.sum(
                    jnp.where(lane == 2 * j + e, r.lse[rows], 0.0), axis=-1, keepdims=True
                )
                delta = jnp.sum(head_lanes(e, inner), axis=-1, keepdims=True)
                shifted = mm_t(keys, jnp.concatenate([qe, with_terms(r.qenc[rows], lse)], axis=1))
                probs = jnp.exp(shifted)
                none = jnp.zeros((QB, 128), BF16)
                moved = mm_t(values, jnp.concatenate([de, with_terms(none, delta)], axis=1))
                ds = (probs * moved).astype(BF16)
                dk = mm(ds, qe)
                dv = mm(probs.astype(BF16), de)
                for kk in range(2):
                    half = slice(kk * T, (kk + 1) * T)
                    at = 2 * D + kk * 128
                    if k == 0 and e == 0:
                        r.big[0:T, at : at + 128] = dk[half]
                        r.big[0:T, at + 256 : at + 384] = dv[half]
                    else:
                        r.big[0:T, at : at + 128] += dk[half]
                        r.big[0:T, at + 256 : at + 384] += dv[half]
                dq = dq + mm(turned[e], ds)
            r.hid[rows, cols] = (dq.T * scale).astype(BF16)
            if k == 0:
                for step, act in halfway:
                    pl.when(j == step)(lambda act=act: (act(), None)[1])

        def part(core, what):
            at = pl.multiple_of(2 * D + core * 128 + what * 256, 128)
            return r.big[0:T, pl.ds(at, 128)]

        @pl.when(j >= 2)
        def _():
            dkv_copy(j - 2).wait_send()

        for what in range(2):
            mine = pl.ds(pl.multiple_of(j * 256 + what * 128, 128), 128)
            r.big[0:T, mine] = part(c, what)
            r.cot[:, pl.ds(pl.multiple_of(lax.rem(j, 2) * 256 + what * 128, 128), 128)] = part(
                oc, what
            ).astype(BF16)
        dkv_copy(j).start()

        @pl.when(j == 2)
        def _():
            pairs_back(0)

    def dkv_copy(j):
        slot = lax.rem(j, 2)
        return remote(
            r.cot.at[:, pl.ds(pl.multiple_of(slot * 256, 128), 256)],
            r.dkvr.at[:, pl.ds(pl.multiple_of(j * 256, 128), 256)],
            r.s_js.at[j],
            r.s_jr.at[j],
            sibling,
        )

    def pairs_back(m):
        parts, weights = [], []
        for j in (2 * m, 2 * m + 1):
            dkv_copy(j).wait_recv()
            if m == 1:
                dkv_copy(j).wait_send()
            both = slice(j * 256, (j + 1) * 256)
            dkv = r.big[0:T, both] + r.dkvr[:, both].astype(F32)
            own = slice(j * 128, (j + 1) * 128)
            parts += [r.hid[0:T, own], dkv.astype(BF16)]
            for base in (0, D, 2 * D):
                weights.append(r.w[QKV][:, base + j * 128 : base + (j + 1) * 128])
        pairs = jnp.concatenate(parts, axis=1)
        share = mm_t(pairs, jnp.concatenate(weights, axis=1))
        if m == 0:
            r.big[0:T, 3 * D : 4 * D] = share
        else:
            r.big[0:T, 3 * D : 4 * D] += share
        r.dg[:, m * 768 : (m + 1) * 768] = mm(r.tr[...], pairs).astype(BF16)

    acts = []
    for k in range(HEADS // 2):
        halfway += [(k, act) for _, act in turns_of(1)]
        if k == 2:
            enlist(U_QKV0)
            acts.append((2, lambda: red0(U_QKV0)))
        acts += [(k, act) for _, act in turns_of(1)]
    loop(HEADS // 2, attend_back, acts)
    pairs_back(1)
    reduce_start(U_QKV1)
    turn()

    def qkv_back(i):
        rows = rows_of(i)
        r.gs[rows] += ln_back(2, r.big[rows, 3 * D : 4 * D], r.y2[rows])

    loop(NB, qkv_back)

    def point_back(i):
        rows = rows_of(i, T)
        f2 = r.gs[rows].astype(BF16)
        r.a4[rows] = f2
        for k in range(FF // CH):
            cols = slice(k * CH, (k + 1) * CH)
            d = mm_t(f2, r.w[POINT][cols])
            r.hid[rows_of(i, T, 16), cols] = d.astype(BF16)

    loop(1, point_back)
    edge_send(2, r.hid[T : T + 16], r.hid[16:32])
    turn()

    def grad_point(k):
        cols = rows_of(k, GC)
        r.w[POINT][cols] = mm_tn(r.sep[:, cols], r.a4[...]).astype(BF16)

    loop(FF // GC, grad_point)
    reduce_start(U_POINT0, U_POINT1)
    turn()
    r.hid[0:16], r.hid[T + 16 : T + 32] = edge_take(2)

    def depth_back(j):
        cols = pl.ds(pl.multiple_of(j * 256, 256), 256)
        gain, shift = r.midp[0:1, cols], r.midp[1:2, cols]
        sums = [jnp.zeros((8, 256), F32) for _ in range(9)]
        for b in range(T // MB):
            lo = b * MB
            taps = mm(r.ms[b], r.hid[window(b) : window(b) + MW, cols])
            a3 = r.nm[lo : lo + MB, cols].astype(F32) * gain + shift
            total = jnp.zeros((MB, 256), F32)
            here = r.hid[16 + lo : 16 + lo + MB, cols].astype(F32)
            for o in range(-4, 5):
                i = TAPS.index(-o) if o else 0
                moved = taps[i * MB : (i + 1) * MB] if o else here
                total = total + moved * r.midp[6 + o : 7 + o, cols]
                part = moved * a3
                for g in range(MB // 8):
                    sums[o + 4] = sums[o + 4] + part[g * 8 : (g + 1) * 8]
            r.big[lo + 8 : lo + 8 + MB, cols] = total
        for o in range(9):
            r.g8[2 + o : 3 + o, cols] = jnp.sum(sums[o], axis=0, keepdims=True)

    loop(FF // 256, depth_back, turns_of(FF // 256))

    def mid_back(i):
        rows, erows = rows_of(i, RM), rows_of(i, RM, 8)
        e = r.big[erows]
        unit = r.nm[rows].astype(F32)
        eg = e * r.midp[0:1]
        m1 = jnp.mean(eg, axis=-1, keepdims=True)
        m2 = jnp.mean(eg * unit, axis=-1, keepdims=True)
        r.g8[0:1] += jnp.sum(e * unit, axis=0, keepdims=True)
        r.g8[1:2] += jnp.sum(e, axis=0, keepdims=True)
        dmid = r.rm[rows] * (eg - m1 - unit * m2)
        r.dgl[rows] = (dmid * r.dgl[rows].astype(F32)).astype(BF16)
        right = dmid[:, 0:H] * r.dgr[rows].astype(F32)
        r.pext[0, erows] = right.astype(BF16).astype(F32)

    loop(T // RM, mid_back, turns_of(T // RM))
    edge_send(3, r.pext[0, T : T + 8], r.pext[0, 8:16])
    r.tr[...] = r.a2[...].T

    def grad_left(k):
        cols = rows_of(k, GC)
        r.sep[:, cols] = mm(r.tr[...], r.dgl[:, cols]).astype(BF16)

    half = FF // GC // 2
    lax.fori_loop(0, half, lambda k, _: (grad_left(k), 0)[1], 0)
    reduce_start(U_LEFT0)
    turn()
    lax.fori_loop(half, 2 * half, lambda k, _: (grad_left(k), 0)[1], 0)
    reduce_start(U_LEFT1)
    turn()
    top, bottom = edge_take(3)
    r.pext[0, 0:8] = top
    r.pext[0, T + 8 : T + 16] = bottom
    for k in range(T // 128):
        lo = k * 128
        for o in (-1, 0, 1):
            moved = r.pext[0, lo + 8 - o : lo + 136 - o]
            if o:
                moved = moved * jnp.concatenate([mask(-o, lo, 128)] * (H // 128), axis=1)
            r.hid[lo : lo + 128, (o + 1) * H : (o + 2) * H] = moved.astype(BF16)
    for o in range(3):
        cols = slice(o * H, (o + 1) * H)
        r.dkvr[:, cols] = mm(r.tr[...], r.hid[0:T, cols]).astype(BF16)
    reduce_start(U_CONV)
    turn()

    def branch_back(i):
        rows = rows_of(i)
        e = mm_t(r.dgl[rows], r.w[LEFT][...])
        for o in range(3):
            e = e + mm_t(r.hid[rows, o * H : (o + 1) * H], r.w[CONV][o])
        r.gs[rows] += ln_back(1, e, r.y1[rows])

    loop(NB, branch_back, turns_of(NB))

    def gate_back(i):
        rows = rows_of(i)
        g = r.gs[rows]
        r.sg[rows, 0:D] = (g * r.sg[rows, 0:D].astype(F32)).astype(BF16)
        r.sg[rows, D : 2 * D] = (g * r.sg[rows, D : 2 * D].astype(F32)).astype(BF16)

    loop(NB, gate_back)
    r.tr[...] = r.a1[...].T

    def grad_glu(k):
        cols = rows_of(k, D)
        to = pl.ds(pl.multiple_of(k * D + 2 * D, D), D)
        r.hid[0:T, to] = mm(r.tr[...], r.sg[:, cols]).astype(BF16)

    grad_glu(0)
    reduce_start(U_GLU0)
    turn()
    grad_glu(1)
    reduce_start(U_GLU1)
    turn()

    def glu_back(i):
        rows = rows_of(i)
        e = mm_t(r.sg[rows], r.w[GLU][...])
        total = r.gs[rows] + ln_back(0, e, r.xin[rows].astype(F32))
        r.a5[rows] = total.astype(BF16)

    loop(NB, glu_back, turns_of(NB))
    r.gsm[0:16] = r.g8[:, 0 : FF // 2].astype(BF16)
    r.gsm[16:32] = r.g8[:, FF // 2 : FF].astype(BF16)
    reduce_start(SMALL)
    move(TAIL[0])
    tokens_out(r.a5, r.o_ig, 3)
    move(TAIL[1])
    while any(ahead.values()):
        move(range(UNITS))

    for u in range(UNITS):
        red_end(u)
    tokens_out_done(r.osend, r.o_out, 2)
    tokens_out_done(r.a5, r.o_ig, 3)
    tokens_in_sent(r.x, r.xin, 0)
    tokens_in_sent(r.ct, r.cot, 1)
    seg_sent()
    for t in range(1, n):
        small_copy(t).wait_send()


def local(
    inputs,
    segment_ids,
    cotangent,
    norm_gain,
    norm_bias,
    glu_weight,
    left_weight,
    conv_weight,
    mid_gain,
    mid_bias,
    depth_weight,
    point_weight,
    qkv_weight,
    out_weight,
    ffn_in,
    ffn_out,
):
    seqs, span, width = inputs.shape
    n = lax.axis_size("seq")
    plan = Plan(
        lax.axis_size("dp"), n, seqs, span, width, ffn_in.shape[1], conv_weight.shape[2]
    )
    q = lax.axis_index("seq")

    def placed(piece, repeats):
        if repeats == 1:
            return piece
        size = piece.shape[-1]
        tiled = jnp.tile(piece, (1,) * (piece.ndim - 1) + (repeats,))
        at = lax.broadcasted_iota(jnp.int32, tiled.shape, tiled.ndim - 1) // size
        return jnp.where(at == q % repeats, tiled, jnp.zeros_like(tiled))

    segs = placed(segment_ids, plan.sr)
    norms = placed(jnp.concatenate([norm_gain, norm_bias], 0), plan.nr)
    rows = plan.spack
    at = lax.broadcasted_iota(jnp.int32, (rows, plan.FFn), 0)
    small = jnp.pad(norms, ((0, rows - 8), (0, plan.FFn - plan.nw)))
    small = jnp.where(at == 8, mid_gain[None], jnp.where(at == 9, mid_bias[None], small))
    taps = jnp.pad(depth_weight, ((10, rows - 10 - depth_weight.shape[0]), (0, 0)))
    small = jnp.where(at >= 10, taps, small)
    weights = [None] * WEIGHTS
    weights[GLU], weights[CONV], weights[LEFT] = glu_weight, conv_weight, left_weight
    weights[POINT], weights[QKV], weights[OUT] = point_weight, qkv_weight, out_weight
    weights[FIN], weights[FOUT] = ffn_in, ffn_out

    shapes = []
    plan.buffers(shapes.append)
    out_shape = [jax.ShapeDtypeStruct(inputs.shape, BF16)] * 2
    out_shape += [jax.ShapeDtypeStruct(plan.piece(w, plan.kr(w)), BF16) for w in range(WEIGHTS)]
    out_shape += [jax.ShapeDtypeStruct((32, plan.FF // 2), BF16)]
    hbm = pl.BlockSpec(memory_space=pl.ANY)
    got = pl.pallas_call(
        lambda *refs: kernel(plan, *refs),
        out_shape=out_shape,
        in_specs=[hbm] * INPUTS,
        out_specs=[hbm] * OUTPUTS,
        scratch_shapes=shapes,
        compiler_params=pltpu.CompilerParams(
            collective_id=0, has_side_effects=True, vmem_limit_bytes=64 << 20
        ),
        name="cell",
    )(inputs, segs, cotangent, small, *weights)
    out = unpacked(plan, got)
    return (
        out[0],
        out[1],
        out[2 + WEIGHTS],
        out[3 + WEIGHTS],
        out[2 + GLU],
        out[2 + LEFT],
        out[2 + CONV],
        out[4 + WEIGHTS].reshape(-1),
        out[5 + WEIGHTS].reshape(-1),
        out[6 + WEIGHTS],
        out[2 + POINT],
        out[2 + QKV],
        out[2 + OUT],
        out[2 + FIN],
        out[2 + FOUT],
    )


def unpacked(plan, parts):
    count = 2 + WEIGHTS
    dn = plan.D // plan.n
    wide = [jax.ShapeDtypeStruct(p.shape, F32) for p in parts[:count]]
    conv, qkv, H = 2 + CONV, 2 + QKV, plan.HALF
    wide[conv] = jax.ShapeDtypeStruct((3, plan.kr(CONV), H), F32)
    tiny = [(4, dn), (4, dn), (1, plan.FFn), (1, plan.FFn), (9, plan.FFn)]
    out_shape = wide + [jax.ShapeDtypeStruct(shape, F32) for shape in tiny]

    def body(*refs):
        ins, outs = refs[:count], refs[count + 1 : 2 * count + 1]
        sums, tinies = refs[count], refs[2 * count + 1 : 2 * count + 6]
        near, far = refs[2 * count + 6 : 3 * count + 6], refs[3 * count + 6 : 4 * count + 6]
        came, went = refs[4 * count + 6], refs[4 * count + 7]

        def arrive(i):
            return pltpu.make_async_copy(ins[i], near[i], came.at[i])

        def leave(i):
            return pltpu.make_async_copy(far[i], outs[i], went.at[i])

        for i in range(count):
            arrive(i).start()
        q = lax.axis_index("seq")
        whole = jnp.concatenate([sums[0:16].astype(F32), sums[16:32].astype(F32)], axis=1)
        rolled = pltpu.roll(whole, (plan.FF - q * plan.FFn) % plan.FF, 1)[:, 0 : plan.FFn]
        tinies[2][...] = rolled[0:1]
        tinies[3][...] = rolled[1:2]
        tinies[4][...] = rolled[2:11]
        for k in range(2):
            row = whole[11 + k : 12 + k]
            rows = [row[:, i * plan.D : (i + 1) * plan.D] for i in range(4)]
            both = jnp.concatenate(rows + rows, axis=0)
            tinies[k][...] = pltpu.roll(both, (plan.D - q * dn) % plan.D, 1)[0:4, 0:dn]
        for i in range(count):
            arrive(i).wait()
            if i == conv:
                for k in range(3):
                    far[i][k] = near[i][:, k * H : (k + 1) * H].astype(F32)
            elif i == qkv:
                for k in range(12):
                    to = (k % 3) * plan.D + k // 3 * 128
                    far[i][:, to : to + 128] = near[i][:, k * 128 : (k + 1) * 128].astype(F32)
            else:
                far[i][...] = near[i][...].astype(F32)
            leave(i).start()
        for i in range(count):
            leave(i).wait()

    hbm = pl.BlockSpec(memory_space=pl.ANY)
    vmem = pl.BlockSpec(memory_space=pltpu.VMEM)
    return pl.pallas_call(
        body,
        out_shape=out_shape,
        in_specs=[hbm] * count + [vmem],
        out_specs=[hbm] * count + [vmem] * len(tiny),
        scratch_shapes=[pltpu.VMEM(p.shape, BF16) for p in parts[:count]]
        + [pltpu.VMEM(shape.shape, F32) for shape in wide]
        + [pltpu.SemaphoreType.DMA((count,))] * 2,
        compiler_params=pltpu.CompilerParams(vmem_limit_bytes=64 << 20),
    )(*parts)


def solution(mesh):
    in_specs = (
        P("dp", "seq", None),
        P("dp", "seq"),
        P("dp", "seq", None),
        P(None, "seq"),
        P(None, "seq"),
        P("seq", None),
        P("seq", None),
        P(None, "seq", None),
        P("seq"),
        P("seq"),
        P(None, "seq"),
        P("seq", None),
        P("seq", None),
        P("seq", None),
        P("seq", None),
        P("seq", None),
    )
    out_specs = (
        P("dp", "seq", None),
        P("dp", "seq", None),
        P(None, "seq"),
        P(None, "seq"),
        P("seq", None),
        P("seq", None),
        P(None, "seq", None),
        P("seq"),
        P("seq"),
        P(None, "seq"),
        P("seq", None),
        P("seq", None),
        P("seq", None),
        P("seq", None),
        P("seq", None),
    )
    return jax.shard_map(local, mesh=mesh, in_specs=in_specs, out_specs=out_specs, check_vma=False)
```
